32 devices in a mesh: dp: 16 (over z, y, core), ctx: 2 (over x).
Axes of the slice: x: 2, y: 2, z: 4, core: 2. Of those that a mesh axis runs over, the one named last changes fastest.
Arguments:
- tokens: bfloat16 [16, 1024, 768], P('dp', 'ctx'), may hold values from -6 to 6
- w_query: bfloat16 [768, 768], P('dp'), may hold values from -0.21875 to 0.21875
- w_key: bfloat16 [768, 768], P('dp'), may hold values from -0.21875 to 0.21875
- w_value: bfloat16 [768, 768], P('dp'), may hold values from -0.21875 to 0.21875
- w_out: bfloat16 [768, 768], P('dp')
- w_up: bfloat16 [768, 3072], P('dp'), may hold values from -0.21875 to 0.21875
- w_down: bfloat16 [3072, 768], P('dp'), may hold values from -0.109375 to 0.109375
- gain_attn: bfloat16 [768], P('dp'), may hold values from 0.5 to 1.5
- gain_ffn: bfloat16 [768], P('dp'), may hold values from 0.5 to 1.5
- teacher: bfloat16 [16, 1024, 768], P('dp', 'ctx'), may hold values from -6 to 6
- seq_lengths: int32 [16], P('dp'), may hold values from 1 to 1024, 10240 in all
- tok_perm: int32 [16, 1024], P('dp'), may hold values from 0 to 1023, as said below
- valid_count: int32 [1], replicated, may hold values from 512 to 16384
Outputs:
- activations: bfloat16 [16, 1024, 768], P('dp', 'ctx')
- loss: float32 [1], replicated
- token_grad: float32 [16, 1024, 768], P('dp', 'ctx')
- w_query_grad: float32 [768, 768], P('dp')
- w_key_grad: float32 [768, 768], P('dp')
- w_value_grad: float32 [768, 768], P('dp')
- w_out_grad: float32 [768, 768], P('dp')
- w_up_grad: float32 [768, 3072], P('dp')
- w_down_grad: float32 [3072, 768], P('dp')
- gain_attn_grad: float32 [768], P('dp')
- gain_ffn_grad: float32 [768], P('dp')
The draws below stay inside these ranges and needn't reach their ends.
Inputs may be any that keep to these rules, and one draw needn't show every extreme that they name: `tok_perm`: each row is a permutation of 0 to 1023. With G = 2 and B = 512 // G, dealt row c * 512 + t * B + j (0 <= j < B) holds a position from t * 512 to (t + 1) * 512 - 1. `seq_lengths`: the longest sequence has exactly 1024 valid tokens; all together have 5 * 1024 * 2.
All inputs are finite; a program needn't handle non-finite values. No bound on the sum of `seq_lengths` on one device may be relied on, other than what follows from the above.
Results may differ from the reference program's by a relative error of at most 0.023.
Values may be sent and summed in bfloat16 or wider, within the bound.
A program may use at most 192 MiB of HBM per device.

```python
import math
import jax
import jax.numpy as jnp
import numpy as np
from jax import lax

HEADS = 12
HEAD_DIM = 64
FF = 3072
D = 768
SPAN = 512
SEQ_LEN = 1024
SEQS = 16
TOKENS = 16384


def draw_w_out(key, part):
    spread = (0.22 * SEQ_LEN / D) ** 0.5
    values = jax.random.normal(key, (D, D), jnp.float32) * spread
    return values.astype(jnp.bfloat16)


def draw_tok_perm(key, part):
    groups = SEQ_LEN // SPAN
    per_peer = SPAN // groups
    ranks_base = jnp.broadcast_to(jnp.arange(SPAN, dtype=jnp.int32), (SEQS, groups, SPAN))
    shuffled = jax.random.permutation(key, ranks_base, axis=2, independent=True)
    blocks = shuffled.reshape(SEQS, groups, groups, per_peer)
    anchor = blocks + (jnp.arange(groups, dtype=jnp.int32) * SPAN)[None, :, None, None]
    return jnp.transpose(anchor, (0, 2, 1, 3)).reshape(SEQS, SEQ_LEN).astype(jnp.int32)


def levels(key, extent, split, least, largest):
    def one(axis_at, blocks):
        steps = jax.random.uniform(jax.random.fold_in(jax.random.fold_in(key, 6), axis_at), (blocks,), jnp.float32, least / len(split), largest / len(split))
        return jnp.repeat(jnp.exp(steps), extent[axis_at] // blocks).reshape((-1,) + (1,) * (len(extent) - axis_at - 1))

    level = one(*split[0])
    for cut in split[1:]:
        level = level * one(*cut)
    return level


def split_up(amount, total, limit, skew):
    weights = [(1 << 20) // math.isqrt(standing ** skew) + 1 for standing in range(2, amount + 1)]
    spare, counts = total - limit - (amount - 1), [1] * (amount - 1)
    while spare > 0:
        free = [i for i in range(amount - 1) if counts[i] < limit]
        pool, left = sum([weights[i] for i in free]), spare
        for i in free:
            addition = min(limit - counts[i], max(1, left * weights[i] // pool), spare)
            counts[i] = counts[i] + addition
            spare = spare - addition
    return np.array([limit] + counts)


def uneven_parts(own_key, count, total, bound, lean):
    if count == 2:
        one = jax.random.randint(own_key, (), max(1, total - bound), min(bound, total - 1) + 1)
        return jnp.stack([one, total - one])
    lengths = jnp.asarray(split_up(count, total, bound, lean), jnp.int32)
    pairs = (count - 1) // 2
    source_of, sink = lengths[1:1 + 2 * pairs:2], lengths[2:2 + 2 * pairs:2]
    room = jnp.minimum(source_of - 1, bound - sink)
    passed = jax.random.randint(jax.random.fold_in(own_key, 1), (pairs,), 0, 1 << 20) % (room + 1)
    lengths = lengths.at[1:1 + 2 * pairs:2].set(source_of - passed).at[2:2 + 2 * pairs:2].set(sink + passed)
    return lengths[jax.random.permutation(jax.random.fold_in(own_key, 2), count)]


def scatter_about(key, dims, deviation, most, pieces=(), kind=jnp.bfloat16):
    drawn = jax.random.normal(key, dims, jnp.float32) * deviation
    if len(pieces) > 0:
        drawn = levels(key, dims, pieces, -0.22, 0.18) * drawn
    return jnp.clip(drawn, min=-most, max=most).astype(kind)


def setup_inputs(seed: int = 0) -> dict:
    seeds = jax.random.split(jax.random.key(seed), 14)
    return {
        "tokens": scatter_about(seeds[0], (SEQS, SEQ_LEN, D), 1.0, 6.0, ((0, 16), (1, 2))),
        "w_query": scatter_about(seeds[1], (D, D), D ** -0.5, 0.21875, ((0, 16),)),
        "w_key": scatter_about(seeds[2], (D, D), D ** -0.5, 0.21875, ((0, 16),)),
        "w_value": scatter_about(seeds[3], (D, D), D ** -0.5, 0.21875, ((0, 16),)),
        "w_out": draw_w_out(jax.random.fold_in(seeds[13], 71), 0),
        "w_up": scatter_about(seeds[5], (D, FF), D ** -0.5, 0.21875, ((0, 16),)),
        "w_down": scatter_about(seeds[6], (FF, D), FF ** -0.5, 0.109375, ((0, 16),)),
        "gain_attn": jnp.clip(1.0 + 0.1 * jax.random.normal(seeds[7], (D,), jnp.float32), 0.5, 1.5).astype(jnp.bfloat16),
        "gain_ffn": jnp.clip(1.0 + 0.1 * jax.random.normal(seeds[8], (D,), jnp.float32), 0.5, 1.5).astype(jnp.bfloat16),
        "teacher": scatter_about(seeds[9], (SEQS, SEQ_LEN, D), 1.0, 6.0, ((0, 16), (1, 2))),
        "seq_lengths": uneven_parts(seeds[10], SEQS, 5 * SEQ_LEN * SEQS // 8, SEQ_LEN, 2).astype(jnp.int32),
        "tok_perm": draw_tok_perm(jax.random.fold_in(seeds[13], 71), 0),
        "valid_count": jax.random.randint(seeds[12], (1,), TOKENS // 32, TOKENS + 1).astype(jnp.int32),
    }


EPSILON = 1e-06
SCORE_SCALE = 0.125
MASKED = -1e+30

@jax.custom_vjp
def low(v):
    return lax.optimization_barrier(v.astype(jnp.bfloat16)).astype(jnp.float32)

@jax.custom_vjp
def low_back(v):
    return v

def low_keep(v):
    return (low(v), None)

def low_pass(kept, grad):
    return (grad,)

def back_keep(v):
    return (v, None)

def back_low(kept, grad):
    return (low(grad),)
low.defvjp(low_keep, low_pass)
low_back.defvjp(back_keep, back_low)

def matmul(left_mat, right_mat):
    return jnp.dot(left_mat, right_mat, precision=lax.Precision.HIGHEST, preferred_element_type=jnp.float32)

def gelu_exact(values):
    return 0.5 * values * (1.0 + lax.erf(values * 0.7071067811865476))

def norm_rows(hidden, gain_row):
    center = hidden - lax.optimization_barrier(jnp.mean(hidden, axis=-1, keepdims=True))
    spread = lax.optimization_barrier(jnp.mean(center * center, axis=-1, keepdims=True))
    return center * lax.rsqrt(spread + EPSILON) * gain_row

def attend(queries, keys, values, counted):
    keys_heads = keys.reshape(SEQ_LEN, HEADS, HEAD_DIM)
    values_heads = values.reshape(SEQ_LEN, HEADS, HEAD_DIM)

    def one_block(query_block):
        query_heads = query_block.reshape(SPAN, HEADS, HEAD_DIM)
        scores = jnp.einsum('qhe,khe->hqk', query_heads, keys_heads, precision=lax.Precision.HIGHEST) * SCORE_SCALE
        scores = low_back(scores)
        scores = jnp.where(counted[None, None, :], scores, MASKED)
        row_max = lax.optimization_barrier(jnp.max(scores, axis=-1, keepdims=True))
        exps_row = jnp.exp(scores - row_max)
        soft_weights = low(exps_row / lax.optimization_barrier(jnp.sum(exps_row, axis=-1, keepdims=True)))
        mixed_out = jnp.einsum('hqk,khe->qhe', soft_weights, values_heads, precision=lax.Precision.HIGHEST)
        return mixed_out.reshape(SPAN, HEADS * HEAD_DIM)
    blocks = lax.map(jax.checkpoint(one_block), queries.reshape(SEQ_LEN // SPAN, SPAN, HEADS * HEAD_DIM))
    return blocks.reshape(SEQ_LEN, HEADS * HEAD_DIM)

def one_sequence(params, tokens_seq, target_seq, length, dealt_order):
    query_w, key_w, value_w, out_w, up_w, down_w, gain_first, gain_second = params
    counted = dealt_order < length
    queries = low(low_back(matmul(tokens_seq, query_w)))
    keys = low(low_back(matmul(tokens_seq, key_w)))
    values = low(low_back(matmul(tokens_seq, value_w)))
    mixed_out = low(low_back(attend(queries, keys, values, counted)))
    branch = low_back(matmul(mixed_out, out_w))
    normed = norm_rows(tokens_seq + branch, gain_first)
    upward = low_back(matmul(low(normed), up_w))
    active = low(gelu_exact(upward))
    down_out = low_back(matmul(active, down_w))
    result = low(low_back(norm_rows(normed + down_out, gain_second)))
    ordered = jnp.zeros_like(result).at[dealt_order].set(result)
    live_rows = (jnp.arange(SEQ_LEN, dtype=jnp.int32) < length)[:, None]
    difference = ordered - target_seq
    square_sum = jnp.sum(jnp.where(live_rows, difference * difference, 0.0))
    return (ordered, square_sum)

def reference(tokens, w_query, w_key, w_value, w_out, w_up, w_down, gain_attn, gain_ffn, teacher, seq_lengths, tok_perm, valid_count):
    params = tuple((weight.astype(jnp.float32) for weight in (w_query, w_key, w_value, w_out, w_up, w_down, gain_attn, gain_ffn)))
    inputs = tokens.astype(jnp.float32)
    targets = teacher.astype(jnp.float32)
    valid_total = valid_count[0].astype(jnp.float32)

    def objective(weights, layer_in):

        def per_seq(running, seq_item):
            tokens_seq, target_seq, length, dealt_order = seq_item
            ordered, square_sum = one_sequence(weights, tokens_seq, target_seq, length, dealt_order)
            return (running + square_sum, ordered)
        square_total, ordered = lax.scan(per_seq, jnp.zeros((), jnp.float32), (layer_in, targets, seq_lengths, tok_perm))
        loss_value = square_total / (2.0 * D * valid_total)
        return (square_total * (0.5 * TOKENS) / valid_total, (loss_value, ordered))
    scaled, pullback, extras = jax.vjp(objective, params, inputs, has_aux=True)
    weight_grads, input_grad = pullback(jnp.ones_like(scaled))
    loss_value, ordered = extras
    return (ordered.astype(jnp.bfloat16), loss_value.reshape(1), input_grad, weight_grads[0], weight_grads[1], weight_grads[2], weight_grads[3], weight_grads[4], weight_grads[5], weight_grads[6], weight_grads[7])
```

```python
import functools
import math

import jax
import jax.numpy as jnp
from jax import lax
from jax.experimental import pallas as pl
from jax.experimental.pallas import tpu as pltpu
from jax.sharding import PartitionSpec as P

HEAD_DIM = 64


EPSILON = 1e-06
SCORE_SCALE = 0.125
MASKED = -1e30
MESH = pl.DeviceIdType.MESH
MIB = 1024 * 1024


def gelu_exact(values):
    return 0.5 * values * (1.0 + lax.erf(values * 0.7071067811865476))


def norm_forward(hidden, gain_row):
    center = hidden - jnp.mean(hidden, axis=-1, keepdims=True)
    inverse = lax.rsqrt(jnp.mean(center * center, axis=-1, keepdims=True) + EPSILON)
    normal = center * inverse
    return (normal * gain_row, normal, inverse)


def norm_backward(grad_norm, gain_row, normal, inverse):
    scaled = grad_norm * gain_row
    grad_input = inverse * (
        scaled
        - jnp.mean(scaled, axis=-1, keepdims=True)
        - normal * jnp.mean(scaled * normal, axis=-1, keepdims=True)
    )
    return (grad_input, jnp.sum(grad_norm * normal, axis=0))


def row_product(left_mat, right_mat):
    return lax.dot_general(
        left_mat, right_mat, (((0,), (0,)), ((), ())), preferred_element_type=jnp.float32
    )


def by_transpose(left_mat, right_mat):
    return lax.dot_general(
        left_mat, right_mat, (((1,), (1,)), ((), ())), preferred_element_type=jnp.float32
    )


def shards(
    tokens,
    w_query,
    w_key,
    w_value,
    w_out,
    w_up,
    w_down,
    gain_attn,
    gain_ffn,
    teacher,
    seq_lengths,
    tok_perm,
    valid_count,
):
    ctx_count = lax.axis_size("ctx")
    ctx_rank = lax.axis_index("ctx")
    dp_count = lax.axis_size("dp")
    layer_in = tokens[0]
    span_rows, model_width = layer_in.shape
    head_count = model_width // HEAD_DIM
    dealt_order = tok_perm[0]
    seq_len = dealt_order.shape[0]
    length = seq_lengths[0]
    keep_all = dealt_order < length
    per_peer = span_rows // ctx_count
    query_weight, key_weight, value_weight, out_weight, gain_first = (
        lax.all_gather(w_query, "dp", axis=0, tiled=True),
        lax.all_gather(w_key, "dp", axis=0, tiled=True),
        lax.all_gather(w_value, "dp", axis=0, tiled=True),
        lax.all_gather(w_out, "dp", axis=0, tiled=True),
        lax.all_gather(gain_attn, "dp", axis=0, tiled=True),
    )
    up_weight, down_weight, gain_second = (
        lax.all_gather(w_up, "dp", axis=0, tiled=True),
        lax.all_gather(w_down, "dp", axis=0, tiled=True),
        lax.all_gather(gain_ffn, "dp", axis=0, tiled=True),
    )
    queries = jnp.dot(layer_in, query_weight, preferred_element_type=jnp.float32).astype(
        jnp.bfloat16
    )
    keys_own = jnp.dot(layer_in, key_weight, preferred_element_type=jnp.float32).astype(
        jnp.bfloat16
    )
    values_own = jnp.dot(layer_in, value_weight, preferred_element_type=jnp.float32).astype(
        jnp.bfloat16
    )
    query_heads = queries.reshape(span_rows, head_count, HEAD_DIM)
    initial = (
        jnp.full((head_count, span_rows), MASKED, jnp.float32),
        jnp.zeros((head_count, span_rows), jnp.float32),
        jnp.zeros((head_count, span_rows, HEAD_DIM), jnp.float32),
    )
    fold_state = initial
    key_piece = lax.all_gather(keys_own, "ctx", axis=0, tiled=True)
    value_piece = lax.all_gather(values_own, "ctx", axis=0, tiled=True)
    piece_rows = key_piece.shape[0]
    block_rows = math.gcd(piece_rows, span_rows)
    key_blocks = key_piece.reshape(piece_rows // block_rows, block_rows, head_count, HEAD_DIM)
    value_blocks = value_piece.reshape(piece_rows // block_rows, block_rows, head_count, HEAD_DIM)

    def step_block(block_state, block_item):
        running_max, running_sum, accumulated = block_state
        key_block, value_block, block_index = block_item
        key_keep = lax.dynamic_slice_in_dim(keep_all, block_index * block_rows, block_rows)
        scores = (
            jnp.einsum("qhe,khe->hqk", query_heads, key_block, preferred_element_type=jnp.float32)
            * SCORE_SCALE
        )
        scores = jnp.where(key_keep[None, None, :], scores, MASKED)
        new_max = jnp.maximum(running_max, jnp.max(scores, axis=-1))
        factor = jnp.exp(running_max - new_max)
        soft_weights = jnp.where(key_keep[None, None, :], jnp.exp(scores - new_max[..., None]), 0.0)
        running_sum = running_sum * factor + jnp.sum(soft_weights, axis=-1)
        accumulated = accumulated * factor[..., None] + jnp.einsum(
            "hqk,khe->hqe",
            soft_weights.astype(jnp.bfloat16),
            value_block,
            preferred_element_type=jnp.float32,
        )
        return ((new_max, running_sum, accumulated), None)

    block_indices = jnp.arange(piece_rows // block_rows, dtype=jnp.int32)
    fold_state, unused = lax.scan(step_block, fold_state, (key_blocks, value_blocks, block_indices))
    run_max, run_sum, accumulated = fold_state
    log_total = run_max + jnp.log(run_sum)
    attn_full = jnp.transpose(accumulated / run_sum[..., None], (1, 0, 2)).reshape(
        span_rows, model_width
    )
    attn_low = attn_full.astype(jnp.bfloat16)
    gain_first32 = gain_first.astype(jnp.float32)
    gain_second32 = gain_second.astype(jnp.float32)
    branch = jnp.dot(attn_low, out_weight, preferred_element_type=jnp.float32)
    normed, normal_first, inverse_first = norm_forward(
        layer_in.astype(jnp.float32) + branch, gain_first32
    )
    normed_low = normed.astype(jnp.bfloat16)
    upward = jnp.dot(normed_low, up_weight, preferred_element_type=jnp.float32)
    active, gelu_pull = jax.vjp(gelu_exact, upward)
    active_low = active.astype(jnp.bfloat16)
    down_out = jnp.dot(active_low, down_weight, preferred_element_type=jnp.float32)
    result, normal_second, inverse_second = norm_forward(normed + down_out, gain_second32)
    result_low = result.astype(jnp.bfloat16)
    arrived = lax.all_to_all(result_low, "ctx", split_axis=0, concat_axis=0, tiled=True)
    sources = (
        jnp.arange(ctx_count, dtype=jnp.int32)[:, None] * span_rows
        + ctx_rank * per_peer
        + jnp.arange(per_peer, dtype=jnp.int32)[None, :]
    ).reshape(span_rows)
    local_pos = jnp.take(dealt_order, sources) - ctx_rank * span_rows
    in_order = jnp.zeros_like(arrived).at[local_pos].set(arrived)
    target = teacher[0].astype(jnp.float32)
    live_rows = (ctx_rank * span_rows + jnp.arange(span_rows, dtype=jnp.int32) < length)[:, None]
    residual_err = jnp.where(live_rows, in_order.astype(jnp.float32) - target, 0.0)
    total_sq = lax.psum(jnp.sum(residual_err * residual_err), ("dp", "ctx"))
    valid_total = valid_count[0].astype(jnp.float32)
    loss_value = (total_sq / (2.0 * model_width * valid_total)).reshape(1)
    grad_scale = seq_len * dp_count / valid_total
    grad_order = (residual_err * grad_scale).astype(jnp.bfloat16)
    outgoing = jnp.take(grad_order, local_pos, axis=0)
    grad_result = lax.all_to_all(outgoing, "ctx", split_axis=0, concat_axis=0, tiled=True).astype(
        jnp.float32
    )
    grad_sum_second, grad_gain_second = norm_backward(
        grad_result, gain_second32, normal_second, inverse_second
    )
    down_grad_low = grad_sum_second.astype(jnp.bfloat16)
    grad_down_w = row_product(active_low, down_grad_low)
    grad_active = by_transpose(down_grad_low, down_weight)
    grad_upward = gelu_pull(grad_active)[0].astype(jnp.bfloat16)
    grad_up_w = row_product(normed_low, grad_upward)
    grad_normed = grad_sum_second + by_transpose(grad_upward, up_weight)
    grad_hidden, grad_gain_first = norm_backward(
        grad_normed, gain_first32, normal_first, inverse_first
    )
    branch_grad = grad_hidden.astype(jnp.bfloat16)
    grad_out_w = row_product(attn_low, branch_grad)
    attn_grad_low = by_transpose(branch_grad, out_weight).astype(jnp.bfloat16)
    grad_heads = attn_grad_low.reshape(span_rows, head_count, HEAD_DIM)
    row_delta = jnp.sum(
        (attn_grad_low.astype(jnp.float32) * attn_full).reshape(span_rows, head_count, HEAD_DIM),
        axis=-1,
    ).T
    keys_all, values_all = (
        lax.all_gather(keys_own, "ctx", axis=0, tiled=True),
        lax.all_gather(values_own, "ctx", axis=0, tiled=True),
    )
    blocks_count = seq_len // span_rows
    key_stack = keys_all.reshape(blocks_count, span_rows, head_count, HEAD_DIM)
    value_stack = values_all.reshape(blocks_count, span_rows, head_count, HEAD_DIM)

    def score_terms(
        query_block, grad_block, total_block, delta_block, key_block, value_block, key_keep
    ):
        scores = (
            jnp.einsum("qhe,khe->hqk", query_block, key_block, preferred_element_type=jnp.float32)
            * SCORE_SCALE
        )
        soft_weights = jnp.where(
            key_keep[None, None, :], jnp.exp(scores - total_block[..., None]), 0.0
        )
        prob_grad = jnp.einsum(
            "qhe,khe->hqk", grad_block, value_block, preferred_element_type=jnp.float32
        )
        score_grad = (soft_weights * (prob_grad - delta_block[..., None])).astype(jnp.bfloat16)
        return (soft_weights, score_grad)

    def back_block(query_grad, block_item):
        key_block, value_block, block_index = block_item
        key_keep = lax.dynamic_slice_in_dim(keep_all, block_index * span_rows, span_rows)
        soft_weights, score_grad = score_terms(
            query_heads, grad_heads, log_total, row_delta, key_block, value_block, key_keep
        )
        value_grad = jnp.einsum(
            "hqk,qhe->khe",
            soft_weights.astype(jnp.bfloat16),
            grad_heads,
            preferred_element_type=jnp.float32,
        )
        query_grad = query_grad + SCORE_SCALE * jnp.einsum(
            "hqk,khe->qhe", score_grad, key_block, preferred_element_type=jnp.float32
        )
        key_grad = SCORE_SCALE * jnp.einsum(
            "hqk,qhe->khe", score_grad, query_heads, preferred_element_type=jnp.float32
        )
        return (query_grad, (key_grad, value_grad))

    query_grad, (key_grads, value_grads) = lax.scan(
        back_block,
        jnp.zeros((span_rows, head_count, HEAD_DIM), jnp.float32),
        (key_stack, value_stack, jnp.arange(blocks_count, dtype=jnp.int32)),
    )
    key_grad_sum, value_grad_sum = (
        lax.psum_scatter(
            key_grads.reshape(seq_len, model_width).astype(jnp.bfloat16),
            "ctx",
            scatter_dimension=0,
            tiled=True,
        ).astype(jnp.float32),
        lax.psum_scatter(
            value_grads.reshape(seq_len, model_width).astype(jnp.bfloat16),
            "ctx",
            scatter_dimension=0,
            tiled=True,
        ).astype(jnp.float32),
    )
    query_grad_low = query_grad.reshape(span_rows, model_width).astype(jnp.bfloat16)
    key_grad_low = key_grad_sum.astype(jnp.bfloat16)
    value_grad_low = value_grad_sum.astype(jnp.bfloat16)
    grad_query_w = row_product(layer_in, query_grad_low)
    grad_key_w = row_product(layer_in, key_grad_low)
    grad_value_w = row_product(layer_in, value_grad_low)
    token_grad = (
        grad_hidden
        + by_transpose(query_grad_low, query_weight)
        + by_transpose(key_grad_low, key_weight)
        + by_transpose(value_grad_low, value_weight)
    )
    up_part, down_part, second_part = (
        lax.psum_scatter(
            grad_up_w.astype(jnp.bfloat16), "dp", scatter_dimension=0, tiled=True
        ).astype(jnp.float32),
        lax.psum_scatter(
            grad_down_w.astype(jnp.bfloat16), "dp", scatter_dimension=0, tiled=True
        ).astype(jnp.float32),
        lax.psum_scatter(
            grad_gain_second.astype(jnp.bfloat16), "dp", scatter_dimension=0, tiled=True
        ).astype(jnp.float32),
    )
    query_part, key_part, value_part, out_part, first_part = (
        lax.psum_scatter(
            grad_query_w.astype(jnp.bfloat16), "dp", scatter_dimension=0, tiled=True
        ).astype(jnp.float32),
        lax.psum_scatter(
            grad_key_w.astype(jnp.bfloat16), "dp", scatter_dimension=0, tiled=True
        ).astype(jnp.float32),
        lax.psum_scatter(
            grad_value_w.astype(jnp.bfloat16), "dp", scatter_dimension=0, tiled=True
        ).astype(jnp.float32),
        lax.psum_scatter(
            grad_out_w.astype(jnp.bfloat16), "dp", scatter_dimension=0, tiled=True
        ).astype(jnp.float32),
        lax.psum_scatter(
            grad_gain_first.astype(jnp.bfloat16), "dp", scatter_dimension=0, tiled=True
        ).astype(jnp.float32),
    )
    summed = (
        lax.psum(query_part.astype(jnp.bfloat16), "ctx").astype(jnp.float32),
        lax.psum(key_part.astype(jnp.bfloat16), "ctx").astype(jnp.float32),
        lax.psum(value_part.astype(jnp.bfloat16), "ctx").astype(jnp.float32),
        lax.psum(out_part.astype(jnp.bfloat16), "ctx").astype(jnp.float32),
        lax.psum(up_part.astype(jnp.bfloat16), "ctx").astype(jnp.float32),
        lax.psum(down_part.astype(jnp.bfloat16), "ctx").astype(jnp.float32),
        lax.psum(first_part.astype(jnp.bfloat16), "ctx").astype(jnp.float32),
        lax.psum(second_part.astype(jnp.bfloat16), "ctx").astype(jnp.float32),
    )
    query_sum, key_sum, value_sum, out_sum, up_sum, down_sum, first_sum, second_sum = summed
    return (
        in_order[None],
        loss_value,
        token_grad[None],
        query_sum,
        key_sum,
        value_sum,
        out_sum,
        up_sum,
        down_sum,
        first_sum,
        second_sum,
    )


class Chunk:
    def __init__(self, rows, cols, first):
        self.rows, self.cols, self.half = rows, cols, cols // 2
        self.first, self.second = first, cols // 2 - first


class Place:
    def __init__(self):
        dp = lax.axis_index("dp")
        self.x = lax.axis_index("ctx")
        self.z, self.y, self.c = dp // 4, (dp // 2) % 2, dp % 2
        self.xo, self.yo, self.co = 1 - self.x, 1 - self.y, 1 - self.c
        self.to_x = (dp, self.xo)
        self.to_y = (self.z * 4 + self.yo * 2 + self.c, self.x)
        self.to_c = (self.z * 4 + self.y * 2 + self.co, self.x)
        self.z_up = [(self.z + k) % 4 for k in range(4)]
        self.z_down = [(self.z + 4 - k) % 4 for k in range(4)]
        self.to_z = [(self.z_up[k] * 4 + self.y * 2 + self.c, self.x) for k in range(4)]

    def partners(self):
        return [self.to_x, self.to_y, self.to_c] + self.to_z[1:]

    def barrier(self):
        semaphore = pltpu.get_barrier_semaphore()
        for partner in self.partners():
            pl.semaphore_signal(semaphore, inc=1, device_id=partner, device_id_type=MESH)
        pl.semaphore_wait(semaphore, 6)


class Links:
    def __init__(self, send, recv):
        self.send, self.recv, self.used, self.all = send, recv, 0, []

    def start(self, src, dst, partner):
        at = self.used
        self.used += 1
        copy = pltpu.make_async_remote_copy(
            src_ref=src,
            dst_ref=dst,
            send_sem=self.send.at[at],
            recv_sem=self.recv.at[at],
            device_id=partner,
            device_id_type=MESH,
        )
        copy.start()
        self.all.append(copy)
        return copy

    def drain(self):
        for copy in self.all:
            copy.wait_send()


def columns(start, size):
    return pl.ds(pl.multiple_of(start, 128), size)


class Gather:
    def __init__(self, chunk, shard, whole, place, links, own_sem):
        self.chunk, self.shard, self.whole = chunk, shard, whole
        self.p, self.links = place, links
        self.own = pltpu.make_async_copy(shard, whole.at[place.z, place.y, place.c], own_sem)

    def half(self, x):
        return columns(x * self.chunk.half, self.chunk.half)

    def first(self, x):
        return columns(x * self.chunk.half, self.chunk.first)

    def second(self, x):
        return columns(x * self.chunk.half + self.chunk.first, self.chunk.second)

    def step0(self):
        p, whole, shard = self.p, self.whole, self.shard
        mine = self.half(p.x)
        self.own.start()
        self.from_z = [
            self.links.start(
                shard.at[:, mine], whole.at[p.z, p.y, p.c, :, mine], p.to_z[k]
            )
            for k in range(1, 4)
        ]
        self.y_own = self.links.start(
            shard.at[:, mine], whole.at[p.z, p.y, p.c, :, mine], p.to_y
        )
        self.from_c = [self.links.start(shard, whole.at[p.z, p.y, p.c], p.to_c)]

    def step1(self):
        p, whole = self.p, self.whole
        mine = self.half(p.x)
        self.from_x, self.from_y = [], [self.y_own]
        for k in range(1, 4):
            self.from_z[k - 1].wait_recv()
            piece = whole.at[p.z_down[k], p.y, p.c, :, mine]
            self.from_x.append(self.links.start(piece, piece, p.to_x))
            self.from_y.append(self.links.start(piece, piece, p.to_y))
            self.from_c.append(self.links.start(piece, piece, p.to_c))

    def step2(self):
        p, whole = self.p, self.whole
        other = self.half(p.xo)
        self.own.wait()
        for k in range(1, 4):
            self.from_x[k - 1].wait_recv()
            piece = whole.at[p.z_down[k], p.y, p.c, :, other]
            self.from_c.append(self.links.start(piece, piece, p.to_c))
        piece = whole.at[:, p.y, p.c, :, self.first(p.xo)]
        self.first_y = self.links.start(piece, piece, p.to_y)
        for copy in self.from_y:
            copy.wait_recv()
        piece = whole.at[:, p.yo, p.c, :, self.second(p.x)]
        self.second_x = self.links.start(piece, piece, p.to_x)
        piece = whole.at[:, p.yo, p.c, :, self.half(p.x)]
        self.from_c.append(self.links.start(piece, piece, p.to_c))

    def step3(self):
        p, whole = self.p, self.whole
        self.first_y.wait_recv()
        piece = whole.at[:, p.yo, p.c, :, self.first(p.xo)]
        self.from_c.append(self.links.start(piece, piece, p.to_c))
        self.second_x.wait_recv()
        piece = whole.at[:, p.yo, p.c, :, self.second(p.xo)]
        self.from_c.append(self.links.start(piece, piece, p.to_c))

    def step4(self):
        for copy in self.from_c:
            copy.wait_recv()


GATHER_COPIES = 23


def reduce_scratch(chunk):
    rows, bf16 = chunk.rows, jnp.bfloat16
    return [
        pltpu.VMEM((4, 2, rows, chunk.cols), bf16),
        pltpu.VMEM((4, 2, rows, chunk.second), bf16),
        pltpu.VMEM((2, 4, rows, chunk.first), bf16),
        pltpu.VMEM((4, rows, chunk.second), bf16),
        pltpu.VMEM((4, rows, chunk.first), bf16),
        pltpu.VMEM((3, rows, chunk.half), bf16),
    ]


REDUCE_COPIES = 10


class Reduce(Gather):
    def __init__(self, chunk, grads, out, place, links, scratch):
        self.chunk, self.grads, self.out = chunk, grads, out
        self.p, self.links = place, links
        self.core_in, self.x_in, self.y_in, self.y_in2, self.x_in2, self.z_in = scratch

    def add(self, outer, at, source):
        steps = self.chunk.rows // 16

        def body(i, carry):
            rows = pl.ds(pl.multiple_of((i % steps) * 16, 16), 16)
            target = at(i // steps, rows)
            given = source(i // steps, rows)
            self.grads[target] = (
                self.grads[target].astype(jnp.float32) + given.astype(jnp.float32)
            ).astype(jnp.bfloat16)
            return carry

        lax.fori_loop(0, outer * steps, body, 0)

    def step0(self):
        p = self.p
        self.by_core = self.links.start(self.grads.at[:, :, p.co], self.core_in, p.to_c)

    def step1(self):
        p, grads = self.p, self.grads
        self.by_core.wait_recv()
        everything = pl.ds(0, self.chunk.cols)
        self.add(
            8,
            lambda i, rows: (i // 2, i % 2, p.c, rows, everything),
            lambda i, rows: self.core_in[i // 2, i % 2, rows, :],
        )
        self.by_x = self.links.start(grads.at[:, :, p.c, :, self.second(p.xo)], self.x_in, p.to_x)
        self.by_y = [
            self.links.start(grads.at[:, p.yo, p.c, :, self.first(h)], self.y_in.at[h], p.to_y)
            for h in range(2)
        ]

    def step2(self):
        p, grads = self.p, self.grads
        for h in range(2):
            self.by_y[h].wait_recv()
            cut = self.first(h)
            self.add(
                4,
                lambda i, rows: (i, p.y, p.c, rows, cut),
                lambda i, rows: self.y_in[h, i, rows, :],
            )
        self.by_x2 = self.links.start(grads.at[:, p.y, p.c, :, self.first(p.xo)], self.x_in2, p.to_x)
        self.by_x.wait_recv()
        cut2 = self.second(p.x)
        self.add(
            8,
            lambda i, rows: (i // 2, i % 2, p.c, rows, cut2),
            lambda i, rows: self.x_in[i // 2, i % 2, rows, :],
        )
        self.by_y2 = self.links.start(grads.at[:, p.yo, p.c, :, cut2], self.y_in2, p.to_y)

    def step3(self):
        p, grads = self.p, self.grads
        self.by_x2.wait_recv()
        cut = self.first(p.x)
        self.add(
            4, lambda i, rows: (i, p.y, p.c, rows, cut), lambda i, rows: self.x_in2[i, rows, :]
        )
        self.by_y2.wait_recv()
        cut2 = self.second(p.x)
        self.add(
            4, lambda i, rows: (i, p.y, p.c, rows, cut2), lambda i, rows: self.y_in2[i, rows, :]
        )
        mine = self.half(p.x)
        self.by_z = [
            self.links.start(grads.at[p.z_up[k], p.y, p.c, :, mine], self.z_in.at[k - 1], p.to_z[k])
            for k in range(1, 4)
        ]

    def step4(self):
        p = self.p
        mine = self.half(p.x)
        for copy in self.by_z:
            copy.wait_recv()

        def body(i, carry):
            rows = pl.ds(pl.multiple_of(i * 16, 16), 16)
            total = self.grads[p.z, p.y, p.c, rows, mine].astype(jnp.float32)
            for k in range(3):
                total = total + self.z_in[k, rows, :].astype(jnp.float32)
            self.out[rows, mine] = total.astype(jnp.bfloat16)
            return carry

        lax.fori_loop(0, self.chunk.rows // 16, body, 0)
        self.last = self.links.start(self.out.at[:, mine], self.out.at[:, mine], p.to_x)

    def step5(self):
        self.last.wait_recv()


class Total:
    def __init__(self, value, core_in, x_in, y_in, by_z, place, links):
        self.value, self.core_in, self.x_in, self.y_in, self.by_z = value, core_in, x_in, y_in, by_z
        self.p, self.links = place, links

    def step0(self):
        self.copy = self.links.start(self.value.at[0], self.core_in, self.p.to_c)

    def step1(self):
        self.copy.wait_recv()
        self.value[1] = self.value[0] + self.core_in[...]
        self.copy = self.links.start(self.value.at[1], self.x_in, self.p.to_x)

    def step2(self):
        self.copy.wait_recv()
        self.value[2] = self.value[1] + self.x_in[...]
        self.copy = self.links.start(self.value.at[2], self.y_in, self.p.to_y)

    def step3(self):
        self.copy.wait_recv()
        z = self.p.z
        self.by_z[z] = self.value[2] + self.y_in[...]
        self.copies = [
            self.links.start(self.by_z.at[z], self.by_z.at[z], self.p.to_z[k]) for k in range(1, 4)
        ]

    def step4(self):
        for copy in self.copies:
            copy.wait_recv()
        return ((self.by_z[0] + self.by_z[1]) + self.by_z[2]) + self.by_z[3]


TOTAL_COPIES = 6


def gather_kernel(chunks, *refs):
    n = len(chunks)
    shards, tokens, teach = refs[:n], refs[n], refs[n + 1]
    wholes, tokens_all, teach_in = refs[n + 2 : 2 * n + 2], refs[2 * n + 2], refs[2 * n + 3]
    send, recv, own_sem = refs[2 * n + 4 :]
    place = Place()
    links = Links(send, recv)
    place.barrier()
    work = [
        Gather(chunk, shards[i], wholes[i], place, links, own_sem.at[i])
        for i, chunk in enumerate(chunks)
    ]
    own_tokens = pltpu.make_async_copy(tokens, tokens_all.at[place.x], own_sem.at[n])
    own_tokens.start()
    swap = []
    for item in work:
        item.step0()
    swap.append(links.start(tokens, tokens_all.at[place.x], place.to_x))
    swap.append(links.start(teach, teach_in, place.to_x))
    for s in range(n + 3):
        for i, item in enumerate(work):
            if s - i == 0:
                item.step1()
            if s - i == 1:
                item.step2()
            if s - i == 2:
                item.step3()
            if s - i == 3:
                item.step4()
    for copy in swap:
        copy.wait_recv()
    own_tokens.wait()
    links.drain()


def gather_all(chunks, shards, tokens, teach):
    bf16 = jnp.bfloat16
    n = len(chunks)
    out_shape = [jax.ShapeDtypeStruct((4, 2, 2, c.rows, c.cols), bf16) for c in chunks]
    out_shape += [
        jax.ShapeDtypeStruct((2,) + tokens.shape, bf16),
        jax.ShapeDtypeStruct(teach.shape, bf16),
    ]
    copies = GATHER_COPIES * n + 2
    return pl.pallas_call(
        functools.partial(gather_kernel, chunks),
        out_shape=out_shape,
        in_specs=[pl.BlockSpec(memory_space=pl.ANY)] * (n + 2),
        out_specs=[pl.BlockSpec(memory_space=pl.ANY)] * (n + 2),
        scratch_shapes=[
            pltpu.SemaphoreType.DMA((copies,)),
            pltpu.SemaphoreType.DMA((copies,)),
            pltpu.SemaphoreType.DMA((n + 1,)),
        ],
        compiler_params=pltpu.CompilerParams(collective_id=0, has_side_effects=True),
    )(*shards, tokens, teach)


def reduce_kernel(chunks, *refs):
    n = len(chunks)
    grads, error, result = refs[:n], refs[n], refs[n + 1]
    outs, total_out, result_in = refs[n + 2 : 2 * n + 2], refs[2 * n + 2], refs[2 * n + 3]
    rest = refs[2 * n + 4 :]
    send, recv = rest[:2]
    value, core_in, x_in, y_in, by_z = rest[2:7]
    scratch = rest[7:]
    place = Place()
    links = Links(send, recv)
    value[0] = error[...]
    place.barrier()
    total = Total(value, core_in, x_in, y_in, by_z, place, links)
    work = [
        Reduce(chunk, grads[i], outs[i], place, links, scratch[6 * i : 6 * i + 6])
        for i, chunk in enumerate(chunks)
    ]
    total.step0()
    work[0].step0()
    swap = links.start(result, result_in, place.to_x)
    for item in work[1:]:
        item.step0()
    total.step1()
    for s in range(n + 4):
        if s < 2:
            getattr(total, "step" + str(s + 2))()
        for i, item in enumerate(work):
            if 0 <= s - i < 5:
                getattr(item, "step" + str(s - i + 1))()
    total_out[...] = total.step4()
    swap.wait_recv()
    links.drain()


def reduce_all(chunks, grads, error, result):
    bf16 = jnp.bfloat16
    n = len(chunks)
    out_shape = [jax.ShapeDtypeStruct((c.rows, c.cols), bf16) for c in chunks]
    out_shape += [
        jax.ShapeDtypeStruct((8, 128), jnp.float32),
        jax.ShapeDtypeStruct(result.shape, bf16),
    ]
    copies = REDUCE_COPIES * n + TOTAL_COPIES + 1
    small = pltpu.VMEM((8, 128), jnp.float32)
    vmem = pl.BlockSpec(memory_space=pltpu.VMEM)
    anywhere = pl.BlockSpec(memory_space=pl.ANY)
    return pl.pallas_call(
        functools.partial(reduce_kernel, chunks),
        out_shape=out_shape,
        in_specs=[vmem] * (n + 1) + [anywhere],
        out_specs=[vmem] * (n + 1) + [anywhere],
        scratch_shapes=[
            pltpu.SemaphoreType.DMA((copies,)),
            pltpu.SemaphoreType.DMA((copies,)),
            pltpu.VMEM((3, 8, 128), jnp.float32),
            small,
            small,
            small,
            pltpu.VMEM((4, 8, 128), jnp.float32),
        ]
        + sum([reduce_scratch(c) for c in chunks], []),
        compiler_params=pltpu.CompilerParams(
            collective_id=1, has_side_effects=True, vmem_limit_bytes=56 * MIB
        ),
    )(*grads, error, result)


def pick_rows(index, source):
    chosen = index[:, None] == jnp.arange(source.shape[0], dtype=jnp.int32)[None, :]
    return jnp.dot(
        chosen.astype(jnp.bfloat16), source, preferred_element_type=jnp.float32
    ).astype(jnp.bfloat16)


def fused_shards(
    tokens,
    w_query,
    w_key,
    w_value,
    w_out,
    w_up,
    w_down,
    gain_attn,
    gain_ffn,
    teacher,
    seq_lengths,
    tok_perm,
    valid_count,
):
    bf16, f32 = jnp.bfloat16, jnp.float32
    rank = lax.axis_index("ctx")
    dp_count = lax.axis_size("dp")
    layer_in = tokens[0]
    span, width = layer_in.shape
    ff = w_up.shape[1]
    shard = w_query.shape[0]
    head_count = width // HEAD_DIM
    order = tok_perm[0]
    seq_len = order.shape[0]
    length = seq_lengths[0]
    counted = order < length
    block = span // 2

    def column_block(gain):
        return jnp.pad(gain[:, None], ((0, 0), (0, 127)))

    chunks = (
        Chunk(shard, 3 * width, 640),
        Chunk(shard, width + 256, 256),
        Chunk(shard, ff, 896),
        Chunk(w_down.shape[0], width, 256),
    )
    shards_in = (
        jnp.concatenate([w_query, w_key, w_value], axis=1),
        jnp.concatenate([w_out, column_block(gain_attn), column_block(gain_ffn)], axis=1),
        w_up,
        w_down,
    )
    by_block = order.reshape(2, 2, block)
    mine_here = jnp.take(by_block, rank, axis=1)
    own_pos = jnp.take(mine_here, rank, axis=0) - rank * span
    peer_pos = jnp.take(mine_here, 1 - rank, axis=0) - rank * span
    teach_own = pick_rows(own_pos, teacher[0])
    teach_send = pick_rows(peer_pos, teacher[0])
    qkv, out_gain, up_all, down_all, tokens_all, teach_in = gather_all(
        chunks, shards_in, layer_in, teach_send
    )
    qkv = qkv.reshape(width, 3 * width)
    out_gain = out_gain.reshape(width, width + 256)
    up_weight = up_all.reshape(width, ff)
    down_weight = down_all.reshape(ff, width)
    out_weight = out_gain[:, :width]
    gain_first = out_gain[:, width].astype(f32)
    gain_second = out_gain[:, width + 128].astype(f32)
    both = tokens_all.reshape(seq_len, width)
    teach_dealt = jnp.where(
        rank == 0,
        jnp.concatenate([teach_own, teach_in]),
        jnp.concatenate([teach_in, teach_own]),
    ).astype(f32)

    def project(rows, which):
        return jnp.dot(
            rows, qkv[:, which * width : (which + 1) * width], preferred_element_type=f32
        ).astype(bf16)

    queries = project(layer_in, 0).reshape(span, head_count, HEAD_DIM)
    keys = project(both, 1).reshape(seq_len, head_count, HEAD_DIM)
    values = project(both, 2).reshape(seq_len, head_count, HEAD_DIM)
    scores = jnp.einsum("qhe,khe->hqk", queries, keys, preferred_element_type=f32) * SCORE_SCALE
    scores = jnp.where(counted[None, None, :], scores, MASKED)
    top = jnp.max(scores, axis=-1, keepdims=True)
    weights = jnp.exp(scores - top)
    total = jnp.sum(weights, axis=-1)
    mixed = jnp.einsum("hqk,khe->hqe", weights.astype(bf16), values, preferred_element_type=f32)
    log_total = top[..., 0] + jnp.log(total)
    attn_full = jnp.transpose(mixed / total[..., None], (1, 0, 2)).reshape(span, width)
    attn_low = attn_full.astype(bf16)
    branch = jnp.dot(attn_low, out_weight, preferred_element_type=f32)
    normed, normal_first, inverse_first = norm_forward(layer_in.astype(f32) + branch, gain_first)
    normed_low = normed.astype(bf16)
    upward = jnp.dot(normed_low, up_weight, preferred_element_type=f32)
    active, gelu_pull = jax.vjp(gelu_exact, upward)
    active_low = active.astype(bf16)
    down_out = jnp.dot(active_low, down_weight, preferred_element_type=f32)
    result, normal_second, inverse_second = norm_forward(normed + down_out, gain_second)
    result_low = result.astype(bf16)
    own_order = lax.dynamic_slice_in_dim(order, rank * span, span)
    live = (own_order < length)[:, None]
    error = jnp.where(live, result_low.astype(f32) - teach_dealt, 0.0)
    square = jnp.sum(error * error)
    valid_total = valid_count[0].astype(f32)
    grad_scale = seq_len * dp_count / valid_total
    grad_result = (error * grad_scale).astype(bf16).astype(f32)
    grad_sum_second, grad_gain_second = norm_backward(
        grad_result, gain_second, normal_second, inverse_second
    )
    down_grad_low = grad_sum_second.astype(bf16)
    grad_down_w = row_product(active_low, down_grad_low)
    grad_active = by_transpose(down_grad_low, down_weight)
    grad_upward = gelu_pull(grad_active)[0].astype(bf16)
    grad_up_w = row_product(normed_low, grad_upward)
    grad_normed = grad_sum_second + by_transpose(grad_upward, up_weight)
    grad_hidden, grad_gain_first = norm_backward(
        grad_normed, gain_first, normal_first, inverse_first
    )
    branch_grad = grad_hidden.astype(bf16)
    grad_out_w = row_product(attn_low, branch_grad)
    attn_grad_low = by_transpose(branch_grad, out_weight).astype(bf16)
    grad_heads = attn_grad_low.reshape(span, head_count, HEAD_DIM)
    row_delta = jnp.sum(
        (attn_grad_low.astype(f32) * attn_full).reshape(span, head_count, HEAD_DIM), axis=-1
    ).T
    scores = jnp.einsum("qhe,khe->hqk", queries, keys, preferred_element_type=f32) * SCORE_SCALE
    soft = jnp.where(counted[None, None, :], jnp.exp(scores - log_total[..., None]), 0.0)
    prob_grad = jnp.einsum("qhe,khe->hqk", grad_heads, values, preferred_element_type=f32)
    score_grad = (soft * (prob_grad - row_delta[..., None])).astype(bf16)
    value_grad = jnp.einsum("hqk,qhe->khe", soft.astype(bf16), grad_heads, preferred_element_type=f32)
    query_grad = SCORE_SCALE * jnp.einsum("hqk,khe->qhe", score_grad, keys, preferred_element_type=f32)
    key_grad = SCORE_SCALE * jnp.einsum("hqk,qhe->khe", score_grad, queries, preferred_element_type=f32)
    both_grads = jnp.concatenate(
        [key_grad.reshape(seq_len, width), value_grad.reshape(seq_len, width)], axis=1
    )
    theirs = lax.dynamic_slice_in_dim(both_grads, (1 - rank) * span, span).astype(bf16)
    arrived = lax.ppermute(theirs, "ctx", [(0, 1), (1, 0)])
    kv_grad = (
        lax.dynamic_slice_in_dim(both_grads, rank * span, span) + arrived.astype(f32)
    ).astype(bf16)
    qkv_grad = jnp.concatenate([query_grad.reshape(span, width).astype(bf16), kv_grad], axis=1)
    grad_qkv_w = row_product(layer_in, qkv_grad)
    token_grad = grad_hidden + by_transpose(qkv_grad, qkv)
    whole_grads = [
        grad_qkv_w,
        jnp.concatenate(
            [grad_out_w, column_block(grad_gain_first), column_block(grad_gain_second)], axis=1
        ),
        grad_up_w,
        grad_down_w,
    ]
    whole_grads = [
        g.astype(bf16).reshape(4, 2, 2, c.rows, c.cols) for g, c in zip(whole_grads, chunks)
    ]
    result_send = lax.dynamic_slice_in_dim(result_low, (1 - rank) * block, block)
    result_own = lax.dynamic_slice_in_dim(result_low, rank * block, block)
    down_sum, up_sum, out_sum, qkv_sum, square_sum, result_in = reduce_all(
        (chunks[3], chunks[2], chunks[1], chunks[0]),
        (whole_grads[3], whole_grads[2], whole_grads[1], whole_grads[0]),
        jnp.full((8, 128), square, f32),
        result_send,
    )
    loss = (square_sum[0, 0] / (2.0 * width * valid_total)).reshape(1)
    placed = jnp.concatenate([own_pos, peer_pos])
    rows = jnp.arange(span, dtype=jnp.int32)
    in_order = jnp.dot(
        (rows[:, None] == placed[None, :]).astype(bf16),
        jnp.concatenate([result_own, result_in]),
        preferred_element_type=f32,
    ).astype(bf16)
    qkv_sum, out_sum = qkv_sum.astype(f32), out_sum.astype(f32)
    return (
        in_order[None],
        loss,
        token_grad[None],
        qkv_sum[:, :width],
        qkv_sum[:, width : 2 * width],
        qkv_sum[:, 2 * width :],
        out_sum[:, :width],
        up_sum.astype(f32),
        down_sum.astype(f32),
        out_sum[:, width],
        out_sum[:, width + 128],
    )


def solution(mesh):
    in_specs = (
        P("dp", "ctx", None),
        P("dp", None),
        P("dp", None),
        P("dp", None),
        P("dp", None),
        P("dp", None),
        P("dp", None),
        P("dp"),
        P("dp"),
        P("dp", "ctx", None),
        P("dp"),
        P("dp", None),
        P(),
    )
    out_specs = (
        P("dp", "ctx", None),
        P(),
        P("dp", "ctx", None),
        P("dp", None),
        P("dp", None),
        P("dp", None),
        P("dp", None),
        P("dp", None),
        P("dp", None),
        P("dp"),
        P("dp"),
    )
    body = fused_shards if dict(mesh.shape) == {"dp": 16, "ctx": 2} else shards
    return jax.shard_map(body, mesh=mesh, in_specs=in_specs, out_specs=out_specs, check_vma=False)
```

```python
import functools
import math

import jax
import jax.numpy as jnp
from jax import lax
from jax.experimental import pallas as pl
from jax.experimental.pallas import tpu as pltpu
from jax.sharding import PartitionSpec as P

HEAD_DIM = 64


EPSILON = 1e-06
SCORE_SCALE = 0.125
MASKED = -1e30
MESH = pl.DeviceIdType.MESH
MIB = 1024 * 1024


def gelu_exact(values):
    return 0.5 * values * (1.0 + lax.erf(values * 0.7071067811865476))


def norm_forward(hidden, gain_row):
    center = hidden - jnp.mean(hidden, axis=-1, keepdims=True)
    inverse = lax.rsqrt(jnp.mean(center * center, axis=-1, keepdims=True) + EPSILON)
    normal = center * inverse
    return (normal * gain_row, normal, inverse)


def norm_backward(grad_norm, gain_row, normal, inverse):
    scaled = grad_norm * gain_row
    grad_input = inverse * (
        scaled
        - jnp.mean(scaled, axis=-1, keepdims=True)
        - normal * jnp.mean(scaled * normal, axis=-1, keepdims=True)
    )
    return (grad_input, jnp.sum(grad_norm * normal, axis=0))


def row_product(left_mat, right_mat):
    return lax.dot_general(
        left_mat, right_mat, (((0,), (0,)), ((), ())), preferred_element_type=jnp.float32
    )


def by_transpose(left_mat, right_mat):
    return lax.dot_general(
        left_mat, right_mat, (((1,), (1,)), ((), ())), preferred_element_type=jnp.float32
    )


def shards(
    tokens,
    w_query,
    w_key,
    w_value,
    w_out,
    w_up,
    w_down,
    gain_attn,
    gain_ffn,
    teacher,
    seq_lengths,
    tok_perm,
    valid_count,
):
    ctx_count = lax.axis_size("ctx")
    ctx_rank = lax.axis_index("ctx")
    dp_count = lax.axis_size("dp")
    layer_in = tokens[0]
    span_rows, model_width = layer_in.shape
    head_count = model_width // HEAD_DIM
    dealt_order = tok_perm[0]
    seq_len = dealt_order.shape[0]
    length = seq_lengths[0]
    keep_all = dealt_order < length
    per_peer = span_rows // ctx_count
    query_weight, key_weight, value_weight, out_weight, gain_first = (
        lax.all_gather(w_query, "dp", axis=0, tiled=True),
        lax.all_gather(w_key, "dp", axis=0, tiled=True),
        lax.all_gather(w_value, "dp", axis=0, tiled=True),
        lax.all_gather(w_out, "dp", axis=0, tiled=True),
        lax.all_gather(gain_attn, "dp", axis=0, tiled=True),
    )
    up_weight, down_weight, gain_second = (
        lax.all_gather(w_up, "dp", axis=0, tiled=True),
        lax.all_gather(w_down, "dp", axis=0, tiled=True),
        lax.all_gather(gain_ffn, "dp", axis=0, tiled=True),
    )
    queries = jnp.dot(layer_in, query_weight, preferred_element_type=jnp.float32).astype(
        jnp.bfloat16
    )
    keys_own = jnp.dot(layer_in, key_weight, preferred_element_type=jnp.float32).astype(
        jnp.bfloat16
    )
    values_own = jnp.dot(layer_in, value_weight, preferred_element_type=jnp.float32).astype(
        jnp.bfloat16
    )
    query_heads = queries.reshape(span_rows, head_count, HEAD_DIM)
    initial = (
        jnp.full((head_count, span_rows), MASKED, jnp.float32),
        jnp.zeros((head_count, span_rows), jnp.float32),
        jnp.zeros((head_count, span_rows, HEAD_DIM), jnp.float32),
    )
    fold_state = initial
    key_piece = lax.all_gather(keys_own, "ctx", axis=0, tiled=True)
    value_piece = lax.all_gather(values_own, "ctx", axis=0, tiled=True)
    piece_rows = key_piece.shape[0]
    block_rows = math.gcd(piece_rows, span_rows)
    key_blocks = key_piece.reshape(piece_rows // block_rows, block_rows, head_count, HEAD_DIM)
    value_blocks = value_piece.reshape(piece_rows // block_rows, block_rows, head_count, HEAD_DIM)

    def step_block(block_state, block_item):
        running_max, running_sum, accumulated = block_state
        key_block, value_block, block_index = block_item
        key_keep = lax.dynamic_slice_in_dim(keep_all, block_index * block_rows, block_rows)
        scores = (
            jnp.einsum("qhe,khe->hqk", query_heads, key_block, preferred_element_type=jnp.float32)
            * SCORE_SCALE
        )
        scores = jnp.where(key_keep[None, None, :], scores, MASKED)
        new_max = jnp.maximum(running_max, jnp.max(scores, axis=-1))
        factor = jnp.exp(running_max - new_max)
        soft_weights = jnp.where(key_keep[None, None, :], jnp.exp(scores - new_max[..., None]), 0.0)
        running_sum = running_sum * factor + jnp.sum(soft_weights, axis=-1)
        accumulated = accumulated * factor[..., None] + jnp.einsum(
            "hqk,khe->hqe",
            soft_weights.astype(jnp.bfloat16),
            value_block,
            preferred_element_type=jnp.float32,
        )
        return ((new_max, running_sum, accumulated), None)

    block_indices = jnp.arange(piece_rows // block_rows, dtype=jnp.int32)
    fold_state, unused = lax.scan(step_block, fold_state, (key_blocks, value_blocks, block_indices))
    run_max, run_sum, accumulated = fold_state
    log_total = run_max + jnp.log(run_sum)
    attn_full = jnp.transpose(accumulated / run_sum[..., None], (1, 0, 2)).reshape(
        span_rows, model_width
    )
    attn_low = attn_full.astype(jnp.bfloat16)
    gain_first32 = gain_first.astype(jnp.float32)
    gain_second32 = gain_second.astype(jnp.float32)
    branch = jnp.dot(attn_low, out_weight, preferred_element_type=jnp.float32)
    normed, normal_first, inverse_first = norm_forward(
        layer_in.astype(jnp.float32) + branch, gain_first32
    )
    normed_low = normed.astype(jnp.bfloat16)
    upward = jnp.dot(normed_low, up_weight, preferred_element_type=jnp.float32)
    active, gelu_pull = jax.vjp(gelu_exact, upward)
    active_low = active.astype(jnp.bfloat16)
    down_out = jnp.dot(active_low, down_weight, preferred_element_type=jnp.float32)
    result, normal_second, inverse_second = norm_forward(normed + down_out, gain_second32)
    result_low = result.astype(jnp.bfloat16)
    arrived = lax.all_to_all(result_low, "ctx", split_axis=0, concat_axis=0, tiled=True)
    sources = (
        jnp.arange(ctx_count, dtype=jnp.int32)[:, None] * span_rows
        + ctx_rank * per_peer
        + jnp.arange(per_peer, dtype=jnp.int32)[None, :]
    ).reshape(span_rows)
    local_pos = jnp.take(dealt_order, sources) - ctx_rank * span_rows
    in_order = jnp.zeros_like(arrived).at[local_pos].set(arrived)
    target = teacher[0].astype(jnp.float32)
    live_rows = (ctx_rank * span_rows + jnp.arange(span_rows, dtype=jnp.int32) < length)[:, None]
    residual_err = jnp.where(live_rows, in_order.astype(jnp.float32) - target, 0.0)
    total_sq = lax.psum(jnp.sum(residual_err * residual_err), ("dp", "ctx"))
    valid_total = valid_count[0].astype(jnp.float32)
    loss_value = (total_sq / (2.0 * model_width * valid_total)).reshape(1)
    grad_scale = seq_len * dp_count / valid_total
    grad_order = (residual_err * grad_scale).astype(jnp.bfloat16)
    outgoing = jnp.take(grad_order, local_pos, axis=0)
    grad_result = lax.all_to_all(outgoing, "ctx", split_axis=0, concat_axis=0, tiled=True).astype(
        jnp.float32
    )
    grad_sum_second, grad_gain_second = norm_backward(
        grad_result, gain_second32, normal_second, inverse_second
    )
    down_grad_low = grad_sum_second.astype(jnp.bfloat16)
    grad_down_w = row_product(active_low, down_grad_low)
    grad_active = by_transpose(down_grad_low, down_weight)
    grad_upward = gelu_pull(grad_active)[0].astype(jnp.bfloat16)
    grad_up_w = row_product(normed_low, grad_upward)
    grad_normed = grad_sum_second + by_transpose(grad_upward, up_weight)
    grad_hidden, grad_gain_first = norm_backward(
        grad_normed, gain_first32, normal_first, inverse_first
    )
    branch_grad = grad_hidden.astype(jnp.bfloat16)
    grad_out_w = row_product(attn_low, branch_grad)
    attn_grad_low = by_transpose(branch_grad, out_weight).astype(jnp.bfloat16)
    grad_heads = attn_grad_low.reshape(span_rows, head_count, HEAD_DIM)
    row_delta = jnp.sum(
        (attn_grad_low.astype(jnp.float32) * attn_full).reshape(span_rows, head_count, HEAD_DIM),
        axis=-1,
    ).T
    keys_all, values_all = (
        lax.all_gather(keys_own, "ctx", axis=0, tiled=True),
        lax.all_gather(values_own, "ctx", axis=0, tiled=True),
    )
    blocks_count = seq_len // span_rows
    key_stack = keys_all.reshape(blocks_count, span_rows, head_count, HEAD_DIM)
    value_stack = values_all.reshape(blocks_count, span_rows, head_count, HEAD_DIM)

    def score_terms(
        query_block, grad_block, total_block, delta_block, key_block, value_block, key_keep
    ):
        scores = (
            jnp.einsum("qhe,khe->hqk", query_block, key_block, preferred_element_type=jnp.float32)
            * SCORE_SCALE
        )
        soft_weights = jnp.where(
            key_keep[None, None, :], jnp.exp(scores - total_block[..., None]), 0.0
        )
        prob_grad = jnp.einsum(
            "qhe,khe->hqk", grad_block, value_block, preferred_element_type=jnp.float32
        )
        score_grad = (soft_weights * (prob_grad - delta_block[..., None])).astype(jnp.bfloat16)
        return (soft_weights, score_grad)

    def back_block(query_grad, block_item):
        key_block, value_block, block_index = block_item
        key_keep = lax.dynamic_slice_in_dim(keep_all, block_index * span_rows, span_rows)
        soft_weights, score_grad = score_terms(
            query_heads, grad_heads, log_total, row_delta, key_block, value_block, key_keep
        )
        value_grad = jnp.einsum(
            "hqk,qhe->khe",
            soft_weights.astype(jnp.bfloat16),
            grad_heads,
            preferred_element_type=jnp.float32,
        )
        query_grad = query_grad + SCORE_SCALE * jnp.einsum(
            "hqk,khe->qhe", score_grad, key_block, preferred_element_type=jnp.float32
        )
        key_grad = SCORE_SCALE * jnp.einsum(
            "hqk,qhe->khe", score_grad, query_heads, preferred_element_type=jnp.float32
        )
        return (query_grad, (key_grad, value_grad))

    query_grad, (key_grads, value_grads) = lax.scan(
        back_block,
        jnp.zeros((span_rows, head_count, HEAD_DIM), jnp.float32),
        (key_stack, value_stack, jnp.arange(blocks_count, dtype=jnp.int32)),
    )
    key_grad_sum, value_grad_sum = (
        lax.psum_scatter(
            key_grads.reshape(seq_len, model_width).astype(jnp.bfloat16),
            "ctx",
            scatter_dimension=0,
            tiled=True,
        ).astype(jnp.float32),
        lax.psum_scatter(
            value_grads.reshape(seq_len, model_width).astype(jnp.bfloat16),
            "ctx",
            scatter_dimension=0,
            tiled=True,
        ).astype(jnp.float32),
    )
    query_grad_low = query_grad.reshape(span_rows, model_width).astype(jnp.bfloat16)
    key_grad_low = key_grad_sum.astype(jnp.bfloat16)
    value_grad_low = value_grad_sum.astype(jnp.bfloat16)
    grad_query_w = row_product(layer_in, query_grad_low)
    grad_key_w = row_product(layer_in, key_grad_low)
    grad_value_w = row_product(layer_in, value_grad_low)
    token_grad = (
        grad_hidden
        + by_transpose(query_grad_low, query_weight)
        + by_transpose(key_grad_low, key_weight)
        + by_transpose(value_grad_low, value_weight)
    )
    up_part, down_part, second_part = (
        lax.psum_scatter(
            grad_up_w.astype(jnp.bfloat16), "dp", scatter_dimension=0, tiled=True
        ).astype(jnp.float32),
        lax.psum_scatter(
            grad_down_w.astype(jnp.bfloat16), "dp", scatter_dimension=0, tiled=True
        ).astype(jnp.float32),
        lax.psum_scatter(
            grad_gain_second.astype(jnp.bfloat16), "dp", scatter_dimension=0, tiled=True
        ).astype(jnp.float32),
    )
    query_part, key_part, value_part, out_part, first_part = (
        lax.psum_scatter(
            grad_query_w.astype(jnp.bfloat16), "dp", scatter_dimension=0, tiled=True
        ).astype(jnp.float32),
        lax.psum_scatter(
            grad_key_w.astype(jnp.bfloat16), "dp", scatter_dimension=0, tiled=True
        ).astype(jnp.float32),
        lax.psum_scatter(
            grad_value_w.astype(jnp.bfloat16), "dp", scatter_dimension=0, tiled=True
        ).astype(jnp.float32),
        lax.psum_scatter(
            grad_out_w.astype(jnp.bfloat16), "dp", scatter_dimension=0, tiled=True
        ).astype(jnp.float32),
        lax.psum_scatter(
            grad_gain_first.astype(jnp.bfloat16), "dp", scatter_dimension=0, tiled=True
        ).astype(jnp.float32),
    )
    summed = (
        lax.psum(query_part.astype(jnp.bfloat16), "ctx").astype(jnp.float32),
        lax.psum(key_part.astype(jnp.bfloat16), "ctx").astype(jnp.float32),
        lax.psum(value_part.astype(jnp.bfloat16), "ctx").astype(jnp.float32),
        lax.psum(out_part.astype(jnp.bfloat16), "ctx").astype(jnp.float32),
        lax.psum(up_part.astype(jnp.bfloat16), "ctx").astype(jnp.float32),
        lax.psum(down_part.astype(jnp.bfloat16), "ctx").astype(jnp.float32),
        lax.psum(first_part.astype(jnp.bfloat16), "ctx").astype(jnp.float32),
        lax.psum(second_part.astype(jnp.bfloat16), "ctx").astype(jnp.float32),
    )
    query_sum, key_sum, value_sum, out_sum, up_sum, down_sum, first_sum, second_sum = summed
    return (
        in_order[None],
        loss_value,
        token_grad[None],
        query_sum,
        key_sum,
        value_sum,
        out_sum,
        up_sum,
        down_sum,
        first_sum,
        second_sum,
    )


class Place:
    def __init__(self):
        dp = lax.axis_index("dp")
        self.x = lax.axis_index("ctx")
        self.z, self.y, self.c = dp // 4, (dp // 2) % 2, dp % 2
        self.xo, self.yo, self.co = 1 - self.x, 1 - self.y, 1 - self.c
        self.to_x = (dp, self.xo)
        self.to_y = (self.z * 4 + self.yo * 2 + self.c, self.x)
        self.to_c = (self.z * 4 + self.y * 2 + self.co, self.x)
        self.z_up = [(self.z + k) % 4 for k in range(4)]
        self.z_down = [(self.z + 4 - k) % 4 for k in range(4)]
        self.to_z = [(self.z_up[k] * 4 + self.y * 2 + self.c, self.x) for k in range(4)]

    def barrier(self):
        semaphore = pltpu.get_barrier_semaphore()
        for partner in [self.to_x, self.to_y, self.to_c] + self.to_z[1:]:
            pl.semaphore_signal(semaphore, inc=1, device_id=partner, device_id_type=MESH)
        pl.semaphore_wait(semaphore, 6)


class Links:
    def __init__(self, send, recv):
        self.send, self.recv, self.used, self.all = send, recv, 0, []

    def start(self, src, dst, partner):
        at = self.used
        self.used += 1
        copy = pltpu.make_async_remote_copy(
            src_ref=src,
            dst_ref=dst,
            send_sem=self.send.at[at],
            recv_sem=self.recv.at[at],
            device_id=partner,
            device_id_type=MESH,
        )
        copy.start()
        self.all.append(copy)
        return copy

    def sent(self, copy):
        copy.wait_send()
        self.all = [other for other in self.all if other is not copy]

    def drain(self):
        for copy in self.all:
            copy.wait_send()


class Cut:
    def __init__(self, width, first):
        self.full = width // 2
        self.one, self.two = first, width // 2 - first

    def half(self, x):
        return pl.ds(pl.multiple_of(x * self.full, 128), self.full)

    def first(self, x):
        return pl.ds(pl.multiple_of(x * self.full, 128), self.one)

    def second(self, x):
        return pl.ds(pl.multiple_of(x * self.full + self.one, 128), self.two)


class Gather:
    copies = 23

    def __init__(self, rows, cut, shard, whole, place, links, own_sem):
        self.rows, self.cut, self.shard, self.whole = rows, cut, shard, whole
        self.p, self.links = place, links
        self.own = pltpu.make_async_copy(
            shard.at[rows], whole.at[place.z, place.y, place.c, rows], own_sem
        )

    def piece(self, z, y, cols):
        return self.whole.at[z, y, self.p.c, self.rows, cols]

    def push(self, piece, partner):
        return self.links.start(piece, piece, partner)

    def step0(self):
        p, rows = self.p, self.rows
        mine = self.cut.half(p.x)
        source, target = self.shard.at[rows, mine], self.piece(p.z, p.y, mine)
        self.from_z = [self.links.start(source, target, p.to_z[k]) for k in range(1, 4)]
        self.own.start()
        self.from_y = [self.links.start(source, target, p.to_y)]
        self.from_c = [
            self.links.start(self.shard.at[rows], self.whole.at[p.z, p.y, p.c, rows], p.to_c)
        ]

    def step1(self):
        p = self.p
        self.from_x = []
        for k in range(1, 4):
            self.from_z[k - 1].wait_recv()
            piece = self.piece(p.z_down[k], p.y, self.cut.half(p.x))
            self.from_x.append(self.push(piece, p.to_x))
            self.from_y.append(self.push(piece, p.to_y))
            self.from_c.append(self.push(piece, p.to_c))

    def step2(self):
        p, cut, every = self.p, self.cut, slice(None)
        self.own.wait()
        for k in range(1, 4):
            self.from_x[k - 1].wait_recv()
        self.first_y = self.push(self.piece(every, p.y, cut.first(p.xo)), p.to_y)
        for k in range(1, 4):
            self.from_c.append(self.push(self.piece(p.z_down[k], p.y, cut.half(p.xo)), p.to_c))
        for copy in self.from_y:
            copy.wait_recv()
        self.second_x = self.push(self.piece(every, p.yo, cut.second(p.x)), p.to_x)
        self.from_c.append(self.push(self.piece(every, p.yo, cut.half(p.x)), p.to_c))

    def step3(self):
        p, cut, every = self.p, self.cut, slice(None)
        self.first_y.wait_recv()
        self.from_c.append(self.push(self.piece(every, p.yo, cut.first(p.xo)), p.to_c))
        self.second_x.wait_recv()
        self.from_c.append(self.push(self.piece(every, p.yo, cut.second(p.xo)), p.to_c))

    def step4(self):
        for copy in self.from_c:
            copy.wait_recv()


class Reduce:
    copies = 10

    def __init__(self, rows, at, first_row, cut, grads, out, place, links, scratch):
        self.rows, self.cut, self.grads, self.out = rows, cut, grads, out
        self.at, self.here = pl.ds(at, rows), pl.ds(first_row, rows)
        self.at0, self.here0 = at, first_row
        self.p, self.links = place, links
        self.core_in, self.x_in, self.y_in, self.y_in2, self.x_in2, self.z_in = scratch
        self.block = max(b for b in range(16, min(rows, 96) + 1, 16) if rows % b == 0)
        self.stage = 0

    def add(self, outer, target, source):
        steps = self.rows // self.block

        def body(i, carry):
            first = pl.multiple_of((i % steps) * self.block, 16)
            put = target(i // steps, pl.ds(self.at0 + first, self.block))
            given = source(i // steps, pl.ds(self.here0 + first, self.block))
            self.grads[put] = (
                self.grads[put].astype(jnp.float32) + given.astype(jnp.float32)
            ).astype(jnp.bfloat16)
            return carry

        lax.fori_loop(0, outer * steps, body, 0)

    def step0(self):
        p = self.p
        self.by_core = self.links.start(
            self.grads.at[:, :, p.co, self.at], self.core_in.at[:, :, self.here], p.to_c
        )

    def step1(self):
        p, cut, grads = self.p, self.cut, self.grads
        self.by_core.wait_recv()
        self.add(
            8,
            lambda i, rows: (i // 2, i % 2, p.c, rows),
            lambda i, rows: self.core_in[i // 2, i % 2, rows],
        )
        self.by_y = [
            self.links.start(
                grads.at[:, p.yo, p.c, self.at, cut.first(h)], self.y_in.at[h, :, self.here], p.to_y
            )
            for h in range(2)
        ]
        self.by_x = self.links.start(
            grads.at[:, :, p.c, self.at, cut.second(p.xo)], self.x_in.at[:, :, self.here], p.to_x
        )

    def step2(self):
        p, cut, grads = self.p, self.cut, self.grads
        for h in range(2):
            self.by_y[h].wait_recv()
            self.add(
                4,
                lambda i, rows: (i, p.y, p.c, rows, cut.first(h)),
                lambda i, rows: self.y_in[h, i, rows],
            )
        self.by_x2 = self.links.start(
            grads.at[:, p.y, p.c, self.at, cut.first(p.xo)], self.x_in2.at[:, self.here], p.to_x
        )
        self.by_x.wait_recv()
        self.add(
            8,
            lambda i, rows: (i // 2, i % 2, p.c, rows, cut.second(p.x)),
            lambda i, rows: self.x_in[i // 2, i % 2, rows],
        )
        self.by_y2 = self.links.start(
            grads.at[:, p.yo, p.c, self.at, cut.second(p.x)], self.y_in2.at[:, self.here], p.to_y
        )

    def step3(self):
        p, cut, grads = self.p, self.cut, self.grads
        self.by_x2.wait_recv()
        self.add(
            4,
            lambda i, rows: (i, p.y, p.c, rows, cut.first(p.x)),
            lambda i, rows: self.x_in2[i, rows],
        )
        self.by_y2.wait_recv()
        self.add(
            4,
            lambda i, rows: (i, p.y, p.c, rows, cut.second(p.x)),
            lambda i, rows: self.y_in2[i, rows],
        )
        self.by_z = [
            self.links.start(
                grads.at[p.z_up[k], p.y, p.c, self.at, cut.half(p.x)],
                self.z_in.at[k - 1, self.here],
                p.to_z[k],
            )
            for k in range(1, 4)
        ]

    def step4(self):
        p, mine = self.p, self.cut.half(self.p.x)
        for copy in self.by_z:
            copy.wait_recv()

        def body(i, carry):
            first = pl.multiple_of(i * self.block, 16)
            rows = pl.ds(self.here0 + first, self.block)
            total = self.grads[p.z, p.y, p.c, pl.ds(self.at0 + first, self.block), mine].astype(
                jnp.float32
            )
            for k in range(3):
                total = total + self.z_in[k, rows].astype(jnp.float32)
            self.out[rows, mine] = total.astype(jnp.bfloat16)
            return carry

        lax.fori_loop(0, self.rows // self.block, body, 0)
        done = self.out.at[self.here, mine]
        self.last = self.links.start(done, done, p.to_x)

    def step5(self):
        self.last.wait_recv()

    def beat(self):
        getattr(self, "step" + str(self.stage))()
        self.stage += 1


def reduce_scratch(rows, cut, width):
    bf16 = jnp.bfloat16
    return [
        pltpu.VMEM((4, 2, rows, width), bf16),
        pltpu.VMEM((4, 2, rows, cut.two), bf16),
        pltpu.VMEM((2, 4, rows, cut.one), bf16),
        pltpu.VMEM((4, rows, cut.two), bf16),
        pltpu.VMEM((4, rows, cut.one), bf16),
        pltpu.VMEM((3, rows, cut.full), bf16),
    ]


class Total:
    copies = 6

    def __init__(self, value, core_in, x_in, y_in, by_z, place, links):
        self.value, self.core_in, self.x_in, self.y_in, self.by_z = value, core_in, x_in, y_in, by_z
        self.p, self.links = place, links
        self.stage = 0

    def step0(self):
        self.copy = self.links.start(self.value.at[0], self.core_in, self.p.to_c)

    def step1(self):
        self.copy.wait_recv()
        self.value[1] = self.value[0] + self.core_in[...]
        self.copy = self.links.start(self.value.at[1], self.x_in, self.p.to_x)

    def step2(self):
        self.copy.wait_recv()
        self.value[2] = self.value[1] + self.x_in[...]
        self.copy = self.links.start(self.value.at[2], self.y_in, self.p.to_y)

    def step3(self):
        self.copy.wait_recv()
        z = self.p.z
        self.by_z[z] = self.value[2] + self.y_in[...]
        self.spread = [
            self.links.start(self.by_z.at[z], self.by_z.at[z], self.p.to_z[k]) for k in range(1, 4)
        ]

    def step4(self):
        for copy in self.spread:
            copy.wait_recv()

    def step5(self):
        pass

    def sum(self):
        return ((self.by_z[0] + self.by_z[1]) + self.by_z[2]) + self.by_z[3]

    def beat(self):
        getattr(self, "step" + str(self.stage))()
        self.stage += 1


ROOT_HALF = 0.7071067811865476
DENSITY = 0.3989422804014327


def dot(left, right):
    return jnp.dot(left, right, preferred_element_type=jnp.float32)


def layer_kernel(s, *refs):
    (tokens, packed, teacher, order_row, order_col, length, valid) = refs[:7]
    (ordered_out, total_out, token_out, grads_out) = refs[7:11]
    (W, G, tok, qs, ks, vs, dO, stat, attn, n1, r1, low1, act, gp, acc, teach, res_in, low2, gains, sums) = refs[11:31]
    total_refs, (send, recv, local), scratch = refs[31:36], refs[36:39], refs[39:]
    f32, bf16 = jnp.float32, jnp.bfloat16
    span, width, shard, downs = s.span, s.width, s.shard, s.downs
    pairs = width // 128
    third = width // 3
    half = width // 2
    place = Place()
    x, xo = place.x, place.xo
    cut = s.cut
    links = Links(send, recv)

    def own(first, size):
        return pl.ds(pl.multiple_of(x * span + first, 16), size)

    def other(first, size):
        return pl.ds(pl.multiple_of(xo * span + first, 16), size)

    def loop(count, body):
        def step(i, carry):
            body(i)
            return carry

        lax.fori_loop(0, count, step, 0)

    def by_columns(first, n):
        cols = pl.ds(pl.multiple_of(n * third, 128), third)
        rows = pl.ds(pl.multiple_of(first, 16), shard)
        return W[:, :, :, rows, cols].reshape(width, third)

    def half_rows(first, m):
        rows = pl.ds(pl.multiple_of(first, 16), shard)
        return W[pl.ds(2 * m, 2), :, :, rows, :].reshape(half, width)

    def down_block(p, y):
        return W[p, y, :, s.down0 : s.down0 + downs, :].reshape(2 * downs, width)

    gathers = [
        Gather(pl.ds(a, b - a), cut, packed, W, place, links, local.at[i])
        for i, (a, b) in enumerate(s.gather_rows)
    ]
    n_gather = len(gathers)
    order = sorted(
        [(step + s.lag * i, i, step) for i in range(n_gather) for step in range(5)]
    )
    ready = [order.index(entry) for entry in order if entry[2] == 4]
    done = [0]

    def run_until(index):
        while done[0] <= index:
            entry = order[done[0]]
            getattr(gathers[entry[1]], "step" + str(entry[2]))()
            done[0] += 1

    def tick(count):
        run_until(min(done[0] + count, len(order)) - 1)

    place.barrier()
    own_tokens = pltpu.make_async_copy(tokens, tok.at[own(0, span)], local.at[n_gather])
    own_tokens.start()
    own_teacher = pltpu.make_async_copy(teacher, gp.at[0], local.at[n_gather + 1])
    own_teacher.start()
    run_until(0)
    send_tokens = links.start(tokens, tok.at[own(0, span)], place.to_x)
    length_now = length[0]
    iota_rows = lax.broadcasted_iota(jnp.int32, (s.block, span), 1)

    def pick(c):
        rows = pl.ds(pl.multiple_of(c * span + x * s.block, 16), s.block)
        position = order_col[rows, :] - x * span
        chosen = iota_rows == jnp.concatenate([position] * (span // 128), axis=1)
        return jnp.where(chosen, 1.0, 0.0).astype(bf16)

    own_teacher.wait()
    for n in range(3):
        cols = slice(n * third, (n + 1) * third)
        gp[1, : s.block, cols] = dot(pick(xo), gp[0, :, cols]).astype(bf16)
        teach[x, :, cols] = dot(pick(x), gp[0, :, cols]).astype(bf16)
    run_until(ready[0])
    teach_copy = links.start(gp.at[1, pl.ds(0, s.block)], teach.at[x], place.to_x)

    own_tokens.wait()

    def project(rows, which):
        def body(n):
            cols = pl.ds(pl.multiple_of(n * third, 128), third)
            for first, target, scale in which:
                value = dot(tok[rows, :], by_columns(first, n)).astype(bf16)
                target[rows, cols] = value * scale if scale != 1.0 else value

        loop(3, body)

    sets = ((0, qs, SCORE_SCALE), (shard, ks, 1.0), (2 * shard, vs, 1.0))
    project(own(0, span), sets)
    tick(s.tick_project)
    send_tokens.wait_recv()
    project(other(0, span), sets)
    tick(s.tick_project)

    lane = lax.broadcasted_iota(jnp.int32, (1, 128), 1)
    even32 = lane < HEAD_DIM
    even = jnp.where(even32, 1.0, 0.0).astype(bf16)
    odd = jnp.where(even32, 0.0, 1.0).astype(bf16)
    bias_row = jnp.where(order_row[0:1, :] < length_now, 0.0, MASKED)
    rows_q = s.rows_q

    def attend(pair):
        lanes = pl.ds(pair * 128, 128)

        def body(b):
            rows = own(b * rows_q, rows_q)
            query, key, value = qs[rows, lanes], ks[:, lanes], vs[:, lanes]
            tops, mixed = [], []
            for keep, rest in ((even, odd), (odd, even)):
                scores = (
                    lax.dot_general(
                        query * keep, key, (((1,), (1,)), ((), ())), preferred_element_type=f32
                    )
                    + bias_row
                )
                top = jnp.max(scores, axis=1, keepdims=True)
                weight = jnp.exp(scores - top).astype(bf16)
                tops.append(top)
                mixed.append(dot(weight, value * keep + rest))
            part = jnp.where(even32, mixed[0], mixed[1])
            total = pltpu.roll(jnp.where(even32, mixed[1], mixed[0]), HEAD_DIM, 1)
            out = pl.ds(pl.multiple_of(b * rows_q, 16), rows_q)
            attn[out, lanes] = (part / total).astype(bf16)
            log_total = jnp.where(even32, tops[0], tops[1]) + jnp.log(total)
            log_rows = log_total.T
            for h in range(2):
                stat[x, 0, pl.ds(2 * pair + h, 1), pl.ds(pl.multiple_of(b * rows_q, 128), rows_q)] = (
                    log_rows[h * HEAD_DIM : h * HEAD_DIM + 1, :]
                )

        loop(span // rows_q, body)

    for pair in range(pairs):
        attend(pair)
        tick(s.tick_attend)

    run_until(ready[1])
    device = lax.broadcasted_iota(jnp.int32, (16, width), 0)
    feature = lax.broadcasted_iota(jnp.int32, (16, width), 1)
    mine = (feature // shard) == device
    spread = jnp.where(
        lax.broadcasted_iota(jnp.int32, (128, width), 1) % shard
        == lax.broadcasted_iota(jnp.int32, (128, width), 0),
        1.0,
        0.0,
    ).astype(bf16)
    gain_rows = W[:, :, :, s.gain0 : s.gain0 + 16, :128].reshape(16, 16, 128).astype(f32)
    for g in range(2):
        wide = dot(gain_rows[:, g, :].astype(bf16), spread)
        gains[g : g + 1, :] = jnp.sum(jnp.where(mine, wide, 0.0), axis=0, keepdims=True)

    def branch(n):
        cols = pl.ds(pl.multiple_of(n * third, 128), third)
        acc[:, cols] = dot(attn[...], by_columns(s.out0, n))

    loop(3, branch)
    rows_n = s.rows_n

    def wide_column(column):
        return jnp.broadcast_to(column, (rows_n, 128))

    def first_norm(b):
        first = pl.multiple_of(b * rows_n, 16)
        rows = pl.ds(first, rows_n)
        hidden = tok[own(first, rows_n), :].astype(f32) + acc[rows, :]
        center = hidden - jnp.mean(hidden, axis=1, keepdims=True)
        inverse = lax.rsqrt(jnp.mean(center * center, axis=1, keepdims=True) + EPSILON)
        normal = center * inverse
        n1[rows, :] = normal
        r1[rows, :] = wide_column(inverse)
        low1[rows, :] = (normal * gains[0:1, :]).astype(bf16)

    loop(span // rows_n, first_norm)
    tick(s.tick_norm)

    teach_copy.wait_recv()
    links.sent(teach_copy)
    run_until(ready[s.up_ready])

    def upward(t):
        p, n = t // 3, t % 3
        cols = pl.ds(pl.multiple_of(n * third, 128), third)
        value = dot(low1[...], by_columns(s.up0 + p * shard, n))
        cdf = 0.5 * (1.0 + lax.erf(value * ROOT_HALF))
        act[p, :, cols] = (value * cdf).astype(bf16)
        gp[p, :, cols] = (cdf + value * (jnp.exp(-0.5 * value * value) * DENSITY)).astype(bf16)

    loop(3 * s.panels, upward)
    run_until(len(order) - 1)

    def downward(n):
        cols = pl.ds(pl.multiple_of(n * third, 128), third)
        value = None
        for p in range(s.panels):
            weight = W[p, :, :, s.down0 : s.down0 + downs, cols].reshape(width, third)
            part = dot(act[p], weight)
            value = part if value is None else value + part
        acc[:, cols] = value

    loop(3, downward)

    sums[...] = jnp.zeros_like(sums)
    valid_total = jnp.full((1, 1), valid[0], jnp.int32).astype(f32)
    grad_scale = s.tokens / valid_total

    def fold(values):
        return jnp.sum(values.reshape(rows_n // 8, 8, width), axis=0)

    def second_norm(b):
        first = pl.multiple_of(b * rows_n, 16)
        rows = pl.ds(first, rows_n)
        hidden = n1[rows, :] * gains[0:1, :] + acc[rows, :]
        center = hidden - jnp.mean(hidden, axis=1, keepdims=True)
        inverse = lax.rsqrt(jnp.mean(center * center, axis=1, keepdims=True) + EPSILON)
        normal = center * inverse
        gain = gains[1:2, :]
        result = (normal * gain).astype(bf16)
        per = s.block // rows_n
        at = pl.ds(pl.multiple_of((b % per) * rows_n, 16), rows_n)
        target = teach[b // per, at, :].astype(f32)
        teach[b // per, at, :] = result
        live = order_col[own(first, rows_n), 0:1] < length_now
        error = jnp.where(live, result.astype(f32) - target, 0.0)
        sums[2] += fold(error * error)
        grad = (error * grad_scale).astype(bf16).astype(f32)
        sums[1] += fold(grad * normal)
        scaled = grad * gain
        grad_sum = inverse * (
            scaled
            - jnp.mean(scaled, axis=1, keepdims=True)
            - normal * jnp.mean(scaled * normal, axis=1, keepdims=True)
        )
        acc[rows, :] = grad_sum
        low2[rows, :] = grad_sum.astype(bf16)

    loop(span // rows_n, second_norm)
    links.drain()
    links.all = []
    send_result = links.start(teach.at[xo], res_in, place.to_x)
    total_refs[0][0] = jnp.broadcast_to(
        jnp.sum(jnp.sum(sums[2], axis=0, keepdims=True), axis=1, keepdims=True), (8, 128)
    )
    total = Total(*total_refs, place, links)

    waiting, active = [total], []

    def beat():
        for item in list(active):
            item.beat()
            if item.stage > 5:
                active.remove(item)
        if waiting:
            item = waiting.pop(0)
            item.beat()
            active.append(item)

    def enter(name):
        for a, b in s.reduce_rows[name]:
            in_weights = name == "last"
            waiting.append(
                Reduce(
                    b - a,
                    a + s.down0 if in_weights else a - s.out0,
                    a,
                    cut,
                    W if in_weights else G,
                    grads_out,
                    place,
                    links,
                    scratch,
                )
            )

    def turned(left, right):
        return lax.dot_general(left, right, (((0,), (0,)), ((), ())), preferred_element_type=f32)

    def by_turned(left, right):
        return lax.dot_general(left, right, (((1,), (1,)), ((), ())), preferred_element_type=f32)

    def down_grad(t):
        p, y = t // 2, t % 2
        cols = pl.ds(pl.multiple_of(y * half, 128), half)
        value = turned(act[p, :, cols], low2[...]).astype(bf16)
        G[p, y, :, s.down0 - s.out0 : s.down0 - s.out0 + downs, :] = value.reshape(2, downs, width)

    loop(2 * s.panels, down_grad)
    enter("down")
    beat()
    beat()

    def active_grad(t):
        p, y = t // 2, t % 2
        cols = pl.ds(pl.multiple_of(y * half, 128), half)
        value = by_turned(low2[...], down_block(p, y))
        gp[p, :, cols] = (value * gp[p, :, cols].astype(f32)).astype(bf16)

    loop(2 * s.panels, active_grad)
    beat()

    def put_grad(first, m, value):
        rows = pl.ds(pl.multiple_of(first, 16), shard)
        return (pl.ds(2 * m, 2), slice(None), slice(None), rows, slice(None)), value.astype(
            bf16
        ).reshape(2, 2, 2, shard, width)

    def up_grad(t):
        m, p = t // s.panels, t % s.panels
        cols = pl.ds(pl.multiple_of(m * half, 128), half)
        where, value = put_grad(
            s.up0 - s.out0 + p * shard, m, turned(low1[:, cols], gp[p])
        )
        G[where] = value

    loop(2 * s.panels, up_grad)
    enter("up")
    beat()

    def normed_grad(m):
        cols = pl.ds(pl.multiple_of(m * half, 128), half)
        value = acc[:, cols]
        for p in range(s.panels):
            value = value + by_turned(gp[p], half_rows(s.up0 + p * shard, m))
        acc[:, cols] = value

    loop(2, normed_grad)
    beat()

    def first_back(b):
        rows = pl.ds(pl.multiple_of(b * rows_n, 16), rows_n)
        grad, normal = acc[rows, :], n1[rows, :]
        sums[0] += fold(grad * normal)
        scaled = grad * gains[0:1, :]
        hidden_grad = r1[rows, 0:1] * (
            scaled
            - jnp.mean(scaled, axis=1, keepdims=True)
            - normal * jnp.mean(scaled * normal, axis=1, keepdims=True)
        )
        acc[rows, :] = hidden_grad
        low2[rows, :] = hidden_grad.astype(bf16)

    loop(span // rows_n, first_back)

    def attn_grad(m):
        cols = pl.ds(pl.multiple_of(m * half, 128), half)
        dO[own(0, span), cols] = by_turned(low2[...], half_rows(s.out0, m)).astype(bf16)

    loop(2, attn_grad)
    head = lax.broadcasted_iota(jnp.int32, (16, width), 0)
    in_head = jnp.where((feature // HEAD_DIM) == head, 1.0, 0.0)

    def head_delta(b):
        first = pl.multiple_of(b * 128, 128)
        rows = pl.ds(first, 128)
        product = dO[own(first, 128), :].astype(f32) * attn[rows, :].astype(f32)
        stat[x, 1, :, rows] = lax.dot_general(
            in_head,
            product,
            (((1,), (1,)), ((), ())),
            precision=lax.Precision.HIGHEST,
            preferred_element_type=f32,
        )

    loop(span // 128, head_delta)
    send_grad = links.start(dO.at[own(0, span)], dO.at[own(0, span)], place.to_x)
    send_stat = links.start(stat.at[x], stat.at[x], place.to_x)

    def out_grad(m):
        cols = pl.ds(pl.multiple_of(m * half, 128), half)
        where, value = put_grad(0, m, turned(attn[:, cols], low2[...]))
        G[where] = value

    loop(2, out_grad)
    pieces = []
    for g in range(2):
        row = jnp.sum(sums[g], axis=0, keepdims=True)
        split = jnp.where(mine, jnp.broadcast_to(row, (16, width)), 0.0).astype(bf16)
        pieces.append(by_turned(split, spread))
    at_row = lax.broadcasted_iota(jnp.int32, (16, 16, 128), 1)
    gain_block = jnp.where(
        at_row == 0, pieces[0][:, None, :], jnp.where(at_row == 1, pieces[1][:, None, :], 0.0)
    ).astype(bf16)
    G[:, :, :, shard : shard + 16, :128] = gain_block.reshape(4, 2, 2, 16, 128)
    G[:, :, :, shard : shard + 16, 128:] = jnp.zeros((4, 2, 2, 16, width - 128), bf16)
    enter("out")
    beat()

    rows_k = s.rows_k

    def block_terms(key, value, bias, query, grad, log_row, delta_row):
        scores = by_turned(key, query) + bias
        p = jnp.exp(scores - log_row)
        score_grad = (p * (by_turned(value, grad) - delta_row)).astype(bf16)
        return p.astype(bf16), score_grad

    def key_bias(rows):
        column = jnp.where(order_col[rows, :] < length_now, 0.0, MASKED)
        return jnp.concatenate([column] * (span // 128), axis=1)

    def back_other(pair):
        lanes = pl.ds(pair * 128, 128)

        def body(b):
            rows = other(b * rows_k, rows_k)
            key, value, bias = ks[rows, lanes], vs[rows, lanes], key_bias(rows)
            query, grad = qs[own(0, span), lanes], dO[own(0, span), lanes]
            result = jnp.zeros((span, 128), f32)
            for h, keep in enumerate((even, odd)):
                at = pl.ds(2 * pair + h, 1)
                p, score_grad = block_terms(
                    key, value, bias, query * keep, grad * keep, stat[x, 0, at, :], stat[x, 1, at, :]
                )
                result = result + turned(score_grad, key * keep)
            n1[:, lanes] += result

        n1[:, lanes] = jnp.zeros((span, 128), f32)
        loop(span // rows_k, body)

    def back_own(pair):
        lanes = pl.ds(pair * 128, 128)

        def body(b):
            first = pl.multiple_of(b * rows_k, 16)
            rows = own(first, rows_k)
            key, value, bias = ks[rows, lanes], vs[rows, lanes], key_bias(rows)
            result = jnp.zeros((span, 128), f32)
            key_grad = jnp.zeros((rows_k, 128), f32)
            value_grad = jnp.zeros((rows_k, 128), f32)
            for side in (x, xo):
                whole = pl.ds(pl.multiple_of(side * span, 16), span)
                query, grad = qs[whole, lanes], dO[whole, lanes]
                for h, keep in enumerate((even, odd)):
                    at = pl.ds(2 * pair + h, 1)
                    query_h, grad_h = query * keep, grad * keep
                    p, score_grad = block_terms(
                        key, value, bias, query_h, grad_h, stat[side, 0, at, :], stat[side, 1, at, :]
                    )
                    value_grad = value_grad + dot(p, grad_h)
                    key_grad = key_grad + dot(score_grad, query_h)
                    if side is x:
                        result = result + turned(score_grad, key * keep)
            out = pl.ds(first, rows_k)
            n1[:, lanes] += result
            act[1, out, lanes] = key_grad.astype(bf16)
            act[2, out, lanes] = value_grad.astype(bf16)

        loop(span // rows_k, body)
        act[0, :, lanes] = (n1[:, lanes] * SCORE_SCALE).astype(bf16)

    for pair in range(pairs):
        back_other(pair)
        if pair in s.beats_other:
            beat()
    send_grad.wait_recv()
    send_stat.wait_recv()
    for pair in range(pairs):
        back_own(pair)
        if pair in s.beats_own:
            beat()

    def weight_grad(t):
        j, m = t // 2, t % 2
        cols = pl.ds(pl.multiple_of(m * half, 128), half)
        where, value = put_grad(s.down0 + j * shard, m, turned(tok[own(0, span), cols], act[j]))
        W[where] = value

    loop(6, weight_grad)
    enter("last")
    beat()

    def input_grad(m):
        cols = pl.ds(pl.multiple_of(m * half, 128), half)
        value = acc[:, cols]
        for j in range(3):
            value = value + by_turned(act[j], half_rows(j * shard, m))
        acc[:, cols] = value

    loop(2, input_grad)
    token_copy = pltpu.make_async_copy(acc, token_out, local.at[n_gather])
    token_copy.start()
    beat()
    send_result.wait_recv()

    def place_rows(n):
        cols = pl.ds(pl.multiple_of(n * third, 128), third)
        value = None
        position = lax.broadcasted_iota(jnp.int32, (span, s.block), 0) + x * span
        for c, rows in ((x, teach[x, :, cols]), (xo, res_in[:, cols])):
            at = order_row[0:1, pl.ds(pl.multiple_of(c * span + x * s.block, 128), s.block)]
            chosen = jnp.where(position == at, 1.0, 0.0).astype(bf16)
            part = dot(chosen, rows)
            value = part if value is None else value + part
        low2[:, cols] = value.astype(bf16)

    loop(3, place_rows)
    ordered_copy = pltpu.make_async_copy(low2, ordered_out, local.at[n_gather + 1])
    ordered_copy.start()
    while waiting or active:
        beat()
    total_out[...] = total.sum()
    token_copy.wait()
    ordered_copy.wait()
    links.drain()


class Sizes:
    def __init__(self, span, width, ff, shard, downs, tokens):
        self.span, self.width, self.shard, self.downs, self.tokens = span, width, shard, downs, tokens
        self.panels = ff // width
        self.block = span // 2
        self.out0 = 3 * shard
        self.gain0 = 4 * shard
        self.up0 = self.gain0 + 16
        self.down0 = self.up0 + self.panels * shard
        self.rows = self.down0 + downs
        self.cut = Cut(width, 2 * (width // 6))
        self.lag = 1.01
        up_half = self.up0 + self.panels // 2 * shard
        up_end = self.down0
        self.gather_rows = (
            (0, self.out0),
            (self.out0, up_half),
            (up_half, up_end),
            (up_end, up_end + downs // 2),
            (up_end + downs // 2, self.rows),
        )
        self.up_ready = 2
        self.reduce_rows = {
            "down": ((up_end, up_end + downs // 2), (up_end + downs // 2, self.rows)),
            "up": ((self.up0, up_half), (up_half, up_end)),
            "out": ((self.out0, self.up0),),
            "last": ((0, shard), (shard, self.out0)),
        }
        self.tick_project, self.tick_attend, self.tick_norm = 1, 2, 1
        self.rows_q, self.rows_n, self.rows_k = 128, 64, 256
        self.beats_other, self.beats_own = (1, 3, 5), (0, 1, 2, 3, 4, 5)


def layer(s, tokens, packed, teacher, order_row, order_col, length, valid):
    bf16, f32 = jnp.bfloat16, jnp.float32
    span, width = s.span, s.width
    both = 2 * span
    anywhere = pl.BlockSpec(memory_space=pl.ANY)
    vmem = pl.BlockSpec(memory_space=pltpu.VMEM)
    smem = pl.BlockSpec(memory_space=pltpu.SMEM)
    reduces = sum(len(v) for v in s.reduce_rows.values())
    copies = (
        Gather.copies * len(s.gather_rows) + Reduce.copies * reduces + Total.copies + 6
    )
    small = pltpu.VMEM((8, 128), f32)
    scratch = [
        pltpu.VMEM((4, 2, 2, s.rows, width), bf16),
        pltpu.VMEM((4, 2, 2, s.rows - s.out0, width), bf16),
        pltpu.VMEM((both, width), bf16),
        pltpu.VMEM((both, width), bf16),
        pltpu.VMEM((both, width), bf16),
        pltpu.VMEM((both, width), bf16),
        pltpu.VMEM((both, width), bf16),
        pltpu.VMEM((2, 2, 16, span), f32),
        pltpu.VMEM((span, width), bf16),
        pltpu.VMEM((span, width), f32),
        pltpu.VMEM((span, 128), f32),
        pltpu.VMEM((span, width), bf16),
        pltpu.VMEM((s.panels, span, width), bf16),
        pltpu.VMEM((s.panels, span, width), bf16),
        pltpu.VMEM((span, width), f32),
        pltpu.VMEM((2, s.block, width), bf16),
        pltpu.VMEM((s.block, width), bf16),
        pltpu.VMEM((span, width), bf16),
        pltpu.VMEM((8, width), f32),
        pltpu.VMEM((3, 8, width), f32),
        pltpu.VMEM((3, 8, 128), f32),
        small,
        small,
        small,
        pltpu.VMEM((4, 8, 128), f32),
        pltpu.SemaphoreType.DMA((copies,)),
        pltpu.SemaphoreType.DMA((copies,)),
        pltpu.SemaphoreType.DMA((len(s.gather_rows) + 2,)),
    ] + reduce_scratch(s.rows, s.cut, width)
    return pl.pallas_call(
        functools.partial(layer_kernel, s),
        out_shape=[
            jax.ShapeDtypeStruct((span, width), bf16),
            jax.ShapeDtypeStruct((8, 128), f32),
            jax.ShapeDtypeStruct((span, width), f32),
            jax.ShapeDtypeStruct((s.rows, width), bf16),
        ],
        in_specs=[anywhere, anywhere, anywhere, vmem, vmem, smem, smem],
        out_specs=[anywhere, vmem, anywhere, vmem],
        scratch_shapes=scratch,
        compiler_params=pltpu.CompilerParams(
            collective_id=0, has_side_effects=True, vmem_limit_bytes=s.vmem
        ),
    )(tokens, packed, teacher, order_row, order_col, length, valid)


def fused_shards(
    tokens,
    w_query,
    w_key,
    w_value,
    w_out,
    w_up,
    w_down,
    gain_attn,
    gain_ffn,
    teacher,
    seq_lengths,
    tok_perm,
    valid_count,
):
    f32 = jnp.float32
    dp_count = lax.axis_size("dp")
    span, width = tokens.shape[1:]
    shard, ff = w_up.shape
    seq_len = tok_perm.shape[1]
    s = Sizes(span, width, ff, shard, w_down.shape[0], seq_len * dp_count)
    s.vmem = 63 * MIB
    gain_rows = jnp.pad(jnp.stack([gain_attn, gain_ffn]), ((0, 14), (0, width - shard)))
    up_rows = jnp.transpose(w_up.reshape(shard, s.panels, width), (1, 0, 2)).reshape(-1, width)
    packed = jnp.concatenate([w_query, w_key, w_value, w_out, gain_rows, up_rows, w_down])
    order = tok_perm[0]
    ordered, total, token_grad, grads = layer(
        s,
        tokens[0],
        packed,
        teacher[0],
        jnp.broadcast_to(order[None, :], (8, seq_len)),
        jnp.broadcast_to(order[:, None], (seq_len, 128)),
        seq_lengths,
        valid_count,
    )
    loss = (total[0, 0] / (2.0 * width * valid_count[0].astype(f32))).reshape(1)
    grads = grads.astype(f32)
    up = grads[s.up0 : s.down0].reshape(s.panels, shard, width)
    return (
        ordered[None],
        loss,
        token_grad[None],
        grads[:shard],
        grads[shard : 2 * shard],
        grads[2 * shard : 3 * shard],
        grads[s.out0 : s.gain0],
        jnp.transpose(up, (1, 0, 2)).reshape(shard, ff),
        grads[s.down0 :],
        grads[s.gain0, :shard],
        grads[s.gain0 + 1, :shard],
    )


def solution(mesh):
    in_specs = (
        P("dp", "ctx", None),
        P("dp", None),
        P("dp", None),
        P("dp", None),
        P("dp", None),
        P("dp", None),
        P("dp", None),
        P("dp"),
        P("dp"),
        P("dp", "ctx", None),
        P("dp"),
        P("dp", None),
        P(),
    )
    out_specs = (
        P("dp", "ctx", None),
        P(),
        P("dp", "ctx", None),
        P("dp", None),
        P("dp", None),
        P("dp", None),
        P("dp", None),
        P("dp", None),
        P("dp", None),
        P("dp"),
        P("dp"),
    )
    body = fused_shards if dict(mesh.shape) == {"dp": 16, "ctx": 2} else shards
    return jax.shard_map(body, mesh=mesh, in_specs=in_specs, out_specs=out_specs, check_vma=False)
```

```python
import functools
import math

import jax
import jax.numpy as jnp
from jax import lax
from jax.experimental import pallas as pl
from jax.experimental.pallas import tpu as pltpu
from jax.sharding import PartitionSpec as P

HEAD_DIM = 64


EPSILON = 1e-06
SCORE_SCALE = 0.125
MASKED = -1e30
MESH = pl.DeviceIdType.MESH
MIB = 1024 * 1024


GATHER_SPLIT = (3, 4, 5, 6, 7, 8, 9)
EARLY = 3
FORWARD = ((0, 1, 2, 3, 4, 5, 6, 7, 8, 9, 10, 11), (), (0, 0, 0, 1, 2, 1, 1, 3, 2, 2), (3, 4, 5), (6,), (3, 4, 7, 3), (5, 6, 8, 9), (4, 7, 10, 4), (5,), (5, 6, 8, 10, 9, 6, 11), (7, 10), (), (7, 8), (8, 11), (), (9, 11), (), (), (), (9,), (), (), (), (), (), (), (), (), (), ())
BACKWARD = ((0, 1), (0, 2), (1, 3), (2, 4), (3,), (0, 4, 5), (1,), (5, 6), (), (7,), (2, 6, 7, 1), (8,), (0, 1, 3, 8), (0, 2), (4, 9), (2, 3), (9, 5), (), (4,), (), (6,), (3, 4, 5, 6, 7, 8), (5, 6, 10), (9, 7, 10), (7, 11), (8, 11, 10), (8, 9, 12), (11, 12, 9), (10,), (10, 11, 12, 11, 12, 12))


def gelu_exact(values):
    return 0.5 * values * (1.0 + lax.erf(values * 0.7071067811865476))


def norm_forward(hidden, gain_row):
    center = hidden - jnp.mean(hidden, axis=-1, keepdims=True)
    inverse = lax.rsqrt(jnp.mean(center * center, axis=-1, keepdims=True) + EPSILON)
    normal = center * inverse
    return (normal * gain_row, normal, inverse)


def norm_backward(grad_norm, gain_row, normal, inverse):
    scaled = grad_norm * gain_row
    grad_input = inverse * (
        scaled
        - jnp.mean(scaled, axis=-1, keepdims=True)
        - normal * jnp.mean(scaled * normal, axis=-1, keepdims=True)
    )
    return (grad_input, jnp.sum(grad_norm * normal, axis=0))


def row_product(left_mat, right_mat):
    return lax.dot_general(
        left_mat, right_mat, (((0,), (0,)), ((), ())), preferred_element_type=jnp.float32
    )


def by_transpose(left_mat, right_mat):
    return lax.dot_general(
        left_mat, right_mat, (((1,), (1,)), ((), ())), preferred_element_type=jnp.float32
    )


def shards(
    tokens,
    w_query,
    w_key,
    w_value,
    w_out,
    w_up,
    w_down,
    gain_attn,
    gain_ffn,
    teacher,
    seq_lengths,
    tok_perm,
    valid_count,
):
    ctx_count = lax.axis_size("ctx")
    ctx_rank = lax.axis_index("ctx")
    dp_count = lax.axis_size("dp")
    layer_in = tokens[0]
    span_rows, model_width = layer_in.shape
    head_count = model_width // HEAD_DIM
    dealt_order = tok_perm[0]
    seq_len = dealt_order.shape[0]
    length = seq_lengths[0]
    keep_all = dealt_order < length
    per_peer = span_rows // ctx_count
    query_weight, key_weight, value_weight, out_weight, gain_first = (
        lax.all_gather(w_query, "dp", axis=0, tiled=True),
        lax.all_gather(w_key, "dp", axis=0, tiled=True),
        lax.all_gather(w_value, "dp", axis=0, tiled=True),
        lax.all_gather(w_out, "dp", axis=0, tiled=True),
        lax.all_gather(gain_attn, "dp", axis=0, tiled=True),
    )
    up_weight, down_weight, gain_second = (
        lax.all_gather(w_up, "dp", axis=0, tiled=True),
        lax.all_gather(w_down, "dp", axis=0, tiled=True),
        lax.all_gather(gain_ffn, "dp", axis=0, tiled=True),
    )
    queries = jnp.dot(layer_in, query_weight, preferred_element_type=jnp.float32).astype(
        jnp.bfloat16
    )
    keys_own = jnp.dot(layer_in, key_weight, preferred_element_type=jnp.float32).astype(
        jnp.bfloat16
    )
    values_own = jnp.dot(layer_in, value_weight, preferred_element_type=jnp.float32).astype(
        jnp.bfloat16
    )
    query_heads = queries.reshape(span_rows, head_count, HEAD_DIM)
    initial = (
        jnp.full((head_count, span_rows), MASKED, jnp.float32),
        jnp.zeros((head_count, span_rows), jnp.float32),
        jnp.zeros((head_count, span_rows, HEAD_DIM), jnp.float32),
    )
    fold_state = initial
    key_piece = lax.all_gather(keys_own, "ctx", axis=0, tiled=True)
    value_piece = lax.all_gather(values_own, "ctx", axis=0, tiled=True)
    piece_rows = key_piece.shape[0]
    block_rows = math.gcd(piece_rows, span_rows)
    key_blocks = key_piece.reshape(piece_rows // block_rows, block_rows, head_count, HEAD_DIM)
    value_blocks = value_piece.reshape(piece_rows // block_rows, block_rows, head_count, HEAD_DIM)

    def step_block(block_state, block_item):
        running_max, running_sum, accumulated = block_state
        key_block, value_block, block_index = block_item
        key_keep = lax.dynamic_slice_in_dim(keep_all, block_index * block_rows, block_rows)
        scores = (
            jnp.einsum("qhe,khe->hqk", query_heads, key_block, preferred_element_type=jnp.float32)
            * SCORE_SCALE
        )
        scores = jnp.where(key_keep[None, None, :], scores, MASKED)
        new_max = jnp.maximum(running_max, jnp.max(scores, axis=-1))
        factor = jnp.exp(running_max - new_max)
        soft_weights = jnp.where(key_keep[None, None, :], jnp.exp(scores - new_max[..., None]), 0.0)
        running_sum = running_sum * factor + jnp.sum(soft_weights, axis=-1)
        accumulated = accumulated * factor[..., None] + jnp.einsum(
            "hqk,khe->hqe",
            soft_weights.astype(jnp.bfloat16),
            value_block,
            preferred_element_type=jnp.float32,
        )
        return ((new_max, running_sum, accumulated), None)

    block_indices = jnp.arange(piece_rows // block_rows, dtype=jnp.int32)
    fold_state, unused = lax.scan(step_block, fold_state, (key_blocks, value_blocks, block_indices))
    run_max, run_sum, accumulated = fold_state
    log_total = run_max + jnp.log(run_sum)
    attn_full = jnp.transpose(accumulated / run_sum[..., None], (1, 0, 2)).reshape(
        span_rows, model_width
    )
    attn_low = attn_full.astype(jnp.bfloat16)
    gain_first32 = gain_first.astype(jnp.float32)
    gain_second32 = gain_second.astype(jnp.float32)
    branch = jnp.dot(attn_low, out_weight, preferred_element_type=jnp.float32)
    normed, normal_first, inverse_first = norm_forward(
        layer_in.astype(jnp.float32) + branch, gain_first32
    )
    normed_low = normed.astype(jnp.bfloat16)
    upward = jnp.dot(normed_low, up_weight, preferred_element_type=jnp.float32)
    active, gelu_pull = jax.vjp(gelu_exact, upward)
    active_low = active.astype(jnp.bfloat16)
    down_out = jnp.dot(active_low, down_weight, preferred_element_type=jnp.float32)
    result, normal_second, inverse_second = norm_forward(normed + down_out, gain_second32)
    result_low = result.astype(jnp.bfloat16)
    arrived = lax.all_to_all(result_low, "ctx", split_axis=0, concat_axis=0, tiled=True)
    sources = (
        jnp.arange(ctx_count, dtype=jnp.int32)[:, None] * span_rows
        + ctx_rank * per_peer
        + jnp.arange(per_peer, dtype=jnp.int32)[None, :]
    ).reshape(span_rows)
    local_pos = jnp.take(dealt_order, sources) - ctx_rank * span_rows
    in_order = jnp.zeros_like(arrived).at[local_pos].set(arrived)
    target = teacher[0].astype(jnp.float32)
    live_rows = (ctx_rank * span_rows + jnp.arange(span_rows, dtype=jnp.int32) < length)[:, None]
    residual_err = jnp.where(live_rows, in_order.astype(jnp.float32) - target, 0.0)
    total_sq = lax.psum(jnp.sum(residual_err * residual_err), ("dp", "ctx"))
    valid_total = valid_count[0].astype(jnp.float32)
    loss_value = (total_sq / (2.0 * model_width * valid_total)).reshape(1)
    grad_scale = seq_len * dp_count / valid_total
    grad_order = (residual_err * grad_scale).astype(jnp.bfloat16)
    outgoing = jnp.take(grad_order, local_pos, axis=0)
    grad_result = lax.all_to_all(outgoing, "ctx", split_axis=0, concat_axis=0, tiled=True).astype(
        jnp.float32
    )
    grad_sum_second, grad_gain_second = norm_backward(
        grad_result, gain_second32, normal_second, inverse_second
    )
    down_grad_low = grad_sum_second.astype(jnp.bfloat16)
    grad_down_w = row_product(active_low, down_grad_low)
    grad_active = by_transpose(down_grad_low, down_weight)
    grad_upward = gelu_pull(grad_active)[0].astype(jnp.bfloat16)
    grad_up_w = row_product(normed_low, grad_upward)
    grad_normed = grad_sum_second + by_transpose(grad_upward, up_weight)
    grad_hidden, grad_gain_first = norm_backward(
        grad_normed, gain_first32, normal_first, inverse_first
    )
    branch_grad = grad_hidden.astype(jnp.bfloat16)
    grad_out_w = row_product(attn_low, branch_grad)
    attn_grad_low = by_transpose(branch_grad, out_weight).astype(jnp.bfloat16)
    grad_heads = attn_grad_low.reshape(span_rows, head_count, HEAD_DIM)
    row_delta = jnp.sum(
        (attn_grad_low.astype(jnp.float32) * attn_full).reshape(span_rows, head_count, HEAD_DIM),
        axis=-1,
    ).T
    keys_all, values_all = (
        lax.all_gather(keys_own, "ctx", axis=0, tiled=True),
        lax.all_gather(values_own, "ctx", axis=0, tiled=True),
    )
    blocks_count = seq_len // span_rows
    key_stack = keys_all.reshape(blocks_count, span_rows, head_count, HEAD_DIM)
    value_stack = values_all.reshape(blocks_count, span_rows, head_count, HEAD_DIM)

    def score_terms(
        query_block, grad_block, total_block, delta_block, key_block, value_block, key_keep
    ):
        scores = (
            jnp.einsum("qhe,khe->hqk", query_block, key_block, preferred_element_type=jnp.float32)
            * SCORE_SCALE
        )
        soft_weights = jnp.where(
            key_keep[None, None, :], jnp.exp(scores - total_block[..., None]), 0.0
        )
        prob_grad = jnp.einsum(
            "qhe,khe->hqk", grad_block, value_block, preferred_element_type=jnp.float32
        )
        score_grad = (soft_weights * (prob_grad - delta_block[..., None])).astype(jnp.bfloat16)
        return (soft_weights, score_grad)

    def back_block(query_grad, block_item):
        key_block, value_block, block_index = block_item
        key_keep = lax.dynamic_slice_in_dim(keep_all, block_index * span_rows, span_rows)
        soft_weights, score_grad = score_terms(
            query_heads, grad_heads, log_total, row_delta, key_block, value_block, key_keep
        )
        value_grad = jnp.einsum(
            "hqk,qhe->khe",
            soft_weights.astype(jnp.bfloat16),
            grad_heads,
            preferred_element_type=jnp.float32,
        )
        query_grad = query_grad + SCORE_SCALE * jnp.einsum(
            "hqk,khe->qhe", score_grad, key_block, preferred_element_type=jnp.float32
        )
        key_grad = SCORE_SCALE * jnp.einsum(
            "hqk,qhe->khe", score_grad, query_heads, preferred_element_type=jnp.float32
        )
        return (query_grad, (key_grad, value_grad))

    query_grad, (key_grads, value_grads) = lax.scan(
        back_block,
        jnp.zeros((span_rows, head_count, HEAD_DIM), jnp.float32),
        (key_stack, value_stack, jnp.arange(blocks_count, dtype=jnp.int32)),
    )
    key_grad_sum, value_grad_sum = (
        lax.psum_scatter(
            key_grads.reshape(seq_len, model_width).astype(jnp.bfloat16),
            "ctx",
            scatter_dimension=0,
            tiled=True,
        ).astype(jnp.float32),
        lax.psum_scatter(
            value_grads.reshape(seq_len, model_width).astype(jnp.bfloat16),
            "ctx",
            scatter_dimension=0,
            tiled=True,
        ).astype(jnp.float32),
    )
    query_grad_low = query_grad.reshape(span_rows, model_width).astype(jnp.bfloat16)
    key_grad_low = key_grad_sum.astype(jnp.bfloat16)
    value_grad_low = value_grad_sum.astype(jnp.bfloat16)
    grad_query_w = row_product(layer_in, query_grad_low)
    grad_key_w = row_product(layer_in, key_grad_low)
    grad_value_w = row_product(layer_in, value_grad_low)
    token_grad = (
        grad_hidden
        + by_transpose(query_grad_low, query_weight)
        + by_transpose(key_grad_low, key_weight)
        + by_transpose(value_grad_low, value_weight)
    )
    up_part, down_part, second_part = (
        lax.psum_scatter(
            grad_up_w.astype(jnp.bfloat16), "dp", scatter_dimension=0, tiled=True
        ).astype(jnp.float32),
        lax.psum_scatter(
            grad_down_w.astype(jnp.bfloat16), "dp", scatter_dimension=0, tiled=True
        ).astype(jnp.float32),
        lax.psum_scatter(
            grad_gain_second.astype(jnp.bfloat16), "dp", scatter_dimension=0, tiled=True
        ).astype(jnp.float32),
    )
    query_part, key_part, value_part, out_part, first_part = (
        lax.psum_scatter(
            grad_query_w.astype(jnp.bfloat16), "dp", scatter_dimension=0, tiled=True
        ).astype(jnp.float32),
        lax.psum_scatter(
            grad_key_w.astype(jnp.bfloat16), "dp", scatter_dimension=0, tiled=True
        ).astype(jnp.float32),
        lax.psum_scatter(
            grad_value_w.astype(jnp.bfloat16), "dp", scatter_dimension=0, tiled=True
        ).astype(jnp.float32),
        lax.psum_scatter(
            grad_out_w.astype(jnp.bfloat16), "dp", scatter_dimension=0, tiled=True
        ).astype(jnp.float32),
        lax.psum_scatter(
            grad_gain_first.astype(jnp.bfloat16), "dp", scatter_dimension=0, tiled=True
        ).astype(jnp.float32),
    )
    summed = (
        lax.psum(query_part.astype(jnp.bfloat16), "ctx").astype(jnp.float32),
        lax.psum(key_part.astype(jnp.bfloat16), "ctx").astype(jnp.float32),
        lax.psum(value_part.astype(jnp.bfloat16), "ctx").astype(jnp.float32),
        lax.psum(out_part.astype(jnp.bfloat16), "ctx").astype(jnp.float32),
        lax.psum(up_part.astype(jnp.bfloat16), "ctx").astype(jnp.float32),
        lax.psum(down_part.astype(jnp.bfloat16), "ctx").astype(jnp.float32),
        lax.psum(first_part.astype(jnp.bfloat16), "ctx").astype(jnp.float32),
        lax.psum(second_part.astype(jnp.bfloat16), "ctx").astype(jnp.float32),
    )
    query_sum, key_sum, value_sum, out_sum, up_sum, down_sum, first_sum, second_sum = summed
    return (
        in_order[None],
        loss_value,
        token_grad[None],
        query_sum,
        key_sum,
        value_sum,
        out_sum,
        up_sum,
        down_sum,
        first_sum,
        second_sum,
    )


class Place:
    def __init__(self):
        dp = lax.axis_index("dp")
        self.x = lax.axis_index("ctx")
        self.z, self.y, self.c = dp // 4, (dp // 2) % 2, dp % 2
        self.xo, self.yo, self.co = 1 - self.x, 1 - self.y, 1 - self.c
        self.to_x = (dp, self.xo)
        self.to_y = (self.z * 4 + self.yo * 2 + self.c, self.x)
        self.to_c = (self.z * 4 + self.y * 2 + self.co, self.x)
        self.z_up = [(self.z + k) % 4 for k in range(4)]
        self.z_down = [(self.z + 4 - k) % 4 for k in range(4)]
        self.to_z = [(self.z_up[k] * 4 + self.y * 2 + self.c, self.x) for k in range(4)]

    def barrier(self):
        semaphore = pltpu.get_barrier_semaphore()
        for partner in [self.to_x, self.to_y, self.to_c] + self.to_z[1:]:
            pl.semaphore_signal(semaphore, inc=1, device_id=partner, device_id_type=MESH)
        pl.semaphore_wait(semaphore, 6)


class Links:
    def __init__(self, send, recv):
        self.send, self.recv, self.used, self.all = send, recv, 0, []

    def start(self, src, dst, partner):
        at = self.used
        self.used += 1
        copy = pltpu.make_async_remote_copy(
            src_ref=src,
            dst_ref=dst,
            send_sem=self.send.at[at],
            recv_sem=self.recv.at[at],
            device_id=partner,
            device_id_type=MESH,
        )
        copy.start()
        self.all.append(copy)
        return copy

    def sent(self, copy):
        copy.wait_send()
        self.all = [other for other in self.all if other is not copy]

    def drain(self):
        for copy in self.all:
            copy.wait_send()
        self.all = []


class Gather:
    copies = 20

    def __init__(self, block, early, shard, whole, place, links, own_sem):
        first, last, self.split = block[:3]
        self.early = early
        self.rows = pl.ds(first, last - first)
        self.width = block[3] if len(block) > 3 else whole.shape[-1]
        self.shard, self.whole = shard, whole
        self.p, self.links = place, links
        self.own = pltpu.make_async_copy(
            shard.at[self.rows, self.cols()],
            whole.at[place.z, place.y, place.c, self.rows, self.cols()],
            own_sem,
        )
        self.last = 4 if self.split else 3

    def cols(self):
        return pl.ds(0, self.width)

    def half(self, x):
        if not self.split:
            return self.cols()
        size = self.width // 2
        return pl.ds(pl.multiple_of(x * size, 128), size)

    def piece(self, z, y, cols):
        return self.whole.at[z, y, self.p.c, self.rows, cols]

    def push(self, piece, partner):
        return self.links.start(piece, piece, partner)

    def step0(self):
        p = self.p
        mine = self.half(p.x)
        source, target = self.shard.at[self.rows, mine], self.piece(p.z, p.y, mine)
        self.from_z = [self.links.start(source, target, p.to_z[k]) for k in range(1, 4)]
        self.own.start()
        if self.early:
            self.spread()

    def spread(self):
        p = self.p
        mine = self.half(p.x)
        self.from_y = [
            self.links.start(self.shard.at[self.rows, mine], self.piece(p.z, p.y, mine), p.to_y)
        ]
        self.from_c = [
            self.links.start(
                self.shard.at[self.rows, self.cols()], self.piece(p.z, p.y, self.cols()), p.to_c
            )
        ]

    def step1(self):
        p = self.p
        if not self.early:
            self.spread()
        self.from_x = []
        for k in range(1, 4):
            self.from_z[k - 1].wait_recv()
            piece = self.piece(p.z_down[k], p.y, self.half(p.x))
            self.from_y.append(self.push(piece, p.to_y))
            if self.split:
                self.from_x.append(self.push(piece, p.to_x))
            self.from_c.append(self.push(piece, p.to_c))

    def step2(self):
        p, every = self.p, slice(None)
        for copy in self.from_y:
            copy.wait_recv()
        piece = self.piece(every, p.yo, self.half(p.x))
        if self.split:
            self.across = self.push(piece, p.to_x)
        self.from_c.append(self.push(piece, p.to_c))
        for k, copy in enumerate(self.from_x):
            copy.wait_recv()
            piece = self.piece(p.z_down[k + 1], p.y, self.half(p.xo))
            self.from_c.append(self.push(piece, p.to_c))

    def step3(self):
        if self.split:
            self.across.wait_recv()
            piece = self.piece(slice(None), self.p.yo, self.half(self.p.xo))
            self.from_c.append(self.push(piece, self.p.to_c))
        else:
            self.step4()

    def step4(self):
        for copy in self.from_c:
            copy.wait_recv()
        self.own.wait()


class Reduce:
    copies = 7

    def __init__(self, block, at, grads, out, place, links, core_in, bufs):
        first, last, self.split = block[:3]
        self.col0, self.width = (0, grads.shape[-1]) if len(block) < 4 else block[3]
        self.rows = last - first
        self.at0, self.here0 = at, first
        self.at, self.here = pl.ds(at, self.rows), pl.ds(first, self.rows)
        self.grads, self.out = grads, out
        self.p, self.links = place, links
        self.core_in, self.bufs = core_in, bufs
        limit = max(48, 96 * 768 // self.width)
        self.block = max(b for b in range(16, min(self.rows, limit) + 1, 16) if self.rows % b == 0)
        self.stage = 0
        self.last = 5 if self.split else 4

    def cols(self):
        return pl.ds(self.col0, self.width)

    def half(self, x):
        if not self.split:
            return self.cols()
        size = self.width // 2
        return pl.ds(pl.multiple_of(self.col0 + x * size, 128), size)

    def low(self):
        return pl.ds(self.col0, self.width // 2)

    def high(self):
        return pl.ds(self.col0 + self.width // 2, self.width // 2) if self.split else self.cols()

    def add(self, outer, target, source):
        steps = self.rows // self.block

        def body(i, carry):
            first = pl.multiple_of((i % steps) * self.block, 16)
            put = target(i // steps, pl.ds(self.at0 + first, self.block))
            given = source(i // steps, pl.ds(self.here0 + first, self.block))
            self.grads[put] = (
                self.grads[put].astype(jnp.float32) + given.astype(jnp.float32)
            ).astype(jnp.bfloat16)
            return carry

        lax.fori_loop(0, outer * steps, body, 0)

    def step0(self):
        p = self.p
        self.by_core = self.links.start(
            self.grads.at[:, :, p.co, self.at, self.cols()],
            self.core_in.at[:, :, self.here, self.cols()],
            p.to_c,
        )

    def add_core(self, y):
        p = self.p
        self.add(
            4,
            lambda i, rows: (i, y, p.c, rows, self.cols()),
            lambda i, rows: self.core_in[i, y, rows, self.cols()],
        )

    def send_y(self):
        p = self.p
        self.by_y = self.links.start(
            self.grads.at[:, p.yo, p.c, self.at, self.half(p.x)],
            self.bufs.at[pl.ds(0, 4), self.here, self.high()],
            p.to_y,
        )

    def step1(self):
        p = self.p
        self.by_core.wait_recv()
        self.add_core(p.yo)
        if not self.split:
            self.send_y()
        self.add_core(p.y)
        if self.split:
            self.by_x = [
                self.links.start(
                    self.grads.at[:, y, p.c, self.at, self.half(p.xo)],
                    self.bufs.at[pl.ds(4 * i, 4), self.here, self.low()],
                    p.to_x,
                )
                for i, y in enumerate((p.yo, p.y))
            ]

    def add_x(self, i, y):
        p = self.p
        self.by_x[i].wait_recv()
        self.add(
            4,
            lambda j, rows: (j, y, p.c, rows, self.half(p.x)),
            lambda j, rows: self.bufs[4 * i + j, rows, self.low()],
        )

    def step2(self):
        if self.split:
            self.add_x(0, self.p.yo)
            self.send_y()
            self.add_x(1, self.p.y)
        else:
            self.reduce_y()

    def reduce_y(self):
        p = self.p
        self.by_y.wait_recv()
        self.add(
            4,
            lambda i, rows: (i, p.y, p.c, rows, self.half(p.x)),
            lambda i, rows: self.bufs[i, rows, self.high()],
        )
        self.by_z = [
            self.links.start(
                self.grads.at[p.z_up[k], p.y, p.c, self.at, self.half(p.x)],
                self.bufs.at[3 + k, self.here, self.high()],
                p.to_z[k],
            )
            for k in range(1, 4)
        ]

    def reduce_z(self, put):
        p = self.p
        for copy in self.by_z:
            copy.wait_recv()

        def body(i, carry):
            first = pl.multiple_of(i * self.block, 16)
            rows = pl.ds(self.here0 + first, self.block)
            place = (p.z, p.y, p.c, pl.ds(self.at0 + first, self.block), self.half(p.x))
            total = self.grads[place].astype(jnp.float32)
            for k in range(3):
                total = total + self.bufs[4 + k, rows, self.high()].astype(jnp.float32)
            put(rows, place, total.astype(jnp.bfloat16))
            return carry

        lax.fori_loop(0, self.rows // self.block, body, 0)

    def step3(self):
        p = self.p
        if self.split:
            self.reduce_y()
            return

        def put(rows, place, value):
            self.grads[place] = value

        self.reduce_z(put)
        self.by_x = self.links.start(
            self.grads.at[p.z, p.y, p.c, self.at, self.cols()],
            self.bufs.at[7, self.here, self.cols()],
            p.to_x,
        )

    def step4(self):
        p = self.p
        if self.split:

            def put(rows, place, value):
                self.out[rows, self.half(p.x)] = value

            self.reduce_z(put)
            done = self.out.at[self.here, self.half(p.x)]
            self.by_x = self.links.start(done, done, p.to_x)
            return
        self.by_x.wait_recv()

        def body(i, carry):
            first = pl.multiple_of(i * self.block, 16)
            rows = pl.ds(self.here0 + first, self.block)
            own = self.grads[p.z, p.y, p.c, pl.ds(self.at0 + first, self.block), self.cols()]
            self.out[rows, self.cols()] = (
                own.astype(jnp.float32) + self.bufs[7, rows, self.cols()].astype(jnp.float32)
            ).astype(jnp.bfloat16)
            return carry

        lax.fori_loop(0, self.rows // self.block, body, 0)

    def step5(self):
        self.by_x.wait_recv()

    def beat(self):
        getattr(self, "step" + str(self.stage))()
        self.stage += 1


class Total:
    copies = 6
    last = 4

    def __init__(self, value, core_in, x_in, y_in, by_z, place, links):
        self.value, self.core_in, self.x_in, self.y_in, self.by_z = value, core_in, x_in, y_in, by_z
        self.p, self.links = place, links
        self.stage = 0

    def step0(self):
        self.copy = self.links.start(self.value.at[0], self.core_in, self.p.to_c)

    def step1(self):
        self.copy.wait_recv()
        self.value[1] = self.value[0] + self.core_in[...]
        self.copy = self.links.start(self.value.at[1], self.x_in, self.p.to_x)

    def step2(self):
        self.copy.wait_recv()
        self.value[2] = self.value[1] + self.x_in[...]
        self.copy = self.links.start(self.value.at[2], self.y_in, self.p.to_y)

    def step3(self):
        self.copy.wait_recv()
        z = self.p.z
        self.by_z[z] = self.value[2] + self.y_in[...]
        self.spread = [
            self.links.start(self.by_z.at[z], self.by_z.at[z], self.p.to_z[k]) for k in range(1, 4)
        ]

    def step4(self):
        for copy in self.spread:
            copy.wait_recv()

    def sum(self):
        return ((self.by_z[0] + self.by_z[1]) + self.by_z[2]) + self.by_z[3]

    def beat(self):
        getattr(self, "step" + str(self.stage))()
        self.stage += 1


ROOT_HALF = 0.7071067811865476
DENSITY = 0.3989422804014327


def dot(left, right):
    return jnp.dot(left, right, preferred_element_type=jnp.float32)


def layer_kernel(s, *refs):
    (tokens, packed, teacher, order_row, length, valid) = refs[:6]
    (ordered_out, total_out, token_out, grads_out) = refs[6:10]
    (W, G, tok, qs, ks, vs, dO, stat, attn, n1, r1, low1, act, gp, acc, teach, res_in, low2, gains, sums) = refs[10:30]
    total_refs, (send, recv, local), (order_col, core_in, bufs) = refs[30:35], refs[35:38], refs[38:]
    f32, bf16 = jnp.float32, jnp.bfloat16
    span, width, shard, downs = s.span, s.width, s.shard, s.downs
    pairs = width // 128
    third = width // 3
    half = width // 2
    place = Place()
    x, xo = place.x, place.xo
    links = Links(send, recv)

    def own(first, size):
        return pl.ds(pl.multiple_of(x * span + first, 16), size)

    def other(first, size):
        return pl.ds(pl.multiple_of(xo * span + first, 16), size)

    def loop(count, body):
        def step(i, carry):
            body(i)
            return carry

        lax.fori_loop(0, count, step, 0)

    def by_columns(first, n):
        cols = pl.ds(pl.multiple_of(n * third, 128), third)
        rows = pl.ds(pl.multiple_of(first, 16), shard)
        return W[:, :, :, rows, cols].reshape(width, third)

    def half_rows(first, m):
        rows = pl.ds(pl.multiple_of(first, 16), shard)
        return W[pl.ds(2 * m, 2), :, :, rows, :].reshape(half, width)

    gathers = [
        Gather(block, i < s.early, packed, W, place, links, local.at[i])
        for i, block in enumerate(s.gather_blocks)
    ]
    n_gather = len(gathers)
    stages = [0] * n_gather
    forward = iter(s.forward)

    def advance():
        for i in next(forward):
            getattr(gathers[i], "step" + str(stages[i]))()
            stages[i] += 1

    def arrived(first, last):
        advance()
        for i, block in enumerate(s.gather_blocks):
            if block[0] < last and block[1] > first:
                assert stages[i] > gathers[i].last

    place.barrier()
    own_tokens = pltpu.make_async_copy(tokens, tok.at[own(0, span)], local.at[n_gather])
    own_tokens.start()
    own_teacher = pltpu.make_async_copy(teacher, gp.at[0], local.at[n_gather + 1])
    own_teacher.start()
    send_tokens = links.start(tokens, tok.at[own(0, span)], place.to_x)
    advance()
    order_col[...] = jnp.broadcast_to(order_row[...].astype(f32), (128, 2 * span)).T
    length_now = length[0]
    length_float = length_now.astype(f32)
    iota_rows = lax.broadcasted_iota(jnp.int32, (s.block, span), 1)

    def pick(c):
        rows = pl.ds(pl.multiple_of(c * span + x * s.block, 16), s.block)
        position = order_col[rows, :].astype(jnp.int32) - x * span
        chosen = iota_rows == jnp.concatenate([position] * (span // 128), axis=1)
        return jnp.where(chosen, 1.0, 0.0).astype(bf16)

    own_teacher.wait()
    for n in range(3):
        cols = slice(n * third, (n + 1) * third)
        gp[1, : s.block, cols] = dot(pick(xo), gp[0, :, cols]).astype(bf16)
        teach[x, :, cols] = dot(pick(x), gp[0, :, cols]).astype(bf16)
    teach_copy = links.start(gp.at[1, pl.ds(0, s.block)], teach.at[x], place.to_x)
    advance()
    arrived(0, s.out0)

    own_tokens.wait()

    def project(rows, which):
        def body(n):
            cols = pl.ds(pl.multiple_of(n * third, 128), third)
            for first, target, scale in which:
                value = dot(tok[rows, :], by_columns(first, n)).astype(bf16)
                target[rows, cols] = value * scale if scale != 1.0 else value

        loop(3, body)

    sets = ((0, qs, SCORE_SCALE), (shard, ks, 1.0), (2 * shard, vs, 1.0))
    project(own(0, span), sets)
    advance()
    send_tokens.wait_recv()
    project(other(0, span), sets)
    advance()

    lane = lax.broadcasted_iota(jnp.int32, (1, 128), 1)
    even32 = lane < HEAD_DIM
    even = jnp.where(even32, 1.0, 0.0).astype(bf16)
    odd = jnp.where(even32, 0.0, 1.0).astype(bf16)
    bias_row = jnp.where(order_row[0:1, :] < length_now, 0.0, MASKED)
    rows_q = s.rows_q

    def attend(pair):
        lanes = pl.ds(pair * 128, 128)

        def body(b):
            rows = own(b * rows_q, rows_q)
            query, key, value = qs[rows, lanes], ks[:, lanes], vs[:, lanes]
            tops, mixed = [], []
            for keep, rest in ((even, odd), (odd, even)):
                scores = (
                    lax.dot_general(
                        query * keep, key, (((1,), (1,)), ((), ())), preferred_element_type=f32
                    )
                    + bias_row
                )
                top = jnp.max(scores, axis=1, keepdims=True)
                weight = jnp.exp(scores - top).astype(bf16)
                tops.append(top)
                mixed.append(dot(weight, value * keep + rest))
            part = jnp.where(even32, mixed[0], mixed[1])
            total = pltpu.roll(jnp.where(even32, mixed[1], mixed[0]), HEAD_DIM, 1)
            out = pl.ds(pl.multiple_of(b * rows_q, 16), rows_q)
            attn[out, lanes] = (part / total).astype(bf16)
            log_total = jnp.where(even32, tops[0], tops[1]) + jnp.log(total)
            log_rows = log_total.T
            for h in range(2):
                stat[x, 0, pl.ds(2 * pair + h, 1), pl.ds(pl.multiple_of(b * rows_q, 128), rows_q)] = (
                    log_rows[h * HEAD_DIM : h * HEAD_DIM + 1, :]
                )

        loop(span // rows_q, body)

    for pair in range(pairs):
        attend(pair)
        advance()

    arrived(s.out0, s.up0)
    device = lax.broadcasted_iota(jnp.int32, (16, width), 0)
    feature = lax.broadcasted_iota(jnp.int32, (16, width), 1)
    mine = (feature // shard) == device
    spread = jnp.where(
        lax.broadcasted_iota(jnp.int32, (128, width), 1) % shard
        == lax.broadcasted_iota(jnp.int32, (128, width), 0),
        1.0,
        0.0,
    ).astype(bf16)
    gain_rows = W[:, :, :, s.gain0 : s.gain0 + 16, :128].reshape(16, 16, 128).astype(f32)
    for g in range(2):
        wide = dot(gain_rows[:, g, :].astype(bf16), spread)
        gains[g : g + 1, :] = jnp.sum(jnp.where(mine, wide, 0.0), axis=0, keepdims=True)

    def branch(n):
        cols = pl.ds(pl.multiple_of(n * third, 128), third)
        acc[:, cols] = dot(attn[...], by_columns(s.out0, n))

    loop(3, branch)
    advance()
    rows_n = s.rows_n

    def wide_column(column):
        return jnp.broadcast_to(column, (rows_n, 128))

    def first_norm(b):
        first = pl.multiple_of(b * rows_n, 16)
        rows = pl.ds(first, rows_n)
        hidden = tok[own(first, rows_n), :].astype(f32) + acc[rows, :]
        center = hidden - jnp.mean(hidden, axis=1, keepdims=True)
        inverse = lax.rsqrt(jnp.mean(center * center, axis=1, keepdims=True) + EPSILON)
        normal = center * inverse
        n1[rows, :] = normal
        r1[rows, :] = wide_column(inverse)
        low1[rows, :] = (normal * gains[0:1, :]).astype(bf16)

    loop(span // rows_n, first_norm)
    advance()

    teach_copy.wait_recv()
    links.sent(teach_copy)

    def upward(p):
        def body(n):
            cols = pl.ds(pl.multiple_of(n * third, 128), third)
            value = dot(low1[...], by_columns(s.up0 + p * shard, n))
            cdf = 0.5 * (1.0 + lax.erf(value * ROOT_HALF))
            act[p, :, cols] = (value * cdf).astype(bf16)
            gp[p, :, cols] = (cdf + value * (jnp.exp(-0.5 * value * value) * DENSITY)).astype(bf16)

        loop(3, body)

    def downward(p):
        def body(n):
            cols = pl.ds(pl.multiple_of(n * third, 128), third)
            value = dot(act[p], by_columns(s.down0 + p * shard, n))
            acc[:, cols] = value if p == 0 else acc[:, cols] + value

        loop(3, body)

    for p in range(s.panels):
        arrived(s.up0 + p * shard, s.up0 + (p + 1) * shard)
        upward(p)
        advance()
        arrived(s.down0 + p * shard, s.down0 + (p + 1) * shard)
        downward(p)
        advance()

    sums[...] = jnp.zeros_like(sums)
    valid_total = jnp.full((1, 1), valid[0], jnp.int32).astype(f32)
    grad_scale = s.tokens / valid_total

    def fold(values):
        return jnp.sum(values.reshape(rows_n // 8, 8, width), axis=0)

    def second_norm(b):
        first = pl.multiple_of(b * rows_n, 16)
        rows = pl.ds(first, rows_n)
        hidden = n1[rows, :] * gains[0:1, :] + acc[rows, :]
        center = hidden - jnp.mean(hidden, axis=1, keepdims=True)
        inverse = lax.rsqrt(jnp.mean(center * center, axis=1, keepdims=True) + EPSILON)
        normal = center * inverse
        gain = gains[1:2, :]
        result = (normal * gain).astype(bf16)
        per = s.block // rows_n
        at = pl.ds(pl.multiple_of((b % per) * rows_n, 16), rows_n)
        target = teach[b // per, at, :].astype(f32)
        teach[b // per, at, :] = result
        live = order_col[own(first, rows_n), 0:1] < length_float
        error = jnp.where(live, result.astype(f32) - target, 0.0)
        sums[2] += fold(error * error)
        grad = (error * grad_scale).astype(bf16).astype(f32)
        sums[1] += fold(grad * normal)
        scaled = grad * gain
        grad_sum = inverse * (
            scaled
            - jnp.mean(scaled, axis=1, keepdims=True)
            - normal * jnp.mean(scaled * normal, axis=1, keepdims=True)
        )
        acc[rows, :] = grad_sum
        low2[rows, :] = grad_sum.astype(bf16)

    loop(span // rows_n, second_norm)
    links.drain()
    send_result = links.start(teach.at[xo], res_in, place.to_x)
    total_refs[0][0] = jnp.broadcast_to(
        jnp.sum(jnp.sum(sums[2], axis=0, keepdims=True), axis=1, keepdims=True), (8, 128)
    )
    total = Total(*total_refs, place, links)

    reduces = [total]
    backward = iter(s.backward)

    def beat():
        for i in next(backward):
            reduces[i].beat()

    def enter(block, in_weights=False):
        first = block[0]
        reduces.append(
            Reduce(
                block,
                first + s.down0 if in_weights else first - s.out0,
                W if in_weights else G,
                grads_out,
                place,
                links,
                core_in,
                bufs,
            )
        )

    def turned(left, right):
        return lax.dot_general(left, right, (((0,), (0,)), ((), ())), preferred_element_type=f32)

    def by_turned(left, right):
        return lax.dot_general(left, right, (((1,), (1,)), ((), ())), preferred_element_type=f32)

    def put_grad(first, m, value):
        rows = pl.ds(pl.multiple_of(first, 16), shard)
        return (pl.ds(2 * m, 2), slice(None), slice(None), rows, slice(None)), value.astype(
            bf16
        ).reshape(2, 2, 2, shard, width)

    def panel_grad(first, left, right):
        def body(m):
            cols = pl.ds(pl.multiple_of(m * half, 128), half)
            where, value = put_grad(first - s.out0, m, turned(left[:, cols], right[...]))
            G[where] = value

        loop(2, body)

    for p in range(s.panels):
        panel_grad(s.down0 + p * shard, act.at[p], low2)
        enter(s.down_blocks[p])
        beat()

    def active_grad(p):
        def body(m):
            cols = pl.ds(pl.multiple_of(m * half, 128), half)
            value = by_turned(low2[...], half_rows(s.down0 + p * shard, m))
            gp[p, :, cols] = (value * gp[p, :, cols].astype(f32)).astype(bf16)

        loop(2, body)

    for p in range(s.panels):
        active_grad(p)
        beat()
        panel_grad(s.up0 + p * shard, low1, gp.at[p])
        enter(s.up_blocks[p])
        beat()

    def normed_grad(m):
        cols = pl.ds(pl.multiple_of(m * half, 128), half)
        value = acc[:, cols]
        for p in range(s.panels):
            value = value + by_turned(gp[p], half_rows(s.up0 + p * shard, m))
        acc[:, cols] = value

    loop(2, normed_grad)
    beat()

    def first_back(b):
        rows = pl.ds(pl.multiple_of(b * rows_n, 16), rows_n)
        grad, normal = acc[rows, :], n1[rows, :]
        sums[0] += fold(grad * normal)
        scaled = grad * gains[0:1, :]
        hidden_grad = r1[rows, 0:1] * (
            scaled
            - jnp.mean(scaled, axis=1, keepdims=True)
            - normal * jnp.mean(scaled * normal, axis=1, keepdims=True)
        )
        acc[rows, :] = hidden_grad
        low2[rows, :] = hidden_grad.astype(bf16)

    loop(span // rows_n, first_back)
    beat()

    def attn_grad(m):
        cols = pl.ds(pl.multiple_of(m * half, 128), half)
        dO[own(0, span), cols] = by_turned(low2[...], half_rows(s.out0, m)).astype(bf16)

    loop(2, attn_grad)
    head = lax.broadcasted_iota(jnp.int32, (16, width), 0)
    in_head = jnp.where((feature // HEAD_DIM) == head, 1.0, 0.0)

    def head_delta(b):
        first = pl.multiple_of(b * 128, 128)
        rows = pl.ds(first, 128)
        product = dO[own(first, 128), :].astype(f32) * attn[rows, :].astype(f32)
        stat[x, 1, :, rows] = lax.dot_general(
            in_head,
            product,
            (((1,), (1,)), ((), ())),
            precision=lax.Precision.HIGHEST,
            preferred_element_type=f32,
        )

    loop(span // 128, head_delta)
    send_grad = links.start(dO.at[own(0, span)], dO.at[own(0, span)], place.to_x)
    send_stat = links.start(stat.at[x], stat.at[x], place.to_x)

    panel_grad(s.out0, attn, low2)
    pieces = []
    for g in range(2):
        row = jnp.sum(sums[g], axis=0, keepdims=True)
        split = jnp.where(mine, jnp.broadcast_to(row, (16, width)), 0.0).astype(bf16)
        pieces.append(by_turned(split, spread))
    at_row = lax.broadcasted_iota(jnp.int32, (16, 16, 128), 1)
    gain_block = jnp.where(
        at_row == 0, pieces[0][:, None, :], jnp.where(at_row == 1, pieces[1][:, None, :], 0.0)
    ).astype(bf16)
    G[:, :, :, shard : shard + 16, :128] = gain_block.reshape(4, 2, 2, 16, 128)
    G[:, :, :, shard : shard + 16, 128:] = jnp.zeros((4, 2, 2, 16, width - 128), bf16)
    enter(s.out_block)
    beat()

    rows_k = s.rows_k

    def block_terms(key, value, bias, query, grad, log_row, delta_row):
        scores = by_turned(key, query) + bias
        p = jnp.exp(scores - log_row)
        score_grad = (p * (by_turned(value, grad) - delta_row)).astype(bf16)
        return p.astype(bf16), score_grad

    def key_bias(rows):
        column = jnp.where(order_col[rows, :] < length_float, 0.0, MASKED)
        return jnp.concatenate([column] * (span // 128), axis=1)

    def back_other(pair):
        lanes = pl.ds(pair * 128, 128)

        def body(b):
            rows = other(b * rows_k, rows_k)
            key, value, bias = ks[rows, lanes], vs[rows, lanes], key_bias(rows)
            query, grad = qs[own(0, span), lanes], dO[own(0, span), lanes]
            result = jnp.zeros((span, 128), f32)
            for h, keep in enumerate((even, odd)):
                at = pl.ds(2 * pair + h, 1)
                p, score_grad = block_terms(
                    key, value, bias, query * keep, grad * keep, stat[x, 0, at, :], stat[x, 1, at, :]
                )
                result = result + turned(score_grad, key * keep)
            n1[:, lanes] += result

        n1[:, lanes] = jnp.zeros((span, 128), f32)
        loop(span // rows_k, body)

    def back_own(pair):
        lanes = pl.ds(pair * 128, 128)

        def body(b):
            first = pl.multiple_of(b * rows_k, 16)
            rows = own(first, rows_k)
            key, value, bias = ks[rows, lanes], vs[rows, lanes], key_bias(rows)
            result = jnp.zeros((span, 128), f32)
            key_grad = jnp.zeros((rows_k, 128), f32)
            value_grad = jnp.zeros((rows_k, 128), f32)
            for side in (x, xo):
                whole = pl.ds(pl.multiple_of(side * span, 16), span)
                query, grad = qs[whole, lanes], dO[whole, lanes]
                for h, keep in enumerate((even, odd)):
                    at = pl.ds(2 * pair + h, 1)
                    query_h, grad_h = query * keep, grad * keep
                    p, score_grad = block_terms(
                        key, value, bias, query_h, grad_h, stat[side, 0, at, :], stat[side, 1, at, :]
                    )
                    value_grad = value_grad + dot(p, grad_h)
                    key_grad = key_grad + dot(score_grad, query_h)
                    if side is x:
                        result = result + turned(score_grad, key * keep)
            out = pl.ds(first, rows_k)
            n1[:, lanes] += result
            act[1, out, lanes] = key_grad.astype(bf16)
            act[2, out, lanes] = value_grad.astype(bf16)

        loop(span // rows_k, body)
        act[0, :, lanes] = (n1[:, lanes] * SCORE_SCALE).astype(bf16)

    def weight_grad(j, columns):
        def body(m):
            cols = pl.ds(pl.multiple_of(m * half, 128), half)
            value = turned(tok[own(0, span), cols], act[j, :, columns]).astype(bf16)
            W[
                pl.ds(2 * m, 2), :, :, s.down0 + j * shard : s.down0 + (j + 1) * shard, columns
            ] = value.reshape(2, 2, 2, shard, 256)

        loop(2, body)

    for pair in range(pairs):
        back_other(pair)
        beat()
    send_grad.wait_recv()
    send_stat.wait_recv()
    for pair in range(pairs):
        back_own(pair)
        if pair % 2 == 1:
            for j in range(3):
                weight_grad(j, slice((pair - 1) * 128, (pair + 1) * 128))
            enter(s.last_blocks[pair // 2], True)
        beat()

    def input_grad(m):
        cols = pl.ds(pl.multiple_of(m * half, 128), half)
        value = acc[:, cols]
        for j in range(3):
            value = value + by_turned(act[j], half_rows(j * shard, m))
        acc[:, cols] = value

    loop(2, input_grad)
    token_copy = pltpu.make_async_copy(acc, token_out, local.at[n_gather])
    token_copy.start()
    beat()
    send_result.wait_recv()

    def place_rows(n):
        cols = pl.ds(pl.multiple_of(n * third, 128), third)
        value = None
        position = lax.broadcasted_iota(jnp.int32, (span, s.block), 0) + x * span
        for c, rows in ((x, teach[x, :, cols]), (xo, res_in[:, cols])):
            at = order_row[0:1, pl.ds(pl.multiple_of(c * span + x * s.block, 128), s.block)]
            chosen = jnp.where(position == at, 1.0, 0.0).astype(bf16)
            part = dot(chosen, rows)
            value = part if value is None else value + part
        low2[:, cols] = value.astype(bf16)

    loop(3, place_rows)
    ordered_copy = pltpu.make_async_copy(low2, ordered_out, local.at[n_gather + 1])
    ordered_copy.start()
    beat()
    beat()
    assert all(item.stage > item.last for item in reduces)
    total_out[...] = total.sum()
    token_copy.wait()
    ordered_copy.wait()
    links.drain()


class Sizes:
    def __init__(self, span, width, ff, shard, downs, tokens):
        self.span, self.width, self.shard, self.downs, self.tokens = span, width, shard, downs, tokens
        self.panels = ff // width
        self.block = span // 2
        self.out0 = 3 * shard
        self.gain0 = 4 * shard
        self.up0 = self.gain0 + 16
        self.down0 = self.up0 + self.panels * shard
        self.rows = self.down0 + downs
        panels = [self.up0 + p * shard for p in range(self.panels)]
        lower = [self.down0 + p * shard for p in range(self.panels)]
        blocks = [(j * shard, (j + 1) * shard) for j in range(3)] + [(self.out0, self.up0)]
        for up, down in zip(panels, lower):
            blocks += [(up, up + shard), (down, down + shard)]
        self.gather_blocks = tuple(b + (i in GATHER_SPLIT,) for i, b in enumerate(blocks))
        self.early = EARLY
        self.up_blocks = [(up, up + shard, False) for up in panels]
        self.down_blocks = [(down, down + shard, False) for down in lower]
        self.out_block = (self.out0, self.up0, False)
        self.last_blocks = [(0, self.out0, False, (256 * j, 256)) for j in range(width // 256)]
        self.forward, self.backward = FORWARD, BACKWARD
        self.rows_q, self.rows_n, self.rows_k = 128, 64, 256


def layer(s, tokens, packed, teacher, order_row, length, valid):
    bf16, f32 = jnp.bfloat16, jnp.float32
    span, width = s.span, s.width
    both = 2 * span
    anywhere = pl.BlockSpec(memory_space=pl.ANY)
    vmem = pl.BlockSpec(memory_space=pltpu.VMEM)
    smem = pl.BlockSpec(memory_space=pltpu.SMEM)
    reduces = 2 * s.panels + 1 + len(s.last_blocks)
    copies = Gather.copies * len(s.gather_blocks) + Reduce.copies * reduces + Total.copies + 6
    small = pltpu.VMEM((8, 128), f32)
    scratch = [
        pltpu.VMEM((4, 2, 2, s.rows, width), bf16),
        pltpu.VMEM((4, 2, 2, s.rows - s.out0, width), bf16),
        pltpu.VMEM((both, width), bf16),
        pltpu.VMEM((both, width), bf16),
        pltpu.VMEM((both, width), bf16),
        pltpu.VMEM((both, width), bf16),
        pltpu.VMEM((both, width), bf16),
        pltpu.VMEM((2, 2, 16, span), f32),
        pltpu.VMEM((span, width), bf16),
        pltpu.VMEM((span, width), f32),
        pltpu.VMEM((span, 128), f32),
        pltpu.VMEM((span, width), bf16),
        pltpu.VMEM((s.panels, span, width), bf16),
        pltpu.VMEM((s.panels, span, width), bf16),
        pltpu.VMEM((span, width), f32),
        pltpu.VMEM((2, s.block, width), bf16),
        pltpu.VMEM((s.block, width), bf16),
        pltpu.VMEM((span, width), bf16),
        pltpu.VMEM((8, width), f32),
        pltpu.VMEM((3, 8, width), f32),
        pltpu.VMEM((3, 8, 128), f32),
        small,
        small,
        small,
        pltpu.VMEM((4, 8, 128), f32),
        pltpu.SemaphoreType.DMA((copies,)),
        pltpu.SemaphoreType.DMA((copies,)),
        pltpu.SemaphoreType.DMA((len(s.gather_blocks) + 2,)),
        pltpu.VMEM((both, 128), f32),
        pltpu.VMEM((4, 2, s.rows, width), bf16),
        pltpu.VMEM((8, s.rows, width), bf16),
    ]
    return pl.pallas_call(
        functools.partial(layer_kernel, s),
        out_shape=[
            jax.ShapeDtypeStruct((span, width), bf16),
            jax.ShapeDtypeStruct((8, 128), f32),
            jax.ShapeDtypeStruct((span, width), f32),
            jax.ShapeDtypeStruct((s.rows, width), bf16),
        ],
        in_specs=[anywhere, anywhere, anywhere, vmem, smem, smem],
        out_specs=[anywhere, vmem, anywhere, vmem],
        scratch_shapes=scratch,
        compiler_params=pltpu.CompilerParams(
            collective_id=0, has_side_effects=True, vmem_limit_bytes=s.vmem
        ),
    )(tokens, packed, teacher, order_row, length, valid)


def fused_shards(
    tokens,
    w_query,
    w_key,
    w_value,
    w_out,
    w_up,
    w_down,
    gain_attn,
    gain_ffn,
    teacher,
    seq_lengths,
    tok_perm,
    valid_count,
):
    f32 = jnp.float32
    dp_count = lax.axis_size("dp")
    span, width = tokens.shape[1:]
    shard, ff = w_up.shape
    seq_len = tok_perm.shape[1]
    s = Sizes(span, width, ff, shard, w_down.shape[0], seq_len * dp_count)
    s.vmem = 63 * MIB
    gain_rows = jnp.pad(jnp.stack([gain_attn, gain_ffn]), ((0, 14), (0, width - shard)))
    up_rows = jnp.transpose(
        w_up.reshape(shard, dp_count, s.panels, shard), (2, 0, 1, 3)
    ).reshape(-1, width)
    packed = jnp.concatenate([w_query, w_key, w_value, w_out, gain_rows, up_rows, w_down])
    ordered, total, token_grad, grads = layer(
        s, tokens[0], packed, teacher[0], tok_perm, seq_lengths, valid_count
    )
    loss = (total[0, 0] / (2.0 * width * valid_count[0].astype(f32))).reshape(1)
    grads = grads.astype(f32)
    up = grads[s.up0 : s.down0].reshape(s.panels, shard, dp_count, shard)
    return (
        ordered[None],
        loss,
        token_grad[None],
        grads[:shard],
        grads[shard : 2 * shard],
        grads[2 * shard : 3 * shard],
        grads[s.out0 : s.gain0],
        jnp.transpose(up, (1, 2, 0, 3)).reshape(shard, ff),
        grads[s.down0 :],
        grads[s.gain0, :shard],
        grads[s.gain0 + 1, :shard],
    )


def solution(mesh):
    in_specs = (
        P("dp", "ctx", None),
        P("dp", None),
        P("dp", None),
        P("dp", None),
        P("dp", None),
        P("dp", None),
        P("dp", None),
        P("dp"),
        P("dp"),
        P("dp", "ctx", None),
        P("dp"),
        P("dp", None),
        P(),
    )
    out_specs = (
        P("dp", "ctx", None),
        P(),
        P("dp", "ctx", None),
        P("dp", None),
        P("dp", None),
        P("dp", None),
        P("dp", None),
        P("dp", None),
        P("dp", None),
        P("dp"),
        P("dp"),
    )
    body = fused_shards if dict(mesh.shape) == {"dp": 16, "ctx": 2} else shards
    return jax.shard_map(body, mesh=mesh, in_specs=in_specs, out_specs=out_specs, check_vma=False)
```

```python
import functools
import math

import jax
import jax.numpy as jnp
from jax import lax
from jax.experimental import pallas as pl
from jax.experimental.pallas import tpu as pltpu
from jax.sharding import PartitionSpec as P

HEAD_DIM = 64


EPSILON = 1e-06
SCORE_SCALE = 0.125
MASKED = -1e30
MESH = pl.DeviceIdType.MESH
MIB = 1024 * 1024


GATHER_SPLIT = (1, 3, 5, 6, 7, 8, 9)
REDUCE_SPLIT = (1, 2, 7, 8, 9, 11)
EARLY = 4
FORWARD = ((0, 1, 2, 3, 4, 5, 6, 7, 8, 9, 10), (), (0, 1, 0, 0, 2, 2, 3, 2, 1, 3, 4, 1, 5, 1), (), (3, 4, 6), (3,), (4, 5, 7), (6,), (8,), (5,), (5, 7), (), (), (6, 9), (), (6,), (), (8,), (), (), (7, 7), (10,), (9, 8, 8), (), (9, 10, 9), (), (10,), ())
BACKWARD = ((0, 1), (0, 2), (3,), (), (1, 4), (), (2, 5), (), (3, 0, 6), (4,), (5, 7), (0, 1, 2, 0, 6, 7, 4), (), (8,), (3, 1, 5, 8), (2,), (4,), (6,), (), (5, 7), (9,), (1, 3, 2), (10,), (), (8, 6, 4, 9, 10, 5, 2, 11), (6,), (7, 8, 11, 12), (9, 3, 12), (11, 10), (7, 8, 9, 3, 10, 12, 11, 8, 12, 11, 9, 10, 9, 10, 12, 12))


def gelu_exact(values):
    return 0.5 * values * (1.0 + lax.erf(values * 0.7071067811865476))


def norm_forward(hidden, gain_row):
    center = hidden - jnp.mean(hidden, axis=-1, keepdims=True)
    inverse = lax.rsqrt(jnp.mean(center * center, axis=-1, keepdims=True) + EPSILON)
    normal = center * inverse
    return (normal * gain_row, normal, inverse)


def norm_backward(grad_norm, gain_row, normal, inverse):
    scaled = grad_norm * gain_row
    grad_input = inverse * (
        scaled
        - jnp.mean(scaled, axis=-1, keepdims=True)
        - normal * jnp.mean(scaled * normal, axis=-1, keepdims=True)
    )
    return (grad_input, jnp.sum(grad_norm * normal, axis=0))


def row_product(left_mat, right_mat):
    return lax.dot_general(
        left_mat, right_mat, (((0,), (0,)), ((), ())), preferred_element_type=jnp.float32
    )


def by_transpose(left_mat, right_mat):
    return lax.dot_general(
        left_mat, right_mat, (((1,), (1,)), ((), ())), preferred_element_type=jnp.float32
    )


def shards(
    tokens,
    w_query,
    w_key,
    w_value,
    w_out,
    w_up,
    w_down,
    gain_attn,
    gain_ffn,
    teacher,
    seq_lengths,
    tok_perm,
    valid_count,
):
    ctx_count = lax.axis_size("ctx")
    ctx_rank = lax.axis_index("ctx")
    dp_count = lax.axis_size("dp")
    layer_in = tokens[0]
    span_rows, model_width = layer_in.shape
    head_count = model_width // HEAD_DIM
    dealt_order = tok_perm[0]
    seq_len = dealt_order.shape[0]
    length = seq_lengths[0]
    keep_all = dealt_order < length
    per_peer = span_rows // ctx_count
    query_weight, key_weight, value_weight, out_weight, gain_first = (
        lax.all_gather(w_query, "dp", axis=0, tiled=True),
        lax.all_gather(w_key, "dp", axis=0, tiled=True),
        lax.all_gather(w_value, "dp", axis=0, tiled=True),
        lax.all_gather(w_out, "dp", axis=0, tiled=True),
        lax.all_gather(gain_attn, "dp", axis=0, tiled=True),
    )
    up_weight, down_weight, gain_second = (
        lax.all_gather(w_up, "dp", axis=0, tiled=True),
        lax.all_gather(w_down, "dp", axis=0, tiled=True),
        lax.all_gather(gain_ffn, "dp", axis=0, tiled=True),
    )
    queries = jnp.dot(layer_in, query_weight, preferred_element_type=jnp.float32).astype(
        jnp.bfloat16
    )
    keys_own = jnp.dot(layer_in, key_weight, preferred_element_type=jnp.float32).astype(
        jnp.bfloat16
    )
    values_own = jnp.dot(layer_in, value_weight, preferred_element_type=jnp.float32).astype(
        jnp.bfloat16
    )
    query_heads = queries.reshape(span_rows, head_count, HEAD_DIM)
    initial = (
        jnp.full((head_count, span_rows), MASKED, jnp.float32),
        jnp.zeros((head_count, span_rows), jnp.float32),
        jnp.zeros((head_count, span_rows, HEAD_DIM), jnp.float32),
    )
    fold_state = initial
    key_piece = lax.all_gather(keys_own, "ctx", axis=0, tiled=True)
    value_piece = lax.all_gather(values_own, "ctx", axis=0, tiled=True)
    piece_rows = key_piece.shape[0]
    block_rows = math.gcd(piece_rows, span_rows)
    key_blocks = key_piece.reshape(piece_rows // block_rows, block_rows, head_count, HEAD_DIM)
    value_blocks = value_piece.reshape(piece_rows // block_rows, block_rows, head_count, HEAD_DIM)

    def step_block(block_state, block_item):
        running_max, running_sum, accumulated = block_state
        key_block, value_block, block_index = block_item
        key_keep = lax.dynamic_slice_in_dim(keep_all, block_index * block_rows, block_rows)
        scores = (
            jnp.einsum("qhe,khe->hqk", query_heads, key_block, preferred_element_type=jnp.float32)
            * SCORE_SCALE
        )
        scores = jnp.where(key_keep[None, None, :], scores, MASKED)
        new_max = jnp.maximum(running_max, jnp.max(scores, axis=-1))
        factor = jnp.exp(running_max - new_max)
        soft_weights = jnp.where(key_keep[None, None, :], jnp.exp(scores - new_max[..., None]), 0.0)
        running_sum = running_sum * factor + jnp.sum(soft_weights, axis=-1)
        accumulated = accumulated * factor[..., None] + jnp.einsum(
            "hqk,khe->hqe",
            soft_weights.astype(jnp.bfloat16),
            value_block,
            preferred_element_type=jnp.float32,
        )
        return ((new_max, running_sum, accumulated), None)

    block_indices = jnp.arange(piece_rows // block_rows, dtype=jnp.int32)
    fold_state, unused = lax.scan(step_block, fold_state, (key_blocks, value_blocks, block_indices))
    run_max, run_sum, accumulated = fold_state
    log_total = run_max + jnp.log(run_sum)
    attn_full = jnp.transpose(accumulated / run_sum[..., None], (1, 0, 2)).reshape(
        span_rows, model_width
    )
    attn_low = attn_full.astype(jnp.bfloat16)
    gain_first32 = gain_first.astype(jnp.float32)
    gain_second32 = gain_second.astype(jnp.float32)
    branch = jnp.dot(attn_low, out_weight, preferred_element_type=jnp.float32)
    normed, normal_first, inverse_first = norm_forward(
        layer_in.astype(jnp.float32) + branch, gain_first32
    )
    normed_low = normed.astype(jnp.bfloat16)
    upward = jnp.dot(normed_low, up_weight, preferred_element_type=jnp.float32)
    active, gelu_pull = jax.vjp(gelu_exact, upward)
    active_low = active.astype(jnp.bfloat16)
    down_out = jnp.dot(active_low, down_weight, preferred_element_type=jnp.float32)
    result, normal_second, inverse_second = norm_forward(normed + down_out, gain_second32)
    result_low = result.astype(jnp.bfloat16)
    arrived = lax.all_to_all(result_low, "ctx", split_axis=0, concat_axis=0, tiled=True)
    sources = (
        jnp.arange(ctx_count, dtype=jnp.int32)[:, None] * span_rows
        + ctx_rank * per_peer
        + jnp.arange(per_peer, dtype=jnp.int32)[None, :]
    ).reshape(span_rows)
    local_pos = jnp.take(dealt_order, sources) - ctx_rank * span_rows
    in_order = jnp.zeros_like(arrived).at[local_pos].set(arrived)
    target = teacher[0].astype(jnp.float32)
    live_rows = (ctx_rank * span_rows + jnp.arange(span_rows, dtype=jnp.int32) < length)[:, None]
    residual_err = jnp.where(live_rows, in_order.astype(jnp.float32) - target, 0.0)
    total_sq = lax.psum(jnp.sum(residual_err * residual_err), ("dp", "ctx"))
    valid_total = valid_count[0].astype(jnp.float32)
    loss_value = (total_sq / (2.0 * model_width * valid_total)).reshape(1)
    grad_scale = seq_len * dp_count / valid_total
    grad_order = (residual_err * grad_scale).astype(jnp.bfloat16)
    outgoing = jnp.take(grad_order, local_pos, axis=0)
    grad_result = lax.all_to_all(outgoing, "ctx", split_axis=0, concat_axis=0, tiled=True).astype(
        jnp.float32
    )
    grad_sum_second, grad_gain_second = norm_backward(
        grad_result, gain_second32, normal_second, inverse_second
    )
    down_grad_low = grad_sum_second.astype(jnp.bfloat16)
    grad_down_w = row_product(active_low, down_grad_low)
    grad_active = by_transpose(down_grad_low, down_weight)
    grad_upward = gelu_pull(grad_active)[0].astype(jnp.bfloat16)
    grad_up_w = row_product(normed_low, grad_upward)
    grad_normed = grad_sum_second + by_transpose(grad_upward, up_weight)
    grad_hidden, grad_gain_first = norm_backward(
        grad_normed, gain_first32, normal_first, inverse_first
    )
    branch_grad = grad_hidden.astype(jnp.bfloat16)
    grad_out_w = row_product(attn_low, branch_grad)
    attn_grad_low = by_transpose(branch_grad, out_weight).astype(jnp.bfloat16)
    grad_heads = attn_grad_low.reshape(span_rows, head_count, HEAD_DIM)
    row_delta = jnp.sum(
        (attn_grad_low.astype(jnp.float32) * attn_full).reshape(span_rows, head_count, HEAD_DIM),
        axis=-1,
    ).T
    keys_all, values_all = (
        lax.all_gather(keys_own, "ctx", axis=0, tiled=True),
        lax.all_gather(values_own, "ctx", axis=0, tiled=True),
    )
    blocks_count = seq_len // span_rows
    key_stack = keys_all.reshape(blocks_count, span_rows, head_count, HEAD_DIM)
    value_stack = values_all.reshape(blocks_count, span_rows, head_count, HEAD_DIM)

    def score_terms(
        query_block, grad_block, total_block, delta_block, key_block, value_block, key_keep
    ):
        scores = (
            jnp.einsum("qhe,khe->hqk", query_block, key_block, preferred_element_type=jnp.float32)
            * SCORE_SCALE
        )
        soft_weights = jnp.where(
            key_keep[None, None, :], jnp.exp(scores - total_block[..., None]), 0.0
        )
        prob_grad = jnp.einsum(
            "qhe,khe->hqk", grad_block, value_block, preferred_element_type=jnp.float32
        )
        score_grad = (soft_weights * (prob_grad - delta_block[..., None])).astype(jnp.bfloat16)
        return (soft_weights, score_grad)

    def back_block(query_grad, block_item):
        key_block, value_block, block_index = block_item
        key_keep = lax.dynamic_slice_in_dim(keep_all, block_index * span_rows, span_rows)
        soft_weights, score_grad = score_terms(
            query_heads, grad_heads, log_total, row_delta, key_block, value_block, key_keep
        )
        value_grad = jnp.einsum(
            "hqk,qhe->khe",
            soft_weights.astype(jnp.bfloat16),
            grad_heads,
            preferred_element_type=jnp.float32,
        )
        query_grad = query_grad + SCORE_SCALE * jnp.einsum(
            "hqk,khe->qhe", score_grad, key_block, preferred_element_type=jnp.float32
        )
        key_grad = SCORE_SCALE * jnp.einsum(
            "hqk,qhe->khe", score_grad, query_heads, preferred_element_type=jnp.float32
        )
        return (query_grad, (key_grad, value_grad))

    query_grad, (key_grads, value_grads) = lax.scan(
        back_block,
        jnp.zeros((span_rows, head_count, HEAD_DIM), jnp.float32),
        (key_stack, value_stack, jnp.arange(blocks_count, dtype=jnp.int32)),
    )
    key_grad_sum, value_grad_sum = (
        lax.psum_scatter(
            key_grads.reshape(seq_len, model_width).astype(jnp.bfloat16),
            "ctx",
            scatter_dimension=0,
            tiled=True,
        ).astype(jnp.float32),
        lax.psum_scatter(
            value_grads.reshape(seq_len, model_width).astype(jnp.bfloat16),
            "ctx",
            scatter_dimension=0,
            tiled=True,
        ).astype(jnp.float32),
    )
    query_grad_low = query_grad.reshape(span_rows, model_width).astype(jnp.bfloat16)
    key_grad_low = key_grad_sum.astype(jnp.bfloat16)
    value_grad_low = value_grad_sum.astype(jnp.bfloat16)
    grad_query_w = row_product(layer_in, query_grad_low)
    grad_key_w = row_product(layer_in, key_grad_low)
    grad_value_w = row_product(layer_in, value_grad_low)
    token_grad = (
        grad_hidden
        + by_transpose(query_grad_low, query_weight)
        + by_transpose(key_grad_low, key_weight)
        + by_transpose(value_grad_low, value_weight)
    )
    up_part, down_part, second_part = (
        lax.psum_scatter(
            grad_up_w.astype(jnp.bfloat16), "dp", scatter_dimension=0, tiled=True
        ).astype(jnp.float32),
        lax.psum_scatter(
            grad_down_w.astype(jnp.bfloat16), "dp", scatter_dimension=0, tiled=True
        ).astype(jnp.float32),
        lax.psum_scatter(
            grad_gain_second.astype(jnp.bfloat16), "dp", scatter_dimension=0, tiled=True
        ).astype(jnp.float32),
    )
    query_part, key_part, value_part, out_part, first_part = (
        lax.psum_scatter(
            grad_query_w.astype(jnp.bfloat16), "dp", scatter_dimension=0, tiled=True
        ).astype(jnp.float32),
        lax.psum_scatter(
            grad_key_w.astype(jnp.bfloat16), "dp", scatter_dimension=0, tiled=True
        ).astype(jnp.float32),
        lax.psum_scatter(
            grad_value_w.astype(jnp.bfloat16), "dp", scatter_dimension=0, tiled=True
        ).astype(jnp.float32),
        lax.psum_scatter(
            grad_out_w.astype(jnp.bfloat16), "dp", scatter_dimension=0, tiled=True
        ).astype(jnp.float32),
        lax.psum_scatter(
            grad_gain_first.astype(jnp.bfloat16), "dp", scatter_dimension=0, tiled=True
        ).astype(jnp.float32),
    )
    summed = (
        lax.psum(query_part.astype(jnp.bfloat16), "ctx").astype(jnp.float32),
        lax.psum(key_part.astype(jnp.bfloat16), "ctx").astype(jnp.float32),
        lax.psum(value_part.astype(jnp.bfloat16), "ctx").astype(jnp.float32),
        lax.psum(out_part.astype(jnp.bfloat16), "ctx").astype(jnp.float32),
        lax.psum(up_part.astype(jnp.bfloat16), "ctx").astype(jnp.float32),
        lax.psum(down_part.astype(jnp.bfloat16), "ctx").astype(jnp.float32),
        lax.psum(first_part.astype(jnp.bfloat16), "ctx").astype(jnp.float32),
        lax.psum(second_part.astype(jnp.bfloat16), "ctx").astype(jnp.float32),
    )
    query_sum, key_sum, value_sum, out_sum, up_sum, down_sum, first_sum, second_sum = summed
    return (
        in_order[None],
        loss_value,
        token_grad[None],
        query_sum,
        key_sum,
        value_sum,
        out_sum,
        up_sum,
        down_sum,
        first_sum,
        second_sum,
    )


class Place:
    def __init__(self):
        dp = lax.axis_index("dp")
        self.x = lax.axis_index("ctx")
        self.z, self.y, self.c = dp // 4, (dp // 2) % 2, dp % 2
        self.xo, self.yo, self.co = 1 - self.x, 1 - self.y, 1 - self.c
        self.to_x = (dp, self.xo)
        self.to_y = (self.z * 4 + self.yo * 2 + self.c, self.x)
        self.to_c = (self.z * 4 + self.y * 2 + self.co, self.x)
        self.z_up = [(self.z + k) % 4 for k in range(4)]
        self.z_down = [(self.z + 4 - k) % 4 for k in range(4)]
        self.to_z = [(self.z_up[k] * 4 + self.y * 2 + self.c, self.x) for k in range(4)]

    def barrier(self):
        semaphore = pltpu.get_barrier_semaphore()
        for partner in [self.to_x, self.to_y, self.to_c] + self.to_z[1:]:
            pl.semaphore_signal(semaphore, inc=1, device_id=partner, device_id_type=MESH)
        pl.semaphore_wait(semaphore, 6)


class Links:
    def __init__(self, send, recv):
        self.send, self.recv, self.used, self.flying = send, recv, 0, []
        self.free = list(range(send.shape[0]))

    def start(self, src, dst, partner):
        if not self.free:
            self.sent(self.flying[0][0])
        at = self.free.pop(0)
        copy = pltpu.make_async_remote_copy(
            src_ref=src,
            dst_ref=dst,
            send_sem=self.send.at[at],
            recv_sem=self.recv.at[self.used],
            device_id=partner,
            device_id_type=MESH,
        )
        self.used += 1
        copy.start()
        self.flying.append((copy, at))
        return copy

    def sent(self, copy):
        for entry in list(self.flying):
            if entry[0] is copy:
                copy.wait_send()
                self.free.append(entry[1])
        self.flying = [entry for entry in self.flying if entry[0] is not copy]

    def drain(self):
        for copy, at in list(self.flying):
            self.sent(copy)


class Gather:
    def __init__(self, block, early, shard, shift, whole, place, links, own_sem):
        first, last, self.split, self.col0, self.width = block
        self.early = early
        self.rows = pl.ds(first, last - first)
        self.shard, self.shift, self.whole = shard, shift, whole
        self.p, self.links = place, links
        self.own = pltpu.make_async_copy(
            shard.at[:, self.cols(shift)],
            whole.at[place.z, place.y, place.c, self.rows, self.cols()],
            own_sem,
        )
        self.last = 4 if self.split else 3

    def cols(self, shift=0):
        return pl.ds(self.col0 + shift, self.width)

    def half(self, x, shift=0):
        if not self.split:
            return self.cols(shift)
        size = self.width // 2
        return pl.ds(pl.multiple_of(self.col0 + shift + x * size, 128), size)

    def piece(self, z, y, cols):
        return self.whole.at[z, y, self.p.c, self.rows, cols]

    def push(self, piece, partner):
        return self.links.start(piece, piece, partner)

    def step0(self):
        p = self.p
        source = self.shard.at[:, self.half(p.x, self.shift)]
        target = self.piece(p.z, p.y, self.half(p.x))
        self.from_z = [self.links.start(source, target, p.to_z[k]) for k in range(1, 4)]
        self.own.start()
        if self.early:
            self.own_y()

    def own_y(self):
        p = self.p
        source = self.shard.at[:, self.half(p.x, self.shift)]
        self.from_y = [self.links.start(source, self.piece(p.z, p.y, self.half(p.x)), p.to_y)]

    def step1(self):
        p = self.p
        if not self.early:
            self.own_y()
        self.from_x = []
        for k in range(1, 4):
            self.from_z[k - 1].wait_recv()
            piece = self.piece(p.z_down[k], p.y, self.half(p.x))
            self.from_y.append(self.push(piece, p.to_y))
            if self.split:
                self.from_x.append(self.push(piece, p.to_x))
        self.own.wait()
        self.from_c = [self.push(self.piece(slice(None), p.y, self.half(p.x)), p.to_c)]

    def step2(self):
        p, every = self.p, slice(None)
        for copy in self.from_y:
            copy.wait_recv()
        piece = self.piece(every, p.yo, self.half(p.x))
        if self.split:
            self.across = self.push(piece, p.to_x)
        self.from_c.append(self.push(piece, p.to_c))
        if self.split:
            for copy in self.from_x:
                copy.wait_recv()
            self.from_c.append(self.push(self.piece(every, p.y, self.half(p.xo)), p.to_c))

    def step3(self):
        if self.split:
            self.across.wait_recv()
            piece = self.piece(slice(None), self.p.yo, self.half(self.p.xo))
            self.from_c.append(self.push(piece, self.p.to_c))
        else:
            self.step4()

    def step4(self):
        for copy in self.from_c:
            copy.wait_recv()


class Reduce:
    def __init__(self, block, at, grads, out, out0, shift, place, links, here, core_in, bufs):
        first, last, self.split, self.col0, self.width = block
        self.rows = last - first
        self.at0, self.here0, self.out0, self.shift = at, here, out0, shift
        self.at, self.here = pl.ds(at, self.rows), pl.ds(here, self.rows)
        self.grads, self.out = grads, out
        self.p, self.links = place, links
        self.core_in, self.bufs = core_in, bufs
        limit = max(48, 96 * 768 // self.width)
        self.block = max(b for b in range(16, min(self.rows, limit) + 1, 16) if self.rows % b == 0)
        self.stage = 0
        self.last = 5 if self.split else 4

    def cols(self, shift=0):
        return pl.ds(self.col0 + shift, self.width)

    def half(self, x, shift=0):
        if not self.split:
            return self.cols(shift)
        size = self.width // 2
        return pl.ds(pl.multiple_of(self.col0 + shift + x * size, 128), size)

    def low(self):
        return pl.ds(self.col0, self.width // 2)

    def high(self):
        return pl.ds(self.col0 + self.width // 2, self.width // 2) if self.split else self.cols()

    def add(self, outer, target, source):
        steps = self.rows // self.block

        def body(i, carry):
            first = pl.multiple_of((i % steps) * self.block, 16)
            put = target(i // steps, pl.ds(self.at0 + first, self.block))
            given = source(i // steps, pl.ds(self.here0 + first, self.block))
            self.grads[put] = (
                self.grads[put].astype(jnp.float32) + given.astype(jnp.float32)
            ).astype(jnp.bfloat16)
            return carry

        lax.fori_loop(0, outer * steps, body, 0)

    def step0(self):
        p = self.p
        self.by_core = self.links.start(
            self.grads.at[:, :, p.co, self.at, self.cols()],
            self.core_in.at[:, :, self.here, self.cols()],
            p.to_c,
        )

    def add_core(self, y):
        p = self.p
        self.add(
            4,
            lambda i, rows: (i, y, p.c, rows, self.cols()),
            lambda i, rows: self.core_in[i, y, rows, self.cols()],
        )

    def send_y(self):
        p = self.p
        self.by_y = self.links.start(
            self.grads.at[:, p.yo, p.c, self.at, self.half(p.x)],
            self.bufs(0, slice(None)).at[:, self.here, self.high()],
            p.to_y,
        )

    def step1(self):
        p = self.p
        self.by_core.wait_recv()
        self.add_core(p.yo)
        if not self.split:
            self.send_y()
        self.add_core(p.y)
        if self.split:
            self.by_x = [
                self.links.start(
                    self.grads.at[:, y, p.c, self.at, self.half(p.xo)],
                    self.bufs(i, slice(None)).at[:, self.here, self.low()],
                    p.to_x,
                )
                for i, y in enumerate((p.yo, p.y))
            ]

    def add_x(self, i, y):
        p = self.p
        self.by_x[i].wait_recv()
        self.add(
            4,
            lambda j, rows: (j, y, p.c, rows, self.half(p.x)),
            lambda j, rows: self.bufs(i, j)[rows, self.low()],
        )

    def step2(self):
        if self.split:
            self.add_x(0, self.p.yo)
            self.send_y()
            self.add_x(1, self.p.y)
        else:
            self.reduce_y()

    def reduce_y(self):
        p = self.p
        self.by_y.wait_recv()
        self.add(
            4,
            lambda i, rows: (i, p.y, p.c, rows, self.half(p.x)),
            lambda i, rows: self.bufs(0, i)[rows, self.high()],
        )
        self.by_z = [
            self.links.start(
                self.grads.at[p.z_up[k], p.y, p.c, self.at, self.half(p.x)],
                self.bufs(1, k - 1).at[self.here, self.high()],
                p.to_z[k],
            )
            for k in range(1, 4)
        ]

    def reduce_z(self, put):
        p = self.p
        for copy in self.by_z:
            copy.wait_recv()

        def body(i, carry):
            first = pl.multiple_of(i * self.block, 16)
            rows = pl.ds(self.here0 + first, self.block)
            place = (p.z, p.y, p.c, pl.ds(self.at0 + first, self.block), self.half(p.x))
            total = self.grads[place].astype(jnp.float32)
            for k in range(3):
                total = total + self.bufs(1, k)[rows, self.high()].astype(jnp.float32)
            put(pl.ds(self.out0 + first, self.block), place, total.astype(jnp.bfloat16))
            return carry

        lax.fori_loop(0, self.rows // self.block, body, 0)

    def step3(self):
        p = self.p
        if self.split:
            self.reduce_y()
            return

        def put(rows, place, value):
            self.grads[place] = value

        self.reduce_z(put)
        self.by_x = self.links.start(
            self.grads.at[p.z, p.y, p.c, self.at, self.cols()],
            self.bufs(1, 3).at[self.here, self.cols()],
            p.to_x,
        )

    def step4(self):
        p = self.p
        if self.split:

            def put(rows, place, value):
                self.out[rows, self.half(p.x, self.shift)] = value

            self.reduce_z(put)
            done = self.out.at[pl.ds(self.out0, self.rows), self.half(p.x, self.shift)]
            self.by_x = self.links.start(done, done, p.to_x)
            return
        self.by_x.wait_recv()

        def body(i, carry):
            first = pl.multiple_of(i * self.block, 16)
            rows = pl.ds(self.here0 + first, self.block)
            own = self.grads[p.z, p.y, p.c, pl.ds(self.at0 + first, self.block), self.cols()]
            self.out[pl.ds(self.out0 + first, self.block), self.cols(self.shift)] = (
                own.astype(jnp.float32) + self.bufs(1, 3)[rows, self.cols()].astype(jnp.float32)
            ).astype(jnp.bfloat16)
            return carry

        lax.fori_loop(0, self.rows // self.block, body, 0)

    def step5(self):
        self.by_x.wait_recv()

    def beat(self):
        getattr(self, "step" + str(self.stage))()
        self.stage += 1


class Total:
    last = 4

    def __init__(self, value, core_in, x_in, y_in, by_z, place, links):
        self.value, self.core_in, self.x_in, self.y_in, self.by_z = value, core_in, x_in, y_in, by_z
        self.p, self.links = place, links
        self.stage = 0

    def step0(self):
        self.copy = self.links.start(self.value.at[0], self.core_in, self.p.to_c)

    def step1(self):
        self.copy.wait_recv()
        self.value[1] = self.value[0] + self.core_in[...]
        self.copy = self.links.start(self.value.at[1], self.x_in, self.p.to_x)

    def step2(self):
        self.copy.wait_recv()
        self.value[2] = self.value[1] + self.x_in[...]
        self.copy = self.links.start(self.value.at[2], self.y_in, self.p.to_y)

    def step3(self):
        self.copy.wait_recv()
        z = self.p.z
        self.by_z[z] = self.value[2] + self.y_in[...]
        self.spread = [
            self.links.start(self.by_z.at[z], self.by_z.at[z], self.p.to_z[k]) for k in range(1, 4)
        ]

    def step4(self):
        for copy in self.spread:
            copy.wait_recv()

    def sum(self):
        return ((self.by_z[0] + self.by_z[1]) + self.by_z[2]) + self.by_z[3]

    def beat(self):
        getattr(self, "step" + str(self.stage))()
        self.stage += 1


ROOT_HALF = 0.7071067811865476
DENSITY = 0.3989422804014327


def dot(left, right):
    return jnp.dot(left, right, preferred_element_type=jnp.float32)


def turned(left, right):
    return lax.dot_general(
        left, right, (((0,), (0,)), ((), ())), preferred_element_type=jnp.float32
    )


def by_turned(left, right):
    return lax.dot_general(
        left, right, (((1,), (1,)), ((), ())), preferred_element_type=jnp.float32
    )


def layer_kernel(s, *refs):
    tokens, teacher, order_row, length, valid = refs[:5]
    weights, (ordered_out, total_out, token_out), outs = refs[5:11], refs[11:14], refs[14:18]
    refs = refs[8:]
    (W, G, tok, qs, ks, vs, dO, stat, attn, n1, r1, low1, act, gp, acc, teach, res_in, low2, gains, sums) = refs[10:30]
    total_refs, (send, recv, local), (order_col, core_in, bufs) = refs[30:35], refs[35:38], refs[38:]
    f32, bf16 = jnp.float32, jnp.bfloat16
    span, width, shard, downs = s.span, s.width, s.shard, s.downs
    pairs = width // 128
    third = width // 3
    place = Place()
    x, xo = place.x, place.xo
    links = Links(send, recv)

    def own(first, size):
        return pl.ds(pl.multiple_of(x * span + first, 16), size)

    def other(first, size):
        return pl.ds(pl.multiple_of(xo * span + first, 16), size)

    def loop(count, body):
        def step(i, carry):
            body(i)
            return carry

        lax.fori_loop(0, count, step, 0)

    def matrix(first):
        return W[:, :, :, first : first + shard, :].reshape(width, width)

    gathers = [
        Gather(block, i < s.early, weights[j], shift, W, place, links, local.at[i])
        for i, (block, (j, shift)) in enumerate(zip(s.gather_blocks, s.sources))
    ]
    n_gather = len(gathers)
    stages = [0] * n_gather
    forward = iter(s.forward)

    def advance():
        for i in next(forward):
            getattr(gathers[i], "step" + str(stages[i]))()
            stages[i] += 1

    def arrived(*blocks):
        advance()
        assert all(stages[i] > gathers[i].last for i in blocks)

    place.barrier()
    own_tokens = pltpu.make_async_copy(tokens, tok.at[own(0, span)], local.at[n_gather])
    own_tokens.start()
    own_teacher = pltpu.make_async_copy(teacher, gp.at[0], local.at[n_gather + 1])
    own_teacher.start()
    send_tokens = links.start(tokens, tok.at[own(0, span)], place.to_x)
    advance()
    order_col[...] = jnp.broadcast_to(order_row[...].astype(f32), (128, 2 * span)).T
    length_now = length[0]
    length_float = length_now.astype(f32)
    iota_rows = lax.broadcasted_iota(jnp.int32, (s.block, span), 1)

    def pick(c):
        rows = pl.ds(pl.multiple_of(c * span + x * s.block, 16), s.block)
        position = order_col[rows, :].astype(jnp.int32) - x * span
        chosen = iota_rows == jnp.concatenate([position] * (span // 128), axis=1)
        return jnp.where(chosen, 1.0, 0.0).astype(bf16)

    own_teacher.wait()
    for n in range(3):
        cols = slice(n * third, (n + 1) * third)
        gp[1, : s.block, cols] = dot(pick(xo), gp[0, :, cols]).astype(bf16)
        teach[x, :, cols] = dot(pick(x), gp[0, :, cols]).astype(bf16)
    teach_copy = links.start(gp.at[1, pl.ds(0, s.block)], teach.at[x], place.to_x)
    advance()
    arrived(0, 1, 2)

    own_tokens.wait()

    def project(rows, which):
        for first, target, scale in which:
            value = dot(tok[rows, :], matrix(first)).astype(bf16)
            target[rows, :] = value * scale if scale != 1.0 else value

    sets = ((0, qs, SCORE_SCALE), (shard, ks, 1.0), (2 * shard, vs, 1.0))
    project(own(0, span), sets)
    advance()
    send_tokens.wait_recv()
    project(other(0, span), sets)
    advance()

    lane = lax.broadcasted_iota(jnp.int32, (1, 128), 1)
    even32 = lane < HEAD_DIM
    even = jnp.where(even32, 1.0, 0.0).astype(bf16)
    odd = jnp.where(even32, 0.0, 1.0).astype(bf16)
    bias_row = jnp.where(order_row[0:1, :] < length_now, 0.0, MASKED)

    def attend(pair):
        lanes = slice(pair * 128, (pair + 1) * 128)
        query, key, value = qs[own(0, span), lanes], ks[:, lanes], vs[:, lanes]
        tops, mixed = [], []
        for keep, rest in ((even, odd), (odd, even)):
            scores = by_turned(query * keep, key) + bias_row
            top = jnp.max(scores, axis=1, keepdims=True)
            weight = jnp.exp(scores - top).astype(bf16)
            tops.append(top)
            mixed.append(dot(weight, value * keep + rest))
        part = jnp.where(even32, mixed[0], mixed[1])
        total = pltpu.roll(jnp.where(even32, mixed[1], mixed[0]), HEAD_DIM, 1)
        attn[:, lanes] = (part / total).astype(bf16)
        log_rows = (jnp.where(even32, tops[0], tops[1]) + jnp.log(total)).T
        for h in range(2):
            stat[x, 0, 2 * pair + h : 2 * pair + h + 1, :] = log_rows[
                h * HEAD_DIM : h * HEAD_DIM + 1, :
            ]

    for pair in range(pairs):
        attend(pair)
        advance()

    arrived(3)
    device = lax.broadcasted_iota(jnp.int32, (16, width), 0)
    feature = lax.broadcasted_iota(jnp.int32, (16, width), 1)
    mine = (feature // shard) == device
    spread = jnp.where(
        lax.broadcasted_iota(jnp.int32, (128, width), 1) % shard
        == lax.broadcasted_iota(jnp.int32, (128, width), 0),
        1.0,
        0.0,
    ).astype(bf16)
    gain_rows = W[:, :, :, s.gain0 : s.gain0 + 16, :128].reshape(16, 16, 128).astype(f32)
    for g in range(2):
        wide = dot(gain_rows[:, g, :].astype(bf16), spread)
        gains[g : g + 1, :] = jnp.sum(jnp.where(mine, wide, 0.0), axis=0, keepdims=True)

    acc[...] = dot(attn[...], matrix(s.out0))
    advance()
    rows_n = s.rows_n

    def wide_column(column):
        return jnp.broadcast_to(column, (rows_n, 128))

    def first_norm(b):
        first = pl.multiple_of(b * rows_n, 16)
        rows = pl.ds(first, rows_n)
        hidden = tok[own(first, rows_n), :].astype(f32) + acc[rows, :]
        center = hidden - jnp.mean(hidden, axis=1, keepdims=True)
        inverse = lax.rsqrt(jnp.mean(center * center, axis=1, keepdims=True) + EPSILON)
        normal = center * inverse
        n1[rows, :] = normal
        r1[rows, :] = wide_column(inverse)
        low1[rows, :] = (normal * gains[0:1, :]).astype(bf16)

    loop(span // rows_n, first_norm)
    advance()

    teach_copy.wait_recv()
    links.sent(teach_copy)

    def upward(p):
        for n in range(3):
            cols = slice(n * third, (n + 1) * third)
            weight = W[
                :, :, :, s.up0 + p * shard : s.up0 + (p + 1) * shard, cols
            ].reshape(width, third)
            value = dot(low1[...], weight)
            cdf = 0.5 * (1.0 + lax.erf(value * ROOT_HALF))
            act[p, :, cols] = (value * cdf).astype(bf16)
            gp[p, :, cols] = (cdf + value * (jnp.exp(-0.5 * value * value) * DENSITY)).astype(bf16)

    for p in range(s.panels):
        arrived(4 + p)
        upward(p)
        advance()
    for n in range(3):
        arrived(4 + s.panels + n)
        cols = slice(n * third, (n + 1) * third)
        value = None
        for p in range(s.panels):
            part = dot(act[p], W[p, :, :, s.down0 :, cols].reshape(width, third))
            value = part if value is None else value + part
        acc[:, cols] = value
        advance()

    sums[...] = jnp.zeros_like(sums)
    valid_total = jnp.full((1, 1), valid[0], jnp.int32).astype(f32)
    grad_scale = s.tokens / valid_total

    def fold(values):
        return jnp.sum(values.reshape(rows_n // 8, 8, width), axis=0)

    def second_norm(b):
        first = pl.multiple_of(b * rows_n, 16)
        rows = pl.ds(first, rows_n)
        hidden = n1[rows, :] * gains[0:1, :] + acc[rows, :]
        center = hidden - jnp.mean(hidden, axis=1, keepdims=True)
        inverse = lax.rsqrt(jnp.mean(center * center, axis=1, keepdims=True) + EPSILON)
        normal = center * inverse
        gain = gains[1:2, :]
        result = (normal * gain).astype(bf16)
        per = s.block // rows_n
        at = pl.ds(pl.multiple_of((b % per) * rows_n, 16), rows_n)
        target = teach[b // per, at, :].astype(f32)
        teach[b // per, at, :] = result
        live = order_col[own(first, rows_n), 0:1] < length_float
        error = jnp.where(live, result.astype(f32) - target, 0.0)
        sums[2] += fold(error * error)
        grad = (error * grad_scale).astype(bf16).astype(f32)
        sums[1] += fold(grad * normal)
        scaled = grad * gain
        grad_sum = inverse * (
            scaled
            - jnp.mean(scaled, axis=1, keepdims=True)
            - normal * jnp.mean(scaled * normal, axis=1, keepdims=True)
        )
        acc[rows, :] = grad_sum
        low2[rows, :] = grad_sum.astype(bf16)

    loop(span // rows_n, second_norm)
    links.drain()
    send_result = links.start(teach.at[xo], res_in, place.to_x)
    total_refs[0][0] = jnp.broadcast_to(
        jnp.sum(jnp.sum(sums[2], axis=0, keepdims=True), axis=1, keepdims=True), (8, 128)
    )
    total = Total(*total_refs, place, links)

    reduces = [total]
    backward = iter(s.backward)

    def beat():
        for i in next(backward):
            reduces[i].beat()

    def enter(block, out, shift=0, in_weights=False):
        first = block[0]
        reduces.append(
            Reduce(
                block,
                first + s.down0 if in_weights else first - s.out0,
                W if in_weights else G,
                outs[out],
                first if in_weights else 0,
                shift,
                place,
                links,
                first + s.up0 if in_weights else first - s.out0,
                W.at[:, :, 0] if in_weights else core_in,
                (lambda h, j: W.at[j, h, 1]) if in_weights else (lambda h, j: bufs.at[h, j]),
            )
        )

    def panel_grad(first, left, right):
        value = turned(left[...], right[...]).astype(bf16)
        at = first - s.out0
        G[:, :, :, at : at + shard, :] = value.reshape(4, 2, 2, shard, width)

    for n in range(3):
        cols = slice(n * third, (n + 1) * third)
        for p in range(s.panels):
            value = turned(act[p], low2[:, cols]).astype(bf16)
            G[p, :, :, s.down0 - s.out0 :, cols] = value.reshape(2, 2, downs, third)
        enter(s.down_blocks[n], 3)
        beat()

    def active_grad(p):
        value = by_turned(low2[...], W[p, :, :, s.down0 :, :].reshape(width, width))
        gp[p] = (value * gp[p].astype(f32)).astype(bf16)

    for p in range(s.panels):
        active_grad(p)
        beat()
        panel_grad(s.up0 + p * shard, low1, gp.at[p])
        enter(s.up_blocks[p], 2, p * width)
        beat()

    for p in range(s.panels):
        acc[...] += by_turned(gp[p], matrix(s.up0 + p * shard))
    beat()

    def first_back(b):
        rows = pl.ds(pl.multiple_of(b * rows_n, 16), rows_n)
        grad, normal = acc[rows, :], n1[rows, :]
        sums[0] += fold(grad * normal)
        scaled = grad * gains[0:1, :]
        hidden_grad = r1[rows, 0:1] * (
            scaled
            - jnp.mean(scaled, axis=1, keepdims=True)
            - normal * jnp.mean(scaled * normal, axis=1, keepdims=True)
        )
        acc[rows, :] = hidden_grad
        low2[rows, :] = hidden_grad.astype(bf16)

    loop(span // rows_n, first_back)
    beat()

    dO[...] = by_turned(low2[...], matrix(s.out0)).astype(bf16)
    head = lax.broadcasted_iota(jnp.int32, (16, width), 0)
    in_head = jnp.where((feature // HEAD_DIM) == head, 1.0, 0.0)

    def head_delta(b):
        first = pl.multiple_of(b * 128, 128)
        rows = pl.ds(first, 128)
        product = dO[rows, :].astype(f32) * attn[rows, :].astype(f32)
        stat[x, 1, :, rows] = lax.dot_general(
            in_head,
            product,
            (((1,), (1,)), ((), ())),
            precision=lax.Precision.HIGHEST,
            preferred_element_type=f32,
        )

    loop(span // 128, head_delta)
    send_grad = links.start(dO, tok.at[own(0, span)], place.to_x)
    send_stat = links.start(stat.at[x], stat.at[x], place.to_x)

    panel_grad(s.out0, attn, low2)
    pieces = []
    for g in range(2):
        row = jnp.sum(sums[g], axis=0, keepdims=True)
        split = jnp.where(mine, jnp.broadcast_to(row, (16, width)), 0.0).astype(bf16)
        pieces.append(by_turned(split, spread))
    at_row = lax.broadcasted_iota(jnp.int32, (16, 16, 128), 1)
    gain_block = jnp.where(
        at_row == 0, pieces[0][:, None, :], jnp.where(at_row == 1, pieces[1][:, None, :], 0.0)
    ).astype(bf16)
    G[:, :, :, shard : shard + 16, :128] = gain_block.reshape(4, 2, 2, 16, 128)
    G[:, :, :, shard : shard + 16, 128:] = jnp.zeros((4, 2, 2, 16, width - 128), bf16)
    enter(s.out_block, 1)
    beat()

    def block_terms(key, value, bias, query, grad, log_row, delta_row):
        scores = by_turned(key, query) + bias
        p = jnp.exp(scores - log_row)
        score_grad = (p * (by_turned(value, grad) - delta_row)).astype(bf16)
        return p.astype(bf16), score_grad

    def key_side(rows, lanes):
        column = jnp.where(order_col[rows, :] < length_float, 0.0, MASKED)
        return ks[rows, lanes], vs[rows, lanes], jnp.concatenate([column] * (span // 128), axis=1)

    def terms(key, value, bias, side, pair, h, keep):
        lanes = slice(pair * 128, (pair + 1) * 128)
        rows = pl.ds(pl.multiple_of(side * span, 16), span)
        grad = dO[:, lanes] if side is x else tok[rows, lanes]
        query, grad = qs[rows, lanes] * keep, grad * keep
        at = slice(2 * pair + h, 2 * pair + h + 1)
        p, score_grad = block_terms(
            key, value, bias, query, grad, stat[side, 0, at, :], stat[side, 1, at, :]
        )
        return query, grad, p, score_grad

    def back_queries(pair):
        lanes = slice(pair * 128, (pair + 1) * 128)
        result = to_keys = to_values = None
        for rows, mine in ((own(0, span), True), (other(0, span), False)):
            key, value, bias = key_side(rows, lanes)
            for h, keep in enumerate((even, odd)):
                query, grad, p, score_grad = terms(key, value, bias, x, pair, h, keep)
                part = turned(score_grad, key * keep)
                result = part if result is None else result + part
                if mine:
                    value_part, key_part = dot(p, grad), dot(score_grad, query)
                    to_values = value_part if to_values is None else to_values + value_part
                    to_keys = key_part if to_keys is None else to_keys + key_part
        act[0, :, lanes] = (result * SCORE_SCALE).astype(bf16)
        n1[:, lanes] = to_keys
        gp[0, :, lanes] = to_values.astype(bf16)

    def back_keys(pair):
        lanes = slice(pair * 128, (pair + 1) * 128)
        key, value, bias = key_side(own(0, span), lanes)
        to_keys, to_values = n1[:, lanes], gp[0, :, lanes].astype(f32)
        for h, keep in enumerate((even, odd)):
            query, grad, p, score_grad = terms(key, value, bias, xo, pair, h, keep)
            to_values = to_values + dot(p, grad)
            to_keys = to_keys + dot(score_grad, query)
        act[1, :, lanes] = to_keys.astype(bf16)
        act[2, :, lanes] = to_values.astype(bf16)

    def weight_grad(j, columns):
        value = turned(tok[own(0, span), :], act[j, :, columns]).astype(bf16)
        at = s.down0 + j * shard
        W[:, :, :, at : at + shard, columns] = value.reshape(4, 2, 2, shard, value.shape[1])

    for pair in range(pairs):
        back_queries(pair)
        beat()
    weight_grad(0, slice(0, width))
    enter(s.last_blocks[0], 0, in_weights=True)
    beat()
    send_grad.wait_recv()
    send_stat.wait_recv()
    for pair in range(pairs):
        back_keys(pair)
        if pair % 2 == 1:
            for j in (1, 2):
                weight_grad(j, slice((pair - 1) * 128, (pair + 1) * 128))
            enter(s.last_blocks[1 + pair // 2], 0, in_weights=True)
        beat()

    for j in range(3):
        acc[...] += by_turned(act[j], matrix(j * shard))
    token_copy = pltpu.make_async_copy(acc, token_out, local.at[n_gather])
    token_copy.start()
    beat()
    send_result.wait_recv()

    def place_rows(n):
        cols = pl.ds(pl.multiple_of(n * third, 128), third)
        value = None
        position = lax.broadcasted_iota(jnp.int32, (span, s.block), 0) + x * span
        for c, rows in ((x, teach[x, :, cols]), (xo, res_in[:, cols])):
            at = order_row[0:1, pl.ds(pl.multiple_of(c * span + x * s.block, 128), s.block)]
            chosen = jnp.where(position == at, 1.0, 0.0).astype(bf16)
            part = dot(chosen, rows)
            value = part if value is None else value + part
        low2[:, cols] = value.astype(bf16)

    loop(3, place_rows)
    ordered_copy = pltpu.make_async_copy(low2, ordered_out, local.at[n_gather + 1])
    ordered_copy.start()
    beat()
    beat()
    assert all(item.stage > item.last for item in reduces)
    total_out[...] = total.sum()
    token_copy.wait()
    ordered_copy.wait()
    links.drain()


class Sizes:
    def __init__(self, span, width, ff, shard, downs, tokens):
        self.span, self.width, self.shard, self.downs, self.tokens = span, width, shard, downs, tokens
        self.panels = ff // width
        self.block = span // 2
        self.out0 = 3 * shard
        self.gain0 = 4 * shard
        self.up0 = self.gain0 + 16
        self.down0 = self.up0 + self.panels * shard
        self.rows = self.down0 + downs
        blocks = [(j * shard, (j + 1) * shard, 0, width) for j in range(3)]
        blocks += [(self.out0, self.up0, 0, width)]
        for p in range(self.panels):
            blocks += [(self.up0 + p * shard, self.up0 + (p + 1) * shard, 0, width)]
        third = width // 3
        blocks += [(self.down0, self.rows, n * third, third) for n in range(3)]
        self.gather_blocks = [b[:2] + (i in GATHER_SPLIT,) + b[2:] for i, b in enumerate(blocks)]
        self.sources = [(j, 0) for j in range(4)] + [(4, p * width) for p in range(self.panels)]
        self.sources += [(5, 0)] * 3
        self.early = EARLY
        back = blocks[-3:] + blocks[4:-3] + [blocks[3], blocks[0]]
        back += [(shard, self.out0, n * third, third) for n in range(3)]
        back = [b[:2] + (i in REDUCE_SPLIT,) + b[2:] for i, b in enumerate(back)]
        self.down_blocks, self.up_blocks = back[:3], back[3:-5]
        self.out_block, self.last_blocks = back[-5], back[-4:]
        self.forward, self.backward = FORWARD, BACKWARD
        self.rows_n, self.flying = 64, 64


def layer(s, *args):
    bf16, f32 = jnp.bfloat16, jnp.float32
    span, width = s.span, s.width
    both = 2 * span
    anywhere = pl.BlockSpec(memory_space=pl.ANY)
    vmem = pl.BlockSpec(memory_space=pltpu.VMEM)
    smem = pl.BlockSpec(memory_space=pltpu.SMEM)
    back = s.down_blocks + s.up_blocks + [s.out_block] + s.last_blocks
    copies = sum(15 if b[2] else 9 for b in s.gather_blocks)
    copies += sum(8 if b[2] else 6 for b in back) + 6 + 5
    small = pltpu.VMEM((8, 128), f32)
    scratch = [
        pltpu.VMEM((4, 2, 2, s.rows, width), bf16),
        pltpu.VMEM((4, 2, 2, s.rows - s.out0, width), bf16),
        pltpu.VMEM((both, width), bf16),
        pltpu.VMEM((both, width), bf16),
        pltpu.VMEM((both, width), bf16),
        pltpu.VMEM((both, width), bf16),
        pltpu.VMEM((span, width), bf16),
        pltpu.VMEM((2, 2, 16, span), f32),
        pltpu.VMEM((span, width), bf16),
        pltpu.VMEM((span, width), f32),
        pltpu.VMEM((span, 128), f32),
        pltpu.VMEM((span, width), bf16),
        pltpu.VMEM((s.panels, span, width), bf16),
        pltpu.VMEM((s.panels, span, width), bf16),
        pltpu.VMEM((span, width), f32),
        pltpu.VMEM((2, s.block, width), bf16),
        pltpu.VMEM((s.block, width), bf16),
        pltpu.VMEM((span, width), bf16),
        pltpu.VMEM((8, width), f32),
        pltpu.VMEM((3, 8, width), f32),
        pltpu.VMEM((3, 8, 128), f32),
        small,
        small,
        small,
        pltpu.VMEM((4, 8, 128), f32),
        pltpu.SemaphoreType.DMA((s.flying,)),
        pltpu.SemaphoreType.DMA((copies,)),
        pltpu.SemaphoreType.DMA((len(s.gather_blocks) + 2,)),
        pltpu.VMEM((both, 128), f32),
        pltpu.VMEM((4, 2, s.rows - s.out0, width), bf16),
        pltpu.VMEM((2, 4, s.rows - s.out0, width), bf16),
    ]
    return pl.pallas_call(
        functools.partial(layer_kernel, s),
        out_shape=[
            jax.ShapeDtypeStruct((span, width), bf16),
            jax.ShapeDtypeStruct((8, 128), f32),
            jax.ShapeDtypeStruct((span, width), f32),
            jax.ShapeDtypeStruct((s.out0, width), bf16),
            jax.ShapeDtypeStruct((s.up0 - s.out0, width), bf16),
            jax.ShapeDtypeStruct((s.shard, s.panels * width), bf16),
            jax.ShapeDtypeStruct((s.downs, width), bf16),
        ],
        in_specs=[anywhere, anywhere, vmem, smem, smem] + [anywhere] * 6,
        out_specs=[anywhere, vmem, anywhere] + [vmem] * 4,
        scratch_shapes=scratch,
        compiler_params=pltpu.CompilerParams(
            collective_id=0, has_side_effects=True, vmem_limit_bytes=s.vmem
        ),
    )(*args)


def fused_shards(
    tokens,
    w_query,
    w_key,
    w_value,
    w_out,
    w_up,
    w_down,
    gain_attn,
    gain_ffn,
    teacher,
    seq_lengths,
    tok_perm,
    valid_count,
):
    f32 = jnp.float32
    dp_count = lax.axis_size("dp")
    span, width = tokens.shape[1:]
    shard, ff = w_up.shape
    seq_len = tok_perm.shape[1]
    s = Sizes(span, width, ff, shard, w_down.shape[0], seq_len * dp_count)
    s.vmem = 63 * MIB
    gain_rows = jnp.pad(jnp.stack([gain_attn, gain_ffn]), ((0, 14), (0, width - shard)))
    ordered, total, token_grad, qkv, out, up, down = layer(
        s,
        tokens[0],
        teacher[0],
        tok_perm,
        seq_lengths,
        valid_count,
        w_query,
        w_key,
        w_value,
        jnp.concatenate([w_out, gain_rows]),
        w_up,
        w_down,
    )
    loss = (total[0, 0] / (2.0 * width * valid_count[0].astype(f32))).reshape(1)
    return (
        ordered[None],
        loss,
        token_grad[None],
        qkv[:shard].astype(f32),
        qkv[shard : 2 * shard].astype(f32),
        qkv[2 * shard :].astype(f32),
        out[:shard].astype(f32),
        up.astype(f32),
        down.astype(f32),
        out[shard, :shard].astype(f32),
        out[shard + 1, :shard].astype(f32),
    )


def solution(mesh):
    in_specs = (
        P("dp", "ctx", None),
        P("dp", None),
        P("dp", None),
        P("dp", None),
        P("dp", None),
        P("dp", None),
        P("dp", None),
        P("dp"),
        P("dp"),
        P("dp", "ctx", None),
        P("dp"),
        P("dp", None),
        P(),
    )
    out_specs = (
        P("dp", "ctx", None),
        P(),
        P("dp", "ctx", None),
        P("dp", None),
        P("dp", None),
        P("dp", None),
        P("dp", None),
        P("dp", None),
        P("dp", None),
        P("dp"),
        P("dp"),
    )
    body = fused_shards if dict(mesh.shape) == {"dp": 16, "ctx": 2} else shards
    return jax.shard_map(body, mesh=mesh, in_specs=in_specs, out_specs=out_specs, check_vma=False)
```

```python
import functools
import math

import jax
import jax.numpy as jnp
from jax import lax
from jax.experimental import pallas as pl
from jax.experimental.pallas import tpu as pltpu
from jax.sharding import PartitionSpec as P

HEAD_DIM = 64


EPSILON = 1e-06
SCORE_SCALE = 0.125
MASKED = -1e30
MESH = pl.DeviceIdType.MESH
MIB = 1024 * 1024


GATHER_SPLIT = (1, 3, 5, 6, 7, 8, 9)
REDUCE_SPLIT = (1, 2, 7, 8, 9, 11)
EARLY = 4
FORWARD = ((0, 1, 2, 3, 4, 5, 6, 7, 8, 9, 10), (), (0, 1, 0, 0, 2, 2, 3, 2, 1, 3, 4, 1, 5, 1), (), (3, 4, 6), (3,), (4, 5, 7), (6,), (8,), (5,), (5, 7), (), (), (6, 9), (), (6,), (), (8,), (), (), (7, 7), (10,), (9, 8, 8), (), (9, 10, 9), (), (10,), ())
BACKWARD = ((0, 1), (0, 2), (3,), (1, 4), (2, 5), (3, 0, 6), (4, 5, 1, 0, 6, 7), (2, 7, 4), (), (3, 0, 1, 5, 8), (), (8, 4, 6), (2,), (), (5,), (7,), (1, 9), (3, 6, 10), (2, 8, 4, 9, 5, 10, 11), (2, 6, 7, 8, 11, 12), (3, 9, 12), (), (11, 8, 10, 7, 9, 3, 10, 11, 12, 8, 9, 11, 12, 10, 9, 10, 12, 12))


def gelu_exact(values):
    return 0.5 * values * (1.0 + lax.erf(values * 0.7071067811865476))


def norm_forward(hidden, gain_row):
    center = hidden - jnp.mean(hidden, axis=-1, keepdims=True)
    inverse = lax.rsqrt(jnp.mean(center * center, axis=-1, keepdims=True) + EPSILON)
    normal = center * inverse
    return (normal * gain_row, normal, inverse)


def norm_backward(grad_norm, gain_row, normal, inverse):
    scaled = grad_norm * gain_row
    grad_input = inverse * (
        scaled
        - jnp.mean(scaled, axis=-1, keepdims=True)
        - normal * jnp.mean(scaled * normal, axis=-1, keepdims=True)
    )
    return (grad_input, jnp.sum(grad_norm * normal, axis=0))


def row_product(left_mat, right_mat):
    return lax.dot_general(
        left_mat, right_mat, (((0,), (0,)), ((), ())), preferred_element_type=jnp.float32
    )


def by_transpose(left_mat, right_mat):
    return lax.dot_general(
        left_mat, right_mat, (((1,), (1,)), ((), ())), preferred_element_type=jnp.float32
    )


def shards(
    tokens,
    w_query,
    w_key,
    w_value,
    w_out,
    w_up,
    w_down,
    gain_attn,
    gain_ffn,
    teacher,
    seq_lengths,
    tok_perm,
    valid_count,
):
    ctx_count = lax.axis_size("ctx")
    ctx_rank = lax.axis_index("ctx")
    dp_count = lax.axis_size("dp")
    layer_in = tokens[0]
    span_rows, model_width = layer_in.shape
    head_count = model_width // HEAD_DIM
    dealt_order = tok_perm[0]
    seq_len = dealt_order.shape[0]
    length = seq_lengths[0]
    keep_all = dealt_order < length
    per_peer = span_rows // ctx_count
    query_weight, key_weight, value_weight, out_weight, gain_first = (
        lax.all_gather(w_query, "dp", axis=0, tiled=True),
        lax.all_gather(w_key, "dp", axis=0, tiled=True),
        lax.all_gather(w_value, "dp", axis=0, tiled=True),
        lax.all_gather(w_out, "dp", axis=0, tiled=True),
        lax.all_gather(gain_attn, "dp", axis=0, tiled=True),
    )
    up_weight, down_weight, gain_second = (
        lax.all_gather(w_up, "dp", axis=0, tiled=True),
        lax.all_gather(w_down, "dp", axis=0, tiled=True),
        lax.all_gather(gain_ffn, "dp", axis=0, tiled=True),
    )
    queries = jnp.dot(layer_in, query_weight, preferred_element_type=jnp.float32).astype(
        jnp.bfloat16
    )
    keys_own = jnp.dot(layer_in, key_weight, preferred_element_type=jnp.float32).astype(
        jnp.bfloat16
    )
    values_own = jnp.dot(layer_in, value_weight, preferred_element_type=jnp.float32).astype(
        jnp.bfloat16
    )
    query_heads = queries.reshape(span_rows, head_count, HEAD_DIM)
    initial = (
        jnp.full((head_count, span_rows), MASKED, jnp.float32),
        jnp.zeros((head_count, span_rows), jnp.float32),
        jnp.zeros((head_count, span_rows, HEAD_DIM), jnp.float32),
    )
    fold_state = initial
    key_piece = lax.all_gather(keys_own, "ctx", axis=0, tiled=True)
    value_piece = lax.all_gather(values_own, "ctx", axis=0, tiled=True)
    piece_rows = key_piece.shape[0]
    block_rows = math.gcd(piece_rows, span_rows)
    key_blocks = key_piece.reshape(piece_rows // block_rows, block_rows, head_count, HEAD_DIM)
    value_blocks = value_piece.reshape(piece_rows // block_rows, block_rows, head_count, HEAD_DIM)

    def step_block(block_state, block_item):
        running_max, running_sum, accumulated = block_state
        key_block, value_block, block_index = block_item
        key_keep = lax.dynamic_slice_in_dim(keep_all, block_index * block_rows, block_rows)
        scores = (
            jnp.einsum("qhe,khe->hqk", query_heads, key_block, preferred_element_type=jnp.float32)
            * SCORE_SCALE
        )
        scores = jnp.where(key_keep[None, None, :], scores, MASKED)
        new_max = jnp.maximum(running_max, jnp.max(scores, axis=-1))
        factor = jnp.exp(running_max - new_max)
        soft_weights = jnp.where(key_keep[None, None, :], jnp.exp(scores - new_max[..., None]), 0.0)
        running_sum = running_sum * factor + jnp.sum(soft_weights, axis=-1)
        accumulated = accumulated * factor[..., None] + jnp.einsum(
            "hqk,khe->hqe",
            soft_weights.astype(jnp.bfloat16),
            value_block,
            preferred_element_type=jnp.float32,
        )
        return ((new_max, running_sum, accumulated), None)

    block_indices = jnp.arange(piece_rows // block_rows, dtype=jnp.int32)
    fold_state, unused = lax.scan(step_block, fold_state, (key_blocks, value_blocks, block_indices))
    run_max, run_sum, accumulated = fold_state
    log_total = run_max + jnp.log(run_sum)
    attn_full = jnp.transpose(accumulated / run_sum[..., None], (1, 0, 2)).reshape(
        span_rows, model_width
    )
    attn_low = attn_full.astype(jnp.bfloat16)
    gain_first32 = gain_first.astype(jnp.float32)
    gain_second32 = gain_second.astype(jnp.float32)
    branch = jnp.dot(attn_low, out_weight, preferred_element_type=jnp.float32)
    normed, normal_first, inverse_first = norm_forward(
        layer_in.astype(jnp.float32) + branch, gain_first32
    )
    normed_low = normed.astype(jnp.bfloat16)
    upward = jnp.dot(normed_low, up_weight, preferred_element_type=jnp.float32)
    active, gelu_pull = jax.vjp(gelu_exact, upward)
    active_low = active.astype(jnp.bfloat16)
    down_out = jnp.dot(active_low, down_weight, preferred_element_type=jnp.float32)
    result, normal_second, inverse_second = norm_forward(normed + down_out, gain_second32)
    result_low = result.astype(jnp.bfloat16)
    arrived = lax.all_to_all(result_low, "ctx", split_axis=0, concat_axis=0, tiled=True)
    sources = (
        jnp.arange(ctx_count, dtype=jnp.int32)[:, None] * span_rows
        + ctx_rank * per_peer
        + jnp.arange(per_peer, dtype=jnp.int32)[None, :]
    ).reshape(span_rows)
    local_pos = jnp.take(dealt_order, sources) - ctx_rank * span_rows
    in_order = jnp.zeros_like(arrived).at[local_pos].set(arrived)
    target = teacher[0].astype(jnp.float32)
    live_rows = (ctx_rank * span_rows + jnp.arange(span_rows, dtype=jnp.int32) < length)[:, None]
    residual_err = jnp.where(live_rows, in_order.astype(jnp.float32) - target, 0.0)
    total_sq = lax.psum(jnp.sum(residual_err * residual_err), ("dp", "ctx"))
    valid_total = valid_count[0].astype(jnp.float32)
    loss_value = (total_sq / (2.0 * model_width * valid_total)).reshape(1)
    grad_scale = seq_len * dp_count / valid_total
    grad_order = (residual_err * grad_scale).astype(jnp.bfloat16)
    outgoing = jnp.take(grad_order, local_pos, axis=0)
    grad_result = lax.all_to_all(outgoing, "ctx", split_axis=0, concat_axis=0, tiled=True).astype(
        jnp.float32
    )
    grad_sum_second, grad_gain_second = norm_backward(
        grad_result, gain_second32, normal_second, inverse_second
    )
    down_grad_low = grad_sum_second.astype(jnp.bfloat16)
    grad_down_w = row_product(active_low, down_grad_low)
    grad_active = by_transpose(down_grad_low, down_weight)
    grad_upward = gelu_pull(grad_active)[0].astype(jnp.bfloat16)
    grad_up_w = row_product(normed_low, grad_upward)
    grad_normed = grad_sum_second + by_transpose(grad_upward, up_weight)
    grad_hidden, grad_gain_first = norm_backward(
        grad_normed, gain_first32, normal_first, inverse_first
    )
    branch_grad = grad_hidden.astype(jnp.bfloat16)
    grad_out_w = row_product(attn_low, branch_grad)
    attn_grad_low = by_transpose(branch_grad, out_weight).astype(jnp.bfloat16)
    grad_heads = attn_grad_low.reshape(span_rows, head_count, HEAD_DIM)
    row_delta = jnp.sum(
        (attn_grad_low.astype(jnp.float32) * attn_full).reshape(span_rows, head_count, HEAD_DIM),
        axis=-1,
    ).T
    keys_all, values_all = (
        lax.all_gather(keys_own, "ctx", axis=0, tiled=True),
        lax.all_gather(values_own, "ctx", axis=0, tiled=True),
    )
    blocks_count = seq_len // span_rows
    key_stack = keys_all.reshape(blocks_count, span_rows, head_count, HEAD_DIM)
    value_stack = values_all.reshape(blocks_count, span_rows, head_count, HEAD_DIM)

    def score_terms(
        query_block, grad_block, total_block, delta_block, key_block, value_block, key_keep
    ):
        scores = (
            jnp.einsum("qhe,khe->hqk", query_block, key_block, preferred_element_type=jnp.float32)
            * SCORE_SCALE
        )
        soft_weights = jnp.where(
            key_keep[None, None, :], jnp.exp(scores - total_block[..., None]), 0.0
        )
        prob_grad = jnp.einsum(
            "qhe,khe->hqk", grad_block, value_block, preferred_element_type=jnp.float32
        )
        score_grad = (soft_weights * (prob_grad - delta_block[..., None])).astype(jnp.bfloat16)
        return (soft_weights, score_grad)

    def back_block(query_grad, block_item):
        key_block, value_block, block_index = block_item
        key_keep = lax.dynamic_slice_in_dim(keep_all, block_index * span_rows, span_rows)
        soft_weights, score_grad = score_terms(
            query_heads, grad_heads, log_total, row_delta, key_block, value_block, key_keep
        )
        value_grad = jnp.einsum(
            "hqk,qhe->khe",
            soft_weights.astype(jnp.bfloat16),
            grad_heads,
            preferred_element_type=jnp.float32,
        )
        query_grad = query_grad + SCORE_SCALE * jnp.einsum(
            "hqk,khe->qhe", score_grad, key_block, preferred_element_type=jnp.float32
        )
        key_grad = SCORE_SCALE * jnp.einsum(
            "hqk,qhe->khe", score_grad, query_heads, preferred_element_type=jnp.float32
        )
        return (query_grad, (key_grad, value_grad))

    query_grad, (key_grads, value_grads) = lax.scan(
        back_block,
        jnp.zeros((span_rows, head_count, HEAD_DIM), jnp.float32),
        (key_stack, value_stack, jnp.arange(blocks_count, dtype=jnp.int32)),
    )
    key_grad_sum, value_grad_sum = (
        lax.psum_scatter(
            key_grads.reshape(seq_len, model_width).astype(jnp.bfloat16),
            "ctx",
            scatter_dimension=0,
            tiled=True,
        ).astype(jnp.float32),
        lax.psum_scatter(
            value_grads.reshape(seq_len, model_width).astype(jnp.bfloat16),
            "ctx",
            scatter_dimension=0,
            tiled=True,
        ).astype(jnp.float32),
    )
    query_grad_low = query_grad.reshape(span_rows, model_width).astype(jnp.bfloat16)
    key_grad_low = key_grad_sum.astype(jnp.bfloat16)
    value_grad_low = value_grad_sum.astype(jnp.bfloat16)
    grad_query_w = row_product(layer_in, query_grad_low)
    grad_key_w = row_product(layer_in, key_grad_low)
    grad_value_w = row_product(layer_in, value_grad_low)
    token_grad = (
        grad_hidden
        + by_transpose(query_grad_low, query_weight)
        + by_transpose(key_grad_low, key_weight)
        + by_transpose(value_grad_low, value_weight)
    )
    up_part, down_part, second_part = (
        lax.psum_scatter(
            grad_up_w.astype(jnp.bfloat16), "dp", scatter_dimension=0, tiled=True
        ).astype(jnp.float32),
        lax.psum_scatter(
            grad_down_w.astype(jnp.bfloat16), "dp", scatter_dimension=0, tiled=True
        ).astype(jnp.float32),
        lax.psum_scatter(
            grad_gain_second.astype(jnp.bfloat16), "dp", scatter_dimension=0, tiled=True
        ).astype(jnp.float32),
    )
    query_part, key_part, value_part, out_part, first_part = (
        lax.psum_scatter(
            grad_query_w.astype(jnp.bfloat16), "dp", scatter_dimension=0, tiled=True
        ).astype(jnp.float32),
        lax.psum_scatter(
            grad_key_w.astype(jnp.bfloat16), "dp", scatter_dimension=0, tiled=True
        ).astype(jnp.float32),
        lax.psum_scatter(
            grad_value_w.astype(jnp.bfloat16), "dp", scatter_dimension=0, tiled=True
        ).astype(jnp.float32),
        lax.psum_scatter(
            grad_out_w.astype(jnp.bfloat16), "dp", scatter_dimension=0, tiled=True
        ).astype(jnp.float32),
        lax.psum_scatter(
            grad_gain_first.astype(jnp.bfloat16), "dp", scatter_dimension=0, tiled=True
        ).astype(jnp.float32),
    )
    summed = (
        lax.psum(query_part.astype(jnp.bfloat16), "ctx").astype(jnp.float32),
        lax.psum(key_part.astype(jnp.bfloat16), "ctx").astype(jnp.float32),
        lax.psum(value_part.astype(jnp.bfloat16), "ctx").astype(jnp.float32),
        lax.psum(out_part.astype(jnp.bfloat16), "ctx").astype(jnp.float32),
        lax.psum(up_part.astype(jnp.bfloat16), "ctx").astype(jnp.float32),
        lax.psum(down_part.astype(jnp.bfloat16), "ctx").astype(jnp.float32),
        lax.psum(first_part.astype(jnp.bfloat16), "ctx").astype(jnp.float32),
        lax.psum(second_part.astype(jnp.bfloat16), "ctx").astype(jnp.float32),
    )
    query_sum, key_sum, value_sum, out_sum, up_sum, down_sum, first_sum, second_sum = summed
    return (
        in_order[None],
        loss_value,
        token_grad[None],
        query_sum,
        key_sum,
        value_sum,
        out_sum,
        up_sum,
        down_sum,
        first_sum,
        second_sum,
    )


class Place:
    def __init__(self):
        dp = lax.axis_index("dp")
        self.x = lax.axis_index("ctx")
        self.z, self.y, self.c = dp // 4, (dp // 2) % 2, dp % 2
        self.xo, self.yo, self.co = 1 - self.x, 1 - self.y, 1 - self.c
        self.to_x = (dp, self.xo)
        self.to_y = (self.z * 4 + self.yo * 2 + self.c, self.x)
        self.to_c = (self.z * 4 + self.y * 2 + self.co, self.x)
        self.z_up = [(self.z + k) % 4 for k in range(4)]
        self.z_down = [(self.z + 4 - k) % 4 for k in range(4)]
        self.to_z = [(self.z_up[k] * 4 + self.y * 2 + self.c, self.x) for k in range(4)]

    def barrier(self):
        semaphore = pltpu.get_barrier_semaphore()
        for partner in [self.to_x, self.to_y, self.to_c] + self.to_z[1:]:
            pl.semaphore_signal(semaphore, inc=1, device_id=partner, device_id_type=MESH)
        pl.semaphore_wait(semaphore, 6)


class Copy:
    def __init__(self, refs, send, at, recv, to, partner):
        self.refs, self.send, self.at, self.recv, self.to = refs, send, at, recv, to
        self.partner = partner

    def make(self):
        src, dst = self.refs()
        return pltpu.make_async_remote_copy(
            src_ref=src,
            dst_ref=dst,
            send_sem=self.send.at[self.at],
            recv_sem=self.recv.at[self.to],
            device_id=self.partner,
            device_id_type=MESH,
        )

    def wait_send(self):
        self.make().wait_send()

    def wait_recv(self):
        self.make().wait_recv()


class Links:
    def __init__(self, send, recv):
        self.send, self.recv, self.used, self.flying = send, recv, 0, []
        self.free = list(range(send.shape[0]))

    def start(self, refs, partner):
        if not self.free:
            self.sent(self.flying[0][0])
        at = self.free.pop(0)
        copy = Copy(refs, self.send, at, self.recv, self.used, partner)
        self.used += 1
        copy.make().start()
        self.flying.append((copy, at))
        return copy

    def sent(self, copy):
        for entry in list(self.flying):
            if entry[0] is copy:
                copy.wait_send()
                self.free.append(entry[1])
        self.flying = [entry for entry in self.flying if entry[0] is not copy]

    def drain(self):
        for copy, at in list(self.flying):
            self.sent(copy)


class Gather:
    def __init__(self, block, early, shard, shift, whole, place, links, own_sem):
        first, last, self.split, self.col0, self.width = block
        self.early = early
        self.rows = pl.ds(first, last - first)
        self.shard, self.shift, self.whole = shard, shift, whole
        self.p, self.links = place, links
        self.own_sem = own_sem
        self.mine, self.theirs = self.half(place.x), self.half(place.xo)
        self.source = self.half(place.x, shift)
        self.last = 4 if self.split else 3

    def cols(self, shift=0):
        return pl.ds(self.col0 + shift, self.width)

    def half(self, x, shift=0):
        if not self.split:
            return self.cols(shift)
        size = self.width // 2
        return pl.ds(pl.multiple_of(self.col0 + shift + x * size, 128), size)

    def piece(self, z, y, cols):
        return self.whole.at[z, y, self.p.c, self.rows, cols]

    def own(self):
        p = self.p
        return pltpu.make_async_copy(
            self.shard.at[:, self.cols(self.shift)], self.piece(p.z, p.y, self.cols()), self.own_sem()
        )

    def push(self, z, y, cols, partner):
        return self.links.start(lambda: (self.piece(z, y, cols),) * 2, partner)

    def send_own(self, partner):
        p = self.p
        return self.links.start(
            lambda: (self.shard.at[:, self.source], self.piece(p.z, p.y, self.mine)), partner
        )

    def step0(self):
        p = self.p
        self.from_z = [self.send_own(p.to_z[k]) for k in range(1, 4)]
        self.own().start()
        if self.early:
            self.own_y()

    def own_y(self):
        self.from_y = [self.send_own(self.p.to_y)]

    def step1(self):
        p = self.p
        if not self.early:
            self.own_y()
        self.from_x = []
        for k in range(1, 4):
            self.from_z[k - 1].wait_recv()
            piece = (p.z_down[k], p.y, self.mine)
            self.from_y.append(self.push(*piece, p.to_y))
            if self.split:
                self.from_x.append(self.push(*piece, p.to_x))
        self.own().wait()
        self.from_c = [self.push(slice(None), p.y, self.mine, p.to_c)]

    def step2(self):
        p, every = self.p, slice(None)
        for copy in self.from_y:
            copy.wait_recv()
        if self.split:
            self.across = self.push(every, p.yo, self.mine, p.to_x)
        self.from_c.append(self.push(every, p.yo, self.mine, p.to_c))
        if self.split:
            for copy in self.from_x:
                copy.wait_recv()
            self.from_c.append(self.push(every, p.y, self.theirs, p.to_c))

    def step3(self):
        if self.split:
            self.across.wait_recv()
            self.from_c.append(self.push(slice(None), self.p.yo, self.theirs, self.p.to_c))
        else:
            self.step4()

    def step4(self):
        for copy in self.from_c:
            copy.wait_recv()


class Reduce:
    def __init__(self, block, at, grads, out, out0, shift, place, links, here, core_in, bufs):
        first, last, self.split, self.col0, self.width = block
        self.rows = last - first
        self.at0, self.here0, self.out0, self.shift = at, here, out0, shift
        self.at, self.here = pl.ds(at, self.rows), pl.ds(here, self.rows)
        self.grads, self.out = grads, out
        self.p, self.links = place, links
        self.core_in, self.bufs = core_in, bufs
        limit = 32 * 768 // self.width
        self.block = max(b for b in range(16, min(self.rows, limit) + 1, 16) if self.rows % b == 0)
        self.stage = 0
        self.mine, self.theirs = self.half(place.x), self.half(place.xo)
        self.out_mine = self.half(place.x, shift)
        self.last = 5 if self.split else 4

    def cols(self, shift=0):
        return pl.ds(self.col0 + shift, self.width)

    def half(self, x, shift=0):
        if not self.split:
            return self.cols(shift)
        size = self.width // 2
        return pl.ds(pl.multiple_of(self.col0 + shift + x * size, 128), size)

    def low(self):
        return pl.ds(self.col0, self.width // 2)

    def high(self):
        return pl.ds(self.col0 + self.width // 2, self.width // 2) if self.split else self.cols()

    def add(self, outer, target, source):
        steps = self.rows // self.block

        def body(i, carry):
            first = pl.multiple_of((i % steps) * self.block, 16)
            put = target(i // steps, pl.ds(self.at0 + first, self.block))
            given = source(i // steps, pl.ds(self.here0 + first, self.block))
            self.grads[put] = (
                self.grads[put].astype(jnp.float32) + given.astype(jnp.float32)
            ).astype(jnp.bfloat16)
            return carry

        lax.fori_loop(0, outer * steps, body, 0)

    def step0(self):
        p = self.p
        self.by_core = self.links.start(
            lambda: (
                self.grads.at[:, :, p.co, self.at, self.cols()],
                self.core_in().at[:, :, self.here, self.cols()],
            ),
            p.to_c,
        )

    def add_core(self, y):
        p = self.p
        self.add(
            4,
            lambda i, rows: (i, y, p.c, rows, self.cols()),
            lambda i, rows: self.core_in()[i, y, rows, self.cols()],
        )

    def send_y(self):
        p = self.p
        self.by_y = self.links.start(
            lambda: (
                self.grads.at[:, p.yo, p.c, self.at, self.mine],
                self.bufs(0, slice(None)).at[:, self.here, self.high()],
            ),
            p.to_y,
        )

    def step1(self):
        p = self.p
        self.by_core.wait_recv()
        self.add_core(p.yo)
        if not self.split:
            self.send_y()
        self.add_core(p.y)
        if self.split:
            self.by_x = [self.send_x(0, p.yo), self.send_x(1, p.y)]

    def send_x(self, i, y):
        p = self.p
        return self.links.start(
            lambda: (
                self.grads.at[:, y, p.c, self.at, self.theirs],
                self.bufs(i, slice(None)).at[:, self.here, self.low()],
            ),
            p.to_x,
        )

    def add_x(self, i, y):
        p = self.p
        self.by_x[i].wait_recv()
        self.add(
            4,
            lambda j, rows: (j, y, p.c, rows, self.mine),
            lambda j, rows: self.bufs(i, j)[rows, self.low()],
        )

    def step2(self):
        if self.split:
            self.add_x(0, self.p.yo)
            self.send_y()
            self.add_x(1, self.p.y)
        else:
            self.reduce_y()

    def reduce_y(self):
        p = self.p
        self.by_y.wait_recv()
        self.add(
            4,
            lambda i, rows: (i, p.y, p.c, rows, self.mine),
            lambda i, rows: self.bufs(0, i)[rows, self.high()],
        )
        self.by_z = [self.send_z(k) for k in range(1, 4)]

    def send_z(self, k):
        p = self.p
        return self.links.start(
            lambda: (
                self.grads.at[p.z_up[k], p.y, p.c, self.at, self.mine],
                self.bufs(1, k - 1).at[self.here, self.high()],
            ),
            p.to_z[k],
        )

    def reduce_z(self, put):
        p = self.p
        for copy in self.by_z:
            copy.wait_recv()

        def body(i, carry):
            first = pl.multiple_of(i * self.block, 16)
            rows = pl.ds(self.here0 + first, self.block)
            place = (p.z, p.y, p.c, pl.ds(self.at0 + first, self.block), self.mine)
            total = self.grads[place].astype(jnp.float32)
            for k in range(3):
                total = total + self.bufs(1, k)[rows, self.high()].astype(jnp.float32)
            put(pl.ds(self.out0 + first, self.block), place, total.astype(jnp.bfloat16))
            return carry

        lax.fori_loop(0, self.rows // self.block, body, 0)

    def step3(self):
        p = self.p
        if self.split:
            self.reduce_y()
            return

        def put(rows, place, value):
            self.grads[place] = value

        self.reduce_z(put)
        self.by_x = self.links.start(
            lambda: (
                self.grads.at[p.z, p.y, p.c, self.at, self.cols()],
                self.bufs(1, 3).at[self.here, self.cols()],
            ),
            p.to_x,
        )

    def step4(self):
        p = self.p
        if self.split:

            def put(rows, place, value):
                self.out[rows, self.out_mine] = value

            self.reduce_z(put)
            self.by_x = self.links.start(
                lambda: (self.out.at[pl.ds(self.out0, self.rows), self.out_mine],) * 2, p.to_x
            )
            return
        self.by_x.wait_recv()

        def body(i, carry):
            first = pl.multiple_of(i * self.block, 16)
            rows = pl.ds(self.here0 + first, self.block)
            own = self.grads[p.z, p.y, p.c, pl.ds(self.at0 + first, self.block), self.cols()]
            self.out[pl.ds(self.out0 + first, self.block), self.cols(self.shift)] = (
                own.astype(jnp.float32) + self.bufs(1, 3)[rows, self.cols()].astype(jnp.float32)
            ).astype(jnp.bfloat16)
            return carry

        lax.fori_loop(0, self.rows // self.block, body, 0)

    def step5(self):
        self.by_x.wait_recv()

    def beat(self):
        getattr(self, "step" + str(self.stage))()
        self.stage += 1


class Total:
    last = 4

    def __init__(self, value, core_in, x_in, y_in, by_z, place, links):
        self.value, self.core_in, self.x_in, self.y_in, self.by_z = value, core_in, x_in, y_in, by_z
        self.p, self.links = place, links
        self.stage = 0

    def step0(self):
        self.copy = self.links.start(lambda: (self.value.at[0], self.core_in), self.p.to_c)

    def step1(self):
        self.copy.wait_recv()
        self.value[1] = self.value[0] + self.core_in[...]
        self.copy = self.links.start(lambda: (self.value.at[1], self.x_in), self.p.to_x)

    def step2(self):
        self.copy.wait_recv()
        self.value[2] = self.value[1] + self.x_in[...]
        self.copy = self.links.start(lambda: (self.value.at[2], self.y_in), self.p.to_y)

    def step3(self):
        self.copy.wait_recv()
        z = self.p.z
        self.by_z[z] = self.value[2] + self.y_in[...]
        self.spread = [
            self.links.start(lambda: (self.by_z.at[z],) * 2, self.p.to_z[k]) for k in range(1, 4)
        ]

    def step4(self):
        for copy in self.spread:
            copy.wait_recv()

    def sum(self):
        return ((self.by_z[0] + self.by_z[1]) + self.by_z[2]) + self.by_z[3]

    def beat(self):
        getattr(self, "step" + str(self.stage))()
        self.stage += 1


ROOT_HALF = 0.7071067811865476
DENSITY = 0.3989422804014327


def dot(left, right):
    return jnp.dot(left, right, preferred_element_type=jnp.float32)


def turned(left, right):
    return lax.dot_general(
        left, right, (((0,), (0,)), ((), ())), preferred_element_type=jnp.float32
    )


def by_turned(left, right):
    return lax.dot_general(
        left, right, (((1,), (1,)), ((), ())), preferred_element_type=jnp.float32
    )


def layer_kernel(s, *refs):
    tokens, teacher, order_row, length, valid = refs[:5]
    weights, (ordered_out, total_out, token_out), outs = refs[5:11], refs[11:14], refs[14:18]
    refs = refs[8:]
    (W, G, tok, QKV, dO, stat, attn, n1, r1, low1, act, gp, acc, teach, res_in, low2, gains, sums) = refs[10:28]
    total_refs, (send, recv, local), (order_col, core_in, bufs) = refs[28:33], refs[33:36], refs[36:]
    qs, ks, vs = QKV.at[0], QKV.at[1], QKV.at[2]
    f32, bf16 = jnp.float32, jnp.bfloat16
    span, width, shard, downs = s.span, s.width, s.shard, s.downs
    pairs = width // 128
    third = width // 3
    place = Place()
    x, xo = place.x, place.xo
    links = Links(send, recv)

    def own(first, size):
        return pl.ds(pl.multiple_of(x * span + first, 16), size)

    def other(first, size):
        return pl.ds(pl.multiple_of(xo * span + first, 16), size)

    def loop(count, body):
        def step(i, carry):
            body(i)
            return carry

        lax.fori_loop(0, count, step, 0)

    def each(i, count, action):
        for k in range(count):
            pl.when(i == k)(lambda: action())

    def matrix(first):
        return W[:, :, :, pl.ds(pl.multiple_of(first, 16), shard), :].reshape(width, width)

    def semaphore(i):
        return local.at[i]

    gathers = [
        Gather(block, i < s.early, weights[j], shift, W, place, links, functools.partial(semaphore, i))
        for i, (block, (j, shift)) in enumerate(zip(s.gather_blocks, s.sources))
    ]
    n_gather = len(gathers)
    stages = [0] * n_gather
    forward = iter(s.forward)

    def advance():
        for i in next(forward):
            getattr(gathers[i], "step" + str(stages[i]))()
            stages[i] += 1

    def arrived(*blocks):
        advance()
        assert all(stages[i] > gathers[i].last for i in blocks)

    place.barrier()
    own_tokens = pltpu.make_async_copy(tokens, tok.at[own(0, span)], local.at[n_gather])
    own_tokens.start()
    own_teacher = pltpu.make_async_copy(teacher, gp.at[0], local.at[n_gather + 1])
    own_teacher.start()
    send_tokens = links.start(lambda: (tokens, tok.at[own(0, span)]), place.to_x)
    advance()
    order_col[...] = jnp.broadcast_to(order_row[...].astype(f32), (128, 2 * span)).T
    length_now = length[0]
    length_float = length_now.astype(f32)
    iota_rows = lax.broadcasted_iota(jnp.int32, (s.block, span), 1)

    def pick(c):
        rows = pl.ds(pl.multiple_of(c * span + x * s.block, 16), s.block)
        position = order_col[rows, :].astype(jnp.int32) - x * span
        chosen = iota_rows == jnp.concatenate([position] * (span // 128), axis=1)
        return jnp.where(chosen, 1.0, 0.0).astype(bf16)

    own_teacher.wait()
    for n in range(3):
        cols = slice(n * third, (n + 1) * third)
        gp[1, : s.block, cols] = dot(pick(xo), gp[0, :, cols]).astype(bf16)
        teach[x, :, cols] = dot(pick(x), gp[0, :, cols]).astype(bf16)
    teach_copy = links.start(lambda: (gp.at[1, pl.ds(0, s.block)], teach.at[x]), place.to_x)
    advance()
    arrived(0, 1, 2)

    own_tokens.wait()

    def side(i):
        @pl.when(i == 1)
        def _():
            send_tokens.wait_recv()

        rows = pl.ds(pl.multiple_of(jnp.where(i == 0, x, xo) * span, 16), span)

        def project(j):
            scale = jnp.where(j == 0, SCORE_SCALE, 1.0)
            QKV[j, rows, :] = (dot(tok[rows, :], matrix(j * shard)) * scale).astype(bf16)

        loop(3, project)
        each(i, 2, advance)

    loop(2, side)

    lane = lax.broadcasted_iota(jnp.int32, (1, 128), 1)
    even32 = lane < HEAD_DIM
    even = jnp.where(even32, 1.0, 0.0).astype(bf16)
    odd = jnp.where(even32, 0.0, 1.0).astype(bf16)
    bias_row = jnp.where(order_row[0:1, :] < length_now, 0.0, MASKED)

    def attend(pair):
        lanes = pl.ds(pl.multiple_of(pair * 128, 128), 128)
        query, key, value = qs[own(0, span), lanes], ks[:, lanes], vs[:, lanes]
        tops, mixed = [], []
        for keep, rest in ((even, odd), (odd, even)):
            scores = by_turned(query * keep, key) + bias_row
            top = jnp.max(scores, axis=1, keepdims=True)
            weight = jnp.exp(scores - top).astype(bf16)
            tops.append(top)
            mixed.append(dot(weight, value * keep + rest))
        part = jnp.where(even32, mixed[0], mixed[1])
        total = pltpu.roll(jnp.where(even32, mixed[1], mixed[0]), HEAD_DIM, 1)
        attn[:, lanes] = (part / total).astype(bf16)
        log_rows = (jnp.where(even32, tops[0], tops[1]) + jnp.log(total)).T
        for h in range(2):
            stat[x, 0, pl.ds(2 * pair + h, 1), :] = log_rows[
                h * HEAD_DIM : h * HEAD_DIM + 1, :
            ]
        each(pair, pairs, advance)

    loop(pairs, attend)

    arrived(3)
    device = lax.broadcasted_iota(jnp.int32, (16, width), 0)
    feature = lax.broadcasted_iota(jnp.int32, (16, width), 1)
    mine = (feature // shard) == device
    spread = jnp.where(
        lax.broadcasted_iota(jnp.int32, (128, width), 1) % shard
        == lax.broadcasted_iota(jnp.int32, (128, width), 0),
        1.0,
        0.0,
    ).astype(bf16)
    gain_rows = W[:, :, :, s.gain0 : s.gain0 + 16, :128].reshape(16, 16, 128).astype(f32)
    for g in range(2):
        wide = dot(gain_rows[:, g, :].astype(bf16), spread)
        gains[g : g + 1, :] = jnp.sum(jnp.where(mine, wide, 0.0), axis=0, keepdims=True)

    acc[...] = dot(attn[...], matrix(s.out0))
    advance()
    rows_n = s.rows_n

    def wide_column(column):
        return jnp.broadcast_to(column, (rows_n, 128))

    def first_norm(b):
        first = pl.multiple_of(b * rows_n, 16)
        rows = pl.ds(first, rows_n)
        hidden = tok[own(first, rows_n), :].astype(f32) + acc[rows, :]
        center = hidden - jnp.mean(hidden, axis=1, keepdims=True)
        inverse = lax.rsqrt(jnp.mean(center * center, axis=1, keepdims=True) + EPSILON)
        normal = center * inverse
        n1[rows, :] = normal
        r1[rows, :] = wide_column(inverse)
        low1[rows, :] = (normal * gains[0:1, :]).astype(bf16)

    loop(span // rows_n, first_norm)
    advance()

    teach_copy.wait_recv()
    links.sent(teach_copy)

    def ahead(i, count):
        steps = iter(range(count))

        def action():
            if next(steps) > 0:
                advance()
            advance()

        each(i, count, action)

    def upward(p):
        ahead(p, s.panels)
        rows = pl.ds(pl.multiple_of(s.up0 + p * shard, 16), shard)
        for n in range(3):
            cols = slice(n * third, (n + 1) * third)
            value = dot(low1[...], W[:, :, :, rows, cols].reshape(width, third))
            cdf = 0.5 * (1.0 + lax.erf(value * ROOT_HALF))
            act[p, :, cols] = (value * cdf).astype(bf16)
            gp[p, :, cols] = (cdf + value * (jnp.exp(-0.5 * value * value) * DENSITY)).astype(bf16)

    def downward(n):
        ahead(n, 3)
        cols = pl.ds(pl.multiple_of(n * third, 128), third)
        value = None
        for p in range(s.panels):
            part = dot(act[p], W[p, :, :, s.down0 :, cols].reshape(width, third))
            value = part if value is None else value + part
        acc[:, cols] = value

    loop(s.panels, upward)
    advance()
    loop(3, downward)
    advance()
    assert all(stage > item.last for stage, item in zip(stages, gathers))

    sums[...] = jnp.zeros_like(sums)
    valid_total = jnp.full((1, 1), valid[0], jnp.int32).astype(f32)
    grad_scale = s.tokens / valid_total

    def fold(values):
        return jnp.sum(values.reshape(rows_n // 8, 8, width), axis=0)

    def second_norm(b):
        first = pl.multiple_of(b * rows_n, 16)
        rows = pl.ds(first, rows_n)
        hidden = n1[rows, :] * gains[0:1, :] + acc[rows, :]
        center = hidden - jnp.mean(hidden, axis=1, keepdims=True)
        inverse = lax.rsqrt(jnp.mean(center * center, axis=1, keepdims=True) + EPSILON)
        normal = center * inverse
        gain = gains[1:2, :]
        result = (normal * gain).astype(bf16)
        per = s.block // rows_n
        at = pl.ds(pl.multiple_of((b % per) * rows_n, 16), rows_n)
        target = teach[b // per, at, :].astype(f32)
        teach[b // per, at, :] = result
        live = order_col[own(first, rows_n), 0:1] < length_float
        error = jnp.where(live, result.astype(f32) - target, 0.0)
        sums[2] += fold(error * error)
        grad = (error * grad_scale).astype(bf16).astype(f32)
        sums[1] += fold(grad * normal)
        scaled = grad * gain
        grad_sum = inverse * (
            scaled
            - jnp.mean(scaled, axis=1, keepdims=True)
            - normal * jnp.mean(scaled * normal, axis=1, keepdims=True)
        )
        acc[rows, :] = grad_sum
        low2[rows, :] = grad_sum.astype(bf16)

    loop(span // rows_n, second_norm)
    links.drain()
    send_result = links.start(lambda: (teach.at[xo], res_in), place.to_x)
    total_refs[0][0] = jnp.broadcast_to(
        jnp.sum(jnp.sum(sums[2], axis=0, keepdims=True), axis=1, keepdims=True), (8, 128)
    )
    total = Total(*total_refs, place, links)

    reduces = [total]
    backward = iter(s.backward)

    def beat():
        for i in next(backward):
            reduces[i].beat()

    def prepare(block, out, shift=0, in_weights=False):
        first = block[0]
        return Reduce(
            block,
            first + s.down0 if in_weights else first - s.out0,
            W if in_weights else G,
            outs[out],
            first if in_weights else 0,
            shift,
            place,
            links,
            first + s.up0 if in_weights else first - s.out0,
            (lambda: W.at[:, :, 0]) if in_weights else (lambda: core_in),
            (lambda h, j: W.at[j, h, 1]) if in_weights else (lambda h, j: bufs.at[h, j]),
        )

    coming = [prepare(block, 3) for block in s.down_blocks]
    coming += [prepare(block, 2, p * width) for p, block in enumerate(s.up_blocks)]
    coming += [prepare(s.out_block, 1)]
    coming += [prepare(block, 0, in_weights=True) for block in s.last_blocks]

    def enter():
        reduces.append(coming.pop(0))
        beat()

    def panel_grad(first, left, right):
        value = turned(left[...], right[...]).astype(bf16)
        at = pl.ds(pl.multiple_of(first - s.out0, 16), shard)
        G[:, :, :, at, :] = value.reshape(4, 2, 2, shard, width)

    def down_grad(n):
        cols = pl.ds(pl.multiple_of(n * third, 128), third)

        def panel(p):
            value = turned(act[p], low2[:, cols]).astype(bf16)
            G[p, :, :, s.down0 - s.out0 :, cols] = value.reshape(2, 2, downs, third)

        loop(s.panels, panel)
        each(n, 3, enter)

    def up_grad(p):
        value = by_turned(low2[...], W[p, :, :, s.down0 :, :].reshape(width, width))
        gp[p] = (value * gp[p].astype(f32)).astype(bf16)
        panel_grad(s.up0 + p * shard, low1, gp.at[p])
        each(p, s.panels, enter)

    def normed_grad(p):
        acc[...] += by_turned(gp[p], matrix(s.up0 + p * shard))

    loop(3, down_grad)
    loop(s.panels, up_grad)
    loop(s.panels, normed_grad)
    beat()

    def first_back(b):
        rows = pl.ds(pl.multiple_of(b * rows_n, 16), rows_n)
        grad, normal = acc[rows, :], n1[rows, :]
        sums[0] += fold(grad * normal)
        scaled = grad * gains[0:1, :]
        hidden_grad = r1[rows, 0:1] * (
            scaled
            - jnp.mean(scaled, axis=1, keepdims=True)
            - normal * jnp.mean(scaled * normal, axis=1, keepdims=True)
        )
        acc[rows, :] = hidden_grad
        low2[rows, :] = hidden_grad.astype(bf16)

    loop(span // rows_n, first_back)
    beat()

    dO[...] = by_turned(low2[...], matrix(s.out0)).astype(bf16)
    head = lax.broadcasted_iota(jnp.int32, (16, width), 0)
    in_head = jnp.where((feature // HEAD_DIM) == head, 1.0, 0.0)

    def head_delta(b):
        first = pl.multiple_of(b * 128, 128)
        rows = pl.ds(first, 128)
        product = dO[rows, :].astype(f32) * attn[rows, :].astype(f32)
        stat[x, 1, :, rows] = lax.dot_general(
            in_head,
            product,
            (((1,), (1,)), ((), ())),
            precision=lax.Precision.HIGHEST,
            preferred_element_type=f32,
        )

    loop(span // 128, head_delta)
    send_grad = links.start(lambda: (dO, tok.at[own(0, span)]), place.to_x)
    send_stat = links.start(lambda: (stat.at[x],) * 2, place.to_x)

    panel_grad(s.out0, attn, low2)
    pieces = []
    for g in range(2):
        row = jnp.sum(sums[g], axis=0, keepdims=True)
        split = jnp.where(mine, jnp.broadcast_to(row, (16, width)), 0.0).astype(bf16)
        pieces.append(by_turned(split, spread))
    at_row = lax.broadcasted_iota(jnp.int32, (16, 16, 128), 1)
    gain_block = jnp.where(
        at_row == 0, pieces[0][:, None, :], jnp.where(at_row == 1, pieces[1][:, None, :], 0.0)
    ).astype(bf16)
    G[:, :, :, shard : shard + 16, :128] = gain_block.reshape(4, 2, 2, 16, 128)
    G[:, :, :, shard : shard + 16, 128:] = jnp.zeros((4, 2, 2, 16, width - 128), bf16)
    enter()

    def block_terms(key, value, bias, query, grad, log_row, delta_row):
        scores = by_turned(key, query) + bias
        p = jnp.exp(scores - log_row)
        score_grad = (p * (by_turned(value, grad) - delta_row)).astype(bf16)
        return p.astype(bf16), score_grad

    def key_side(rows, lanes):
        column = jnp.where(order_col[rows, :] < length_float, 0.0, MASKED)
        return ks[rows, lanes], vs[rows, lanes], jnp.concatenate([column] * (span // 128), axis=1)

    def pair_lanes(pair):
        return pl.ds(pl.multiple_of(pair * 128, 128), 128)

    def terms(key, value, bias, side, pair, h, keep):
        lanes = pair_lanes(pair)
        rows = pl.ds(pl.multiple_of(side * span, 16), span)
        grad = dO[:, lanes] if side is x else tok[rows, lanes]
        query, grad = qs[rows, lanes] * keep, grad * keep
        at = pl.ds(2 * pair + h, 1)
        p, score_grad = block_terms(
            key, value, bias, query, grad, stat[side, 0, at, :], stat[side, 1, at, :]
        )
        return query, grad, p, score_grad

    def back_queries(pair):
        lanes = pair_lanes(pair)
        result = to_keys = to_values = None
        for rows, mine in ((own(0, span), True), (other(0, span), False)):
            key, value, bias = key_side(rows, lanes)
            for h, keep in enumerate((even, odd)):
                query, grad, p, score_grad = terms(key, value, bias, x, pair, h, keep)
                part = turned(score_grad, key * keep)
                result = part if result is None else result + part
                if mine:
                    value_part, key_part = dot(p, grad), dot(score_grad, query)
                    to_values = value_part if to_values is None else to_values + value_part
                    to_keys = key_part if to_keys is None else to_keys + key_part
        act[0, :, lanes] = (result * SCORE_SCALE).astype(bf16)
        n1[:, lanes] = to_keys
        gp[0, :, lanes] = to_values.astype(bf16)
        each(pair, pairs, beat)

    def back_keys(pair):
        lanes = pair_lanes(pair)
        key, value, bias = key_side(own(0, span), lanes)
        to_keys, to_values = n1[:, lanes], gp[0, :, lanes].astype(f32)
        for h, keep in enumerate((even, odd)):
            query, grad, p, score_grad = terms(key, value, bias, xo, pair, h, keep)
            to_values = to_values + dot(p, grad)
            to_keys = to_keys + dot(score_grad, query)
        act[1, :, lanes] = to_keys.astype(bf16)
        act[2, :, lanes] = to_values.astype(bf16)

    def weight_grad(j, columns):
        value = turned(tok[own(0, span), :], act[j, :, columns]).astype(bf16)
        at = pl.ds(pl.multiple_of(s.down0 + j * shard, 16), shard)
        W[:, :, :, at, columns] = value.reshape(4, 2, 2, shard, value.shape[1])

    def last_pairs(i):
        loop(2, lambda k: back_keys(2 * i + k))
        columns = pl.ds(pl.multiple_of(i * 256, 128), 256)
        loop(2, lambda j: weight_grad(j + 1, columns))
        each(i, pairs // 2, enter)

    loop(pairs, back_queries)
    weight_grad(0, slice(0, width))
    enter()
    send_grad.wait_recv()
    send_stat.wait_recv()
    loop(pairs // 2, last_pairs)

    def input_grad(j):
        acc[...] += by_turned(act[j], matrix(j * shard))

    loop(3, input_grad)
    token_copy = pltpu.make_async_copy(acc, token_out, local.at[n_gather])
    token_copy.start()
    beat()
    send_result.wait_recv()

    def place_rows(n):
        cols = pl.ds(pl.multiple_of(n * third, 128), third)
        value = None
        position = lax.broadcasted_iota(jnp.int32, (span, s.block), 0) + x * span
        for c, rows in ((x, teach[x, :, cols]), (xo, res_in[:, cols])):
            at = order_row[0:1, pl.ds(pl.multiple_of(c * span + x * s.block, 128), s.block)]
            chosen = jnp.where(position == at, 1.0, 0.0).astype(bf16)
            part = dot(chosen, rows)
            value = part if value is None else value + part
        low2[:, cols] = value.astype(bf16)

    loop(3, place_rows)
    ordered_copy = pltpu.make_async_copy(low2, ordered_out, local.at[n_gather + 1])
    ordered_copy.start()
    beat()
    beat()
    assert all(item.stage > item.last for item in reduces)
    total_out[...] = total.sum()
    token_copy.wait()
    ordered_copy.wait()
    links.drain()


class Sizes:
    def __init__(self, span, width, ff, shard, downs, tokens):
        self.span, self.width, self.shard, self.downs, self.tokens = span, width, shard, downs, tokens
        self.panels = ff // width
        self.block = span // 2
        self.out0 = 3 * shard
        self.gain0 = 4 * shard
        self.up0 = self.gain0 + 16
        self.down0 = self.up0 + self.panels * shard
        self.rows = self.down0 + downs
        blocks = [(j * shard, (j + 1) * shard, 0, width) for j in range(3)]
        blocks += [(self.out0, self.up0, 0, width)]
        for p in range(self.panels):
            blocks += [(self.up0 + p * shard, self.up0 + (p + 1) * shard, 0, width)]
        third = width // 3
        blocks += [(self.down0, self.rows, n * third, third) for n in range(3)]
        self.gather_blocks = [b[:2] + (i in GATHER_SPLIT,) + b[2:] for i, b in enumerate(blocks)]
        self.sources = [(j, 0) for j in range(4)] + [(4, p * width) for p in range(self.panels)]
        self.sources += [(5, 0)] * 3
        self.early = EARLY
        back = blocks[-3:] + blocks[4:-3] + [blocks[3], blocks[0]]
        back += [(shard, self.out0, n * third, third) for n in range(3)]
        back = [b[:2] + (i in REDUCE_SPLIT,) + b[2:] for i, b in enumerate(back)]
        self.down_blocks, self.up_blocks = back[:3], back[3:-5]
        self.out_block, self.last_blocks = back[-5], back[-4:]
        self.forward, self.backward = FORWARD, BACKWARD
        self.rows_n, self.flying = 64, 64


def layer(s, *args):
    bf16, f32 = jnp.bfloat16, jnp.float32
    span, width = s.span, s.width
    both = 2 * span
    anywhere = pl.BlockSpec(memory_space=pl.ANY)
    vmem = pl.BlockSpec(memory_space=pltpu.VMEM)
    smem = pl.BlockSpec(memory_space=pltpu.SMEM)
    back = s.down_blocks + s.up_blocks + [s.out_block] + s.last_blocks
    copies = sum(15 if b[2] else 9 for b in s.gather_blocks)
    copies += sum(8 if b[2] else 6 for b in back) + 6 + 5
    small = pltpu.VMEM((8, 128), f32)
    scratch = [
        pltpu.VMEM((4, 2, 2, s.rows, width), bf16),
        pltpu.VMEM((4, 2, 2, s.rows - s.out0, width), bf16),
        pltpu.VMEM((both, width), bf16),
        pltpu.VMEM((3, both, width), bf16),
        pltpu.VMEM((span, width), bf16),
        pltpu.VMEM((2, 2, 16, span), f32),
        pltpu.VMEM((span, width), bf16),
        pltpu.VMEM((span, width), f32),
        pltpu.VMEM((span, 128), f32),
        pltpu.VMEM((span, width), bf16),
        pltpu.VMEM((s.panels, span, width), bf16),
        pltpu.VMEM((s.panels, span, width), bf16),
        pltpu.VMEM((span, width), f32),
        pltpu.VMEM((2, s.block, width), bf16),
        pltpu.VMEM((s.block, width), bf16),
        pltpu.VMEM((span, width), bf16),
        pltpu.VMEM((8, width), f32),
        pltpu.VMEM((3, 8, width), f32),
        pltpu.VMEM((3, 8, 128), f32),
        small,
        small,
        small,
        pltpu.VMEM((4, 8, 128), f32),
        pltpu.SemaphoreType.DMA((s.flying,)),
        pltpu.SemaphoreType.DMA((copies,)),
        pltpu.SemaphoreType.DMA((len(s.gather_blocks) + 2,)),
        pltpu.VMEM((both, 128), f32),
        pltpu.VMEM((4, 2, s.rows - s.out0, width), bf16),
        pltpu.VMEM((2, 4, s.rows - s.out0, width), bf16),
    ]
    return pl.pallas_call(
        functools.partial(layer_kernel, s),
        out_shape=[
            jax.ShapeDtypeStruct((span, width), bf16),
            jax.ShapeDtypeStruct((8, 128), f32),
            jax.ShapeDtypeStruct((span, width), f32),
            jax.ShapeDtypeStruct((s.out0, width), bf16),
            jax.ShapeDtypeStruct((s.up0 - s.out0, width), bf16),
            jax.ShapeDtypeStruct((s.shard, s.panels * width), bf16),
            jax.ShapeDtypeStruct((s.downs, width), bf16),
        ],
        in_specs=[anywhere, anywhere, vmem, smem, smem] + [anywhere] * 6,
        out_specs=[anywhere, vmem, anywhere] + [vmem] * 4,
        scratch_shapes=scratch,
        compiler_params=pltpu.CompilerParams(
            collective_id=0, has_side_effects=True, vmem_limit_bytes=s.vmem
        ),
    )(*args)


def fused_shards(
    tokens,
    w_query,
    w_key,
    w_value,
    w_out,
    w_up,
    w_down,
    gain_attn,
    gain_ffn,
    teacher,
    seq_lengths,
    tok_perm,
    valid_count,
):
    f32 = jnp.float32
    dp_count = lax.axis_size("dp")
    span, width = tokens.shape[1:]
    shard, ff = w_up.shape
    seq_len = tok_perm.shape[1]
    s = Sizes(span, width, ff, shard, w_down.shape[0], seq_len * dp_count)
    s.vmem = 63 * MIB
    gain_rows = jnp.pad(jnp.stack([gain_attn, gain_ffn]), ((0, 14), (0, width - shard)))
    ordered, total, token_grad, qkv, out, up, down = layer(
        s,
        tokens[0],
        teacher[0],
        tok_perm,
        seq_lengths,
        valid_count,
        w_query,
        w_key,
        w_value,
        jnp.concatenate([w_out, gain_rows]),
        w_up,
        w_down,
    )
    loss = (total[0, 0] / (2.0 * width * valid_count[0].astype(f32))).reshape(1)
    return (
        ordered[None],
        loss,
        token_grad[None],
        qkv[:shard].astype(f32),
        qkv[shard : 2 * shard].astype(f32),
        qkv[2 * shard :].astype(f32),
        out[:shard].astype(f32),
        up.astype(f32),
        down.astype(f32),
        out[shard, :shard].astype(f32),
        out[shard + 1, :shard].astype(f32),
    )


def solution(mesh):
    in_specs = (
        P("dp", "ctx", None),
        P("dp", None),
        P("dp", None),
        P("dp", None),
        P("dp", None),
        P("dp", None),
        P("dp", None),
        P("dp"),
        P("dp"),
        P("dp", "ctx", None),
        P("dp"),
        P("dp", None),
        P(),
    )
    out_specs = (
        P("dp", "ctx", None),
        P(),
        P("dp", "ctx", None),
        P("dp", None),
        P("dp", None),
        P("dp", None),
        P("dp", None),
        P("dp", None),
        P("dp", None),
        P("dp"),
        P("dp"),
    )
    body = fused_shards if dict(mesh.shape) == {"dp": 16, "ctx": 2} else shards
    return jax.shard_map(body, mesh=mesh, in_specs=in_specs, out_specs=out_specs, check_vma=False)
```

```python
import functools
import math

import jax
import jax.numpy as jnp
from jax import lax
from jax.experimental import pallas as pl
from jax.experimental.pallas import tpu as pltpu
from jax.sharding import PartitionSpec as P

HEAD_DIM = 64


EPSILON = 1e-06
SCORE_SCALE = 0.125
MASKED = -1e30
MESH = pl.DeviceIdType.MESH
MIB = 1024 * 1024


GATHER_SPLIT = (0, 3, 5, 6, 7, 8, 10)
REDUCE_SPLIT = (1, 2, 7, 8, 9, 11)
EARLY = 11
FORWARD = ((0, 1, 2, 3, 4, 5, 6, 7, 8, 9, 10), (0,), (1, 2, 3, 4, 5, 6, 7, 8, 9, 10, 0, 1, 2, 3, 4, 5, 6, 7, 8, 9, 10, 0, 1, 2, 3, 4, 5, 6, 7, 8, 9, 0, 10, 1, 2, 1, 3, 2, 0, 4, 5, 0), (4, 6, 7, 8), (3, 9, 10), (3, 5), (9,), (5, 6), (6,), (7,), (7,), (), (), (8,), (), (), (), (8,), (), (), (), (10,), (), (), (), (10,), (), ())
BACKWARD = ((0, 1), (0, 2), (3,), (1, 4), (2, 5), (3, 0, 6), (4, 5, 1, 0, 6, 7), (2, 7, 4), (), (3, 0, 1, 5, 8), (), (8, 4, 6), (2,), (), (5,), (7,), (1, 9), (3, 6, 10), (2, 8, 4, 9, 5, 10, 11), (2, 6, 7, 8, 11, 12), (3, 9, 12), (), (11, 8, 10, 7, 9, 3, 10, 11, 12, 8, 9, 11, 12, 10, 9, 10, 12, 12))


def gelu_exact(values):
    return 0.5 * values * (1.0 + lax.erf(values * 0.7071067811865476))


def norm_forward(hidden, gain_row):
    center = hidden - jnp.mean(hidden, axis=-1, keepdims=True)
    inverse = lax.rsqrt(jnp.mean(center * center, axis=-1, keepdims=True) + EPSILON)
    normal = center * inverse
    return (normal * gain_row, normal, inverse)


def norm_backward(grad_norm, gain_row, normal, inverse):
    scaled = grad_norm * gain_row
    grad_input = inverse * (
        scaled
        - jnp.mean(scaled, axis=-1, keepdims=True)
        - normal * jnp.mean(scaled * normal, axis=-1, keepdims=True)
    )
    return (grad_input, jnp.sum(grad_norm * normal, axis=0))


def row_product(left_mat, right_mat):
    return lax.dot_general(
        left_mat, right_mat, (((0,), (0,)), ((), ())), preferred_element_type=jnp.float32
    )


def by_transpose(left_mat, right_mat):
    return lax.dot_general(
        left_mat, right_mat, (((1,), (1,)), ((), ())), preferred_element_type=jnp.float32
    )


def shards(
    tokens,
    w_query,
    w_key,
    w_value,
    w_out,
    w_up,
    w_down,
    gain_attn,
    gain_ffn,
    teacher,
    seq_lengths,
    tok_perm,
    valid_count,
):
    ctx_count = lax.axis_size("ctx")
    ctx_rank = lax.axis_index("ctx")
    dp_count = lax.axis_size("dp")
    layer_in = tokens[0]
    span_rows, model_width = layer_in.shape
    head_count = model_width // HEAD_DIM
    dealt_order = tok_perm[0]
    seq_len = dealt_order.shape[0]
    length = seq_lengths[0]
    keep_all = dealt_order < length
    per_peer = span_rows // ctx_count
    query_weight, key_weight, value_weight, out_weight, gain_first = (
        lax.all_gather(w_query, "dp", axis=0, tiled=True),
        lax.all_gather(w_key, "dp", axis=0, tiled=True),
        lax.all_gather(w_value, "dp", axis=0, tiled=True),
        lax.all_gather(w_out, "dp", axis=0, tiled=True),
        lax.all_gather(gain_attn, "dp", axis=0, tiled=True),
    )
    up_weight, down_weight, gain_second = (
        lax.all_gather(w_up, "dp", axis=0, tiled=True),
        lax.all_gather(w_down, "dp", axis=0, tiled=True),
        lax.all_gather(gain_ffn, "dp", axis=0, tiled=True),
    )
    queries = jnp.dot(layer_in, query_weight, preferred_element_type=jnp.float32).astype(
        jnp.bfloat16
    )
    keys_own = jnp.dot(layer_in, key_weight, preferred_element_type=jnp.float32).astype(
        jnp.bfloat16
    )
    values_own = jnp.dot(layer_in, value_weight, preferred_element_type=jnp.float32).astype(
        jnp.bfloat16
    )
    query_heads = queries.reshape(span_rows, head_count, HEAD_DIM)
    initial = (
        jnp.full((head_count, span_rows), MASKED, jnp.float32),
        jnp.zeros((head_count, span_rows), jnp.float32),
        jnp.zeros((head_count, span_rows, HEAD_DIM), jnp.float32),
    )
    fold_state = initial
    key_piece = lax.all_gather(keys_own, "ctx", axis=0, tiled=True)
    value_piece = lax.all_gather(values_own, "ctx", axis=0, tiled=True)
    piece_rows = key_piece.shape[0]
    block_rows = math.gcd(piece_rows, span_rows)
    key_blocks = key_piece.reshape(piece_rows // block_rows, block_rows, head_count, HEAD_DIM)
    value_blocks = value_piece.reshape(piece_rows // block_rows, block_rows, head_count, HEAD_DIM)

    def step_block(block_state, block_item):
        running_max, running_sum, accumulated = block_state
        key_block, value_block, block_index = block_item
        key_keep = lax.dynamic_slice_in_dim(keep_all, block_index * block_rows, block_rows)
        scores = (
            jnp.einsum("qhe,khe->hqk", query_heads, key_block, preferred_element_type=jnp.float32)
            * SCORE_SCALE
        )
        scores = jnp.where(key_keep[None, None, :], scores, MASKED)
        new_max = jnp.maximum(running_max, jnp.max(scores, axis=-1))
        factor = jnp.exp(running_max - new_max)
        soft_weights = jnp.where(key_keep[None, None, :], jnp.exp(scores - new_max[..., None]), 0.0)
        running_sum = running_sum * factor + jnp.sum(soft_weights, axis=-1)
        accumulated = accumulated * factor[..., None] + jnp.einsum(
            "hqk,khe->hqe",
            soft_weights.astype(jnp.bfloat16),
            value_block,
            preferred_element_type=jnp.float32,
        )
        return ((new_max, running_sum, accumulated), None)

    block_indices = jnp.arange(piece_rows // block_rows, dtype=jnp.int32)
    fold_state, unused = lax.scan(step_block, fold_state, (key_blocks, value_blocks, block_indices))
    run_max, run_sum, accumulated = fold_state
    log_total = run_max + jnp.log(run_sum)
    attn_full = jnp.transpose(accumulated / run_sum[..., None], (1, 0, 2)).reshape(
        span_rows, model_width
    )
    attn_low = attn_full.astype(jnp.bfloat16)
    gain_first32 = gain_first.astype(jnp.float32)
    gain_second32 = gain_second.astype(jnp.float32)
    branch = jnp.dot(attn_low, out_weight, preferred_element_type=jnp.float32)
    normed, normal_first, inverse_first = norm_forward(
        layer_in.astype(jnp.float32) + branch, gain_first32
    )
    normed_low = normed.astype(jnp.bfloat16)
    upward = jnp.dot(normed_low, up_weight, preferred_element_type=jnp.float32)
    active, gelu_pull = jax.vjp(gelu_exact, upward)
    active_low = active.astype(jnp.bfloat16)
    down_out = jnp.dot(active_low, down_weight, preferred_element_type=jnp.float32)
    result, normal_second, inverse_second = norm_forward(normed + down_out, gain_second32)
    result_low = result.astype(jnp.bfloat16)
    arrived = lax.all_to_all(result_low, "ctx", split_axis=0, concat_axis=0, tiled=True)
    sources = (
        jnp.arange(ctx_count, dtype=jnp.int32)[:, None] * span_rows
        + ctx_rank * per_peer
        + jnp.arange(per_peer, dtype=jnp.int32)[None, :]
    ).reshape(span_rows)
    local_pos = jnp.take(dealt_order, sources) - ctx_rank * span_rows
    in_order = jnp.zeros_like(arrived).at[local_pos].set(arrived)
    target = teacher[0].astype(jnp.float32)
    live_rows = (ctx_rank * span_rows + jnp.arange(span_rows, dtype=jnp.int32) < length)[:, None]
    residual_err = jnp.where(live_rows, in_order.astype(jnp.float32) - target, 0.0)
    total_sq = lax.psum(jnp.sum(residual_err * residual_err), ("dp", "ctx"))
    valid_total = valid_count[0].astype(jnp.float32)
    loss_value = (total_sq / (2.0 * model_width * valid_total)).reshape(1)
    grad_scale = seq_len * dp_count / valid_total
    grad_order = (residual_err * grad_scale).astype(jnp.bfloat16)
    outgoing = jnp.take(grad_order, local_pos, axis=0)
    grad_result = lax.all_to_all(outgoing, "ctx", split_axis=0, concat_axis=0, tiled=True).astype(
        jnp.float32
    )
    grad_sum_second, grad_gain_second = norm_backward(
        grad_result, gain_second32, normal_second, inverse_second
    )
    down_grad_low = grad_sum_second.astype(jnp.bfloat16)
    grad_down_w = row_product(active_low, down_grad_low)
    grad_active = by_transpose(down_grad_low, down_weight)
    grad_upward = gelu_pull(grad_active)[0].astype(jnp.bfloat16)
    grad_up_w = row_product(normed_low, grad_upward)
    grad_normed = grad_sum_second + by_transpose(grad_upward, up_weight)
    grad_hidden, grad_gain_first = norm_backward(
        grad_normed, gain_first32, normal_first, inverse_first
    )
    branch_grad = grad_hidden.astype(jnp.bfloat16)
    grad_out_w = row_product(attn_low, branch_grad)
    attn_grad_low = by_transpose(branch_grad, out_weight).astype(jnp.bfloat16)
    grad_heads = attn_grad_low.reshape(span_rows, head_count, HEAD_DIM)
    row_delta = jnp.sum(
        (attn_grad_low.astype(jnp.float32) * attn_full).reshape(span_rows, head_count, HEAD_DIM),
        axis=-1,
    ).T
    keys_all, values_all = (
        lax.all_gather(keys_own, "ctx", axis=0, tiled=True),
        lax.all_gather(values_own, "ctx", axis=0, tiled=True),
    )
    blocks_count = seq_len // span_rows
    key_stack = keys_all.reshape(blocks_count, span_rows, head_count, HEAD_DIM)
    value_stack = values_all.reshape(blocks_count, span_rows, head_count, HEAD_DIM)

    def score_terms(
        query_block, grad_block, total_block, delta_block, key_block, value_block, key_keep
    ):
        scores = (
            jnp.einsum("qhe,khe->hqk", query_block, key_block, preferred_element_type=jnp.float32)
            * SCORE_SCALE
        )
        soft_weights = jnp.where(
            key_keep[None, None, :], jnp.exp(scores - total_block[..., None]), 0.0
        )
        prob_grad = jnp.einsum(
            "qhe,khe->hqk", grad_block, value_block, preferred_element_type=jnp.float32
        )
        score_grad = (soft_weights * (prob_grad - delta_block[..., None])).astype(jnp.bfloat16)
        return (soft_weights, score_grad)

    def back_block(query_grad, block_item):
        key_block, value_block, block_index = block_item
        key_keep = lax.dynamic_slice_in_dim(keep_all, block_index * span_rows, span_rows)
        soft_weights, score_grad = score_terms(
            query_heads, grad_heads, log_total, row_delta, key_block, value_block, key_keep
        )
        value_grad = jnp.einsum(
            "hqk,qhe->khe",
            soft_weights.astype(jnp.bfloat16),
            grad_heads,
            preferred_element_type=jnp.float32,
        )
        query_grad = query_grad + SCORE_SCALE * jnp.einsum(
            "hqk,khe->qhe", score_grad, key_block, preferred_element_type=jnp.float32
        )
        key_grad = SCORE_SCALE * jnp.einsum(
            "hqk,qhe->khe", score_grad, query_heads, preferred_element_type=jnp.float32
        )
        return (query_grad, (key_grad, value_grad))

    query_grad, (key_grads, value_grads) = lax.scan(
        back_block,
        jnp.zeros((span_rows, head_count, HEAD_DIM), jnp.float32),
        (key_stack, value_stack, jnp.arange(blocks_count, dtype=jnp.int32)),
    )
    key_grad_sum, value_grad_sum = (
        lax.psum_scatter(
            key_grads.reshape(seq_len, model_width).astype(jnp.bfloat16),
            "ctx",
            scatter_dimension=0,
            tiled=True,
        ).astype(jnp.float32),
        lax.psum_scatter(
            value_grads.reshape(seq_len, model_width).astype(jnp.bfloat16),
            "ctx",
            scatter_dimension=0,
            tiled=True,
        ).astype(jnp.float32),
    )
    query_grad_low = query_grad.reshape(span_rows, model_width).astype(jnp.bfloat16)
    key_grad_low = key_grad_sum.astype(jnp.bfloat16)
    value_grad_low = value_grad_sum.astype(jnp.bfloat16)
    grad_query_w = row_product(layer_in, query_grad_low)
    grad_key_w = row_product(layer_in, key_grad_low)
    grad_value_w = row_product(layer_in, value_grad_low)
    token_grad = (
        grad_hidden
        + by_transpose(query_grad_low, query_weight)
        + by_transpose(key_grad_low, key_weight)
        + by_transpose(value_grad_low, value_weight)
    )
    up_part, down_part, second_part = (
        lax.psum_scatter(
            grad_up_w.astype(jnp.bfloat16), "dp", scatter_dimension=0, tiled=True
        ).astype(jnp.float32),
        lax.psum_scatter(
            grad_down_w.astype(jnp.bfloat16), "dp", scatter_dimension=0, tiled=True
        ).astype(jnp.float32),
        lax.psum_scatter(
            grad_gain_second.astype(jnp.bfloat16), "dp", scatter_dimension=0, tiled=True
        ).astype(jnp.float32),
    )
    query_part, key_part, value_part, out_part, first_part = (
        lax.psum_scatter(
            grad_query_w.astype(jnp.bfloat16), "dp", scatter_dimension=0, tiled=True
        ).astype(jnp.float32),
        lax.psum_scatter(
            grad_key_w.astype(jnp.bfloat16), "dp", scatter_dimension=0, tiled=True
        ).astype(jnp.float32),
        lax.psum_scatter(
            grad_value_w.astype(jnp.bfloat16), "dp", scatter_dimension=0, tiled=True
        ).astype(jnp.float32),
        lax.psum_scatter(
            grad_out_w.astype(jnp.bfloat16), "dp", scatter_dimension=0, tiled=True
        ).astype(jnp.float32),
        lax.psum_scatter(
            grad_gain_first.astype(jnp.bfloat16), "dp", scatter_dimension=0, tiled=True
        ).astype(jnp.float32),
    )
    summed = (
        lax.psum(query_part.astype(jnp.bfloat16), "ctx").astype(jnp.float32),
        lax.psum(key_part.astype(jnp.bfloat16), "ctx").astype(jnp.float32),
        lax.psum(value_part.astype(jnp.bfloat16), "ctx").astype(jnp.float32),
        lax.psum(out_part.astype(jnp.bfloat16), "ctx").astype(jnp.float32),
        lax.psum(up_part.astype(jnp.bfloat16), "ctx").astype(jnp.float32),
        lax.psum(down_part.astype(jnp.bfloat16), "ctx").astype(jnp.float32),
        lax.psum(first_part.astype(jnp.bfloat16), "ctx").astype(jnp.float32),
        lax.psum(second_part.astype(jnp.bfloat16), "ctx").astype(jnp.float32),
    )
    query_sum, key_sum, value_sum, out_sum, up_sum, down_sum, first_sum, second_sum = summed
    return (
        in_order[None],
        loss_value,
        token_grad[None],
        query_sum,
        key_sum,
        value_sum,
        out_sum,
        up_sum,
        down_sum,
        first_sum,
        second_sum,
    )


class Place:
    def __init__(self):
        dp = lax.axis_index("dp")
        self.x = lax.axis_index("ctx")
        self.z, self.y, self.c = dp // 4, (dp // 2) % 2, dp % 2
        self.xo, self.yo, self.co = 1 - self.x, 1 - self.y, 1 - self.c
        self.to_x = (dp, self.xo)
        self.to_y = (self.z * 4 + self.yo * 2 + self.c, self.x)
        self.to_c = (self.z * 4 + self.y * 2 + self.co, self.x)
        self.z_up = [(self.z + k) % 4 for k in range(4)]
        self.z_down = [(self.z + 4 - k) % 4 for k in range(4)]
        self.to_z = [(self.z_up[k] * 4 + self.y * 2 + self.c, self.x) for k in range(4)]
        z = self.z
        self.above = [(jnp.logical_and(z >= d, z < 3), z > d) for d in range(3)]
        self.below = [(jnp.logical_and(z <= 3 - d, z > 0), z < 3 - d) for d in range(3)]
        self.to_above, self.to_below = self.to_z[1], self.to_z[3]

    def barrier(self):
        semaphore = pltpu.get_barrier_semaphore()
        for partner in [self.to_x, self.to_y, self.to_c] + self.to_z[1:]:
            pl.semaphore_signal(semaphore, inc=1, device_id=partner, device_id_type=MESH)
        pl.semaphore_wait(semaphore, 6)


class Copy:
    def __init__(self, refs, send, at, recv, to, partner, when):
        self.refs, self.send, self.at, self.recv, self.to = refs, send, at, recv, to
        self.partner, self.when = partner, when

    def make(self):
        src, dst = self.refs()
        return pltpu.make_async_remote_copy(
            src_ref=src,
            dst_ref=dst,
            send_sem=self.send.at[self.at],
            recv_sem=self.recv.at[self.to],
            device_id=self.partner,
            device_id_type=MESH,
        )

    def only(self, side, action):
        if self.when is None:
            action()
        else:
            pl.when(self.when[side])(action)

    def start(self):
        self.only(0, lambda: self.make().start())

    def wait_send(self):
        self.only(0, lambda: self.make().wait_send())

    def wait_recv(self):
        self.only(1, lambda: self.make().wait_recv())


class Links:
    def __init__(self, send, recv):
        self.send, self.recv, self.used, self.flying = send, recv, 0, []
        self.free = list(range(send.shape[0]))

    def start(self, refs, partner, when=None):
        if not self.free:
            self.sent(self.flying[0][0])
        at = self.free.pop(0)
        copy = Copy(refs, self.send, at, self.recv, self.used, partner, when)
        self.used += 1
        copy.start()
        self.flying.append((copy, at))
        return copy

    def sent(self, copy):
        for entry in list(self.flying):
            if entry[0] is copy:
                copy.wait_send()
                self.free.append(entry[1])
        self.flying = [entry for entry in self.flying if entry[0] is not copy]

    def drain(self):
        for copy, at in list(self.flying):
            self.sent(copy)


class Gather:
    def __init__(self, block, early, shard, shift, whole, place, links, own_sem):
        first, last, self.split, self.col0, self.width = block
        self.early = early
        self.rows = pl.ds(first, last - first)
        self.shard, self.shift, self.whole = shard, shift, whole
        self.p, self.links = place, links
        self.own_sem = own_sem
        self.mine, self.theirs = self.half(place.x), self.half(place.xo)
        self.source = self.half(place.x, shift)
        self.last = 6 if self.split else 5

    def cols(self, shift=0):
        return pl.ds(self.col0 + shift, self.width)

    def half(self, x, shift=0):
        if not self.split:
            return self.cols(shift)
        size = self.width // 2
        return pl.ds(pl.multiple_of(self.col0 + shift + x * size, 128), size)

    def piece(self, z, y, cols):
        return self.whole.at[z, y, self.p.c, self.rows, cols]

    def own(self):
        p = self.p
        return pltpu.make_async_copy(
            self.shard.at[:, self.cols(self.shift)], self.piece(p.z, p.y, self.cols()), self.own_sem()
        )

    def push(self, z, y, cols, partner, when=None):
        return self.links.start(lambda: (self.piece(z, y, cols),) * 2, partner, when)

    def send_own(self, partner, when=None):
        p = self.p
        return self.links.start(
            lambda: (self.shard.at[:, self.source], self.piece(p.z, p.y, self.mine)), partner, when
        )

    def step0(self):
        p = self.p
        self.up, self.down = self.send_own(p.to_above, p.above[0]), self.send_own(p.to_below, p.below[0])
        self.own().start()
        self.from_x, self.from_y = [], []
        if self.early:
            self.from_y.append(self.send_own(p.to_y))

    def hop(self, d):
        p = self.p
        up, down = self.up, self.down
        up.wait_recv()
        if d < 2:
            self.up = self.push(p.z_down[d + 1], p.y, self.mine, p.to_above, p.above[d + 1])
        down.wait_recv()
        if d < 2:
            self.down = self.push(p.z_up[d + 1], p.y, self.mine, p.to_below, p.below[d + 1])
        for z, there in ((p.z_down[d + 1], p.above[d][1]), (p.z_up[d + 1], p.below[d][1])):
            when = (there, there)
            self.from_y.append(self.push(z, p.y, self.mine, p.to_y, when))
            if self.split:
                self.from_x.append(self.push(z, p.y, self.mine, p.to_x, when))

    def step1(self):
        if not self.early:
            self.from_y.append(self.send_own(self.p.to_y))
        self.hop(0)

    def step2(self):
        self.hop(1)

    def step3(self):
        self.hop(2)
        self.own().wait()
        self.from_c = [self.push(slice(None), self.p.y, self.mine, self.p.to_c)]

    def step4(self):
        p, every = self.p, slice(None)
        for copy in self.from_y:
            copy.wait_recv()
        if self.split:
            self.across = self.push(every, p.yo, self.mine, p.to_x)
        self.from_c.append(self.push(every, p.yo, self.mine, p.to_c))
        if self.split:
            for copy in self.from_x:
                copy.wait_recv()
            self.from_c.append(self.push(every, p.y, self.theirs, p.to_c))

    def step5(self):
        if self.split:
            self.across.wait_recv()
            self.from_c.append(self.push(slice(None), self.p.yo, self.theirs, self.p.to_c))
        else:
            self.step6()

    def step6(self):
        for copy in self.from_c:
            copy.wait_recv()


class Reduce:
    def __init__(self, block, at, grads, out, out0, shift, place, links, here, core_in, bufs):
        first, last, self.split, self.col0, self.width = block
        self.rows = last - first
        self.at0, self.here0, self.out0, self.shift = at, here, out0, shift
        self.at, self.here = pl.ds(at, self.rows), pl.ds(here, self.rows)
        self.grads, self.out = grads, out
        self.p, self.links = place, links
        self.core_in, self.bufs = core_in, bufs
        limit = 32 * 768 // self.width
        self.block = max(b for b in range(16, min(self.rows, limit) + 1, 16) if self.rows % b == 0)
        self.stage = 0
        self.mine, self.theirs = self.half(place.x), self.half(place.xo)
        self.out_mine = self.half(place.x, shift)
        self.last = 5 if self.split else 4

    def cols(self, shift=0):
        return pl.ds(self.col0 + shift, self.width)

    def half(self, x, shift=0):
        if not self.split:
            return self.cols(shift)
        size = self.width // 2
        return pl.ds(pl.multiple_of(self.col0 + shift + x * size, 128), size)

    def low(self):
        return pl.ds(self.col0, self.width // 2)

    def high(self):
        return pl.ds(self.col0 + self.width // 2, self.width // 2) if self.split else self.cols()

    def add(self, outer, target, source):
        steps = self.rows // self.block

        def body(i, carry):
            first = pl.multiple_of((i % steps) * self.block, 16)
            put = target(i // steps, pl.ds(self.at0 + first, self.block))
            given = source(i // steps, pl.ds(self.here0 + first, self.block))
            self.grads[put] = (
                self.grads[put].astype(jnp.float32) + given.astype(jnp.float32)
            ).astype(jnp.bfloat16)
            return carry

        lax.fori_loop(0, outer * steps, body, 0)

    def step0(self):
        p = self.p
        self.by_core = self.links.start(
            lambda: (
                self.grads.at[:, :, p.co, self.at, self.cols()],
                self.core_in().at[:, :, self.here, self.cols()],
            ),
            p.to_c,
        )

    def add_core(self, y):
        p = self.p
        self.add(
            4,
            lambda i, rows: (i, y, p.c, rows, self.cols()),
            lambda i, rows: self.core_in()[i, y, rows, self.cols()],
        )

    def send_y(self):
        p = self.p
        self.by_y = self.links.start(
            lambda: (
                self.grads.at[:, p.yo, p.c, self.at, self.mine],
                self.bufs(0, slice(None)).at[:, self.here, self.high()],
            ),
            p.to_y,
        )

    def step1(self):
        p = self.p
        self.by_core.wait_recv()
        self.add_core(p.yo)
        if not self.split:
            self.send_y()
        self.add_core(p.y)
        if self.split:
            self.by_x = [self.send_x(0, p.yo), self.send_x(1, p.y)]

    def send_x(self, i, y):
        p = self.p
        return self.links.start(
            lambda: (
                self.grads.at[:, y, p.c, self.at, self.theirs],
                self.bufs(i, slice(None)).at[:, self.here, self.low()],
            ),
            p.to_x,
        )

    def add_x(self, i, y):
        p = self.p
        self.by_x[i].wait_recv()
        self.add(
            4,
            lambda j, rows: (j, y, p.c, rows, self.mine),
            lambda j, rows: self.bufs(i, j)[rows, self.low()],
        )

    def step2(self):
        if self.split:
            self.add_x(0, self.p.yo)
            self.send_y()
            self.add_x(1, self.p.y)
        else:
            self.reduce_y()

    def reduce_y(self):
        p = self.p
        self.by_y.wait_recv()
        self.add(
            4,
            lambda i, rows: (i, p.y, p.c, rows, self.mine),
            lambda i, rows: self.bufs(0, i)[rows, self.high()],
        )
        self.by_z = [self.send_z(k) for k in range(1, 4)]

    def send_z(self, k):
        p = self.p
        return self.links.start(
            lambda: (
                self.grads.at[p.z_up[k], p.y, p.c, self.at, self.mine],
                self.bufs(1, k - 1).at[self.here, self.high()],
            ),
            p.to_z[k],
        )

    def reduce_z(self, put):
        p = self.p
        for copy in self.by_z:
            copy.wait_recv()

        def body(i, carry):
            first = pl.multiple_of(i * self.block, 16)
            rows = pl.ds(self.here0 + first, self.block)
            place = (p.z, p.y, p.c, pl.ds(self.at0 + first, self.block), self.mine)
            total = self.grads[place].astype(jnp.float32)
            for k in range(3):
                total = total + self.bufs(1, k)[rows, self.high()].astype(jnp.float32)
            put(pl.ds(self.out0 + first, self.block), place, total.astype(jnp.bfloat16))
            return carry

        lax.fori_loop(0, self.rows // self.block, body, 0)

    def step3(self):
        p = self.p
        if self.split:
            self.reduce_y()
            return

        def put(rows, place, value):
            self.grads[place] = value

        self.reduce_z(put)
        self.by_x = self.links.start(
            lambda: (
                self.grads.at[p.z, p.y, p.c, self.at, self.cols()],
                self.bufs(1, 3).at[self.here, self.cols()],
            ),
            p.to_x,
        )

    def step4(self):
        p = self.p
        if self.split:

            def put(rows, place, value):
                self.out[rows, self.out_mine] = value

            self.reduce_z(put)
            self.by_x = self.links.start(
                lambda: (self.out.at[pl.ds(self.out0, self.rows), self.out_mine],) * 2, p.to_x
            )
            return
        self.by_x.wait_recv()

        def body(i, carry):
            first = pl.multiple_of(i * self.block, 16)
            rows = pl.ds(self.here0 + first, self.block)
            own = self.grads[p.z, p.y, p.c, pl.ds(self.at0 + first, self.block), self.cols()]
            self.out[pl.ds(self.out0 + first, self.block), self.cols(self.shift)] = (
                own.astype(jnp.float32) + self.bufs(1, 3)[rows, self.cols()].astype(jnp.float32)
            ).astype(jnp.bfloat16)
            return carry

        lax.fori_loop(0, self.rows // self.block, body, 0)

    def step5(self):
        self.by_x.wait_recv()

    def beat(self):
        getattr(self, "step" + str(self.stage))()
        self.stage += 1


class Total:
    last = 4

    def __init__(self, value, core_in, x_in, y_in, by_z, place, links):
        self.value, self.core_in, self.x_in, self.y_in, self.by_z = value, core_in, x_in, y_in, by_z
        self.p, self.links = place, links
        self.stage = 0

    def step0(self):
        self.copy = self.links.start(lambda: (self.value.at[0], self.core_in), self.p.to_c)

    def step1(self):
        self.copy.wait_recv()
        self.value[1] = self.value[0] + self.core_in[...]
        self.copy = self.links.start(lambda: (self.value.at[1], self.x_in), self.p.to_x)

    def step2(self):
        self.copy.wait_recv()
        self.value[2] = self.value[1] + self.x_in[...]
        self.copy = self.links.start(lambda: (self.value.at[2], self.y_in), self.p.to_y)

    def step3(self):
        self.copy.wait_recv()
        z = self.p.z
        self.by_z[z] = self.value[2] + self.y_in[...]
        self.spread = [
            self.links.start(lambda: (self.by_z.at[z],) * 2, self.p.to_z[k]) for k in range(1, 4)
        ]

    def step4(self):
        for copy in self.spread:
            copy.wait_recv()

    def sum(self):
        return ((self.by_z[0] + self.by_z[1]) + self.by_z[2]) + self.by_z[3]

    def beat(self):
        getattr(self, "step" + str(self.stage))()
        self.stage += 1


ROOT_HALF = 0.7071067811865476
DENSITY = 0.3989422804014327


def dot(left, right):
    return jnp.dot(left, right, preferred_element_type=jnp.float32)


def turned(left, right):
    return lax.dot_general(
        left, right, (((0,), (0,)), ((), ())), preferred_element_type=jnp.float32
    )


def by_turned(left, right):
    return lax.dot_general(
        left, right, (((1,), (1,)), ((), ())), preferred_element_type=jnp.float32
    )


def layer_kernel(s, *refs):
    tokens, teacher, order_row, length, valid = refs[:5]
    weights, (ordered_out, loss_out, token_out), outs = refs[5:11], refs[11:14], refs[14:18]
    refs = refs[8:]
    (W, G, tok, QKV, dO, stat, attn, n1, r1, low1, act, gp, acc, teach, res_in, low2, gains, sums) = refs[10:28]
    total_refs, (send, recv, local), (order_col, core_in, bufs) = refs[28:33], refs[33:36], refs[36:]
    qs, ks, vs = QKV.at[0], QKV.at[1], QKV.at[2]
    f32, bf16 = jnp.float32, jnp.bfloat16
    span, width, shard, downs = s.span, s.width, s.shard, s.downs
    pairs = width // 128
    third = width // 3
    place = Place()
    x, xo = place.x, place.xo
    links = Links(send, recv)

    def own(first, size):
        return pl.ds(pl.multiple_of(x * span + first, 16), size)

    def other(first, size):
        return pl.ds(pl.multiple_of(xo * span + first, 16), size)

    def loop(count, body):
        def step(i, carry):
            body(i)
            return carry

        lax.fori_loop(0, count, step, 0)

    def each(i, count, action):
        for k in range(count):
            pl.when(i == k)(lambda: action())

    def matrix(first):
        return W[:, :, :, pl.ds(pl.multiple_of(first, 16), shard), :].reshape(width, width)

    def semaphore(i):
        return local.at[i]

    gathers = [
        Gather(block, i < s.early, weights[j], shift, W, place, links, functools.partial(semaphore, i))
        for i, (block, (j, shift)) in enumerate(zip(s.gather_blocks, s.sources))
    ]
    n_gather = len(gathers)
    stages = [0] * n_gather
    forward = iter(s.forward)

    def advance():
        for i in next(forward):
            getattr(gathers[i], "step" + str(stages[i]))()
            stages[i] += 1

    def arrived(*blocks):
        advance()
        assert all(stages[i] > gathers[i].last for i in blocks)

    place.barrier()
    own_tokens = pltpu.make_async_copy(tokens, tok.at[own(0, span)], local.at[n_gather])
    own_tokens.start()
    own_teacher = pltpu.make_async_copy(teacher, gp.at[0], local.at[n_gather + 1])
    own_teacher.start()
    send_tokens = links.start(lambda: (tokens, tok.at[own(0, span)]), place.to_x)
    advance()
    order_col[...] = jnp.broadcast_to(order_row[...].astype(f32), (128, 2 * span)).T
    length_now = length[0]
    length_float = length_now.astype(f32)
    iota_rows = lax.broadcasted_iota(jnp.int32, (s.block, span), 1)

    def pick(c):
        rows = pl.ds(pl.multiple_of(c * span + x * s.block, 16), s.block)
        position = order_col[rows, :].astype(jnp.int32) - x * span
        chosen = iota_rows == jnp.concatenate([position] * (span // 128), axis=1)
        return jnp.where(chosen, 1.0, 0.0).astype(bf16)

    own_teacher.wait()
    for n in range(3):
        cols = slice(n * third, (n + 1) * third)
        gp[1, : s.block, cols] = dot(pick(xo), gp[0, :, cols]).astype(bf16)
        teach[x, :, cols] = dot(pick(x), gp[0, :, cols]).astype(bf16)
    teach_copy = links.start(lambda: (gp.at[1, pl.ds(0, s.block)], teach.at[x]), place.to_x)
    advance()
    arrived(0, 1, 2)

    own_tokens.wait()

    def side(i):
        @pl.when(i == 1)
        def _():
            send_tokens.wait_recv()

        rows = pl.ds(pl.multiple_of(jnp.where(i == 0, x, xo) * span, 16), span)

        def project(j):
            scale = jnp.where(j == 0, SCORE_SCALE, 1.0)
            QKV[j, rows, :] = (dot(tok[rows, :], matrix(j * shard)) * scale).astype(bf16)

        loop(3, project)
        each(i, 2, advance)

    loop(2, side)

    lane = lax.broadcasted_iota(jnp.int32, (1, 128), 1)
    even32 = lane < HEAD_DIM
    even = jnp.where(even32, 1.0, 0.0).astype(bf16)
    odd = jnp.where(even32, 0.0, 1.0).astype(bf16)
    bias_row = jnp.where(order_row[0:1, :] < length_now, 0.0, MASKED)

    def attend(pair):
        lanes = pl.ds(pl.multiple_of(pair * 128, 128), 128)
        query, key, value = qs[own(0, span), lanes], ks[:, lanes], vs[:, lanes]
        tops, mixed = [], []
        for keep, rest in ((even, odd), (odd, even)):
            scores = by_turned(query * keep, key) + bias_row
            top = jnp.max(scores, axis=1, keepdims=True)
            weight = jnp.exp(scores - top).astype(bf16)
            tops.append(top)
            mixed.append(dot(weight, value * keep + rest))
        part = jnp.where(even32, mixed[0], mixed[1])
        total = pltpu.roll(jnp.where(even32, mixed[1], mixed[0]), HEAD_DIM, 1)
        attn[:, lanes] = (part / total).astype(bf16)
        log_rows = (jnp.where(even32, tops[0], tops[1]) + jnp.log(total)).T
        for h in range(2):
            stat[x, 0, pl.ds(2 * pair + h, 1), :] = log_rows[
                h * HEAD_DIM : h * HEAD_DIM + 1, :
            ]
        each(pair, pairs, advance)

    loop(pairs, attend)

    arrived(3)
    device = lax.broadcasted_iota(jnp.int32, (16, width), 0)
    feature = lax.broadcasted_iota(jnp.int32, (16, width), 1)
    mine = (feature // shard) == device
    spread = jnp.where(
        lax.broadcasted_iota(jnp.int32, (128, width), 1) % shard
        == lax.broadcasted_iota(jnp.int32, (128, width), 0),
        1.0,
        0.0,
    ).astype(bf16)
    gain_rows = W[:, :, :, s.gain0 : s.gain0 + 16, :128].reshape(16, 16, 128).astype(f32)
    for g in range(2):
        wide = dot(gain_rows[:, g, :].astype(bf16), spread)
        gains[g : g + 1, :] = jnp.sum(jnp.where(mine, wide, 0.0), axis=0, keepdims=True)

    acc[...] = dot(attn[...], matrix(s.out0))
    advance()
    rows_n = s.rows_n

    def wide_column(column):
        return jnp.broadcast_to(column, (rows_n, 128))

    def first_norm(b):
        first = pl.multiple_of(b * rows_n, 16)
        rows = pl.ds(first, rows_n)
        hidden = tok[own(first, rows_n), :].astype(f32) + acc[rows, :]
        center = hidden - jnp.mean(hidden, axis=1, keepdims=True)
        inverse = lax.rsqrt(jnp.mean(center * center, axis=1, keepdims=True) + EPSILON)
        normal = center * inverse
        n1[rows, :] = normal
        r1[rows, :] = wide_column(inverse)
        low1[rows, :] = (normal * gains[0:1, :]).astype(bf16)

    loop(span // rows_n, first_norm)
    advance()

    teach_copy.wait_recv()
    links.sent(teach_copy)

    def ahead(i, count):
        steps = iter(range(count))

        def action():
            if next(steps) > 0:
                advance()
            advance()

        each(i, count, action)

    def upward(p):
        ahead(p, s.panels)
        rows = pl.ds(pl.multiple_of(s.up0 + p * shard, 16), shard)
        for n in range(3):
            cols = slice(n * third, (n + 1) * third)
            value = dot(low1[...], W[:, :, :, rows, cols].reshape(width, third))
            cdf = 0.5 * (1.0 + lax.erf(value * ROOT_HALF))
            act[p, :, cols] = (value * cdf).astype(bf16)
            gp[p, :, cols] = (cdf + value * (jnp.exp(-0.5 * value * value) * DENSITY)).astype(bf16)

    def downward(n):
        ahead(n, 3)
        cols = pl.ds(pl.multiple_of(n * third, 128), third)
        value = None
        for p in range(s.panels):
            part = dot(act[p], W[p, :, :, s.down0 :, cols].reshape(width, third))
            value = part if value is None else value + part
        acc[:, cols] = value

    loop(s.panels, upward)
    advance()
    loop(3, downward)
    advance()
    assert all(stage > item.last for stage, item in zip(stages, gathers))

    sums[...] = jnp.zeros_like(sums)
    valid_total = jnp.full((1, 1), valid[0], jnp.int32).astype(f32)
    grad_scale = s.tokens / valid_total

    def fold(values):
        return jnp.sum(values.reshape(rows_n // 8, 8, width), axis=0)

    def second_norm(b):
        first = pl.multiple_of(b * rows_n, 16)
        rows = pl.ds(first, rows_n)
        hidden = n1[rows, :] * gains[0:1, :] + acc[rows, :]
        center = hidden - jnp.mean(hidden, axis=1, keepdims=True)
        inverse = lax.rsqrt(jnp.mean(center * center, axis=1, keepdims=True) + EPSILON)
        normal = center * inverse
        gain = gains[1:2, :]
        result = (normal * gain).astype(bf16)
        per = s.block // rows_n
        at = pl.ds(pl.multiple_of((b % per) * rows_n, 16), rows_n)
        target = teach[b // per, at, :].astype(f32)
        teach[b // per, at, :] = result
        live = order_col[own(first, rows_n), 0:1] < length_float
        error = jnp.where(live, result.astype(f32) - target, 0.0)
        sums[2] += fold(error * error)
        grad = (error * grad_scale).astype(bf16).astype(f32)
        sums[1] += fold(grad * normal)
        scaled = grad * gain
        grad_sum = inverse * (
            scaled
            - jnp.mean(scaled, axis=1, keepdims=True)
            - normal * jnp.mean(scaled * normal, axis=1, keepdims=True)
        )
        acc[rows, :] = grad_sum
        low2[rows, :] = grad_sum.astype(bf16)

    loop(span // rows_n, second_norm)
    links.drain()
    send_result = links.start(lambda: (teach.at[xo], res_in), place.to_x)
    total_refs[0][0] = jnp.broadcast_to(
        jnp.sum(jnp.sum(sums[2], axis=0, keepdims=True), axis=1, keepdims=True), (8, 128)
    )
    total = Total(*total_refs, place, links)

    reduces = [total]
    backward = iter(s.backward)

    def beat():
        for i in next(backward):
            reduces[i].beat()

    def prepare(block, out, shift=0, in_weights=False):
        first = block[0]
        return Reduce(
            block,
            first + s.down0 if in_weights else first - s.out0,
            W if in_weights else G,
            outs[out],
            first if in_weights else 0,
            shift,
            place,
            links,
            first + s.up0 if in_weights else first - s.out0,
            (lambda: W.at[:, :, 0]) if in_weights else (lambda: core_in),
            (lambda h, j: W.at[j, h, 1]) if in_weights else (lambda h, j: bufs.at[h, j]),
        )

    coming = [prepare(block, 3) for block in s.down_blocks]
    coming += [prepare(block, 2, p * width) for p, block in enumerate(s.up_blocks)]
    coming += [prepare(s.out_block, 1)]
    coming += [prepare(block, 0, in_weights=True) for block in s.last_blocks]

    def enter():
        reduces.append(coming.pop(0))
        beat()

    def panel_grad(first, left, right):
        value = turned(left[...], right[...]).astype(bf16)
        at = pl.ds(pl.multiple_of(first - s.out0, 16), shard)
        G[:, :, :, at, :] = value.reshape(4, 2, 2, shard, width)

    def down_grad(n):
        cols = pl.ds(pl.multiple_of(n * third, 128), third)

        def panel(p):
            value = turned(act[p], low2[:, cols]).astype(bf16)
            G[p, :, :, s.down0 - s.out0 :, cols] = value.reshape(2, 2, downs, third)

        loop(s.panels, panel)
        each(n, 3, enter)

    def up_grad(p):
        value = by_turned(low2[...], W[p, :, :, s.down0 :, :].reshape(width, width))
        gp[p] = (value * gp[p].astype(f32)).astype(bf16)
        panel_grad(s.up0 + p * shard, low1, gp.at[p])
        each(p, s.panels, enter)

    def normed_grad(p):
        acc[...] += by_turned(gp[p], matrix(s.up0 + p * shard))

    loop(3, down_grad)
    loop(s.panels, up_grad)
    loop(s.panels, normed_grad)
    beat()

    def first_back(b):
        rows = pl.ds(pl.multiple_of(b * rows_n, 16), rows_n)
        grad, normal = acc[rows, :], n1[rows, :]
        sums[0] += fold(grad * normal)
        scaled = grad * gains[0:1, :]
        hidden_grad = r1[rows, 0:1] * (
            scaled
            - jnp.mean(scaled, axis=1, keepdims=True)
            - normal * jnp.mean(scaled * normal, axis=1, keepdims=True)
        )
        acc[rows, :] = hidden_grad
        low2[rows, :] = hidden_grad.astype(bf16)

    loop(span // rows_n, first_back)
    beat()

    dO[...] = by_turned(low2[...], matrix(s.out0)).astype(bf16)
    head = lax.broadcasted_iota(jnp.int32, (16, width), 0)
    in_head = jnp.where((feature // HEAD_DIM) == head, 1.0, 0.0)

    def head_delta(b):
        first = pl.multiple_of(b * 128, 128)
        rows = pl.ds(first, 128)
        product = dO[rows, :].astype(f32) * attn[rows, :].astype(f32)
        stat[x, 1, :, rows] = lax.dot_general(
            in_head,
            product,
            (((1,), (1,)), ((), ())),
            precision=lax.Precision.HIGHEST,
            preferred_element_type=f32,
        )

    loop(span // 128, head_delta)
    send_grad = links.start(lambda: (dO, tok.at[own(0, span)]), place.to_x)
    send_stat = links.start(lambda: (stat.at[x],) * 2, place.to_x)

    panel_grad(s.out0, attn, low2)
    pieces = []
    for g in range(2):
        row = jnp.sum(sums[g], axis=0, keepdims=True)
        split = jnp.where(mine, jnp.broadcast_to(row, (16, width)), 0.0).astype(bf16)
        pieces.append(by_turned(split, spread))
    at_row = lax.broadcasted_iota(jnp.int32, (16, 16, 128), 1)
    gain_block = jnp.where(
        at_row == 0, pieces[0][:, None, :], jnp.where(at_row == 1, pieces[1][:, None, :], 0.0)
    ).astype(bf16)
    G[:, :, :, shard : shard + 16, :128] = gain_block.reshape(4, 2, 2, 16, 128)
    G[:, :, :, shard : shard + 16, 128:] = jnp.zeros((4, 2, 2, 16, width - 128), bf16)
    enter()

    def block_terms(key, value, bias, query, grad, log_row, delta_row):
        scores = by_turned(key, query) + bias
        p = jnp.exp(scores - log_row)
        score_grad = (p * (by_turned(value, grad) - delta_row)).astype(bf16)
        return p.astype(bf16), score_grad

    def key_side(rows, lanes):
        column = jnp.where(order_col[rows, :] < length_float, 0.0, MASKED)
        return ks[rows, lanes], vs[rows, lanes], jnp.concatenate([column] * (span // 128), axis=1)

    def pair_lanes(pair):
        return pl.ds(pl.multiple_of(pair * 128, 128), 128)

    def terms(key, value, bias, side, pair, h, keep):
        lanes = pair_lanes(pair)
        rows = pl.ds(pl.multiple_of(side * span, 16), span)
        grad = dO[:, lanes] if side is x else tok[rows, lanes]
        query, grad = qs[rows, lanes] * keep, grad * keep
        at = pl.ds(2 * pair + h, 1)
        p, score_grad = block_terms(
            key, value, bias, query, grad, stat[side, 0, at, :], stat[side, 1, at, :]
        )
        return query, grad, p, score_grad

    def back_queries(pair):
        lanes = pair_lanes(pair)
        result = to_keys = to_values = None
        for rows, mine in ((own(0, span), True), (other(0, span), False)):
            key, value, bias = key_side(rows, lanes)
            for h, keep in enumerate((even, odd)):
                query, grad, p, score_grad = terms(key, value, bias, x, pair, h, keep)
                part = turned(score_grad, key * keep)
                result = part if result is None else result + part
                if mine:
                    value_part, key_part = dot(p, grad), dot(score_grad, query)
                    to_values = value_part if to_values is None else to_values + value_part
                    to_keys = key_part if to_keys is None else to_keys + key_part
        act[0, :, lanes] = (result * SCORE_SCALE).astype(bf16)
        n1[:, lanes] = to_keys
        gp[0, :, lanes] = to_values.astype(bf16)
        each(pair, pairs, beat)

    def back_keys(pair):
        lanes = pair_lanes(pair)
        key, value, bias = key_side(own(0, span), lanes)
        to_keys, to_values = n1[:, lanes], gp[0, :, lanes].astype(f32)
        for h, keep in enumerate((even, odd)):
            query, grad, p, score_grad = terms(key, value, bias, xo, pair, h, keep)
            to_values = to_values + dot(p, grad)
            to_keys = to_keys + dot(score_grad, query)
        act[1, :, lanes] = to_keys.astype(bf16)
        act[2, :, lanes] = to_values.astype(bf16)

    def weight_grad(j, columns):
        value = turned(tok[own(0, span), :], act[j, :, columns]).astype(bf16)
        at = pl.ds(pl.multiple_of(s.down0 + j * shard, 16), shard)
        W[:, :, :, at, columns] = value.reshape(4, 2, 2, shard, value.shape[1])

    def last_pairs(i):
        loop(2, lambda k: back_keys(2 * i + k))
        columns = pl.ds(pl.multiple_of(i * 256, 128), 256)
        loop(2, lambda j: weight_grad(j + 1, columns))
        each(i, pairs // 2, enter)

    loop(pairs, back_queries)
    weight_grad(0, slice(0, width))
    enter()
    send_grad.wait_recv()
    send_stat.wait_recv()
    loop(pairs // 2, last_pairs)

    def input_grad(j):
        acc[...] += by_turned(act[j], matrix(j * shard))

    loop(3, input_grad)
    token_copy = pltpu.make_async_copy(acc, token_out, local.at[n_gather])
    token_copy.start()
    beat()
    send_result.wait_recv()

    def place_rows(n):
        cols = pl.ds(pl.multiple_of(n * third, 128), third)
        value = None
        position = lax.broadcasted_iota(jnp.int32, (span, s.block), 0) + x * span
        for c, rows in ((x, teach[x, :, cols]), (xo, res_in[:, cols])):
            at = order_row[0:1, pl.ds(pl.multiple_of(c * span + x * s.block, 128), s.block)]
            chosen = jnp.where(position == at, 1.0, 0.0).astype(bf16)
            part = dot(chosen, rows)
            value = part if value is None else value + part
        low2[:, cols] = value.astype(bf16)

    loop(3, place_rows)
    ordered_copy = pltpu.make_async_copy(low2, ordered_out, local.at[n_gather + 1])
    ordered_copy.start()
    beat()
    beat()
    assert all(item.stage > item.last for item in reduces)
    loss_out[0] = jnp.max(total.sum() / (2.0 * width * valid_total))
    token_copy.wait()
    ordered_copy.wait()
    links.drain()


class Sizes:
    def __init__(self, span, width, ff, shard, downs, tokens):
        self.span, self.width, self.shard, self.downs, self.tokens = span, width, shard, downs, tokens
        self.panels = ff // width
        self.block = span // 2
        self.out0 = 3 * shard
        self.gain0 = 4 * shard
        self.up0 = self.gain0 + 16
        self.down0 = self.up0 + self.panels * shard
        self.rows = self.down0 + downs
        blocks = [(j * shard, (j + 1) * shard, 0, width) for j in range(3)]
        blocks += [(self.out0, self.up0, 0, width)]
        for p in range(self.panels):
            blocks += [(self.up0 + p * shard, self.up0 + (p + 1) * shard, 0, width)]
        third = width // 3
        blocks += [(self.down0, self.rows, n * third, third) for n in range(3)]
        self.gather_blocks = [b[:2] + (i in GATHER_SPLIT,) + b[2:] for i, b in enumerate(blocks)]
        self.sources = [(j, 0) for j in range(4)] + [(4, p * width) for p in range(self.panels)]
        self.sources += [(5, 0)] * 3
        self.early = EARLY
        back = blocks[-3:] + blocks[4:-3] + [blocks[3], blocks[0]]
        back += [(shard, self.out0, n * third, third) for n in range(3)]
        back = [b[:2] + (i in REDUCE_SPLIT,) + b[2:] for i, b in enumerate(back)]
        self.down_blocks, self.up_blocks = back[:3], back[3:-5]
        self.out_block, self.last_blocks = back[-5], back[-4:]
        self.forward, self.backward = FORWARD, BACKWARD
        self.rows_n, self.flying = 64, 64


def layer(s, *args):
    bf16, f32 = jnp.bfloat16, jnp.float32
    span, width = s.span, s.width
    both = 2 * span
    anywhere = pl.BlockSpec(memory_space=pl.ANY)
    vmem = pl.BlockSpec(memory_space=pltpu.VMEM)
    smem = pl.BlockSpec(memory_space=pltpu.SMEM)
    back = s.down_blocks + s.up_blocks + [s.out_block] + s.last_blocks
    copies = sum(24 if b[2] else 15 for b in s.gather_blocks)
    copies += sum(8 if b[2] else 6 for b in back) + 6 + 5
    small = pltpu.VMEM((8, 128), f32)
    scratch = [
        pltpu.VMEM((4, 2, 2, s.rows, width), bf16),
        pltpu.VMEM((4, 2, 2, s.rows - s.out0, width), bf16),
        pltpu.VMEM((both, width), bf16),
        pltpu.VMEM((3, both, width), bf16),
        pltpu.VMEM((span, width), bf16),
        pltpu.VMEM((2, 2, 16, span), f32),
        pltpu.VMEM((span, width), bf16),
        pltpu.VMEM((span, width), f32),
        pltpu.VMEM((span, 128), f32),
        pltpu.VMEM((span, width), bf16),
        pltpu.VMEM((s.panels, span, width), bf16),
        pltpu.VMEM((s.panels, span, width), bf16),
        pltpu.VMEM((span, width), f32),
        pltpu.VMEM((2, s.block, width), bf16),
        pltpu.VMEM((s.block, width), bf16),
        pltpu.VMEM((span, width), bf16),
        pltpu.VMEM((8, width), f32),
        pltpu.VMEM((3, 8, width), f32),
        pltpu.VMEM((3, 8, 128), f32),
        small,
        small,
        small,
        pltpu.VMEM((4, 8, 128), f32),
        pltpu.SemaphoreType.DMA((s.flying,)),
        pltpu.SemaphoreType.DMA((copies,)),
        pltpu.SemaphoreType.DMA((len(s.gather_blocks) + 2,)),
        pltpu.VMEM((both, 128), f32),
        pltpu.VMEM((4, 2, s.rows - s.out0, width), bf16),
        pltpu.VMEM((2, 4, s.rows - s.out0, width), bf16),
    ]
    return pl.pallas_call(
        functools.partial(layer_kernel, s),
        out_shape=[
            jax.ShapeDtypeStruct((span, width), bf16),
            jax.ShapeDtypeStruct((1,), f32),
            jax.ShapeDtypeStruct((span, width), f32),
            jax.ShapeDtypeStruct((s.out0, width), bf16),
            jax.ShapeDtypeStruct((s.up0 - s.out0, width), bf16),
            jax.ShapeDtypeStruct((s.shard, s.panels * width), bf16),
            jax.ShapeDtypeStruct((s.downs, width), bf16),
        ],
        in_specs=[anywhere, anywhere, vmem, smem, smem] + [anywhere] * 6,
        out_specs=[anywhere, smem, anywhere] + [vmem] * 4,
        scratch_shapes=scratch,
        compiler_params=pltpu.CompilerParams(
            collective_id=0, has_side_effects=True, vmem_limit_bytes=s.vmem
        ),
    )(*args)


def fused_shards(
    tokens,
    w_query,
    w_key,
    w_value,
    w_out,
    w_up,
    w_down,
    gain_attn,
    gain_ffn,
    teacher,
    seq_lengths,
    tok_perm,
    valid_count,
):
    f32 = jnp.float32
    dp_count = lax.axis_size("dp")
    span, width = tokens.shape[1:]
    shard, ff = w_up.shape
    seq_len = tok_perm.shape[1]
    s = Sizes(span, width, ff, shard, w_down.shape[0], seq_len * dp_count)
    s.vmem = 63 * MIB
    gain_rows = jnp.pad(jnp.stack([gain_attn, gain_ffn]), ((0, 14), (0, width - shard)))
    ordered, loss, token_grad, qkv, out, up, down = layer(
        s,
        tokens[0],
        teacher[0],
        tok_perm,
        seq_lengths,
        valid_count,
        w_query,
        w_key,
        w_value,
        jnp.concatenate([w_out, gain_rows]),
        w_up,
        w_down,
    )
    return (
        ordered[None],
        loss,
        token_grad[None],
        qkv[:shard].astype(f32),
        qkv[shard : 2 * shard].astype(f32),
        qkv[2 * shard :].astype(f32),
        out[:shard].astype(f32),
        up.astype(f32),
        down.astype(f32),
        out[shard, :shard].astype(f32),
        out[shard + 1, :shard].astype(f32),
    )


def solution(mesh):
    in_specs = (
        P("dp", "ctx", None),
        P("dp", None),
        P("dp", None),
        P("dp", None),
        P("dp", None),
        P("dp", None),
        P("dp", None),
        P("dp"),
        P("dp"),
        P("dp", "ctx", None),
        P("dp"),
        P("dp", None),
        P(),
    )
    out_specs = (
        P("dp", "ctx", None),
        P(),
        P("dp", "ctx", None),
        P("dp", None),
        P("dp", None),
        P("dp", None),
        P("dp", None),
        P("dp", None),
        P("dp", None),
        P("dp"),
        P("dp"),
    )
    body = fused_shards if dict(mesh.shape) == {"dp": 16, "ctx": 2} else shards
    return jax.shard_map(body, mesh=mesh, in_specs=in_specs, out_specs=out_specs, check_vma=False)
```

```python
import functools
import math

import jax
import jax.numpy as jnp
from jax import lax
from jax.experimental import pallas as pl
from jax.experimental.pallas import tpu as pltpu
from jax.sharding import PartitionSpec as P

HEAD_DIM = 64


EPSILON = 1e-06
SCORE_SCALE = 0.125
MASKED = -1e30
MESH = pl.DeviceIdType.MESH
MIB = 1024 * 1024


GATHER_SPLIT = (0, 3, 5, 6, 7, 8, 10)
REDUCE_SPLIT = (1, 2, 7, 8, 9, 11)
EARLY = 11
FORWARD = ((0, 1, 2, 3, 4, 5, 6, 7, 8, 9, 10), (0,), (1, 2, 3, 4, 5, 6, 7, 8, 9, 10, 0, 1, 2, 3, 4, 5, 6, 7, 8, 9, 10, 0, 1, 2, 3, 4, 5, 6, 7, 8, 9, 0, 10, 1, 2, 1, 3, 2, 0, 4, 5, 0), (4, 6, 7, 8), (3, 9, 10), (3, 5), (9,), (5, 6), (6,), (7,), (7,), (), (), (8,), (), (), (), (8,), (), (), (), (10,), (), (), (), (10,), (), ())
BACKWARD = ((0, 1), (0, 2), (3,), (1, 4), (2, 5), (3, 0, 6), (4, 5, 1, 0, 6, 7), (2, 7, 4), (), (3, 0, 1, 5, 8), (), (8, 4, 6), (2,), (), (5,), (7,), (1, 9), (3, 6, 10), (2, 8, 4, 9, 5, 10, 11), (2, 6, 7, 8, 11, 12), (3, 9, 12), (), (11, 8, 10, 7, 9, 3, 10, 11, 12, 8, 9, 11, 12, 10, 9, 10, 12, 12))


def gelu_exact(values):
    return 0.5 * values * (1.0 + lax.erf(values * 0.7071067811865476))


def norm_forward(hidden, gain_row):
    center = hidden - jnp.mean(hidden, axis=-1, keepdims=True)
    inverse = lax.rsqrt(jnp.mean(center * center, axis=-1, keepdims=True) + EPSILON)
    normal = center * inverse
    return (normal * gain_row, normal, inverse)


def norm_backward(grad_norm, gain_row, normal, inverse):
    scaled = grad_norm * gain_row
    grad_input = inverse * (
        scaled
        - jnp.mean(scaled, axis=-1, keepdims=True)
        - normal * jnp.mean(scaled * normal, axis=-1, keepdims=True)
    )
    return (grad_input, jnp.sum(grad_norm * normal, axis=0))


def row_product(left_mat, right_mat):
    return lax.dot_general(
        left_mat, right_mat, (((0,), (0,)), ((), ())), preferred_element_type=jnp.float32
    )


def by_transpose(left_mat, right_mat):
    return lax.dot_general(
        left_mat, right_mat, (((1,), (1,)), ((), ())), preferred_element_type=jnp.float32
    )


def shards(
    tokens,
    w_query,
    w_key,
    w_value,
    w_out,
    w_up,
    w_down,
    gain_attn,
    gain_ffn,
    teacher,
    seq_lengths,
    tok_perm,
    valid_count,
):
    ctx_count = lax.axis_size("ctx")
    ctx_rank = lax.axis_index("ctx")
    dp_count = lax.axis_size("dp")
    layer_in = tokens[0]
    span_rows, model_width = layer_in.shape
    head_count = model_width // HEAD_DIM
    dealt_order = tok_perm[0]
    seq_len = dealt_order.shape[0]
    length = seq_lengths[0]
    keep_all = dealt_order < length
    per_peer = span_rows // ctx_count
    query_weight, key_weight, value_weight, out_weight, gain_first = (
        lax.all_gather(w_query, "dp", axis=0, tiled=True),
        lax.all_gather(w_key, "dp", axis=0, tiled=True),
        lax.all_gather(w_value, "dp", axis=0, tiled=True),
        lax.all_gather(w_out, "dp", axis=0, tiled=True),
        lax.all_gather(gain_attn, "dp", axis=0, tiled=True),
    )
    up_weight, down_weight, gain_second = (
        lax.all_gather(w_up, "dp", axis=0, tiled=True),
        lax.all_gather(w_down, "dp", axis=0, tiled=True),
        lax.all_gather(gain_ffn, "dp", axis=0, tiled=True),
    )
    queries = jnp.dot(layer_in, query_weight, preferred_element_type=jnp.float32).astype(
        jnp.bfloat16
    )
    keys_own = jnp.dot(layer_in, key_weight, preferred_element_type=jnp.float32).astype(
        jnp.bfloat16
    )
    values_own = jnp.dot(layer_in, value_weight, preferred_element_type=jnp.float32).astype(
        jnp.bfloat16
    )
    query_heads = queries.reshape(span_rows, head_count, HEAD_DIM)
    initial = (
        jnp.full((head_count, span_rows), MASKED, jnp.float32),
        jnp.zeros((head_count, span_rows), jnp.float32),
        jnp.zeros((head_count, span_rows, HEAD_DIM), jnp.float32),
    )
    fold_state = initial
    key_piece = lax.all_gather(keys_own, "ctx", axis=0, tiled=True)
    value_piece = lax.all_gather(values_own, "ctx", axis=0, tiled=True)
    piece_rows = key_piece.shape[0]
    block_rows = math.gcd(piece_rows, span_rows)
    key_blocks = key_piece.reshape(piece_rows // block_rows, block_rows, head_count, HEAD_DIM)
    value_blocks = value_piece.reshape(piece_rows // block_rows, block_rows, head_count, HEAD_DIM)

    def step_block(block_state, block_item):
        running_max, running_sum, accumulated = block_state
        key_block, value_block, block_index = block_item
        key_keep = lax.dynamic_slice_in_dim(keep_all, block_index * block_rows, block_rows)
        scores = (
            jnp.einsum("qhe,khe->hqk", query_heads, key_block, preferred_element_type=jnp.float32)
            * SCORE_SCALE
        )
        scores = jnp.where(key_keep[None, None, :], scores, MASKED)
        new_max = jnp.maximum(running_max, jnp.max(scores, axis=-1))
        factor = jnp.exp(running_max - new_max)
        soft_weights = jnp.where(key_keep[None, None, :], jnp.exp(scores - new_max[..., None]), 0.0)
        running_sum = running_sum * factor + jnp.sum(soft_weights, axis=-1)
        accumulated = accumulated * factor[..., None] + jnp.einsum(
            "hqk,khe->hqe",
            soft_weights.astype(jnp.bfloat16),
            value_block,
            preferred_element_type=jnp.float32,
        )
        return ((new_max, running_sum, accumulated), None)

    block_indices = jnp.arange(piece_rows // block_rows, dtype=jnp.int32)
    fold_state, unused = lax.scan(step_block, fold_state, (key_blocks, value_blocks, block_indices))
    run_max, run_sum, accumulated = fold_state
    log_total = run_max + jnp.log(run_sum)
    attn_full = jnp.transpose(accumulated / run_sum[..., None], (1, 0, 2)).reshape(
        span_rows, model_width
    )
    attn_low = attn_full.astype(jnp.bfloat16)
    gain_first32 = gain_first.astype(jnp.float32)
    gain_second32 = gain_second.astype(jnp.float32)
    branch = jnp.dot(attn_low, out_weight, preferred_element_type=jnp.float32)
    normed, normal_first, inverse_first = norm_forward(
        layer_in.astype(jnp.float32) + branch, gain_first32
    )
    normed_low = normed.astype(jnp.bfloat16)
    upward = jnp.dot(normed_low, up_weight, preferred_element_type=jnp.float32)
    active, gelu_pull = jax.vjp(gelu_exact, upward)
    active_low = active.astype(jnp.bfloat16)
    down_out = jnp.dot(active_low, down_weight, preferred_element_type=jnp.float32)
    result, normal_second, inverse_second = norm_forward(normed + down_out, gain_second32)
    result_low = result.astype(jnp.bfloat16)
    arrived = lax.all_to_all(result_low, "ctx", split_axis=0, concat_axis=0, tiled=True)
    sources = (
        jnp.arange(ctx_count, dtype=jnp.int32)[:, None] * span_rows
        + ctx_rank * per_peer
        + jnp.arange(per_peer, dtype=jnp.int32)[None, :]
    ).reshape(span_rows)
    local_pos = jnp.take(dealt_order, sources) - ctx_rank * span_rows
    in_order = jnp.zeros_like(arrived).at[local_pos].set(arrived)
    target = teacher[0].astype(jnp.float32)
    live_rows = (ctx_rank * span_rows + jnp.arange(span_rows, dtype=jnp.int32) < length)[:, None]
    residual_err = jnp.where(live_rows, in_order.astype(jnp.float32) - target, 0.0)
    total_sq = lax.psum(jnp.sum(residual_err * residual_err), ("dp", "ctx"))
    valid_total = valid_count[0].astype(jnp.float32)
    loss_value = (total_sq / (2.0 * model_width * valid_total)).reshape(1)
    grad_scale = seq_len * dp_count / valid_total
    grad_order = (residual_err * grad_scale).astype(jnp.bfloat16)
    outgoing = jnp.take(grad_order, local_pos, axis=0)
    grad_result = lax.all_to_all(outgoing, "ctx", split_axis=0, concat_axis=0, tiled=True).astype(
        jnp.float32
    )
    grad_sum_second, grad_gain_second = norm_backward(
        grad_result, gain_second32, normal_second, inverse_second
    )
    down_grad_low = grad_sum_second.astype(jnp.bfloat16)
    grad_down_w = row_product(active_low, down_grad_low)
    grad_active = by_transpose(down_grad_low, down_weight)
    grad_upward = gelu_pull(grad_active)[0].astype(jnp.bfloat16)
    grad_up_w = row_product(normed_low, grad_upward)
    grad_normed = grad_sum_second + by_transpose(grad_upward, up_weight)
    grad_hidden, grad_gain_first = norm_backward(
        grad_normed, gain_first32, normal_first, inverse_first
    )
    branch_grad = grad_hidden.astype(jnp.bfloat16)
    grad_out_w = row_product(attn_low, branch_grad)
    attn_grad_low = by_transpose(branch_grad, out_weight).astype(jnp.bfloat16)
    grad_heads = attn_grad_low.reshape(span_rows, head_count, HEAD_DIM)
    row_delta = jnp.sum(
        (attn_grad_low.astype(jnp.float32) * attn_full).reshape(span_rows, head_count, HEAD_DIM),
        axis=-1,
    ).T
    keys_all, values_all = (
        lax.all_gather(keys_own, "ctx", axis=0, tiled=True),
        lax.all_gather(values_own, "ctx", axis=0, tiled=True),
    )
    blocks_count = seq_len // span_rows
    key_stack = keys_all.reshape(blocks_count, span_rows, head_count, HEAD_DIM)
    value_stack = values_all.reshape(blocks_count, span_rows, head_count, HEAD_DIM)

    def score_terms(
        query_block, grad_block, total_block, delta_block, key_block, value_block, key_keep
    ):
        scores = (
            jnp.einsum("qhe,khe->hqk", query_block, key_block, preferred_element_type=jnp.float32)
            * SCORE_SCALE
        )
        soft_weights = jnp.where(
            key_keep[None, None, :], jnp.exp(scores - total_block[..., None]), 0.0
        )
        prob_grad = jnp.einsum(
            "qhe,khe->hqk", grad_block, value_block, preferred_element_type=jnp.float32
        )
        score_grad = (soft_weights * (prob_grad - delta_block[..., None])).astype(jnp.bfloat16)
        return (soft_weights, score_grad)

    def back_block(query_grad, block_item):
        key_block, value_block, block_index = block_item
        key_keep = lax.dynamic_slice_in_dim(keep_all, block_index * span_rows, span_rows)
        soft_weights, score_grad = score_terms(
            query_heads, grad_heads, log_total, row_delta, key_block, value_block, key_keep
        )
        value_grad = jnp.einsum(
            "hqk,qhe->khe",
            soft_weights.astype(jnp.bfloat16),
            grad_heads,
            preferred_element_type=jnp.float32,
        )
        query_grad = query_grad + SCORE_SCALE * jnp.einsum(
            "hqk,khe->qhe", score_grad, key_block, preferred_element_type=jnp.float32
        )
        key_grad = SCORE_SCALE * jnp.einsum(
            "hqk,qhe->khe", score_grad, query_heads, preferred_element_type=jnp.float32
        )
        return (query_grad, (key_grad, value_grad))

    query_grad, (key_grads, value_grads) = lax.scan(
        back_block,
        jnp.zeros((span_rows, head_count, HEAD_DIM), jnp.float32),
        (key_stack, value_stack, jnp.arange(blocks_count, dtype=jnp.int32)),
    )
    key_grad_sum, value_grad_sum = (
        lax.psum_scatter(
            key_grads.reshape(seq_len, model_width).astype(jnp.bfloat16),
            "ctx",
            scatter_dimension=0,
            tiled=True,
        ).astype(jnp.float32),
        lax.psum_scatter(
            value_grads.reshape(seq_len, model_width).astype(jnp.bfloat16),
            "ctx",
            scatter_dimension=0,
            tiled=True,
        ).astype(jnp.float32),
    )
    query_grad_low = query_grad.reshape(span_rows, model_width).astype(jnp.bfloat16)
    key_grad_low = key_grad_sum.astype(jnp.bfloat16)
    value_grad_low = value_grad_sum.astype(jnp.bfloat16)
    grad_query_w = row_product(layer_in, query_grad_low)
    grad_key_w = row_product(layer_in, key_grad_low)
    grad_value_w = row_product(layer_in, value_grad_low)
    token_grad = (
        grad_hidden
        + by_transpose(query_grad_low, query_weight)
        + by_transpose(key_grad_low, key_weight)
        + by_transpose(value_grad_low, value_weight)
    )
    up_part, down_part, second_part = (
        lax.psum_scatter(
            grad_up_w.astype(jnp.bfloat16), "dp", scatter_dimension=0, tiled=True
        ).astype(jnp.float32),
        lax.psum_scatter(
            grad_down_w.astype(jnp.bfloat16), "dp", scatter_dimension=0, tiled=True
        ).astype(jnp.float32),
        lax.psum_scatter(
            grad_gain_second.astype(jnp.bfloat16), "dp", scatter_dimension=0, tiled=True
        ).astype(jnp.float32),
    )
    query_part, key_part, value_part, out_part, first_part = (
        lax.psum_scatter(
            grad_query_w.astype(jnp.bfloat16), "dp", scatter_dimension=0, tiled=True
        ).astype(jnp.float32),
        lax.psum_scatter(
            grad_key_w.astype(jnp.bfloat16), "dp", scatter_dimension=0, tiled=True
        ).astype(jnp.float32),
        lax.psum_scatter(
            grad_value_w.astype(jnp.bfloat16), "dp", scatter_dimension=0, tiled=True
        ).astype(jnp.float32),
        lax.psum_scatter(
            grad_out_w.astype(jnp.bfloat16), "dp", scatter_dimension=0, tiled=True
        ).astype(jnp.float32),
        lax.psum_scatter(
            grad_gain_first.astype(jnp.bfloat16), "dp", scatter_dimension=0, tiled=True
        ).astype(jnp.float32),
    )
    summed = (
        lax.psum(query_part.astype(jnp.bfloat16), "ctx").astype(jnp.float32),
        lax.psum(key_part.astype(jnp.bfloat16), "ctx").astype(jnp.float32),
        lax.psum(value_part.astype(jnp.bfloat16), "ctx").astype(jnp.float32),
        lax.psum(out_part.astype(jnp.bfloat16), "ctx").astype(jnp.float32),
        lax.psum(up_part.astype(jnp.bfloat16), "ctx").astype(jnp.float32),
        lax.psum(down_part.astype(jnp.bfloat16), "ctx").astype(jnp.float32),
        lax.psum(first_part.astype(jnp.bfloat16), "ctx").astype(jnp.float32),
        lax.psum(second_part.astype(jnp.bfloat16), "ctx").astype(jnp.float32),
    )
    query_sum, key_sum, value_sum, out_sum, up_sum, down_sum, first_sum, second_sum = summed
    return (
        in_order[None],
        loss_value,
        token_grad[None],
        query_sum,
        key_sum,
        value_sum,
        out_sum,
        up_sum,
        down_sum,
        first_sum,
        second_sum,
    )


class Place:
    def __init__(self):
        dp = lax.axis_index("dp")
        self.x = lax.axis_index("ctx")
        self.z, self.y, self.c = dp // 4, (dp // 2) % 2, dp % 2
        self.xo, self.yo, self.co = 1 - self.x, 1 - self.y, 1 - self.c
        self.to_x = (dp, self.xo)
        self.to_y = (self.z * 4 + self.yo * 2 + self.c, self.x)
        self.to_c = (self.z * 4 + self.y * 2 + self.co, self.x)
        self.z_up = [(self.z + k) % 4 for k in range(4)]
        self.z_down = [(self.z + 4 - k) % 4 for k in range(4)]
        self.to_z = [(self.z_up[k] * 4 + self.y * 2 + self.c, self.x) for k in range(4)]
        z = self.z
        self.above = [(jnp.logical_and(z >= d, z < 3), z > d) for d in range(3)]
        self.below = [(jnp.logical_and(z <= 3 - d, z > 0), z < 3 - d) for d in range(3)]
        self.to_above, self.to_below = self.to_z[1], self.to_z[3]

    def barrier(self):
        semaphore = pltpu.get_barrier_semaphore()
        for partner in [self.to_x, self.to_y, self.to_c] + self.to_z[1:]:
            pl.semaphore_signal(semaphore, inc=1, device_id=partner, device_id_type=MESH)
        pl.semaphore_wait(semaphore, 6)


class Copy:
    def __init__(self, refs, send, at, recv, to, partner, when):
        self.refs, self.send, self.at, self.recv, self.to = refs, send, at, recv, to
        self.partner, self.when = partner, when

    def make(self):
        src, dst = self.refs()
        return pltpu.make_async_remote_copy(
            src_ref=src,
            dst_ref=dst,
            send_sem=self.send.at[self.at],
            recv_sem=self.recv.at[self.to],
            device_id=self.partner,
            device_id_type=MESH,
        )

    def only(self, side, action):
        if self.when is None:
            action()
        else:
            pl.when(self.when[side])(action)

    def start(self):
        self.only(0, lambda: self.make().start())

    def wait_send(self):
        self.only(0, lambda: self.make().wait_send())

    def wait_recv(self):
        self.only(1, lambda: self.make().wait_recv())


class Links:
    def __init__(self, send, recv):
        self.send, self.recv, self.used, self.flying = send, recv, 0, []
        self.free = list(range(send.shape[0]))

    def start(self, refs, partner, when=None):
        if not self.free:
            self.sent(self.flying[0][0])
        at = self.free.pop(0)
        copy = Copy(refs, self.send, at, self.recv, self.used, partner, when)
        self.used += 1
        copy.start()
        self.flying.append((copy, at))
        return copy

    def sent(self, copy):
        for entry in list(self.flying):
            if entry[0] is copy:
                copy.wait_send()
                self.free.append(entry[1])
        self.flying = [entry for entry in self.flying if entry[0] is not copy]

    def drain(self):
        for copy, at in list(self.flying):
            self.sent(copy)


class Gather:
    def __init__(self, block, early, shard, shift, whole, place, links, own_sem):
        first, last, self.split, self.col0, self.width = block
        self.early = early
        self.rows = pl.ds(first, last - first)
        self.shard, self.shift, self.whole = shard, shift, whole
        self.p, self.links = place, links
        self.own_sem = own_sem
        self.mine, self.theirs = self.half(place.x), self.half(place.xo)
        self.source = self.half(place.x, shift)
        self.last = 6 if self.split else 5

    def cols(self, shift=0):
        return pl.ds(self.col0 + shift, self.width)

    def half(self, x, shift=0):
        if not self.split:
            return self.cols(shift)
        size = self.width // 2
        return pl.ds(pl.multiple_of(self.col0 + shift + x * size, 128), size)

    def piece(self, z, y, cols):
        return self.whole.at[z, y, self.p.c, self.rows, cols]

    def own(self):
        p = self.p
        return pltpu.make_async_copy(
            self.shard.at[:, self.cols(self.shift)], self.piece(p.z, p.y, self.cols()), self.own_sem()
        )

    def push(self, z, y, cols, partner, when=None):
        return self.links.start(lambda: (self.piece(z, y, cols),) * 2, partner, when)

    def send_own(self, partner, when=None):
        p = self.p
        return self.links.start(
            lambda: (self.shard.at[:, self.source], self.piece(p.z, p.y, self.mine)), partner, when
        )

    def step0(self):
        p = self.p
        self.up, self.down = self.send_own(p.to_above, p.above[0]), self.send_own(p.to_below, p.below[0])
        self.own().start()
        self.from_x, self.from_y = [], []
        if self.early:
            self.from_y.append(self.send_own(p.to_y))

    def hop(self, d):
        p = self.p
        up, down = self.up, self.down
        up.wait_recv()
        if d < 2:
            self.up = self.push(p.z_down[d + 1], p.y, self.mine, p.to_above, p.above[d + 1])
        down.wait_recv()
        if d < 2:
            self.down = self.push(p.z_up[d + 1], p.y, self.mine, p.to_below, p.below[d + 1])
        for z, there in ((p.z_down[d + 1], p.above[d][1]), (p.z_up[d + 1], p.below[d][1])):
            when = (there, there)
            self.from_y.append(self.push(z, p.y, self.mine, p.to_y, when))
            if self.split:
                self.from_x.append(self.push(z, p.y, self.mine, p.to_x, when))

    def step1(self):
        if not self.early:
            self.from_y.append(self.send_own(self.p.to_y))
        self.hop(0)

    def step2(self):
        self.hop(1)

    def step3(self):
        self.hop(2)
        self.own().wait()
        self.from_c = [self.push(slice(None), self.p.y, self.mine, self.p.to_c)]

    def step4(self):
        p, every = self.p, slice(None)
        for copy in self.from_y:
            copy.wait_recv()
        if self.split:
            self.across = self.push(every, p.yo, self.mine, p.to_x)
        self.from_c.append(self.push(every, p.yo, self.mine, p.to_c))
        if self.split:
            for copy in self.from_x:
                copy.wait_recv()
            self.from_c.append(self.push(every, p.y, self.theirs, p.to_c))

    def step5(self):
        if self.split:
            self.across.wait_recv()
            self.from_c.append(self.push(slice(None), self.p.yo, self.theirs, self.p.to_c))
        else:
            self.step6()

    def step6(self):
        for copy in self.from_c:
            copy.wait_recv()


class Reduce:
    def __init__(self, block, at, grads, out, out0, shift, place, links, here, core_in, bufs):
        first, last, self.split, self.col0, self.width = block
        self.rows = last - first
        self.at0, self.here0, self.out0, self.shift = at, here, out0, shift
        self.at, self.here = pl.ds(at, self.rows), pl.ds(here, self.rows)
        self.grads, self.out = grads, out
        self.p, self.links = place, links
        self.core_in, self.bufs = core_in, bufs
        limit = 96 * 768 // self.width
        self.block = max(b for b in range(16, min(self.rows, limit) + 1, 16) if self.rows % b == 0)
        self.stage = 0
        self.mine, self.theirs = self.half(place.x), self.half(place.xo)
        self.out_mine = self.half(place.x, shift)
        self.last = 5 if self.split else 4

    def cols(self, shift=0):
        return pl.ds(self.col0 + shift, self.width)

    def half(self, x, shift=0):
        if not self.split:
            return self.cols(shift)
        size = self.width // 2
        return pl.ds(pl.multiple_of(self.col0 + shift + x * size, 128), size)

    def low(self):
        return pl.ds(self.col0, self.width // 2)

    def high(self):
        return pl.ds(self.col0 + self.width // 2, self.width // 2) if self.split else self.cols()

    def add(self, outer, target, source):
        steps = self.rows // self.block

        def body(i, carry):
            first = pl.multiple_of((i % steps) * self.block, 16)
            put = target(i // steps, pl.ds(self.at0 + first, self.block))
            given = source(i // steps, pl.ds(self.here0 + first, self.block))
            self.grads[put] = self.grads[put] + given
            return carry

        lax.fori_loop(0, outer * steps, body, 0)

    def step0(self):
        p = self.p
        self.by_core = self.links.start(
            lambda: (
                self.grads.at[:, :, p.co, self.at, self.cols()],
                self.core_in().at[:, :, self.here, self.cols()],
            ),
            p.to_c,
        )

    def add_core(self, y):
        p = self.p
        self.add(
            4,
            lambda i, rows: (i, y, p.c, rows, self.cols()),
            lambda i, rows: self.core_in()[i, y, rows, self.cols()],
        )

    def send_y(self):
        p = self.p
        self.by_y = self.links.start(
            lambda: (
                self.grads.at[:, p.yo, p.c, self.at, self.mine],
                self.bufs(0, slice(None)).at[:, self.here, self.high()],
            ),
            p.to_y,
        )

    def step1(self):
        p = self.p
        self.by_core.wait_recv()
        self.add_core(p.yo)
        if not self.split:
            self.send_y()
        self.add_core(p.y)
        if self.split:
            self.by_x = [self.send_x(0, p.yo), self.send_x(1, p.y)]

    def send_x(self, i, y):
        p = self.p
        return self.links.start(
            lambda: (
                self.grads.at[:, y, p.c, self.at, self.theirs],
                self.bufs(i, slice(None)).at[:, self.here, self.low()],
            ),
            p.to_x,
        )

    def add_x(self, i, y):
        p = self.p
        self.by_x[i].wait_recv()
        self.add(
            4,
            lambda j, rows: (j, y, p.c, rows, self.mine),
            lambda j, rows: self.bufs(i, j)[rows, self.low()],
        )

    def step2(self):
        if self.split:
            self.add_x(0, self.p.yo)
            self.send_y()
            self.add_x(1, self.p.y)
        else:
            self.reduce_y()

    def reduce_y(self):
        p = self.p
        self.by_y.wait_recv()
        self.add(
            4,
            lambda i, rows: (i, p.y, p.c, rows, self.mine),
            lambda i, rows: self.bufs(0, i)[rows, self.high()],
        )
        self.by_z = [self.send_z(k) for k in range(1, 4)]

    def send_z(self, k):
        p = self.p
        return self.links.start(
            lambda: (
                self.grads.at[p.z_up[k], p.y, p.c, self.at, self.mine],
                self.bufs(1, k - 1).at[self.here, self.high()],
            ),
            p.to_z[k],
        )

    def reduce_z(self, put):
        p = self.p
        for copy in self.by_z:
            copy.wait_recv()

        def body(i, carry):
            first = pl.multiple_of(i * self.block, 16)
            rows = pl.ds(self.here0 + first, self.block)
            place = (p.z, p.y, p.c, pl.ds(self.at0 + first, self.block), self.mine)
            total = self.grads[place].astype(jnp.float32)
            for k in range(3):
                total = total + self.bufs(1, k)[rows, self.high()].astype(jnp.float32)
            put(pl.ds(self.out0 + first, self.block), place, total.astype(jnp.bfloat16))
            return carry

        lax.fori_loop(0, self.rows // self.block, body, 0)

    def step3(self):
        p = self.p
        if self.split:
            self.reduce_y()
            return

        def put(rows, place, value):
            self.grads[place] = value

        self.reduce_z(put)
        self.by_x = self.links.start(
            lambda: (
                self.grads.at[p.z, p.y, p.c, self.at, self.cols()],
                self.bufs(1, 3).at[self.here, self.cols()],
            ),
            p.to_x,
        )

    def step4(self):
        p = self.p
        if self.split:

            def put(rows, place, value):
                self.out[rows, self.out_mine] = value

            self.reduce_z(put)
            self.by_x = self.links.start(
                lambda: (self.out.at[pl.ds(self.out0, self.rows), self.out_mine],) * 2, p.to_x
            )
            return
        self.by_x.wait_recv()

        def body(i, carry):
            first = pl.multiple_of(i * self.block, 16)
            rows = pl.ds(self.here0 + first, self.block)
            own = self.grads[p.z, p.y, p.c, pl.ds(self.at0 + first, self.block), self.cols()]
            self.out[pl.ds(self.out0 + first, self.block), self.cols(self.shift)] = (
                own.astype(jnp.float32) + self.bufs(1, 3)[rows, self.cols()].astype(jnp.float32)
            ).astype(jnp.bfloat16)
            return carry

        lax.fori_loop(0, self.rows // self.block, body, 0)

    def step5(self):
        self.by_x.wait_recv()

    def beat(self):
        getattr(self, "step" + str(self.stage))()
        self.stage += 1


class Total:
    last = 4

    def __init__(self, value, core_in, x_in, y_in, by_z, place, links):
        self.value, self.core_in, self.x_in, self.y_in, self.by_z = value, core_in, x_in, y_in, by_z
        self.p, self.links = place, links
        self.stage = 0

    def step0(self):
        self.copy = self.links.start(lambda: (self.value.at[0], self.core_in), self.p.to_c)

    def step1(self):
        self.copy.wait_recv()
        self.value[1] = self.value[0] + self.core_in[...]
        self.copy = self.links.start(lambda: (self.value.at[1], self.x_in), self.p.to_x)

    def step2(self):
        self.copy.wait_recv()
        self.value[2] = self.value[1] + self.x_in[...]
        self.copy = self.links.start(lambda: (self.value.at[2], self.y_in), self.p.to_y)

    def step3(self):
        self.copy.wait_recv()
        z = self.p.z
        self.by_z[z] = self.value[2] + self.y_in[...]
        self.spread = [
            self.links.start(lambda: (self.by_z.at[z],) * 2, self.p.to_z[k]) for k in range(1, 4)
        ]

    def step4(self):
        for copy in self.spread:
            copy.wait_recv()

    def sum(self):
        return ((self.by_z[0] + self.by_z[1]) + self.by_z[2]) + self.by_z[3]

    def beat(self):
        getattr(self, "step" + str(self.stage))()
        self.stage += 1


ROOT_HALF = 0.7071067811865476
DENSITY = 0.3989422804014327


def dot(left, right):
    return jnp.dot(left, right, preferred_element_type=jnp.float32)


def turned(left, right):
    return lax.dot_general(
        left, right, (((0,), (0,)), ((), ())), preferred_element_type=jnp.float32
    )


def by_turned(left, right):
    return lax.dot_general(
        left, right, (((1,), (1,)), ((), ())), preferred_element_type=jnp.float32
    )


def layer_kernel(s, *refs):
    tokens, teacher, order_row, length, valid = refs[:5]
    weights, (ordered_out, loss_out, token_out), outs = refs[5:11], refs[11:14], refs[14:18]
    refs = refs[8:]
    (W, G, tok, QKV, dO, stat, attn, n1, r1, low1, act, gp, acc, teach, res_in, low2, gains, sums) = refs[10:28]
    total_refs, (send, recv, local), (order_col, core_in, bufs) = refs[28:33], refs[33:36], refs[36:]
    qs, ks, vs = QKV.at[0], QKV.at[1], QKV.at[2]
    f32, bf16 = jnp.float32, jnp.bfloat16
    span, width, shard, downs = s.span, s.width, s.shard, s.downs
    pairs = width // 128
    third = width // 3
    place = Place()
    x, xo = place.x, place.xo
    links = Links(send, recv)

    def own(first, size):
        return pl.ds(pl.multiple_of(x * span + first, 16), size)

    def other(first, size):
        return pl.ds(pl.multiple_of(xo * span + first, 16), size)

    def loop(count, body):
        def step(i, carry):
            body(i)
            return carry

        lax.fori_loop(0, count, step, 0)

    def each(i, count, action):
        for k in range(count):
            pl.when(i == k)(lambda: action())

    def matrix(first):
        return W[:, :, :, pl.ds(pl.multiple_of(first, 16), shard), :].reshape(width, width)

    def semaphore(i):
        return local.at[i]

    gathers = [
        Gather(block, i < s.early, weights[j], shift, W, place, links, functools.partial(semaphore, i))
        for i, (block, (j, shift)) in enumerate(zip(s.gather_blocks, s.sources))
    ]
    n_gather = len(gathers)
    stages = [0] * n_gather
    forward = iter(s.forward)

    def advance():
        for i in next(forward):
            getattr(gathers[i], "step" + str(stages[i]))()
            stages[i] += 1

    def arrived(*blocks):
        advance()
        assert all(stages[i] > gathers[i].last for i in blocks)

    place.barrier()
    own_tokens = pltpu.make_async_copy(tokens, tok.at[own(0, span)], local.at[n_gather])
    own_tokens.start()
    own_teacher = pltpu.make_async_copy(teacher, gp.at[0], local.at[n_gather + 1])
    own_teacher.start()
    send_tokens = links.start(lambda: (tokens, tok.at[own(0, span)]), place.to_x)
    advance()
    order_col[...] = jnp.broadcast_to(order_row[...].astype(f32), (128, 2 * span)).T
    length_now = length[0]
    length_float = length_now.astype(f32)
    iota_rows = lax.broadcasted_iota(jnp.int32, (s.block, span), 1)

    def pick(c):
        rows = pl.ds(pl.multiple_of(c * span + x * s.block, 16), s.block)
        position = order_col[rows, :].astype(jnp.int32) - x * span
        chosen = iota_rows == jnp.concatenate([position] * (span // 128), axis=1)
        return jnp.where(chosen, 1.0, 0.0).astype(bf16)

    own_teacher.wait()
    for n in range(3):
        cols = slice(n * third, (n + 1) * third)
        gp[1, : s.block, cols] = dot(pick(xo), gp[0, :, cols]).astype(bf16)
        teach[x, :, cols] = dot(pick(x), gp[0, :, cols]).astype(bf16)
    teach_copy = links.start(lambda: (gp.at[1, pl.ds(0, s.block)], teach.at[x]), place.to_x)
    advance()
    arrived(0, 1, 2)

    own_tokens.wait()

    def side(i):
        @pl.when(i == 1)
        def _():
            send_tokens.wait_recv()

        rows = pl.ds(pl.multiple_of(jnp.where(i == 0, x, xo) * span, 16), span)

        def project(j):
            scale = jnp.where(j == 0, SCORE_SCALE, 1.0)
            QKV[j, rows, :] = (dot(tok[rows, :], matrix(j * shard)) * scale).astype(bf16)

        loop(3, project)
        each(i, 2, advance)

    loop(2, side)

    lane = lax.broadcasted_iota(jnp.int32, (1, 128), 1)
    even32 = lane < HEAD_DIM
    even = jnp.where(even32, 1.0, 0.0).astype(bf16)
    odd = jnp.where(even32, 0.0, 1.0).astype(bf16)
    bias_row = jnp.where(order_row[0:1, :] < length_now, 0.0, MASKED)

    def attend(pair):
        lanes = pl.ds(pl.multiple_of(pair * 128, 128), 128)
        query, key, value = qs[own(0, span), lanes], ks[:, lanes], vs[:, lanes]
        tops, mixed = [], []
        for keep, rest in ((even, odd), (odd, even)):
            scores = by_turned(query * keep, key) + bias_row
            top = jnp.max(scores, axis=1, keepdims=True)
            weight = jnp.exp(scores - top).astype(bf16)
            tops.append(top)
            mixed.append(dot(weight, value * keep + rest))
        part = jnp.where(even32, mixed[0], mixed[1])
        total = pltpu.roll(jnp.where(even32, mixed[1], mixed[0]), HEAD_DIM, 1)
        attn[:, lanes] = (part / total).astype(bf16)
        log_rows = (jnp.where(even32, tops[0], tops[1]) + jnp.log(total)).T
        for h in range(2):
            stat[x, 0, pl.ds(2 * pair + h, 1), :] = log_rows[
                h * HEAD_DIM : h * HEAD_DIM + 1, :
            ]
        each(pair, pairs, advance)

    loop(pairs, attend)

    arrived(3)
    device = lax.broadcasted_iota(jnp.int32, (16, width), 0)
    feature = lax.broadcasted_iota(jnp.int32, (16, width), 1)
    mine = (feature // shard) == device
    spread = jnp.where(
        lax.broadcasted_iota(jnp.int32, (128, width), 1) % shard
        == lax.broadcasted_iota(jnp.int32, (128, width), 0),
        1.0,
        0.0,
    ).astype(bf16)
    gain_rows = W[:, :, :, s.gain0 : s.gain0 + 16, :128].reshape(16, 16, 128).astype(f32)
    for g in range(2):
        wide = dot(gain_rows[:, g, :].astype(bf16), spread)
        gains[g : g + 1, :] = jnp.sum(jnp.where(mine, wide, 0.0), axis=0, keepdims=True)

    acc[...] = dot(attn[...], matrix(s.out0))
    advance()
    rows_n = s.rows_n

    def wide_column(column):
        return jnp.broadcast_to(column, (rows_n, 128))

    def first_norm(b):
        first = pl.multiple_of(b * rows_n, 16)
        rows = pl.ds(first, rows_n)
        hidden = tok[own(first, rows_n), :].astype(f32) + acc[rows, :]
        center = hidden - jnp.mean(hidden, axis=1, keepdims=True)
        inverse = lax.rsqrt(jnp.mean(center * center, axis=1, keepdims=True) + EPSILON)
        normal = center * inverse
        n1[rows, :] = normal
        r1[rows, :] = wide_column(inverse)
        low1[rows, :] = (normal * gains[0:1, :]).astype(bf16)

    loop(span // rows_n, first_norm)
    advance()

    teach_copy.wait_recv()
    links.sent(teach_copy)

    def ahead(i, count):
        steps = iter(range(count))

        def action():
            if next(steps) > 0:
                advance()
            advance()

        each(i, count, action)

    def upward(p):
        ahead(p, s.panels)
        rows = pl.ds(pl.multiple_of(s.up0 + p * shard, 16), shard)
        for n in range(3):
            cols = slice(n * third, (n + 1) * third)
            value = dot(low1[...], W[:, :, :, rows, cols].reshape(width, third))
            cdf = 0.5 * (1.0 + lax.erf(value * ROOT_HALF))
            act[p, :, cols] = (value * cdf).astype(bf16)
            gp[p, :, cols] = (cdf + value * (jnp.exp(-0.5 * value * value) * DENSITY)).astype(bf16)

    def downward(n):
        ahead(n, 3)
        cols = pl.ds(pl.multiple_of(n * third, 128), third)
        value = None
        for p in range(s.panels):
            part = dot(act[p], W[p, :, :, s.down0 :, cols].reshape(width, third))
            value = part if value is None else value + part
        acc[:, cols] = value

    loop(s.panels, upward)
    advance()
    loop(3, downward)
    advance()
    assert all(stage > item.last for stage, item in zip(stages, gathers))

    sums[...] = jnp.zeros_like(sums)
    valid_total = jnp.full((1, 1), valid[0], jnp.int32).astype(f32)
    grad_scale = s.tokens / valid_total

    def fold(values):
        return jnp.sum(values.reshape(rows_n // 8, 8, width), axis=0)

    def second_norm(b):
        first = pl.multiple_of(b * rows_n, 16)
        rows = pl.ds(first, rows_n)
        hidden = n1[rows, :] * gains[0:1, :] + acc[rows, :]
        center = hidden - jnp.mean(hidden, axis=1, keepdims=True)
        inverse = lax.rsqrt(jnp.mean(center * center, axis=1, keepdims=True) + EPSILON)
        normal = center * inverse
        gain = gains[1:2, :]
        result = (normal * gain).astype(bf16)
        per = s.block // rows_n
        at = pl.ds(pl.multiple_of((b % per) * rows_n, 16), rows_n)
        target = teach[b // per, at, :].astype(f32)
        teach[b // per, at, :] = result
        live = order_col[own(first, rows_n), 0:1] < length_float
        error = jnp.where(live, result.astype(f32) - target, 0.0)
        sums[2] += fold(error * error)
        grad = (error * grad_scale).astype(bf16).astype(f32)
        sums[1] += fold(grad * normal)
        scaled = grad * gain
        grad_sum = inverse * (
            scaled
            - jnp.mean(scaled, axis=1, keepdims=True)
            - normal * jnp.mean(scaled * normal, axis=1, keepdims=True)
        )
        acc[rows, :] = grad_sum
        low2[rows, :] = grad_sum.astype(bf16)

    loop(span // rows_n, second_norm)
    links.drain()
    send_result = links.start(lambda: (teach.at[xo], res_in), place.to_x)
    total_refs[0][0] = jnp.broadcast_to(
        jnp.sum(jnp.sum(sums[2], axis=0, keepdims=True), axis=1, keepdims=True), (8, 128)
    )
    total = Total(*total_refs, place, links)

    reduces = [total]
    backward = iter(s.backward)

    def beat():
        for i in next(backward):
            reduces[i].beat()

    def prepare(block, out, shift=0, in_weights=False):
        first = block[0]
        return Reduce(
            block,
            first + s.down0 if in_weights else first - s.out0,
            W if in_weights else G,
            outs[out],
            first if in_weights else 0,
            shift,
            place,
            links,
            first + s.up0 if in_weights else first - s.out0,
            (lambda: W.at[:, :, 0]) if in_weights else (lambda: core_in),
            (lambda h, j: W.at[j, h, 1]) if in_weights else (lambda h, j: bufs.at[h, j]),
        )

    coming = [prepare(block, 3) for block in s.down_blocks]
    coming += [prepare(block, 2, p * width) for p, block in enumerate(s.up_blocks)]
    coming += [prepare(s.out_block, 1)]
    coming += [prepare(block, 0, in_weights=True) for block in s.last_blocks]

    def enter():
        reduces.append(coming.pop(0))
        beat()

    def panel_grad(first, left, right):
        value = turned(left[...], right[...]).astype(bf16)
        at = pl.ds(pl.multiple_of(first - s.out0, 16), shard)
        G[:, :, :, at, :] = value.reshape(4, 2, 2, shard, width)

    def down_grad(n):
        cols = pl.ds(pl.multiple_of(n * third, 128), third)

        def panel(p):
            value = turned(act[p], low2[:, cols]).astype(bf16)
            G[p, :, :, s.down0 - s.out0 :, cols] = value.reshape(2, 2, downs, third)

        loop(s.panels, panel)
        each(n, 3, enter)

    def up_grad(p):
        value = by_turned(low2[...], W[p, :, :, s.down0 :, :].reshape(width, width))
        gp[p] = (value * gp[p].astype(f32)).astype(bf16)
        panel_grad(s.up0 + p * shard, low1, gp.at[p])
        each(p, s.panels, enter)

    def normed_grad(p):
        acc[...] += by_turned(gp[p], matrix(s.up0 + p * shard))

    loop(3, down_grad)
    loop(s.panels, up_grad)
    loop(s.panels, normed_grad)
    beat()

    def first_back(b):
        rows = pl.ds(pl.multiple_of(b * rows_n, 16), rows_n)
        grad, normal = acc[rows, :], n1[rows, :]
        sums[0] += fold(grad * normal)
        scaled = grad * gains[0:1, :]
        hidden_grad = r1[rows, 0:1] * (
            scaled
            - jnp.mean(scaled, axis=1, keepdims=True)
            - normal * jnp.mean(scaled * normal, axis=1, keepdims=True)
        )
        acc[rows, :] = hidden_grad
        low2[rows, :] = hidden_grad.astype(bf16)

    loop(span // rows_n, first_back)
    beat()

    dO[...] = by_turned(low2[...], matrix(s.out0)).astype(bf16)
    head = lax.broadcasted_iota(jnp.int32, (16, width), 0)
    in_head = jnp.where((feature // HEAD_DIM) == head, 1.0, 0.0)

    def head_delta(b):
        first = pl.multiple_of(b * 128, 128)
        rows = pl.ds(first, 128)
        product = dO[rows, :].astype(f32) * attn[rows, :].astype(f32)
        stat[x, 1, :, rows] = lax.dot_general(
            in_head,
            product,
            (((1,), (1,)), ((), ())),
            precision=lax.Precision.HIGHEST,
            preferred_element_type=f32,
        )

    loop(span // 128, head_delta)
    send_grad = links.start(lambda: (dO, tok.at[own(0, span)]), place.to_x)
    send_stat = links.start(lambda: (stat.at[x],) * 2, place.to_x)

    panel_grad(s.out0, attn, low2)
    pieces = []
    for g in range(2):
        row = jnp.sum(sums[g], axis=0, keepdims=True)
        split = jnp.where(mine, jnp.broadcast_to(row, (16, width)), 0.0).astype(bf16)
        pieces.append(by_turned(split, spread))
    at_row = lax.broadcasted_iota(jnp.int32, (16, 16, 128), 1)
    gain_block = jnp.where(
        at_row == 0, pieces[0][:, None, :], jnp.where(at_row == 1, pieces[1][:, None, :], 0.0)
    ).astype(bf16)
    G[:, :, :, shard : shard + 16, :128] = gain_block.reshape(4, 2, 2, 16, 128)
    G[:, :, :, shard : shard + 16, 128:] = jnp.zeros((4, 2, 2, 16, width - 128), bf16)
    enter()

    def block_terms(key, value, bias, query, grad, log_row, delta_row):
        scores = by_turned(key, query) + bias
        p = jnp.exp(scores - log_row)
        score_grad = (p * (by_turned(value, grad) - delta_row)).astype(bf16)
        return p.astype(bf16), score_grad

    def key_side(rows, lanes):
        column = jnp.where(order_col[rows, :] < length_float, 0.0, MASKED)
        return ks[rows, lanes], vs[rows, lanes], jnp.concatenate([column] * (span // 128), axis=1)

    def pair_lanes(pair):
        return pl.ds(pl.multiple_of(pair * 128, 128), 128)

    def terms(key, value, bias, side, pair, h, keep):
        lanes = pair_lanes(pair)
        rows = pl.ds(pl.multiple_of(side * span, 16), span)
        grad = dO[:, lanes] if side is x else tok[rows, lanes]
        query, grad = qs[rows, lanes] * keep, grad * keep
        at = pl.ds(2 * pair + h, 1)
        p, score_grad = block_terms(
            key, value, bias, query, grad, stat[side, 0, at, :], stat[side, 1, at, :]
        )
        return query, grad, p, score_grad

    def back_queries(pair):
        lanes = pair_lanes(pair)
        result = to_keys = to_values = None
        for rows, mine in ((own(0, span), True), (other(0, span), False)):
            key, value, bias = key_side(rows, lanes)
            for h, keep in enumerate((even, odd)):
                query, grad, p, score_grad = terms(key, value, bias, x, pair, h, keep)
                part = turned(score_grad, key * keep)
                result = part if result is None else result + part
                if mine:
                    value_part, key_part = dot(p, grad), dot(score_grad, query)
                    to_values = value_part if to_values is None else to_values + value_part
                    to_keys = key_part if to_keys is None else to_keys + key_part
        act[0, :, lanes] = (result * SCORE_SCALE).astype(bf16)
        n1[:, lanes] = to_keys
        gp[0, :, lanes] = to_values.astype(bf16)
        each(pair, pairs, beat)

    def back_keys(pair):
        lanes = pair_lanes(pair)
        key, value, bias = key_side(own(0, span), lanes)
        to_keys, to_values = n1[:, lanes], gp[0, :, lanes].astype(f32)
        for h, keep in enumerate((even, odd)):
            query, grad, p, score_grad = terms(key, value, bias, xo, pair, h, keep)
            to_values = to_values + dot(p, grad)
            to_keys = to_keys + dot(score_grad, query)
        act[1, :, lanes] = to_keys.astype(bf16)
        act[2, :, lanes] = to_values.astype(bf16)

    def weight_grad(j, columns):
        value = turned(tok[own(0, span), :], act[j, :, columns]).astype(bf16)
        at = pl.ds(pl.multiple_of(s.down0 + j * shard, 16), shard)
        W[:, :, :, at, columns] = value.reshape(4, 2, 2, shard, value.shape[1])

    def last_pairs(i):
        loop(2, lambda k: back_keys(2 * i + k))
        columns = pl.ds(pl.multiple_of(i * 256, 128), 256)
        loop(2, lambda j: weight_grad(j + 1, columns))
        each(i, pairs // 2, enter)

    loop(pairs, back_queries)
    weight_grad(0, slice(0, width))
    enter()
    send_grad.wait_recv()
    send_stat.wait_recv()
    loop(pairs // 2, last_pairs)

    def input_grad(j):
        acc[...] += by_turned(act[j], matrix(j * shard))

    loop(3, input_grad)
    token_copy = pltpu.make_async_copy(acc, token_out, local.at[n_gather])
    token_copy.start()
    beat()
    send_result.wait_recv()

    def place_rows(n):
        cols = pl.ds(pl.multiple_of(n * third, 128), third)
        value = None
        position = lax.broadcasted_iota(jnp.int32, (span, s.block), 0) + x * span
        for c, rows in ((x, teach[x, :, cols]), (xo, res_in[:, cols])):
            at = order_row[0:1, pl.ds(pl.multiple_of(c * span + x * s.block, 128), s.block)]
            chosen = jnp.where(position == at, 1.0, 0.0).astype(bf16)
            part = dot(chosen, rows)
            value = part if value is None else value + part
        low2[:, cols] = value.astype(bf16)

    loop(3, place_rows)
    ordered_copy = pltpu.make_async_copy(low2, ordered_out, local.at[n_gather + 1])
    ordered_copy.start()
    beat()
    beat()
    assert all(item.stage > item.last for item in reduces)
    loss_out[0] = jnp.max(total.sum() / (2.0 * width * valid_total))
    token_copy.wait()
    ordered_copy.wait()
    links.drain()


class Sizes:
    def __init__(self, span, width, ff, shard, downs, tokens):
        self.span, self.width, self.shard, self.downs, self.tokens = span, width, shard, downs, tokens
        self.panels = ff // width
        self.block = span // 2
        self.out0 = 3 * shard
        self.gain0 = 4 * shard
        self.up0 = self.gain0 + 16
        self.down0 = self.up0 + self.panels * shard
        self.rows = self.down0 + downs
        blocks = [(j * shard, (j + 1) * shard, 0, width) for j in range(3)]
        blocks += [(self.out0, self.up0, 0, width)]
        for p in range(self.panels):
            blocks += [(self.up0 + p * shard, self.up0 + (p + 1) * shard, 0, width)]
        third = width // 3
        blocks += [(self.down0, self.rows, n * third, third) for n in range(3)]
        self.gather_blocks = [b[:2] + (i in GATHER_SPLIT,) + b[2:] for i, b in enumerate(blocks)]
        self.sources = [(j, 0) for j in range(4)] + [(4, p * width) for p in range(self.panels)]
        self.sources += [(5, 0)] * 3
        self.early = EARLY
        back = blocks[-3:] + blocks[4:-3] + [blocks[3], blocks[0]]
        back += [(shard, self.out0, n * third, third) for n in range(3)]
        back = [b[:2] + (i in REDUCE_SPLIT,) + b[2:] for i, b in enumerate(back)]
        self.down_blocks, self.up_blocks = back[:3], back[3:-5]
        self.out_block, self.last_blocks = back[-5], back[-4:]
        self.forward, self.backward = FORWARD, BACKWARD
        self.rows_n, self.flying = 256, 128


def layer(s, *args):
    bf16, f32 = jnp.bfloat16, jnp.float32
    span, width = s.span, s.width
    both = 2 * span
    anywhere = pl.BlockSpec(memory_space=pl.ANY)
    vmem = pl.BlockSpec(memory_space=pltpu.VMEM)
    smem = pl.BlockSpec(memory_space=pltpu.SMEM)
    back = s.down_blocks + s.up_blocks + [s.out_block] + s.last_blocks
    copies = sum(24 if b[2] else 15 for b in s.gather_blocks)
    copies += sum(8 if b[2] else 6 for b in back) + 6 + 5
    small = pltpu.VMEM((8, 128), f32)
    scratch = [
        pltpu.VMEM((4, 2, 2, s.rows, width), bf16),
        pltpu.VMEM((4, 2, 2, s.rows - s.out0, width), bf16),
        pltpu.VMEM((both, width), bf16),
        pltpu.VMEM((3, both, width), bf16),
        pltpu.VMEM((span, width), bf16),
        pltpu.VMEM((2, 2, 16, span), f32),
        pltpu.VMEM((span, width), bf16),
        pltpu.VMEM((span, width), f32),
        pltpu.VMEM((span, 128), f32),
        pltpu.VMEM((span, width), bf16),
        pltpu.VMEM((s.panels, span, width), bf16),
        pltpu.VMEM((s.panels, span, width), bf16),
        pltpu.VMEM((span, width), f32),
        pltpu.VMEM((2, s.block, width), bf16),
        pltpu.VMEM((s.block, width), bf16),
        pltpu.VMEM((span, width), bf16),
        pltpu.VMEM((8, width), f32),
        pltpu.VMEM((3, 8, width), f32),
        pltpu.VMEM((3, 8, 128), f32),
        small,
        small,
        small,
        pltpu.VMEM((4, 8, 128), f32),
        pltpu.SemaphoreType.DMA((s.flying,)),
        pltpu.SemaphoreType.DMA((copies,)),
        pltpu.SemaphoreType.DMA((len(s.gather_blocks) + 2,)),
        pltpu.VMEM((both, 128), f32),
        pltpu.VMEM((4, 2, s.rows - s.out0, width), bf16),
        pltpu.VMEM((2, 4, s.rows - s.out0, width), bf16),
    ]
    return pl.pallas_call(
        functools.partial(layer_kernel, s),
        out_shape=[
            jax.ShapeDtypeStruct((span, width), bf16),
            jax.ShapeDtypeStruct((1,), f32),
            jax.ShapeDtypeStruct((span, width), f32),
            jax.ShapeDtypeStruct((s.out0, width), bf16),
            jax.ShapeDtypeStruct((s.up0 - s.out0, width), bf16),
            jax.ShapeDtypeStruct((s.shard, s.panels * width), bf16),
            jax.ShapeDtypeStruct((s.downs, width), bf16),
        ],
        in_specs=[anywhere, anywhere, vmem, smem, smem] + [anywhere] * 6,
        out_specs=[anywhere, smem, anywhere] + [vmem] * 4,
        scratch_shapes=scratch,
        compiler_params=pltpu.CompilerParams(
            collective_id=0, has_side_effects=True, vmem_limit_bytes=s.vmem
        ),
    )(*args)


def fused_shards(
    tokens,
    w_query,
    w_key,
    w_value,
    w_out,
    w_up,
    w_down,
    gain_attn,
    gain_ffn,
    teacher,
    seq_lengths,
    tok_perm,
    valid_count,
):
    f32 = jnp.float32
    dp_count = lax.axis_size("dp")
    span, width = tokens.shape[1:]
    shard, ff = w_up.shape
    seq_len = tok_perm.shape[1]
    s = Sizes(span, width, ff, shard, w_down.shape[0], seq_len * dp_count)
    s.vmem = 63 * MIB
    gain_rows = jnp.pad(jnp.stack([gain_attn, gain_ffn]), ((0, 14), (0, width - shard)))
    ordered, loss, token_grad, qkv, out, up, down = layer(
        s,
        tokens[0],
        teacher[0],
        tok_perm,
        seq_lengths,
        valid_count,
        w_query,
        w_key,
        w_value,
        jnp.concatenate([w_out, gain_rows]),
        w_up,
        w_down,
    )
    return (
        ordered[None],
        loss,
        token_grad[None],
        qkv[:shard].astype(f32),
        qkv[shard : 2 * shard].astype(f32),
        qkv[2 * shard :].astype(f32),
        out[:shard].astype(f32),
        up.astype(f32),
        down.astype(f32),
        out[shard, :shard].astype(f32),
        out[shard + 1, :shard].astype(f32),
    )


def solution(mesh):
    in_specs = (
        P("dp", "ctx", None),
        P("dp", None),
        P("dp", None),
        P("dp", None),
        P("dp", None),
        P("dp", None),
        P("dp", None),
        P("dp"),
        P("dp"),
        P("dp", "ctx", None),
        P("dp"),
        P("dp", None),
        P(),
    )
    out_specs = (
        P("dp", "ctx", None),
        P(),
        P("dp", "ctx", None),
        P("dp", None),
        P("dp", None),
        P("dp", None),
        P("dp", None),
        P("dp", None),
        P("dp", None),
        P("dp"),
        P("dp"),
    )
    body = fused_shards if dict(mesh.shape) == {"dp": 16, "ctx": 2} else shards
    return jax.shard_map(body, mesh=mesh, in_specs=in_specs, out_specs=out_specs, check_vma=False)
```

```python
import functools
import math

import jax
import jax.numpy as jnp
from jax import lax
from jax.experimental import pallas as pl
from jax.experimental.pallas import tpu as pltpu
from jax.sharding import PartitionSpec as P

HEAD_DIM = 64


EPSILON = 1e-06
SCORE_SCALE = 0.125
MASKED = -1e30
MESH = pl.DeviceIdType.MESH
MIB = 1024 * 1024


GATHER_SPLIT = (0, 3, 5, 6, 7, 8, 10)
REDUCE_SPLIT = (1, 2, 7, 8, 9, 11)
EARLY = 11
FORWARD = ((0, 1, 2, 3, 4, 5, 6, 7, 8, 9, 10), (0,), (1, 2, 3, 4, 5, 6, 7, 8, 9, 10, 0, 1, 2, 3, 4, 5, 6, 7, 8, 9, 10, 0, 1, 2, 3, 4, 5, 6, 7, 8, 9, 0, 10, 1, 2, 1, 3, 2, 0, 4, 5, 0), (4, 6, 7, 8), (3, 9, 10), (3, 5), (9,), (5, 6), (6,), (7,), (7,), (), (), (8,), (), (), (), (8,), (), (), (), (10,), (), (), (), (10,), (), ())
BACKWARD = ((0, 1), (0, 2), (3,), (1, 4), (2, 5), (3, 0, 6), (4, 5, 1, 0, 6, 7), (2, 7, 4), (), (3, 0, 1, 5, 8), (), (8, 4, 6), (2,), (), (5,), (7,), (1, 9), (3, 6, 10), (2, 8, 4, 9, 5, 10, 11), (2, 6, 7, 8, 11, 12), (3, 9, 12), (), (11, 8, 10, 7, 9, 3, 10, 11, 12, 8, 9, 11, 12, 10, 9, 10, 12, 12))


def gelu_exact(values):
    return 0.5 * values * (1.0 + lax.erf(values * 0.7071067811865476))


def norm_forward(hidden, gain_row):
    center = hidden - jnp.mean(hidden, axis=-1, keepdims=True)
    inverse = lax.rsqrt(jnp.mean(center * center, axis=-1, keepdims=True) + EPSILON)
    normal = center * inverse
    return (normal * gain_row, normal, inverse)


def norm_backward(grad_norm, gain_row, normal, inverse):
    scaled = grad_norm * gain_row
    grad_input = inverse * (
        scaled
        - jnp.mean(scaled, axis=-1, keepdims=True)
        - normal * jnp.mean(scaled * normal, axis=-1, keepdims=True)
    )
    return (grad_input, jnp.sum(grad_norm * normal, axis=0))


def row_product(left_mat, right_mat):
    return lax.dot_general(
        left_mat, right_mat, (((0,), (0,)), ((), ())), preferred_element_type=jnp.float32
    )


def by_transpose(left_mat, right_mat):
    return lax.dot_general(
        left_mat, right_mat, (((1,), (1,)), ((), ())), preferred_element_type=jnp.float32
    )


def shards(
    tokens,
    w_query,
    w_key,
    w_value,
    w_out,
    w_up,
    w_down,
    gain_attn,
    gain_ffn,
    teacher,
    seq_lengths,
    tok_perm,
    valid_count,
):
    ctx_count = lax.axis_size("ctx")
    ctx_rank = lax.axis_index("ctx")
    dp_count = lax.axis_size("dp")
    layer_in = tokens[0]
    span_rows, model_width = layer_in.shape
    head_count = model_width // HEAD_DIM
    dealt_order = tok_perm[0]
    seq_len = dealt_order.shape[0]
    length = seq_lengths[0]
    keep_all = dealt_order < length
    per_peer = span_rows // ctx_count
    query_weight, key_weight, value_weight, out_weight, gain_first = (
        lax.all_gather(w_query, "dp", axis=0, tiled=True),
        lax.all_gather(w_key, "dp", axis=0, tiled=True),
        lax.all_gather(w_value, "dp", axis=0, tiled=True),
        lax.all_gather(w_out, "dp", axis=0, tiled=True),
        lax.all_gather(gain_attn, "dp", axis=0, tiled=True),
    )
    up_weight, down_weight, gain_second = (
        lax.all_gather(w_up, "dp", axis=0, tiled=True),
        lax.all_gather(w_down, "dp", axis=0, tiled=True),
        lax.all_gather(gain_ffn, "dp", axis=0, tiled=True),
    )
    queries = jnp.dot(layer_in, query_weight, preferred_element_type=jnp.float32).astype(
        jnp.bfloat16
    )
    keys_own = jnp.dot(layer_in, key_weight, preferred_element_type=jnp.float32).astype(
        jnp.bfloat16
    )
    values_own = jnp.dot(layer_in, value_weight, preferred_element_type=jnp.float32).astype(
        jnp.bfloat16
    )
    query_heads = queries.reshape(span_rows, head_count, HEAD_DIM)
    initial = (
        jnp.full((head_count, span_rows), MASKED, jnp.float32),
        jnp.zeros((head_count, span_rows), jnp.float32),
        jnp.zeros((head_count, span_rows, HEAD_DIM), jnp.float32),
    )
    fold_state = initial
    key_piece = lax.all_gather(keys_own, "ctx", axis=0, tiled=True)
    value_piece = lax.all_gather(values_own, "ctx", axis=0, tiled=True)
    piece_rows = key_piece.shape[0]
    block_rows = math.gcd(piece_rows, span_rows)
    key_blocks = key_piece.reshape(piece_rows // block_rows, block_rows, head_count, HEAD_DIM)
    value_blocks = value_piece.reshape(piece_rows // block_rows, block_rows, head_count, HEAD_DIM)

    def step_block(block_state, block_item):
        running_max, running_sum, accumulated = block_state
        key_block, value_block, block_index = block_item
        key_keep = lax.dynamic_slice_in_dim(keep_all, block_index * block_rows, block_rows)
        scores = (
            jnp.einsum("qhe,khe->hqk", query_heads, key_block, preferred_element_type=jnp.float32)
            * SCORE_SCALE
        )
        scores = jnp.where(key_keep[None, None, :], scores, MASKED)
        new_max = jnp.maximum(running_max, jnp.max(scores, axis=-1))
        factor = jnp.exp(running_max - new_max)
        soft_weights = jnp.where(key_keep[None, None, :], jnp.exp(scores - new_max[..., None]), 0.0)
        running_sum = running_sum * factor + jnp.sum(soft_weights, axis=-1)
        accumulated = accumulated * factor[..., None] + jnp.einsum(
            "hqk,khe->hqe",
            soft_weights.astype(jnp.bfloat16),
            value_block,
            preferred_element_type=jnp.float32,
        )
        return ((new_max, running_sum, accumulated), None)

    block_indices = jnp.arange(piece_rows // block_rows, dtype=jnp.int32)
    fold_state, unused = lax.scan(step_block, fold_state, (key_blocks, value_blocks, block_indices))
    run_max, run_sum, accumulated = fold_state
    log_total = run_max + jnp.log(run_sum)
    attn_full = jnp.transpose(accumulated / run_sum[..., None], (1, 0, 2)).reshape(
        span_rows, model_width
    )
    attn_low = attn_full.astype(jnp.bfloat16)
    gain_first32 = gain_first.astype(jnp.float32)
    gain_second32 = gain_second.astype(jnp.float32)
    branch = jnp.dot(attn_low, out_weight, preferred_element_type=jnp.float32)
    normed, normal_first, inverse_first = norm_forward(
        layer_in.astype(jnp.float32) + branch, gain_first32
    )
    normed_low = normed.astype(jnp.bfloat16)
    upward = jnp.dot(normed_low, up_weight, preferred_element_type=jnp.float32)
    active, gelu_pull = jax.vjp(gelu_exact, upward)
    active_low = active.astype(jnp.bfloat16)
    down_out = jnp.dot(active_low, down_weight, preferred_element_type=jnp.float32)
    result, normal_second, inverse_second = norm_forward(normed + down_out, gain_second32)
    result_low = result.astype(jnp.bfloat16)
    arrived = lax.all_to_all(result_low, "ctx", split_axis=0, concat_axis=0, tiled=True)
    sources = (
        jnp.arange(ctx_count, dtype=jnp.int32)[:, None] * span_rows
        + ctx_rank * per_peer
        + jnp.arange(per_peer, dtype=jnp.int32)[None, :]
    ).reshape(span_rows)
    local_pos = jnp.take(dealt_order, sources) - ctx_rank * span_rows
    in_order = jnp.zeros_like(arrived).at[local_pos].set(arrived)
    target = teacher[0].astype(jnp.float32)
    live_rows = (ctx_rank * span_rows + jnp.arange(span_rows, dtype=jnp.int32) < length)[:, None]
    residual_err = jnp.where(live_rows, in_order.astype(jnp.float32) - target, 0.0)
    total_sq = lax.psum(jnp.sum(residual_err * residual_err), ("dp", "ctx"))
    valid_total = valid_count[0].astype(jnp.float32)
    loss_value = (total_sq / (2.0 * model_width * valid_total)).reshape(1)
    grad_scale = seq_len * dp_count / valid_total
    grad_order = (residual_err * grad_scale).astype(jnp.bfloat16)
    outgoing = jnp.take(grad_order, local_pos, axis=0)
    grad_result = lax.all_to_all(outgoing, "ctx", split_axis=0, concat_axis=0, tiled=True).astype(
        jnp.float32
    )
    grad_sum_second, grad_gain_second = norm_backward(
        grad_result, gain_second32, normal_second, inverse_second
    )
    down_grad_low = grad_sum_second.astype(jnp.bfloat16)
    grad_down_w = row_product(active_low, down_grad_low)
    grad_active = by_transpose(down_grad_low, down_weight)
    grad_upward = gelu_pull(grad_active)[0].astype(jnp.bfloat16)
    grad_up_w = row_product(normed_low, grad_upward)
    grad_normed = grad_sum_second + by_transpose(grad_upward, up_weight)
    grad_hidden, grad_gain_first = norm_backward(
        grad_normed, gain_first32, normal_first, inverse_first
    )
    branch_grad = grad_hidden.astype(jnp.bfloat16)
    grad_out_w = row_product(attn_low, branch_grad)
    attn_grad_low = by_transpose(branch_grad, out_weight).astype(jnp.bfloat16)
    grad_heads = attn_grad_low.reshape(span_rows, head_count, HEAD_DIM)
    row_delta = jnp.sum(
        (attn_grad_low.astype(jnp.float32) * attn_full).reshape(span_rows, head_count, HEAD_DIM),
        axis=-1,
    ).T
    keys_all, values_all = (
        lax.all_gather(keys_own, "ctx", axis=0, tiled=True),
        lax.all_gather(values_own, "ctx", axis=0, tiled=True),
    )
    blocks_count = seq_len // span_rows
    key_stack = keys_all.reshape(blocks_count, span_rows, head_count, HEAD_DIM)
    value_stack = values_all.reshape(blocks_count, span_rows, head_count, HEAD_DIM)

    def score_terms(
        query_block, grad_block, total_block, delta_block, key_block, value_block, key_keep
    ):
        scores = (
            jnp.einsum("qhe,khe->hqk", query_block, key_block, preferred_element_type=jnp.float32)
            * SCORE_SCALE
        )
        soft_weights = jnp.where(
            key_keep[None, None, :], jnp.exp(scores - total_block[..., None]), 0.0
        )
        prob_grad = jnp.einsum(
            "qhe,khe->hqk", grad_block, value_block, preferred_element_type=jnp.float32
        )
        score_grad = (soft_weights * (prob_grad - delta_block[..., None])).astype(jnp.bfloat16)
        return (soft_weights, score_grad)

    def back_block(query_grad, block_item):
        key_block, value_block, block_index = block_item
        key_keep = lax.dynamic_slice_in_dim(keep_all, block_index * span_rows, span_rows)
        soft_weights, score_grad = score_terms(
            query_heads, grad_heads, log_total, row_delta, key_block, value_block, key_keep
        )
        value_grad = jnp.einsum(
            "hqk,qhe->khe",
            soft_weights.astype(jnp.bfloat16),
            grad_heads,
            preferred_element_type=jnp.float32,
        )
        query_grad = query_grad + SCORE_SCALE * jnp.einsum(
            "hqk,khe->qhe", score_grad, key_block, preferred_element_type=jnp.float32
        )
        key_grad = SCORE_SCALE * jnp.einsum(
            "hqk,qhe->khe", score_grad, query_heads, preferred_element_type=jnp.float32
        )
        return (query_grad, (key_grad, value_grad))

    query_grad, (key_grads, value_grads) = lax.scan(
        back_block,
        jnp.zeros((span_rows, head_count, HEAD_DIM), jnp.float32),
        (key_stack, value_stack, jnp.arange(blocks_count, dtype=jnp.int32)),
    )
    key_grad_sum, value_grad_sum = (
        lax.psum_scatter(
            key_grads.reshape(seq_len, model_width).astype(jnp.bfloat16),
            "ctx",
            scatter_dimension=0,
            tiled=True,
        ).astype(jnp.float32),
        lax.psum_scatter(
            value_grads.reshape(seq_len, model_width).astype(jnp.bfloat16),
            "ctx",
            scatter_dimension=0,
            tiled=True,
        ).astype(jnp.float32),
    )
    query_grad_low = query_grad.reshape(span_rows, model_width).astype(jnp.bfloat16)
    key_grad_low = key_grad_sum.astype(jnp.bfloat16)
    value_grad_low = value_grad_sum.astype(jnp.bfloat16)
    grad_query_w = row_product(layer_in, query_grad_low)
    grad_key_w = row_product(layer_in, key_grad_low)
    grad_value_w = row_product(layer_in, value_grad_low)
    token_grad = (
        grad_hidden
        + by_transpose(query_grad_low, query_weight)
        + by_transpose(key_grad_low, key_weight)
        + by_transpose(value_grad_low, value_weight)
    )
    up_part, down_part, second_part = (
        lax.psum_scatter(
            grad_up_w.astype(jnp.bfloat16), "dp", scatter_dimension=0, tiled=True
        ).astype(jnp.float32),
        lax.psum_scatter(
            grad_down_w.astype(jnp.bfloat16), "dp", scatter_dimension=0, tiled=True
        ).astype(jnp.float32),
        lax.psum_scatter(
            grad_gain_second.astype(jnp.bfloat16), "dp", scatter_dimension=0, tiled=True
        ).astype(jnp.float32),
    )
    query_part, key_part, value_part, out_part, first_part = (
        lax.psum_scatter(
            grad_query_w.astype(jnp.bfloat16), "dp", scatter_dimension=0, tiled=True
        ).astype(jnp.float32),
        lax.psum_scatter(
            grad_key_w.astype(jnp.bfloat16), "dp", scatter_dimension=0, tiled=True
        ).astype(jnp.float32),
        lax.psum_scatter(
            grad_value_w.astype(jnp.bfloat16), "dp", scatter_dimension=0, tiled=True
        ).astype(jnp.float32),
        lax.psum_scatter(
            grad_out_w.astype(jnp.bfloat16), "dp", scatter_dimension=0, tiled=True
        ).astype(jnp.float32),
        lax.psum_scatter(
            grad_gain_first.astype(jnp.bfloat16), "dp", scatter_dimension=0, tiled=True
        ).astype(jnp.float32),
    )
    summed = (
        lax.psum(query_part.astype(jnp.bfloat16), "ctx").astype(jnp.float32),
        lax.psum(key_part.astype(jnp.bfloat16), "ctx").astype(jnp.float32),
        lax.psum(value_part.astype(jnp.bfloat16), "ctx").astype(jnp.float32),
        lax.psum(out_part.astype(jnp.bfloat16), "ctx").astype(jnp.float32),
        lax.psum(up_part.astype(jnp.bfloat16), "ctx").astype(jnp.float32),
        lax.psum(down_part.astype(jnp.bfloat16), "ctx").astype(jnp.float32),
        lax.psum(first_part.astype(jnp.bfloat16), "ctx").astype(jnp.float32),
        lax.psum(second_part.astype(jnp.bfloat16), "ctx").astype(jnp.float32),
    )
    query_sum, key_sum, value_sum, out_sum, up_sum, down_sum, first_sum, second_sum = summed
    return (
        in_order[None],
        loss_value,
        token_grad[None],
        query_sum,
        key_sum,
        value_sum,
        out_sum,
        up_sum,
        down_sum,
        first_sum,
        second_sum,
    )


class Place:
    def __init__(self):
        dp = lax.axis_index("dp")
        self.x = lax.axis_index("ctx")
        self.z, self.y, self.c = dp // 4, (dp // 2) % 2, dp % 2
        self.xo, self.yo, self.co = 1 - self.x, 1 - self.y, 1 - self.c
        self.to_x = (dp, self.xo)
        self.to_y = (self.z * 4 + self.yo * 2 + self.c, self.x)
        self.to_c = (self.z * 4 + self.y * 2 + self.co, self.x)
        self.z_up = [(self.z + k) % 4 for k in range(4)]
        self.z_down = [(self.z + 4 - k) % 4 for k in range(4)]
        self.to_z = [(self.z_up[k] * 4 + self.y * 2 + self.c, self.x) for k in range(4)]
        z = self.z
        self.above = [(jnp.logical_and(z >= d, z < 3), z > d) for d in range(3)]
        self.below = [(jnp.logical_and(z <= 3 - d, z > 0), z < 3 - d) for d in range(3)]
        self.to_above, self.to_below = self.to_z[1], self.to_z[3]

    def barrier(self):
        semaphore = pltpu.get_barrier_semaphore()
        for partner in [self.to_x, self.to_y, self.to_c] + self.to_z[1:]:
            pl.semaphore_signal(semaphore, inc=1, device_id=partner, device_id_type=MESH)
        pl.semaphore_wait(semaphore, 6)


class Copy:
    def __init__(self, refs, send, at, recv, to, partner, when):
        self.refs, self.send, self.at, self.recv, self.to = refs, send, at, recv, to
        self.partner, self.when = partner, when

    def make(self):
        src, dst = self.refs()
        return pltpu.make_async_remote_copy(
            src_ref=src,
            dst_ref=dst,
            send_sem=self.send.at[self.at],
            recv_sem=self.recv.at[self.to],
            device_id=self.partner,
            device_id_type=MESH,
        )

    def only(self, side, action):
        if self.when is None:
            action()
        else:
            pl.when(self.when[side])(action)

    def start(self):
        self.only(0, lambda: self.make().start())

    def wait_send(self):
        self.only(0, lambda: self.make().wait_send())

    def wait_recv(self):
        self.only(1, lambda: self.make().wait_recv())


class Links:
    def __init__(self, send, recv):
        self.send, self.recv, self.used, self.flying = send, recv, 0, []
        self.free = list(range(send.shape[0]))

    def start(self, refs, partner, when=None):
        if not self.free:
            self.sent(self.flying[0][0])
        at = self.free.pop(0)
        copy = Copy(refs, self.send, at, self.recv, self.used, partner, when)
        self.used += 1
        copy.start()
        self.flying.append((copy, at))
        return copy

    def sent(self, copy):
        for entry in list(self.flying):
            if entry[0] is copy:
                copy.wait_send()
                self.free.append(entry[1])
        self.flying = [entry for entry in self.flying if entry[0] is not copy]

    def drain(self):
        for copy, at in list(self.flying):
            self.sent(copy)


class Gather:
    def __init__(self, block, early, shard, shift, whole, place, links, own_sem):
        first, last, self.split, self.col0, self.width = block
        self.early = early
        self.rows = pl.ds(first, last - first)
        self.shard, self.shift, self.whole = shard, shift, whole
        self.p, self.links = place, links
        self.own_sem = own_sem
        self.mine, self.theirs = self.half(place.x), self.half(place.xo)
        self.source = self.half(place.x, shift)
        self.last = 6 if self.split else 5

    def cols(self, shift=0):
        return pl.ds(self.col0 + shift, self.width)

    def half(self, x, shift=0):
        if not self.split:
            return self.cols(shift)
        size = self.width // 2
        return pl.ds(pl.multiple_of(self.col0 + shift + x * size, 128), size)

    def piece(self, z, y, cols):
        return self.whole.at[z, y, self.p.c, self.rows, cols]

    def own(self):
        p = self.p
        return pltpu.make_async_copy(
            self.shard.at[:, self.cols(self.shift)], self.piece(p.z, p.y, self.cols()), self.own_sem()
        )

    def push(self, z, y, cols, partner, when=None):
        return self.links.start(lambda: (self.piece(z, y, cols),) * 2, partner, when)

    def send_own(self, partner, when=None):
        p = self.p
        return self.links.start(
            lambda: (self.shard.at[:, self.source], self.piece(p.z, p.y, self.mine)), partner, when
        )

    def step0(self):
        p = self.p
        self.up, self.down = self.send_own(p.to_above, p.above[0]), self.send_own(p.to_below, p.below[0])
        self.own().start()
        self.from_x, self.from_y = [], []
        if self.early:
            self.from_y.append(self.send_own(p.to_y))

    def hop(self, d):
        p = self.p
        up, down = self.up, self.down
        up.wait_recv()
        if d < 2:
            self.up = self.push(p.z_down[d + 1], p.y, self.mine, p.to_above, p.above[d + 1])
        down.wait_recv()
        if d < 2:
            self.down = self.push(p.z_up[d + 1], p.y, self.mine, p.to_below, p.below[d + 1])
        for z, there in ((p.z_down[d + 1], p.above[d][1]), (p.z_up[d + 1], p.below[d][1])):
            when = (there, there)
            self.from_y.append(self.push(z, p.y, self.mine, p.to_y, when))
            if self.split:
                self.from_x.append(self.push(z, p.y, self.mine, p.to_x, when))

    def step1(self):
        if not self.early:
            self.from_y.append(self.send_own(self.p.to_y))
        self.hop(0)

    def step2(self):
        self.hop(1)

    def step3(self):
        self.hop(2)
        self.own().wait()
        self.from_c = [self.push(slice(None), self.p.y, self.mine, self.p.to_c)]

    def step4(self):
        p, every = self.p, slice(None)
        for copy in self.from_y:
            copy.wait_recv()
        if self.split:
            self.across = self.push(every, p.yo, self.mine, p.to_x)
        self.from_c.append(self.push(every, p.yo, self.mine, p.to_c))
        if self.split:
            for copy in self.from_x:
                copy.wait_recv()
            self.from_c.append(self.push(every, p.y, self.theirs, p.to_c))

    def step5(self):
        if self.split:
            self.across.wait_recv()
            self.from_c.append(self.push(slice(None), self.p.yo, self.theirs, self.p.to_c))
        else:
            self.step6()

    def step6(self):
        for copy in self.from_c:
            copy.wait_recv()


class Reduce:
    def __init__(self, block, at, grads, out, out0, shift, place, links, here, core_in, bufs):
        first, last, self.split, self.col0, self.width = block
        self.rows = last - first
        self.at0, self.here0, self.out0, self.shift = at, here, out0, shift
        self.at, self.here = pl.ds(at, self.rows), pl.ds(here, self.rows)
        self.grads, self.out = grads, out
        self.p, self.links = place, links
        self.core_in, self.bufs = core_in, bufs
        limit = 96 * 768 // self.width
        self.block = max(b for b in range(16, min(self.rows, limit) + 1, 16) if self.rows % b == 0)
        self.stage = 0
        self.mine, self.theirs = self.half(place.x), self.half(place.xo)
        self.out_mine = self.half(place.x, shift)
        self.last = 5 if self.split else 4

    def cols(self, shift=0):
        return pl.ds(self.col0 + shift, self.width)

    def half(self, x, shift=0):
        if not self.split:
            return self.cols(shift)
        size = self.width // 2
        return pl.ds(pl.multiple_of(self.col0 + shift + x * size, 128), size)

    def low(self):
        return pl.ds(self.col0, self.width // 2)

    def high(self):
        return pl.ds(self.col0 + self.width // 2, self.width // 2) if self.split else self.cols()

    def add(self, outer, target, source):
        steps = self.rows // self.block

        def body(i, carry):
            first = pl.multiple_of((i % steps) * self.block, 16)
            put = target(i // steps, pl.ds(self.at0 + first, self.block))
            given = source(i // steps, pl.ds(self.here0 + first, self.block))
            self.grads[put] = self.grads[put] + given
            return carry

        lax.fori_loop(0, outer * steps, body, 0)

    def step0(self):
        p = self.p
        self.by_core = self.links.start(
            lambda: (
                self.grads.at[:, :, p.co, self.at, self.cols()],
                self.core_in().at[:, :, self.here, self.cols()],
            ),
            p.to_c,
        )

    def add_core(self, y):
        p = self.p
        self.add(
            4,
            lambda i, rows: (i, y, p.c, rows, self.cols()),
            lambda i, rows: self.core_in()[i, y, rows, self.cols()],
        )

    def send_y(self):
        p = self.p
        self.by_y = self.links.start(
            lambda: (
                self.grads.at[:, p.yo, p.c, self.at, self.mine],
                self.bufs(0, slice(None)).at[:, self.here, self.high()],
            ),
            p.to_y,
        )

    def step1(self):
        p = self.p
        self.by_core.wait_recv()
        self.add_core(p.yo)
        if not self.split:
            self.send_y()
        self.add_core(p.y)
        if self.split:
            self.by_x = [self.send_x(0, p.yo), self.send_x(1, p.y)]

    def send_x(self, i, y):
        p = self.p
        return self.links.start(
            lambda: (
                self.grads.at[:, y, p.c, self.at, self.theirs],
                self.bufs(i, slice(None)).at[:, self.here, self.low()],
            ),
            p.to_x,
        )

    def add_x(self, i, y):
        p = self.p
        self.by_x[i].wait_recv()
        self.add(
            4,
            lambda j, rows: (j, y, p.c, rows, self.mine),
            lambda j, rows: self.bufs(i, j)[rows, self.low()],
        )

    def step2(self):
        if self.split:
            self.add_x(0, self.p.yo)
            self.send_y()
            self.add_x(1, self.p.y)
        else:
            self.reduce_y()

    def reduce_y(self):
        p = self.p
        self.by_y.wait_recv()
        self.add(
            4,
            lambda i, rows: (i, p.y, p.c, rows, self.mine),
            lambda i, rows: self.bufs(0, i)[rows, self.high()],
        )
        self.by_z = [self.send_z(k) for k in range(1, 4)]

    def send_z(self, k):
        p = self.p
        return self.links.start(
            lambda: (
                self.grads.at[p.z_up[k], p.y, p.c, self.at, self.mine],
                self.bufs(1, k - 1).at[self.here, self.high()],
            ),
            p.to_z[k],
        )

    def reduce_z(self, put):
        p = self.p
        for copy in self.by_z:
            copy.wait_recv()

        def body(i, carry):
            first = pl.multiple_of(i * self.block, 16)
            rows = pl.ds(self.here0 + first, self.block)
            place = (p.z, p.y, p.c, pl.ds(self.at0 + first, self.block), self.mine)
            total = self.grads[place].astype(jnp.float32)
            for k in range(3):
                total = total + self.bufs(1, k)[rows, self.high()].astype(jnp.float32)
            put(pl.ds(self.out0 + first, self.block), place, total.astype(jnp.bfloat16))
            return carry

        lax.fori_loop(0, self.rows // self.block, body, 0)

    def step3(self):
        p = self.p
        if self.split:
            self.reduce_y()
            return

        def put(rows, place, value):
            self.grads[place] = value

        self.reduce_z(put)
        self.by_x = self.links.start(
            lambda: (
                self.grads.at[p.z, p.y, p.c, self.at, self.cols()],
                self.bufs(1, 3).at[self.here, self.cols()],
            ),
            p.to_x,
        )

    def step4(self):
        p = self.p
        if self.split:

            def put(rows, place, value):
                self.out[rows, self.out_mine] = value

            self.reduce_z(put)
            self.by_x = self.links.start(
                lambda: (self.out.at[pl.ds(self.out0, self.rows), self.out_mine],) * 2, p.to_x
            )
            return
        self.by_x.wait_recv()

        def body(i, carry):
            first = pl.multiple_of(i * self.block, 16)
            rows = pl.ds(self.here0 + first, self.block)
            own = self.grads[p.z, p.y, p.c, pl.ds(self.at0 + first, self.block), self.cols()]
            self.out[pl.ds(self.out0 + first, self.block), self.cols(self.shift)] = (
                own.astype(jnp.float32) + self.bufs(1, 3)[rows, self.cols()].astype(jnp.float32)
            ).astype(jnp.bfloat16)
            return carry

        lax.fori_loop(0, self.rows // self.block, body, 0)

    def step5(self):
        self.by_x.wait_recv()

    def beat(self):
        getattr(self, "step" + str(self.stage))()
        self.stage += 1


class Total:
    last = 4

    def __init__(self, value, core_in, x_in, y_in, by_z, place, links):
        self.value, self.core_in, self.x_in, self.y_in, self.by_z = value, core_in, x_in, y_in, by_z
        self.p, self.links = place, links
        self.stage = 0

    def step0(self):
        self.copy = self.links.start(lambda: (self.value.at[0], self.core_in), self.p.to_c)

    def step1(self):
        self.copy.wait_recv()
        self.value[1] = self.value[0] + self.core_in[...]
        self.copy = self.links.start(lambda: (self.value.at[1], self.x_in), self.p.to_x)

    def step2(self):
        self.copy.wait_recv()
        self.value[2] = self.value[1] + self.x_in[...]
        self.copy = self.links.start(lambda: (self.value.at[2], self.y_in), self.p.to_y)

    def step3(self):
        self.copy.wait_recv()
        z = self.p.z
        self.by_z[z] = self.value[2] + self.y_in[...]
        self.spread = [
            self.links.start(lambda: (self.by_z.at[z],) * 2, self.p.to_z[k]) for k in range(1, 4)
        ]

    def step4(self):
        for copy in self.spread:
            copy.wait_recv()

    def sum(self):
        return ((self.by_z[0] + self.by_z[1]) + self.by_z[2]) + self.by_z[3]

    def beat(self):
        getattr(self, "step" + str(self.stage))()
        self.stage += 1


ROOT_HALF = 0.7071067811865476
DENSITY = 0.3989422804014327


def dot(left, right):
    return jnp.dot(left, right, preferred_element_type=jnp.float32)


def turned(left, right):
    return lax.dot_general(
        left, right, (((0,), (0,)), ((), ())), preferred_element_type=jnp.float32
    )


def by_turned(left, right):
    return lax.dot_general(
        left, right, (((1,), (1,)), ((), ())), preferred_element_type=jnp.float32
    )


def layer_kernel(s, *refs):
    tokens, teacher, order_row, length, valid = refs[:5]
    weights, (ordered_out, loss_out, token_out), outs = refs[5:11], refs[11:14], refs[14:18]
    refs = refs[8:]
    (W, G, tok, QKV, dO, stat, attn, n1, r1, low1, act, gp, acc, teach, res_in, low2, gains, sums) = refs[10:28]
    total_refs, (send, recv, local), (order_col, core_in, bufs) = refs[28:33], refs[33:36], refs[36:]
    qs, ks, vs = QKV.at[0], QKV.at[1], QKV.at[2]
    f32, bf16 = jnp.float32, jnp.bfloat16
    span, width, shard, downs = s.span, s.width, s.shard, s.downs
    pairs = width // 128
    third = width // 3
    place = Place()
    x, xo = place.x, place.xo
    links = Links(send, recv)

    def own(first, size):
        return pl.ds(pl.multiple_of(x * span + first, 16), size)

    def other(first, size):
        return pl.ds(pl.multiple_of(xo * span + first, 16), size)

    def loop(count, body):
        def step(i, carry):
            body(i)
            return carry

        lax.fori_loop(0, count, step, 0)

    def each(i, count, action):
        for k in range(count):
            pl.when(i == k)(lambda: action())

    def matrix(first):
        return W[:, :, :, pl.ds(pl.multiple_of(first, 16), shard), :].reshape(width, width)

    def semaphore(i):
        return local.at[i]

    gathers = [
        Gather(block, i < s.early, weights[j], shift, W, place, links, functools.partial(semaphore, i))
        for i, (block, (j, shift)) in enumerate(zip(s.gather_blocks, s.sources))
    ]
    n_gather = len(gathers)
    stages = [0] * n_gather
    forward = iter(s.forward)

    def advance():
        for i in next(forward):
            getattr(gathers[i], "step" + str(stages[i]))()
            stages[i] += 1

    def arrived(*blocks):
        advance()
        assert all(stages[i] > gathers[i].last for i in blocks)

    place.barrier()
    own_tokens = pltpu.make_async_copy(tokens, tok.at[own(0, span)], local.at[n_gather])
    own_tokens.start()
    own_teacher = pltpu.make_async_copy(teacher, gp.at[0], local.at[n_gather + 1])
    own_teacher.start()
    send_tokens = links.start(lambda: (tokens, tok.at[own(0, span)]), place.to_x)
    advance()
    order_col[...] = jnp.broadcast_to(order_row[...].astype(f32), (128, 2 * span)).T
    length_now = length[0]
    length_float = length_now.astype(f32)
    iota_rows = lax.broadcasted_iota(jnp.int32, (s.block, span), 1)

    def pick(c):
        rows = pl.ds(pl.multiple_of(c * span + x * s.block, 16), s.block)
        position = order_col[rows, :].astype(jnp.int32) - x * span
        chosen = iota_rows == jnp.concatenate([position] * (span // 128), axis=1)
        return jnp.where(chosen, 1.0, 0.0).astype(bf16)

    own_teacher.wait()
    for n in range(3):
        cols = slice(n * third, (n + 1) * third)
        low2[: s.block, cols] = dot(pick(xo), gp[0, :, cols]).astype(bf16)
        teach[x, :, cols] = dot(pick(x), gp[0, :, cols]).astype(bf16)
    advance()
    arrived(0, 1, 2)

    own_tokens.wait()

    def side(i):
        @pl.when(i == 1)
        def _():
            send_tokens.wait_recv()

        rows = pl.ds(pl.multiple_of(jnp.where(i == 0, x, xo) * span, 16), span)

        def project(j):
            scale = jnp.where(j == 0, SCORE_SCALE, 1.0)
            QKV[j, rows, :] = (dot(tok[rows, :], matrix(j * shard)) * scale).astype(bf16)

        loop(3, project)
        each(i, 2, advance)

    loop(2, side)

    lane = lax.broadcasted_iota(jnp.int32, (1, 128), 1)
    even32 = lane < HEAD_DIM
    even = jnp.where(even32, 1.0, 0.0).astype(bf16)
    odd = jnp.where(even32, 0.0, 1.0).astype(bf16)
    bias_row = jnp.where(order_row[0:1, :] < length_now, 0.0, MASKED)

    def attend(pair):
        lanes = pl.ds(pl.multiple_of(pair * 128, 128), 128)
        query, key, value = qs[own(0, span), lanes], ks[:, lanes], vs[:, lanes]
        tops, mixed = [], []
        for keep, rest in ((even, odd), (odd, even)):
            scores = by_turned(query * keep, key) + bias_row
            top = jnp.max(scores, axis=1, keepdims=True)
            weight = jnp.exp(scores - top).astype(bf16)
            tops.append(top)
            mixed.append(dot(weight, value * keep + rest))
        part = jnp.where(even32, mixed[0], mixed[1])
        total = pltpu.roll(jnp.where(even32, mixed[1], mixed[0]), HEAD_DIM, 1)
        attn[:, lanes] = (part / total).astype(bf16)
        log_rows = (jnp.where(even32, tops[0], tops[1]) + jnp.log(total)).T
        for h in range(2):
            stat[x, 0, pl.ds(2 * pair + h, 1), :] = log_rows[
                h * HEAD_DIM : h * HEAD_DIM + 1, :
            ]
        each(pair, pairs, advance)

    loop(pairs, attend)
    teach_copy = links.start(lambda: (low2.at[pl.ds(0, s.block)], teach.at[x]), place.to_x)

    arrived(3)
    device = lax.broadcasted_iota(jnp.int32, (16, width), 0)
    feature = lax.broadcasted_iota(jnp.int32, (16, width), 1)
    mine = (feature // shard) == device
    spread = jnp.where(
        lax.broadcasted_iota(jnp.int32, (128, width), 1) % shard
        == lax.broadcasted_iota(jnp.int32, (128, width), 0),
        1.0,
        0.0,
    ).astype(bf16)
    gain_rows = W[:, :, :, s.gain0 : s.gain0 + 16, :128].reshape(16, 16, 128).astype(f32)
    for g in range(2):
        wide = dot(gain_rows[:, g, :].astype(bf16), spread)
        gains[g : g + 1, :] = jnp.sum(jnp.where(mine, wide, 0.0), axis=0, keepdims=True)

    acc[...] = dot(attn[...], matrix(s.out0))
    advance()
    rows_n = s.rows_n

    def wide_column(column):
        return jnp.broadcast_to(column, (rows_n, 128))

    def first_norm(b):
        first = pl.multiple_of(b * rows_n, 16)
        rows = pl.ds(first, rows_n)
        hidden = tok[own(first, rows_n), :].astype(f32) + acc[rows, :]
        center = hidden - jnp.mean(hidden, axis=1, keepdims=True)
        inverse = lax.rsqrt(jnp.mean(center * center, axis=1, keepdims=True) + EPSILON)
        normal = center * inverse
        n1[rows, :] = normal
        r1[rows, :] = wide_column(inverse)
        low1[rows, :] = (normal * gains[0:1, :]).astype(bf16)

    loop(span // rows_n, first_norm)
    advance()


    def ahead(i, count):
        steps = iter(range(count))

        def action():
            if next(steps) > 0:
                advance()
            advance()

        each(i, count, action)

    def upward(p):
        ahead(p, s.panels)
        rows = pl.ds(pl.multiple_of(s.up0 + p * shard, 16), shard)
        for n in range(3):
            cols = slice(n * third, (n + 1) * third)
            value = dot(low1[...], W[:, :, :, rows, cols].reshape(width, third))
            cdf = 0.5 * (1.0 + lax.erf(value * ROOT_HALF))
            act[p, :, cols] = (value * cdf).astype(bf16)
            gp[p, :, cols] = (cdf + value * (jnp.exp(-0.5 * value * value) * DENSITY)).astype(bf16)

    def downward(n):
        ahead(n, 3)
        cols = pl.ds(pl.multiple_of(n * third, 128), third)
        value = None
        for p in range(s.panels):
            part = dot(act[p], W[p, :, :, s.down0 :, cols].reshape(width, third))
            value = part if value is None else value + part
        acc[:, cols] = value

    loop(s.panels, upward)
    advance()
    loop(3, downward)
    advance()
    assert all(stage > item.last for stage, item in zip(stages, gathers))

    teach_copy.wait_recv()
    links.sent(teach_copy)
    sums[...] = jnp.zeros_like(sums)
    valid_total = jnp.full((1, 1), valid[0], jnp.int32).astype(f32)
    grad_scale = s.tokens / valid_total

    def fold(values):
        return jnp.sum(values.reshape(rows_n // 8, 8, width), axis=0)

    def second_norm(b):
        first = pl.multiple_of(b * rows_n, 16)
        rows = pl.ds(first, rows_n)
        hidden = n1[rows, :] * gains[0:1, :] + acc[rows, :]
        center = hidden - jnp.mean(hidden, axis=1, keepdims=True)
        inverse = lax.rsqrt(jnp.mean(center * center, axis=1, keepdims=True) + EPSILON)
        normal = center * inverse
        gain = gains[1:2, :]
        result = (normal * gain).astype(bf16)
        per = s.block // rows_n
        at = pl.ds(pl.multiple_of((b % per) * rows_n, 16), rows_n)
        target = teach[b // per, at, :].astype(f32)
        teach[b // per, at, :] = result
        live = order_col[own(first, rows_n), 0:1] < length_float
        error = jnp.where(live, result.astype(f32) - target, 0.0)
        sums[2] += fold(error * error)
        grad = (error * grad_scale).astype(bf16).astype(f32)
        sums[1] += fold(grad * normal)
        scaled = grad * gain
        grad_sum = inverse * (
            scaled
            - jnp.mean(scaled, axis=1, keepdims=True)
            - normal * jnp.mean(scaled * normal, axis=1, keepdims=True)
        )
        acc[rows, :] = grad_sum
        low2[rows, :] = grad_sum.astype(bf16)

    loop(span // rows_n, second_norm)
    links.drain()
    send_result = links.start(lambda: (teach.at[xo], res_in), place.to_x)
    total_refs[0][0] = jnp.broadcast_to(
        jnp.sum(jnp.sum(sums[2], axis=0, keepdims=True), axis=1, keepdims=True), (8, 128)
    )
    total = Total(*total_refs, place, links)

    reduces = [total]
    backward = iter(s.backward)

    def beat():
        for i in next(backward):
            reduces[i].beat()

    def prepare(block, out, shift=0, in_weights=False):
        first = block[0]
        return Reduce(
            block,
            first + s.down0 if in_weights else first - s.out0,
            W if in_weights else G,
            outs[out],
            first if in_weights else 0,
            shift,
            place,
            links,
            first + s.up0 if in_weights else first - s.out0,
            (lambda: W.at[:, :, 0]) if in_weights else (lambda: core_in),
            (lambda h, j: W.at[j, h, 1]) if in_weights else (lambda h, j: bufs.at[h, j]),
        )

    coming = [prepare(block, 3) for block in s.down_blocks]
    coming += [prepare(block, 2, p * width) for p, block in enumerate(s.up_blocks)]
    coming += [prepare(s.out_block, 1)]
    coming += [prepare(block, 0, in_weights=True) for block in s.last_blocks]

    def enter():
        reduces.append(coming.pop(0))
        beat()

    def panel_grad(first, left, right):
        value = turned(left[...], right[...]).astype(bf16)
        at = pl.ds(pl.multiple_of(first - s.out0, 16), shard)
        G[:, :, :, at, :] = value.reshape(4, 2, 2, shard, width)

    def down_grad(n):
        cols = pl.ds(pl.multiple_of(n * third, 128), third)

        def panel(p):
            value = turned(act[p], low2[:, cols]).astype(bf16)
            G[p, :, :, s.down0 - s.out0 :, cols] = value.reshape(2, 2, downs, third)

        loop(s.panels, panel)
        each(n, 3, enter)

    def up_grad(p):
        value = by_turned(low2[...], W[p, :, :, s.down0 :, :].reshape(width, width))
        gp[p] = (value * gp[p].astype(f32)).astype(bf16)
        panel_grad(s.up0 + p * shard, low1, gp.at[p])
        each(p, s.panels, enter)

    def normed_grad(p):
        acc[...] += by_turned(gp[p], matrix(s.up0 + p * shard))

    loop(3, down_grad)
    loop(s.panels, up_grad)
    loop(s.panels, normed_grad)
    beat()

    def first_back(b):
        rows = pl.ds(pl.multiple_of(b * rows_n, 16), rows_n)
        grad, normal = acc[rows, :], n1[rows, :]
        sums[0] += fold(grad * normal)
        scaled = grad * gains[0:1, :]
        hidden_grad = r1[rows, 0:1] * (
            scaled
            - jnp.mean(scaled, axis=1, keepdims=True)
            - normal * jnp.mean(scaled * normal, axis=1, keepdims=True)
        )
        acc[rows, :] = hidden_grad
        low2[rows, :] = hidden_grad.astype(bf16)

    loop(span // rows_n, first_back)
    beat()

    dO[...] = by_turned(low2[...], matrix(s.out0)).astype(bf16)
    head = lax.broadcasted_iota(jnp.int32, (16, width), 0)
    in_head = jnp.where((feature // HEAD_DIM) == head, 1.0, 0.0)

    def head_delta(b):
        first = pl.multiple_of(b * 128, 128)
        rows = pl.ds(first, 128)
        product = dO[rows, :].astype(f32) * attn[rows, :].astype(f32)
        stat[x, 1, :, rows] = lax.dot_general(
            in_head,
            product,
            (((1,), (1,)), ((), ())),
            precision=lax.Precision.HIGHEST,
            preferred_element_type=f32,
        )

    loop(span // 128, head_delta)
    send_grad = links.start(lambda: (dO, tok.at[own(0, span)]), place.to_x)
    send_stat = links.start(lambda: (stat.at[x],) * 2, place.to_x)

    panel_grad(s.out0, attn, low2)
    pieces = []
    for g in range(2):
        row = jnp.sum(sums[g], axis=0, keepdims=True)
        split = jnp.where(mine, jnp.broadcast_to(row, (16, width)), 0.0).astype(bf16)
        pieces.append(by_turned(split, spread))
    at_row = lax.broadcasted_iota(jnp.int32, (16, 16, 128), 1)
    gain_block = jnp.where(
        at_row == 0, pieces[0][:, None, :], jnp.where(at_row == 1, pieces[1][:, None, :], 0.0)
    ).astype(bf16)
    G[:, :, :, shard : shard + 16, :128] = gain_block.reshape(4, 2, 2, 16, 128)
    G[:, :, :, shard : shard + 16, 128:] = jnp.zeros((4, 2, 2, 16, width - 128), bf16)
    enter()

    def block_terms(key, value, bias, query, grad, log_row, delta_row):
        scores = by_turned(key, query) + bias
        p = jnp.exp(scores - log_row)
        score_grad = (p * (by_turned(value, grad) - delta_row)).astype(bf16)
        return p.astype(bf16), score_grad

    def key_side(rows, lanes):
        column = jnp.where(order_col[rows, :] < length_float, 0.0, MASKED)
        return ks[rows, lanes], vs[rows, lanes], jnp.concatenate([column] * (span // 128), axis=1)

    def pair_lanes(pair):
        return pl.ds(pl.multiple_of(pair * 128, 128), 128)

    def terms(key, value, bias, side, pair, h, keep):
        lanes = pair_lanes(pair)
        rows = pl.ds(pl.multiple_of(side * span, 16), span)
        grad = dO[:, lanes] if side is x else tok[rows, lanes]
        query, grad = qs[rows, lanes] * keep, grad * keep
        at = pl.ds(2 * pair + h, 1)
        p, score_grad = block_terms(
            key, value, bias, query, grad, stat[side, 0, at, :], stat[side, 1, at, :]
        )
        return query, grad, p, score_grad

    def back_queries(pair):
        lanes = pair_lanes(pair)
        result = to_keys = to_values = None
        for rows, mine in ((own(0, span), True), (other(0, span), False)):
            key, value, bias = key_side(rows, lanes)
            for h, keep in enumerate((even, odd)):
                query, grad, p, score_grad = terms(key, value, bias, x, pair, h, keep)
                part = turned(score_grad, key * keep)
                result = part if result is None else result + part
                if mine:
                    value_part, key_part = dot(p, grad), dot(score_grad, query)
                    to_values = value_part if to_values is None else to_values + value_part
                    to_keys = key_part if to_keys is None else to_keys + key_part
        act[0, :, lanes] = (result * SCORE_SCALE).astype(bf16)
        n1[:, lanes] = to_keys
        gp[0, :, lanes] = to_values.astype(bf16)
        each(pair, pairs, beat)

    def back_keys(pair):
        lanes = pair_lanes(pair)
        key, value, bias = key_side(own(0, span), lanes)
        to_keys, to_values = n1[:, lanes], gp[0, :, lanes].astype(f32)
        for h, keep in enumerate((even, odd)):
            query, grad, p, score_grad = terms(key, value, bias, xo, pair, h, keep)
            to_values = to_values + dot(p, grad)
            to_keys = to_keys + dot(score_grad, query)
        act[1, :, lanes] = to_keys.astype(bf16)
        act[2, :, lanes] = to_values.astype(bf16)

    def weight_grad(j, columns):
        value = turned(tok[own(0, span), :], act[j, :, columns]).astype(bf16)
        at = pl.ds(pl.multiple_of(s.down0 + j * shard, 16), shard)
        W[:, :, :, at, columns] = value.reshape(4, 2, 2, shard, value.shape[1])

    def last_pairs(i):
        loop(2, lambda k: back_keys(2 * i + k))
        columns = pl.ds(pl.multiple_of(i * 256, 128), 256)
        loop(2, lambda j: weight_grad(j + 1, columns))
        each(i, pairs // 2, enter)

    loop(pairs, back_queries)
    weight_grad(0, slice(0, width))
    enter()
    send_grad.wait_recv()
    send_stat.wait_recv()
    loop(pairs // 2, last_pairs)

    def input_grad(j):
        acc[...] += by_turned(act[j], matrix(j * shard))

    loop(3, input_grad)
    token_copy = pltpu.make_async_copy(acc, token_out, local.at[n_gather])
    token_copy.start()
    beat()
    send_result.wait_recv()

    def place_rows(n):
        cols = pl.ds(pl.multiple_of(n * third, 128), third)
        value = None
        position = lax.broadcasted_iota(jnp.int32, (span, s.block), 0) + x * span
        for c, rows in ((x, teach[x, :, cols]), (xo, res_in[:, cols])):
            at = order_row[0:1, pl.ds(pl.multiple_of(c * span + x * s.block, 128), s.block)]
            chosen = jnp.where(position == at, 1.0, 0.0).astype(bf16)
            part = dot(chosen, rows)
            value = part if value is None else value + part
        low2[:, cols] = value.astype(bf16)

    loop(3, place_rows)
    ordered_copy = pltpu.make_async_copy(low2, ordered_out, local.at[n_gather + 1])
    ordered_copy.start()
    beat()
    beat()
    assert all(item.stage > item.last for item in reduces)
    loss_out[0] = jnp.max(total.sum() / (2.0 * width * valid_total))
    token_copy.wait()
    ordered_copy.wait()
    links.drain()


class Sizes:
    def __init__(self, span, width, ff, shard, downs, tokens):
        self.span, self.width, self.shard, self.downs, self.tokens = span, width, shard, downs, tokens
        self.panels = ff // width
        self.block = span // 2
        self.out0 = 3 * shard
        self.gain0 = 4 * shard
        self.up0 = self.gain0 + 16
        self.down0 = self.up0 + self.panels * shard
        self.rows = self.down0 + downs
        blocks = [(j * shard, (j + 1) * shard, 0, width) for j in range(3)]
        blocks += [(self.out0, self.up0, 0, width)]
        for p in range(self.panels):
            blocks += [(self.up0 + p * shard, self.up0 + (p + 1) * shard, 0, width)]
        third = width // 3
        blocks += [(self.down0, self.rows, n * third, third) for n in range(3)]
        self.gather_blocks = [b[:2] + (i in GATHER_SPLIT,) + b[2:] for i, b in enumerate(blocks)]
        self.sources = [(j, 0) for j in range(4)] + [(4, p * width) for p in range(self.panels)]
        self.sources += [(5, 0)] * 3
        self.early = EARLY
        back = blocks[-3:] + blocks[4:-3] + [blocks[3], blocks[0]]
        back += [(shard, self.out0, n * third, third) for n in range(3)]
        back = [b[:2] + (i in REDUCE_SPLIT,) + b[2:] for i, b in enumerate(back)]
        self.down_blocks, self.up_blocks = back[:3], back[3:-5]
        self.out_block, self.last_blocks = back[-5], back[-4:]
        self.forward, self.backward = FORWARD, BACKWARD
        self.rows_n, self.flying = 256, 128


def layer(s, *args):
    bf16, f32 = jnp.bfloat16, jnp.float32
    span, width = s.span, s.width
    both = 2 * span
    anywhere = pl.BlockSpec(memory_space=pl.ANY)
    vmem = pl.BlockSpec(memory_space=pltpu.VMEM)
    smem = pl.BlockSpec(memory_space=pltpu.SMEM)
    back = s.down_blocks + s.up_blocks + [s.out_block] + s.last_blocks
    copies = sum(24 if b[2] else 15 for b in s.gather_blocks)
    copies += sum(8 if b[2] else 6 for b in back) + 6 + 5
    small = pltpu.VMEM((8, 128), f32)
    scratch = [
        pltpu.VMEM((4, 2, 2, s.rows, width), bf16),
        pltpu.VMEM((4, 2, 2, s.rows - s.out0, width), bf16),
        pltpu.VMEM((both, width), bf16),
        pltpu.VMEM((3, both, width), bf16),
        pltpu.VMEM((span, width), bf16),
        pltpu.VMEM((2, 2, 16, span), f32),
        pltpu.VMEM((span, width), bf16),
        pltpu.VMEM((span, width), f32),
        pltpu.VMEM((span, 128), f32),
        pltpu.VMEM((span, width), bf16),
        pltpu.VMEM((s.panels, span, width), bf16),
        pltpu.VMEM((s.panels, span, width), bf16),
        pltpu.VMEM((span, width), f32),
        pltpu.VMEM((2, s.block, width), bf16),
        pltpu.VMEM((s.block, width), bf16),
        pltpu.VMEM((span, width), bf16),
        pltpu.VMEM((8, width), f32),
        pltpu.VMEM((3, 8, width), f32),
        pltpu.VMEM((3, 8, 128), f32),
        small,
        small,
        small,
        pltpu.VMEM((4, 8, 128), f32),
        pltpu.SemaphoreType.DMA((s.flying,)),
        pltpu.SemaphoreType.DMA((copies,)),
        pltpu.SemaphoreType.DMA((len(s.gather_blocks) + 2,)),
        pltpu.VMEM((both, 128), f32),
        pltpu.VMEM((4, 2, s.rows - s.out0, width), bf16),
        pltpu.VMEM((2, 4, s.rows - s.out0, width), bf16),
    ]
    return pl.pallas_call(
        functools.partial(layer_kernel, s),
        out_shape=[
            jax.ShapeDtypeStruct((span, width), bf16),
            jax.ShapeDtypeStruct((1,), f32),
            jax.ShapeDtypeStruct((span, width), f32),
            jax.ShapeDtypeStruct((s.out0, width), bf16),
            jax.ShapeDtypeStruct((s.up0 - s.out0, width), bf16),
            jax.ShapeDtypeStruct((s.shard, s.panels * width), bf16),
            jax.ShapeDtypeStruct((s.downs, width), bf16),
        ],
        in_specs=[anywhere, anywhere, vmem, smem, smem] + [anywhere] * 6,
        out_specs=[anywhere, smem, anywhere] + [vmem] * 4,
        scratch_shapes=scratch,
        compiler_params=pltpu.CompilerParams(
            collective_id=0, has_side_effects=True, vmem_limit_bytes=s.vmem
        ),
    )(*args)


def fused_shards(
    tokens,
    w_query,
    w_key,
    w_value,
    w_out,
    w_up,
    w_down,
    gain_attn,
    gain_ffn,
    teacher,
    seq_lengths,
    tok_perm,
    valid_count,
):
    f32 = jnp.float32
    dp_count = lax.axis_size("dp")
    span, width = tokens.shape[1:]
    shard, ff = w_up.shape
    seq_len = tok_perm.shape[1]
    s = Sizes(span, width, ff, shard, w_down.shape[0], seq_len * dp_count)
    s.vmem = 63 * MIB
    gain_rows = jnp.pad(jnp.stack([gain_attn, gain_ffn]), ((0, 14), (0, width - shard)))
    ordered, loss, token_grad, qkv, out, up, down = layer(
        s,
        tokens[0],
        teacher[0],
        tok_perm,
        seq_lengths,
        valid_count,
        w_query,
        w_key,
        w_value,
        jnp.concatenate([w_out, gain_rows]),
        w_up,
        w_down,
    )
    return (
        ordered[None],
        loss,
        token_grad[None],
        qkv[:shard].astype(f32),
        qkv[shard : 2 * shard].astype(f32),
        qkv[2 * shard :].astype(f32),
        out[:shard].astype(f32),
        up.astype(f32),
        down.astype(f32),
        out[shard, :shard].astype(f32),
        out[shard + 1, :shard].astype(f32),
    )


def solution(mesh):
    in_specs = (
        P("dp", "ctx", None),
        P("dp", None),
        P("dp", None),
        P("dp", None),
        P("dp", None),
        P("dp", None),
        P("dp", None),
        P("dp"),
        P("dp"),
        P("dp", "ctx", None),
        P("dp"),
        P("dp", None),
        P(),
    )
    out_specs = (
        P("dp", "ctx", None),
        P(),
        P("dp", "ctx", None),
        P("dp", None),
        P("dp", None),
        P("dp", None),
        P("dp", None),
        P("dp", None),
        P("dp", None),
        P("dp"),
        P("dp"),
    )
    body = fused_shards if dict(mesh.shape) == {"dp": 16, "ctx": 2} else shards
    return jax.shard_map(body, mesh=mesh, in_specs=in_specs, out_specs=out_specs, check_vma=False)
```
